32 devices in a mesh: ctx: 8 (over z, y), head: 4 (over x, core).
Axes of the slice: x: 2, y: 2, z: 4, core: 2. Of those that a mesh axis runs over, the one named last changes fastest.
Arguments:
- sec_q: bfloat16 [1024, 1536], P('ctx', 'head'), may hold values from -7 to 7
- sec_k: bfloat16 [1024, 1536], P('ctx', 'head'), may hold values from -6 to 6
- sec_v: bfloat16 [1024, 1536], P('ctx', 'head'), may hold values from -6 to 6
- hist_k: bfloat16 [256, 1536], P('ctx', 'head'), may hold values from -6 to 6
- hist_v: bfloat16 [256, 1536], P('ctx', 'head'), may hold values from -6 to 6
- frame_levels: int32 [8, 2], replicated, may hold values from 0 to 2, as said below
- frame_counts: int32 [8], replicated, may hold values from 1 to 2, as said below
- w_out: bfloat16 [1536, 3072], P('head'), may hold values from -0.15625 to 0.15625
- grad_out: bfloat16 [1024, 3072], P('ctx', 'head'), may hold values from -6 to 6
Outputs:
- out: bfloat16 [1024, 3072], P('ctx', 'head')
- grad_sec_q: bfloat16 [1024, 1536], P('ctx', 'head')
- grad_sec_k: bfloat16 [1024, 1536], P('ctx', 'head')
- grad_sec_v: bfloat16 [1024, 1536], P('ctx', 'head')
- grad_hist_k: bfloat16 [256, 1536], P('ctx', 'head')
- grad_hist_v: bfloat16 [256, 1536], P('ctx', 'head')
The draws below stay inside these ranges and needn't reach their ends.
Inputs may be any that keep to these rules, and one draw needn't show every extreme that they name: `frame_levels`: only the first frame_counts[o] levels of owner o count; the tokens of one owner never exceed 32, and in every draw some owner has exactly 32. `frame_counts`: in every draw some owner has 2 frames.
All inputs are finite; a program needn't handle non-finite values.
Results may differ from the reference program's by a relative error of at most 0.033.
Values may be sent and summed in bfloat16 or wider, within the bound.
No kernel may reach another device: no remote copies, remote signals or barrier semaphores. Data moves between devices by JAX's collectives and lax.ppermute only.
A program may use at most 192 MiB of HBM per device.

```python
import math
import jax
import jax.numpy as jnp
from jax import lax

D = 3072
HEADS = 12
HDIM = 128
FTOK = 16
FMAX = 2
HW = 1536
HCAP = 32
SEC = 1024
HIST = 256
N_CTX = 8


def shared_keys(key):
    return jax.random.truncated_normal(key, -6.0, 6.0, (SEC, HW), jnp.float32)


def draw_sec_q(key, part):
    key = jax.random.fold_in(key, 11)
    values_drawn = jax.random.truncated_normal(key, -6.0, 6.0, (SEC, HW), jnp.float32)
    return values_drawn.astype(jnp.bfloat16)


def draw_sec_k(key, part):
    shared = shared_keys(key)
    return shared.astype(jnp.bfloat16)


def frame_plan(key):
    key = jax.random.fold_in(key, 23)
    key_levels, key_counts, key_full = jax.random.split(key, 3)
    levels = jax.random.randint(key_levels, (N_CTX, FMAX), 0, 3)
    pick = jax.random.randint(key_counts, (N_CTX,), 0, 4)
    counts = jnp.where(pick > 0, FMAX, 1)
    full_owner = jax.random.randint(key_full, (), 0, N_CTX)
    is_full = jnp.arange(N_CTX) == full_owner
    levels = jnp.where(is_full[:, None], 0, levels)
    counts = jnp.where(is_full, FMAX, counts)
    return (levels.astype(jnp.int32), counts.astype(jnp.int32))


def draw_frame_levels(key, part):
    return frame_plan(key)[0]


def draw_frame_counts(key, part):
    return frame_plan(key)[1]


def block_levels(key, extent, cuts, low, high):
    def one(position, shards_of):
        heights = jax.random.uniform(jax.random.fold_in(jax.random.fold_in(key, 6), position), (shards_of,), jnp.float32, low / len(cuts), high / len(cuts))
        return jnp.repeat(jnp.exp(heights), extent[position] // shards_of).reshape((-1,) + (1,) * (len(extent) - position - 1))

    level = one(*cuts[0])
    for cut in cuts[1:]:
        level = level * one(*cut)
    return level


def centred(own_key, extent, deviation, bound, cuts=(), held_as=jnp.bfloat16):
    loudness = block_levels(own_key, extent, cuts, -0.22, 0.18) if cuts else 1.0
    result = jax.random.normal(own_key, extent, jnp.float32) * deviation * loudness
    return jnp.minimum(jnp.maximum(result, -bound), bound).astype(held_as)


def setup_inputs(seed: int = 0) -> dict:
    key_of = jax.random.split(jax.random.key(seed), 10)
    return {
        "sec_q": draw_sec_q(jax.random.fold_in(key_of[9], 71), 0),
        "sec_k": draw_sec_k(jax.random.fold_in(key_of[9], 71), 0),
        "sec_v": centred(key_of[2], (SEC, HW), 1.0, 6.0, ((0, 8), (1, 4))),
        "hist_k": centred(key_of[3], (HIST, HW), 1.0, 6.0, ((0, 8), (1, 4))),
        "hist_v": centred(key_of[4], (HIST, HW), 1.0, 6.0, ((0, 8), (1, 4))),
        "frame_levels": draw_frame_levels(jax.random.fold_in(key_of[9], 71), 0),
        "frame_counts": draw_frame_counts(jax.random.fold_in(key_of[9], 71), 0),
        "w_out": centred(key_of[7], (HW, D), HW ** -0.5, 0.15625, ((0, 4),)),
        "grad_out": centred(key_of[8], (SEC, D), 1.0, 6.0, ((0, 8), (1, 4))),
    }


NEG_FILL = -1e+30

def owner_token_counts(frame_levels, frame_counts):
    frame_index = jnp.arange(FMAX, dtype=jnp.int32)[None, :]
    per_frame = jnp.where(frame_index < frame_counts[:, None], jnp.right_shift(jnp.int32(FTOK), 2 * frame_levels), 0)
    return lax.optimization_barrier(jnp.sum(per_frame, axis=1)).astype(jnp.int32)

def reference(sec_q, sec_k, sec_v, hist_k, hist_v, frame_levels, frame_counts, w_out, grad_out):
    score_scale = 1.0 / math.sqrt(HDIM)
    owner_tokens = owner_token_counts(frame_levels, frame_counts)
    hist_valid = (jnp.arange(HCAP, dtype=jnp.int32)[None, :] < owner_tokens[:, None]).reshape(HIST)
    key_valid = jnp.concatenate([jnp.ones((SEC,), dtype=bool), hist_valid])
    all_keys = jnp.concatenate([sec_k, hist_k], axis=0)
    all_values = jnp.concatenate([sec_v, hist_v], axis=0)
    d_attn = lax.dot_general(grad_out, w_out, (((1,), (1,)), ((), ())), preferred_element_type=jnp.float32).astype(jnp.bfloat16)
    block_rows = min(512, SEC)
    block_count = SEC // block_rows

    def by_head(stacked):
        return stacked.reshape(stacked.shape[0], HEADS, HDIM).transpose(1, 0, 2)

    def one_head(operands):
        query_h, key_h, value_h, dattn_h = operands

        def block_step(carry_pair, block_pair):
            grad_key, grad_value = carry_pair
            query_b, dattn_b = block_pair
            scores = jnp.dot(query_b, key_h.T, preferred_element_type=jnp.float32) * score_scale
            scores = jnp.where(key_valid[None, :], scores, NEG_FILL)
            row_top = lax.optimization_barrier(jnp.max(scores, axis=1, keepdims=True))
            log_total = row_top + jnp.log(lax.optimization_barrier(jnp.sum(jnp.exp(scores - row_top), axis=1, keepdims=True)))
            prob_b = jnp.where(key_valid[None, :], jnp.exp(scores - log_total), 0.0).astype(jnp.bfloat16)
            attn_b = jnp.dot(prob_b, value_h, preferred_element_type=jnp.float32).astype(jnp.bfloat16)
            row_delta = lax.optimization_barrier(jnp.sum(attn_b.astype(jnp.float32) * dattn_b.astype(jnp.float32), axis=1, keepdims=True))
            dprobs = jnp.dot(dattn_b, value_h.T, preferred_element_type=jnp.float32)
            dscores = (prob_b.astype(jnp.float32) * (dprobs - row_delta)).astype(jnp.bfloat16)
            grad_query = (jnp.dot(dscores, key_h, preferred_element_type=jnp.float32) * score_scale).astype(jnp.bfloat16)
            grad_key = grad_key + jnp.dot(dscores.T, query_b, preferred_element_type=jnp.float32)
            grad_value = grad_value + jnp.dot(prob_b.T, dattn_b, preferred_element_type=jnp.float32)
            return ((grad_key, grad_value), (attn_b, grad_query))
        zero_grads = jnp.zeros((SEC + HIST, HDIM), jnp.float32)
        query_blocks = query_h.reshape(block_count, block_rows, HDIM)
        dattn_blocks = dattn_h.reshape(block_count, block_rows, HDIM)
        sums_pair, outputs_pair = lax.scan(block_step, (zero_grads, zero_grads), (query_blocks, dattn_blocks))
        attn_full = outputs_pair[0].reshape(SEC, HDIM)
        grad_query_full = outputs_pair[1].reshape(SEC, HDIM)
        grad_key_full = (sums_pair[0] * score_scale).astype(jnp.bfloat16)
        grad_value_full = sums_pair[1].astype(jnp.bfloat16)
        return (attn_full, grad_query_full, grad_key_full, grad_value_full)
    results = lax.map(one_head, (by_head(sec_q), by_head(all_keys), by_head(all_values), by_head(d_attn)))

    def merged(stacked):
        return stacked.transpose(1, 0, 2).reshape(stacked.shape[1], HW)
    attn = merged(results[0])
    out = jnp.dot(attn, w_out, preferred_element_type=jnp.float32).astype(jnp.bfloat16)
    grad_sec_q = merged(results[1])
    grad_keys = merged(results[2])
    grad_values = merged(results[3])
    return (out, grad_sec_q, grad_keys[:SEC], grad_values[:SEC], grad_keys[SEC:], grad_values[SEC:])
```

```python
import math

import jax
import jax.numpy as jnp
from jax import lax
from jax.sharding import PartitionSpec as P

HDIM = 128
FTOK = 16
FMAX = 2
NEG_FILL = -1e30
AXES = ("ctx", "head")


def contract_rows(left_side, right_side):
    return lax.dot_general(
        left_side, right_side, (((0,), (0,)), ((), ())), preferred_element_type=jnp.float32
    )


def contract_cols(left_side, right_side):
    return lax.dot_general(
        left_side, right_side, (((1,), (1,)), ((), ())), preferred_element_type=jnp.float32
    )


def head_slice(stacked, head_idx):
    return stacked[:, head_idx * HDIM : (head_idx + 1) * HDIM]


def owner_token_counts(frame_levels, frame_counts):
    frame_index = jnp.arange(FMAX, dtype=jnp.int32)[None, :]
    per_frame = jnp.where(
        frame_index < frame_counts[:, None], jnp.right_shift(jnp.int32(FTOK), 2 * frame_levels), 0
    )
    return jnp.sum(per_frame, axis=1)


def from_ahead(block, axis, step):
    count = lax.axis_size(axis)
    return lax.ppermute(block, axis, [((i + step) % count, i) for i in range(count)])


def gather_direct(block, axis, dim):
    count = lax.axis_size(axis)
    parts = [block] + [from_ahead(block, axis, step) for step in range(1, count)]
    doubled = jnp.concatenate(parts + parts[:-1], axis=dim)
    size = block.shape[dim]
    first = lax.rem(count - lax.axis_index(axis), count)
    return lax.dynamic_slice_in_dim(doubled, first * size, count * size, dim)


def reduce_direct(partial, axis):
    count = lax.axis_size(axis)
    me = lax.axis_index(axis)
    size = partial.shape[1] // count
    total = None
    for step in range(count):
        share = lax.dynamic_slice_in_dim(partial, lax.rem(me + step, count) * size, size, 1)
        if step:
            share = lax.ppermute(
                share.astype(jnp.bfloat16), axis, [(i, (i + step) % count) for i in range(count)]
            ).astype(jnp.float32)
        total = share if total is None else total + share
    return total


def shards(sec_q, sec_k, sec_v, hist_k, hist_v, frame_levels, frame_counts, w_out, grad_out):
    score_scale = 1.0 / math.sqrt(HDIM)
    rows = sec_q.shape[0]
    width = sec_q.shape[1]
    heads_here = width // HDIM
    capacity = hist_k.shape[0]
    owners = lax.axis_size("ctx")
    me = lax.axis_index("ctx")
    small = owners <= 8

    grad_full = gather_direct(grad_out, "head", 1)
    packed = jnp.concatenate([sec_q, sec_k, sec_v, hist_k, hist_v], axis=0)
    every = lax.all_gather(packed, "ctx", axis=0, tiled=False)
    all_queries = every[:, :rows].reshape(owners * rows, width)
    all_keys = every[:, rows : 2 * rows].reshape(owners * rows, width)
    all_values = every[:, 2 * rows : 3 * rows].reshape(owners * rows, width)
    all_hist_k = every[:, 3 * rows : 3 * rows + capacity].reshape(owners * capacity, width)
    all_hist_v = every[:, 3 * rows + capacity :].reshape(owners * capacity, width)
    all_keys = jnp.concatenate([all_keys, all_hist_k], axis=0)
    all_values = jnp.concatenate([all_values, all_hist_v], axis=0)
    d_attn = contract_cols(grad_full, w_out).astype(jnp.bfloat16)
    if small:
        all_dattn = gather_direct(d_attn, "ctx", 0)
    else:
        all_dattn = lax.all_gather(d_attn, "ctx", axis=0, tiled=True)

    owner_tokens = owner_token_counts(frame_levels, frame_counts)
    slot_index = jnp.arange(capacity, dtype=jnp.int32)
    hist_valid = (slot_index[None, :] < owner_tokens[:, None]).reshape(owners * capacity)
    key_valid = jnp.concatenate([jnp.ones((owners * rows,), dtype=bool), hist_valid])
    own_count = jnp.sum(jnp.where(jnp.arange(owners, dtype=jnp.int32) == me, owner_tokens, 0))
    own_valid = jnp.concatenate([jnp.ones((rows,), dtype=bool), slot_index < own_count])
    own_keys = jnp.concatenate([sec_k, hist_k], axis=0)
    own_values = jnp.concatenate([sec_v, hist_v], axis=0)

    def totals(query, key, value, dattn):
        scores = contract_cols(query, key) * score_scale
        scores = jnp.where(key_valid[None, :], scores, NEG_FILL)
        top = jnp.max(scores, axis=1, keepdims=True)
        weights = jnp.exp(scores - top)
        total = jnp.sum(weights, axis=1, keepdims=True)
        dprobs = contract_cols(dattn, value)
        delta = jnp.sum(weights * dprobs, axis=1, keepdims=True) / total
        return top + jnp.log(total), delta

    attn_parts, grad_q_parts, key_parts, value_parts = [], [], [], []
    for head in range(heads_here):
        query, key, value, dattn = (
            head_slice(a, head) for a in (all_queries, all_keys, all_values, all_dattn)
        )
        if small:
            lse, delta = totals(query, key, value, dattn)
        else:
            own = totals(head_slice(sec_q, head), key, value, head_slice(d_attn, head))
            lse, delta = (lax.all_gather(a, "ctx", axis=0, tiled=True) for a in own)
        my_lse = lax.dynamic_slice_in_dim(lse, me * rows, rows, 0)
        my_delta = lax.dynamic_slice_in_dim(delta, me * rows, rows, 0)

        def probs_and_dscores(q, k, v, d, valid, lse, delta):
            scores = contract_cols(q, k) * score_scale
            probs = jnp.where(valid[None, :], jnp.exp(scores - lse), 0.0).astype(jnp.bfloat16)
            dprobs = contract_cols(d, v)
            return probs, (probs.astype(jnp.float32) * (dprobs - delta)).astype(jnp.bfloat16)

        probs, dscores = probs_and_dscores(
            head_slice(sec_q, head), key, value, head_slice(d_attn, head), key_valid, my_lse, my_delta
        )
        attn_parts.append(jnp.dot(probs, value, preferred_element_type=jnp.float32))
        grad_q_parts.append(jnp.dot(dscores, key, preferred_element_type=jnp.float32))
        probs, dscores = probs_and_dscores(
            query, head_slice(own_keys, head), head_slice(own_values, head), dattn, own_valid, lse, delta
        )
        key_parts.append(contract_rows(dscores, query))
        value_parts.append(contract_rows(probs, dattn))

    attn = jnp.concatenate(attn_parts, axis=1).astype(jnp.bfloat16)
    partial_out = jnp.dot(attn, w_out, preferred_element_type=jnp.float32)
    out = reduce_direct(partial_out, "head").astype(jnp.bfloat16)
    grad_q = (jnp.concatenate(grad_q_parts, axis=1) * score_scale).astype(jnp.bfloat16)
    grad_keys = (jnp.concatenate(key_parts, axis=1) * score_scale).astype(jnp.bfloat16)
    grad_values = jnp.concatenate(value_parts, axis=1).astype(jnp.bfloat16)
    return (
        out,
        grad_q,
        grad_keys[:rows],
        grad_values[:rows],
        grad_keys[rows:],
        grad_values[rows:],
    )


def solution(mesh):
    split = P("ctx", "head")
    return jax.shard_map(
        shards,
        mesh=mesh,
        in_specs=(split,) * 5 + (P(), P(), P("head", None), split),
        out_specs=(split,) * 6,
        check_vma=False,
    )
```

```python
import functools
import math

import jax
import jax.numpy as jnp
from jax import lax
from jax.experimental import pallas as pl
from jax.experimental.pallas import tpu as pltpu
from jax.sharding import PartitionSpec as P

HDIM = 128
FTOK = 16
FMAX = 2
NEG_FILL = -1e30
SCALE = 1.0 / math.sqrt(HDIM)
F32 = jnp.float32
BF16 = jnp.bfloat16
SQUARE = 4
PAIR = 4


def contract(left, right, left_dim, right_dim):
    return lax.dot_general(
        left, right, (((left_dim,), (right_dim,)), ((), ())), preferred_element_type=F32
    )


def head_slice(stacked, head):
    return stacked[:, head * HDIM : (head + 1) * HDIM]


def swap(block, axis, bit):
    count = lax.axis_size(axis)
    return lax.ppermute(block, axis, [(i, i ^ bit) for i in range(count)])


def local_call(body, name, out_shapes, args, tables=0, flops=0):
    spaces = [pltpu.SMEM] * tables + [pltpu.VMEM] * (len(args) - tables)
    moved = sum(a.size * a.dtype.itemsize for a in args)
    moved += sum(math.prod(o.shape) * o.dtype.itemsize for o in out_shapes)
    return pl.pallas_call(
        body,
        name=name,
        out_shape=out_shapes,
        in_specs=[pl.BlockSpec(memory_space=space) for space in spaces],
        out_specs=[pl.BlockSpec(memory_space=pltpu.VMEM)] * len(out_shapes),
        compiler_params=pltpu.CompilerParams(vmem_limit_bytes=40 * 2**20),
        cost_estimate=pl.CostEstimate(flops=flops, bytes_accessed=moved, transcendentals=0),
    )(*args)


def owner_tokens_at(levels_ref, counts_ref, owner):
    total = jnp.int32(0)
    for frame in range(FMAX):
        tokens = lax.shift_right_logical(jnp.int32(FTOK), 2 * levels_ref[owner, frame])
        total += jnp.where(frame < counts_ref[owner], tokens, 0)
    return total


def square_tokens(levels_ref, counts_ref):
    me = lax.axis_index("ctx")
    return [owner_tokens_at(levels_ref, counts_ref, me ^ step) for step in range(SQUARE)]


def pack_kernel(k_ref, hk_ref, v_ref, hv_ref, kv_ref):
    rows, capacity = k_ref.shape[0], hk_ref.shape[0]
    keys = rows + capacity
    kv_ref[:rows] = k_ref[...]
    kv_ref[rows:keys] = hk_ref[...]
    kv_ref[keys : keys + rows] = v_ref[...]
    kv_ref[keys + rows :] = hv_ref[...]


def dattn_kernel(own_ref, core_ref, near_ref, far_ref, w_ref, out_ref):
    me = lax.axis_index("head")
    size = own_ref.shape[1]
    total = None
    for step, ref in enumerate((own_ref, core_ref, near_ref, far_ref)):
        columns = pl.ds(pl.multiple_of((me ^ step) * size, HDIM), size)
        part = contract(ref[...], w_ref[:, columns], 1, 1)
        total = part if total is None else total + part
    out_ref[...] = total.astype(BF16)


def masked_scores(kv_ref, head, query, tokens, rows, keys):
    scores = contract(head_slice(kv_ref[:keys], head), query, 1, 1) * SCALE
    slot = lax.broadcasted_iota(jnp.int32, scores.shape, 0)
    return jnp.where(slot < rows + tokens, scores, NEG_FILL)


def forward_kernel(
    levels_ref, counts_ref, q_own_ref, q_pair_ref, kv0, kv1, kv2, kv3, own_ref, pair_ref, lse_ref
):
    rows = q_own_ref.shape[0]
    keys = kv0.shape[0] // 2
    tokens = square_tokens(levels_ref, counts_ref)
    lse_ref[...] = jnp.zeros_like(lse_ref)
    for head in range(q_own_ref.shape[1] // HDIM):
        query = jnp.concatenate(
            [head_slice(q_own_ref[...], head), head_slice(q_pair_ref[...], head)], axis=0
        )
        scores = [
            masked_scores(ref, head, query, count, rows, keys)
            for ref, count in zip((kv0, kv1, kv2, kv3), tokens)
        ]
        top = functools.reduce(
            jnp.maximum, [jnp.max(block, axis=0, keepdims=True) for block in scores]
        )
        weights = [jnp.exp(block - top) for block in scores]
        total = sum(jnp.sum(block, axis=0, keepdims=True) for block in weights)
        inverse = 1.0 / total
        attn = sum(
            contract(head_slice(ref[keys:], head), (block * inverse).astype(BF16), 0, 0)
            for ref, block in zip((kv0, kv1, kv2, kv3), weights)
        )
        features = slice(head * HDIM, (head + 1) * HDIM)
        own_ref[features] = attn[:, :rows]
        pair_ref[features] = attn[:, rows:].astype(BF16)
        lse_ref[head : head + 1] = top + jnp.log(total)


def merge_parts(mine, theirs):
    top = jnp.maximum(mine, theirs)
    total = top + jnp.log(jnp.exp(mine - top) + jnp.exp(theirs - top))
    return total, jnp.exp(mine - total), jnp.exp(theirs - total)


def project_kernel(own_ref, pair_ref, lse_ref, lse_pair_ref, w_ref, send_ref, next_ref, keep_ref):
    rows = own_ref.shape[1]
    parts = []
    for head in range(own_ref.shape[0] // HDIM):
        features = slice(head * HDIM, (head + 1) * HDIM)
        _, weight, weight_pair = merge_parts(
            lse_ref[head : head + 1, :rows], lse_pair_ref[head : head + 1, rows:]
        )
        parts.append(own_ref[features] * weight + pair_ref[features].astype(F32) * weight_pair)
    attn = jnp.concatenate(parts, axis=0).astype(BF16)
    me = lax.axis_index("head")
    size = keep_ref.shape[1]

    def columns_of(step):
        columns = pl.ds(pl.multiple_of((me ^ step) * size, HDIM), size)
        return contract(attn, w_ref[:, columns], 0, 0)

    send_ref[:, :size] = columns_of(1).astype(BF16)
    send_ref[:, size:] = columns_of(3).astype(BF16)
    next_ref[...] = columns_of(2)
    keep_ref[...] = columns_of(0)


def add_near_kernel(next_ref, core_ref, out_ref):
    size = next_ref.shape[1]
    out_ref[...] = (next_ref[...] + core_ref[:, size:].astype(F32)).astype(BF16)


def add_out_kernel(keep_ref, core_ref, near_ref, out_ref):
    size = keep_ref.shape[1]
    total = keep_ref[...] + core_ref[:, :size].astype(F32) + near_ref[...].astype(F32)
    out_ref[...] = total.astype(BF16)


def delta_kernel(
    levels_ref, counts_ref, q_own_ref, q_pair_ref, kv0, kv1, kv2, kv3, d_own_ref, d_pair_ref, lse_ref,
    delta_ref,
):
    rows = q_own_ref.shape[0]
    keys = kv0.shape[0] // 2
    tokens = square_tokens(levels_ref, counts_ref)
    delta_ref[...] = jnp.zeros_like(delta_ref)
    for head in range(q_own_ref.shape[1] // HDIM):
        query, dattn = (
            jnp.concatenate([head_slice(a[...], head), head_slice(b[...], head)], axis=0)
            for a, b in ((q_own_ref, q_pair_ref), (d_own_ref, d_pair_ref))
        )
        total = None
        for ref, count in zip((kv0, kv1, kv2, kv3), tokens):
            scores = masked_scores(ref, head, query, count, rows, keys)
            probs = jnp.exp(scores - lse_ref[head : head + 1])
            dprobs = contract(head_slice(ref[keys:], head), dattn, 1, 1)
            part = jnp.sum(probs * dprobs, axis=0, keepdims=True)
            total = part if total is None else total + part
        delta_ref[head : head + 1] = total


def backward_kernel(
    levels_ref, counts_ref, q_own_ref, q_pair_ref, kv0, kv1, kv2, kv3, d_own_ref, d_pair_ref,
    lse_ref, lse_pair_ref, delta_ref, delta_pair_ref,
    dq_own_ref, dq_pair_ref, dkv0, dkv1, dkv2, dkv3,
):
    rows = q_own_ref.shape[0]
    keys = kv0.shape[0] // 2
    tokens = square_tokens(levels_ref, counts_ref)

    def swapped(ref, head):
        row = ref[head : head + 1]
        return jnp.concatenate([row[:, rows:], row[:, :rows]], axis=1)

    for head in range(q_own_ref.shape[1] // HDIM):
        query, dattn = (
            jnp.concatenate([head_slice(a[...], head), head_slice(b[...], head)], axis=0)
            for a, b in ((q_own_ref, q_pair_ref), (d_own_ref, d_pair_ref))
        )
        lse, weight, weight_pair = merge_parts(lse_ref[head : head + 1], swapped(lse_pair_ref, head))
        delta = weight * delta_ref[head : head + 1] + weight_pair * swapped(delta_pair_ref, head)
        features = slice(head * HDIM, (head + 1) * HDIM)
        dquery = None
        for ref, count, out in zip((kv0, kv1, kv2, kv3), tokens, (dkv0, dkv1, dkv2, dkv3)):
            key = head_slice(ref[:keys], head)
            scores = masked_scores(ref, head, query, count, rows, keys)
            probs = jnp.exp(scores - lse).astype(BF16)
            dprobs = contract(head_slice(ref[keys:], head), dattn, 1, 1)
            dscores = (probs.astype(F32) * (dprobs - delta)).astype(BF16)
            out[:keys, features] = (contract(dscores, query, 1, 0) * SCALE).astype(out.dtype)
            out[keys:, features] = contract(probs, dattn, 1, 0).astype(out.dtype)
            part = contract(dscores, key, 0, 0)
            dquery = part if dquery is None else dquery + part
        dq_own_ref[:, features] = dquery[:rows] * SCALE
        dq_pair_ref[:, features] = (dquery[rows:] * SCALE).astype(BF16)


def add_grads_kernel(
    dq_ref, dq_pair_ref, dkv0, dkv1, dkv2, dkv3, q_out, k_out, v_out, hk_out, hv_out
):
    rows, capacity = k_out.shape[0], hk_out.shape[0]
    keys = rows + capacity
    q_out[...] = (dq_ref[...] + dq_pair_ref[...].astype(F32)).astype(BF16)

    def total(begin, size):
        part = slice(begin, begin + size)
        value = dkv0[part]
        for ref in (dkv1, dkv2, dkv3):
            value = value + ref[part].astype(F32)
        return value.astype(BF16)

    k_out[...] = total(0, rows)
    hk_out[...] = total(rows, capacity)
    v_out[...] = total(keys, rows)
    hv_out[...] = total(keys + rows, capacity)


def blocked(sec_q, sec_k, sec_v, hist_k, hist_v, frame_levels, frame_counts, w_out, grad_out):
    shape = jax.ShapeDtypeStruct
    rows, width = sec_q.shape
    heads = width // HDIM
    capacity = hist_k.shape[0]
    keys = rows + capacity
    share = grad_out.shape[1]
    tables = (frame_levels, frame_counts)
    pair_work = 2 * SQUARE * keys * 2 * rows * width

    grad_near = swap(grad_out, "head", 2)
    grad_core = swap(grad_out, "head", 1)
    kv0 = local_call(
        pack_kernel, "pack", [shape((2 * keys, width), BF16)], (sec_k, hist_k, sec_v, hist_v)
    )[0]
    kvs = [kv0] + [swap(kv0, "ctx", step) for step in range(1, SQUARE)]
    q_pair = swap(sec_q, "ctx", PAIR)
    grad_far = swap(grad_near, "head", 1)
    d_attn = local_call(
        dattn_kernel,
        "dattn",
        [shape((rows, width), BF16)],
        (grad_out, grad_core, grad_near, grad_far, w_out),
        flops=2 * rows * width * share * 4,
    )[0]
    d_pair = swap(d_attn, "ctx", PAIR)
    attn_own, attn_pair, lse = local_call(
        forward_kernel,
        "forward",
        [shape((width, rows), F32), shape((width, rows), BF16), shape((8, 2 * rows), F32)],
        (*tables, sec_q, q_pair, *kvs),
        tables=2,
        flops=2 * pair_work,
    )
    lse_pair = swap(lse, "ctx", PAIR)
    attn_got = swap(attn_pair, "ctx", PAIR)
    out_send, out_next, out_keep = local_call(
        project_kernel,
        "project",
        [shape((rows, 2 * share), BF16), shape((rows, share), F32), shape((rows, share), F32)],
        (attn_own, attn_got, lse, lse_pair, w_out),
        flops=2 * rows * width * share * 4,
    )
    out_core = swap(out_send, "head", 1)
    out_near = swap(
        local_call(add_near_kernel, "add_near", [shape((rows, share), BF16)], (out_next, out_core))[0],
        "head",
        2,
    )
    delta = local_call(
        delta_kernel,
        "delta",
        [shape((8, 2 * rows), F32)],
        (*tables, sec_q, q_pair, *kvs, d_attn, d_pair, lse),
        tables=2,
        flops=2 * pair_work,
    )[0]
    delta_pair = swap(delta, "ctx", PAIR)
    dq_own, dq_pair, *dkvs = local_call(
        backward_kernel,
        "backward",
        [shape((rows, width), F32), shape((rows, width), BF16), shape((2 * keys, width), F32)]
        + [shape((2 * keys, width), BF16)] * 3,
        (*tables, sec_q, q_pair, *kvs, d_attn, d_pair, lse, lse_pair, delta, delta_pair),
        tables=2,
        flops=5 * pair_work,
    )
    dq_got = swap(dq_pair, "ctx", PAIR)
    dkv_got = [swap(dkvs[step], "ctx", step) for step in range(1, SQUARE)]
    grad_q, grad_k, grad_v, grad_hk, grad_hv = local_call(
        add_grads_kernel,
        "add_grads",
        [shape((rows, width), BF16)] * 3 + [shape((capacity, width), BF16)] * 2,
        (dq_own, dq_got, dkvs[0], *dkv_got),
    )
    out = local_call(
        add_out_kernel, "add_out", [shape((rows, share), BF16)], (out_keep, out_core, out_near)
    )[0]
    return out, grad_q, grad_k, grad_v, grad_hk, grad_hv


def gathered(sec_q, sec_k, sec_v, hist_k, hist_v, frame_levels, frame_counts, w_out, grad_out):
    rows = sec_q.shape[0]
    capacity = hist_k.shape[0]
    owners = lax.axis_size("ctx")
    me = lax.axis_index("ctx")
    frames = jnp.arange(FMAX, dtype=jnp.int32)[None, :]
    tokens = jnp.where(
        frames < frame_counts[:, None], jnp.right_shift(jnp.int32(FTOK), 2 * frame_levels), 0
    ).sum(axis=1)
    slots = jnp.arange(capacity, dtype=jnp.int32)
    all_valid = jnp.concatenate(
        [jnp.ones((owners * rows,), bool), (slots[None] < tokens[:, None]).reshape(-1)]
    )
    own_valid = jnp.concatenate(
        [jnp.ones((rows,), bool), slots < lax.dynamic_index_in_dim(tokens, me, keepdims=False)]
    )

    def everyone(block, axis=0):
        return lax.all_gather(block, "ctx", axis=axis, tiled=True)

    own_k, own_v = (jnp.concatenate(a, axis=0) for a in ((sec_k, hist_k), (sec_v, hist_v)))
    all_k = jnp.concatenate([everyone(sec_k), everyone(hist_k)], axis=0)
    all_v = jnp.concatenate([everyone(sec_v), everyone(hist_v)], axis=0)
    d_attn = contract(lax.all_gather(grad_out, "head", axis=1, tiled=True), w_out, 1, 1).astype(BF16)
    all_q, all_d = everyone(sec_q), everyone(d_attn)

    def probs_and_dscores(query, key, value, dattn, valid, lse, delta):
        scores = contract(query, key, 1, 1) * SCALE
        probs = jnp.where(valid[None, :], jnp.exp(scores - lse), 0.0).astype(BF16)
        dprobs = contract(dattn, value, 1, 1)
        return probs, (probs.astype(F32) * (dprobs - delta)).astype(BF16)

    attn_parts, q_parts, k_parts, v_parts = [], [], [], []
    for head in range(sec_q.shape[1] // HDIM):
        query, dattn, key, value = (head_slice(a, head) for a in (sec_q, d_attn, all_k, all_v))
        scores = jnp.where(all_valid[None, :], contract(query, key, 1, 1) * SCALE, NEG_FILL)
        lse = jax.nn.logsumexp(scores, axis=1, keepdims=True)
        probs = jnp.where(all_valid[None, :], jnp.exp(scores - lse), 0.0).astype(BF16)
        attn = contract(probs, value, 1, 0).astype(BF16)
        delta = jnp.sum(attn.astype(F32) * dattn.astype(F32), axis=1, keepdims=True)
        _, dscores = probs_and_dscores(query, key, value, dattn, all_valid, lse, delta)
        attn_parts.append(attn)
        q_parts.append(contract(dscores, key, 1, 0))
        query, dattn, key, value = (head_slice(a, head) for a in (all_q, all_d, own_k, own_v))
        probs, dscores = probs_and_dscores(
            query, key, value, dattn, own_valid, everyone(lse), everyone(delta)
        )
        k_parts.append(contract(dscores, query, 0, 0))
        v_parts.append(contract(probs, dattn, 0, 0))
    partial = contract(jnp.concatenate(attn_parts, axis=1), w_out, 1, 0).astype(BF16)
    out = lax.psum_scatter(partial, "head", scatter_dimension=1, tiled=True)
    grad_q, grad_k = (
        (jnp.concatenate(a, axis=1) * SCALE).astype(BF16) for a in (q_parts, k_parts)
    )
    grad_v = jnp.concatenate(v_parts, axis=1).astype(BF16)
    return out, grad_q, grad_k[:rows], grad_v[:rows], grad_k[rows:], grad_v[rows:]


def solution(mesh):
    split = P("ctx", "head")
    plan = blocked if (mesh.shape["ctx"], mesh.shape["head"]) == (2 * SQUARE, 4) else gathered
    return jax.shard_map(
        plan,
        mesh=mesh,
        in_specs=(split,) * 5 + (P(), P(), P("head", None), split),
        out_specs=(split,) * 6,
        check_vma=False,
    )
```

```python
import functools
import math

import jax
import jax.numpy as jnp
from jax import lax
from jax.experimental import pallas as pl
from jax.experimental.pallas import tpu as pltpu
from jax.sharding import PartitionSpec as P

HDIM = 128
FTOK = 16
FMAX = 2
NEG_FILL = -1e30
SCALE = 1.0 / math.sqrt(HDIM)
F32 = jnp.float32
BF16 = jnp.bfloat16
SQUARE = 4
PAIR = 4


def contract(left, right, left_dim, right_dim):
    return lax.dot_general(
        left, right, (((left_dim,), (right_dim,)), ((), ())), preferred_element_type=F32
    )


def head_slice(stacked, head):
    return stacked[:, head * HDIM : (head + 1) * HDIM]


def swap(block, axis, bit):
    count = lax.axis_size(axis)
    return lax.ppermute(block, axis, [(i, i ^ bit) for i in range(count)])


def local_call(body, name, out_shapes, args, tables=0, flops=0):
    spaces = [pltpu.SMEM] * tables + [pltpu.VMEM] * (len(args) - tables)
    moved = sum(a.size * a.dtype.itemsize for a in args)
    moved += sum(math.prod(o.shape) * o.dtype.itemsize for o in out_shapes)
    return pl.pallas_call(
        body,
        name=name,
        out_shape=out_shapes,
        in_specs=[pl.BlockSpec(memory_space=space) for space in spaces],
        out_specs=[pl.BlockSpec(memory_space=pltpu.VMEM)] * len(out_shapes),
        compiler_params=pltpu.CompilerParams(vmem_limit_bytes=40 * 2**20),
        cost_estimate=pl.CostEstimate(flops=flops, bytes_accessed=moved, transcendentals=0),
    )(*args)


def any_call(body, name, out_shapes, args, copies):
    moved = sum(a.size * a.dtype.itemsize for a in args)
    return pl.pallas_call(
        body,
        name=name,
        out_shape=out_shapes,
        in_specs=[pl.BlockSpec(memory_space=pl.ANY)] * len(args),
        out_specs=[pl.BlockSpec(memory_space=pl.ANY)] * len(out_shapes),
        scratch_shapes=[pltpu.SemaphoreType.DMA((copies,))],
        compiler_params=pltpu.CompilerParams(vmem_limit_bytes=60 * 2**20),
        cost_estimate=pl.CostEstimate(flops=0, bytes_accessed=2 * moved, transcendentals=0),
    )(*args)


def copy_all(pairs, sems):
    copies = [
        pltpu.make_async_copy(source, target, sems.at[i]) for i, (source, target) in enumerate(pairs)
    ]
    for copy in copies:
        copy.start()
    for copy in copies:
        copy.wait()


def load_kernel(k_ref, hk_ref, v_ref, hv_ref, kv_out, sems):
    rows, capacity = k_ref.shape[0], hk_ref.shape[0]
    keys = rows + capacity
    copy_all(
        [
            (k_ref, kv_out.at[pl.ds(0, rows)]),
            (v_ref, kv_out.at[pl.ds(keys, rows)]),
            (hk_ref, kv_out.at[pl.ds(rows, capacity)]),
            (hv_ref, kv_out.at[pl.ds(keys + rows, capacity)]),
        ],
        sems,
    )


def limits_kernel(levels_ref, counts_ref, limits_ref):
    me = lax.axis_index("ctx")
    row = lax.broadcasted_iota(jnp.int32, limits_ref.shape, 0)
    limits = jnp.zeros(limits_ref.shape, jnp.int32)
    for step in range(SQUARE):
        total = jnp.int32(0)
        for frame in range(FMAX):
            tokens = lax.shift_right_logical(jnp.int32(FTOK), 2 * levels_ref[me ^ step, frame])
            total += jnp.where(frame < counts_ref[me ^ step], tokens, 0)
        limits = jnp.where(row == step, total, limits)
    limits_ref[...] = limits


def dattn_kernel(own_ref, core_ref, near_ref, far_ref, w_ref, out_ref):
    me = lax.axis_index("head")
    size = own_ref.shape[1]
    total = None
    for step, ref in enumerate((own_ref, core_ref, near_ref, far_ref)):
        columns = pl.ds(pl.multiple_of((me ^ step) * size, HDIM), size)
        part = contract(ref[...], w_ref[:, columns], 1, 1)
        total = part if total is None else total + part
    out_ref[...] = total.astype(BF16)


def both_rows(own_ref, pair_ref, head):
    return jnp.concatenate(
        [head_slice(own_ref[...], head), head_slice(pair_ref[...], head)], axis=0
    )


def forward_kernel(
    limits_ref, q_own_ref, q_pair_ref, d_own_ref, d_pair_ref, kv0, kv1, kv2, kv3,
    stats_ref, own_ref, pair_ref, probs_ref, dprobs_ref,
):
    rows = q_own_ref.shape[0]
    keys = kv0.shape[0] // 2
    blocks = (kv0, kv1, kv2, kv3)
    stats_ref[...] = jnp.zeros_like(stats_ref)
    for head in range(q_own_ref.shape[1] // HDIM):
        query = both_rows(q_own_ref, q_pair_ref, head)
        dattn = both_rows(d_own_ref, d_pair_ref, head)
        scores = []
        for step, ref in enumerate(blocks):
            block = contract(head_slice(ref[:keys], head), query, 1, 1) * SCALE
            slot = lax.broadcasted_iota(jnp.int32, block.shape, 0)
            valid = slot < rows + limits_ref[step : step + 1]
            scores.append(jnp.where(valid, block, NEG_FILL))
        top = functools.reduce(
            jnp.maximum, [jnp.max(block, axis=0, keepdims=True) for block in scores]
        )
        weights = [jnp.exp(block - top) for block in scores]
        total = sum(jnp.sum(block, axis=0, keepdims=True) for block in weights)
        inverse = 1.0 / total
        attn, delta = None, None
        for step, ref in enumerate(blocks):
            value = head_slice(ref[keys:], head)
            probs = weights[step] * inverse
            dprobs = contract(value, dattn, 1, 1)
            part = contract(value, probs.astype(BF16), 0, 0)
            delta_part = jnp.sum(probs * dprobs, axis=0, keepdims=True)
            attn = part if attn is None else attn + part
            delta = delta_part if delta is None else delta + delta_part
            begin = (head * SQUARE + step) * keys
            probs_ref[begin : begin + keys] = probs.astype(probs_ref.dtype)
            dprobs_ref[begin : begin + keys] = dprobs
        features = slice(head * HDIM, (head + 1) * HDIM)
        own_ref[features] = attn[:, :rows]
        pair_ref[features] = attn[:, rows:].astype(BF16)
        stats_ref[head : head + 1] = top + jnp.log(total)
        stats_ref[8 + head : 9 + head] = delta


def merge_parts(mine, theirs):
    top = jnp.maximum(mine, theirs)
    weight, weight_pair = jnp.exp(mine - top), jnp.exp(theirs - top)
    inverse = 1.0 / (weight + weight_pair)
    return weight * inverse, weight_pair * inverse


def project_kernel(own_ref, pair_ref, stats_ref, stats_pair_ref, w_ref, send_ref, next_ref, keep_ref):
    rows = own_ref.shape[1]
    parts = []
    for head in range(own_ref.shape[0] // HDIM):
        features = slice(head * HDIM, (head + 1) * HDIM)
        weight, weight_pair = merge_parts(
            stats_ref[head : head + 1, :rows], stats_pair_ref[head : head + 1, rows:]
        )
        parts.append(own_ref[features] * weight + pair_ref[features].astype(F32) * weight_pair)
    attn = jnp.concatenate(parts, axis=0).astype(BF16)
    me = lax.axis_index("head")
    size = keep_ref.shape[1]

    def columns_of(step):
        columns = pl.ds(pl.multiple_of((me ^ step) * size, HDIM), size)
        return contract(attn, w_ref[:, columns], 0, 0)

    send_ref[:, :size] = columns_of(1).astype(BF16)
    send_ref[:, size:] = columns_of(3).astype(BF16)
    next_ref[...] = columns_of(2)
    keep_ref[...] = columns_of(0)


def add_near_kernel(next_ref, core_ref, out_ref):
    size = next_ref.shape[1]
    out_ref[...] = (next_ref[...] + core_ref[:, size:].astype(F32)).astype(BF16)


def add_out_kernel(keep_ref, core_ref, near_ref, out_ref):
    size = keep_ref.shape[1]
    total = keep_ref[...] + core_ref[:, :size].astype(F32) + near_ref[...].astype(F32)
    out_ref[...] = total.astype(BF16)


def backward_kernel(
    q_own_ref, q_pair_ref, d_own_ref, d_pair_ref, kv0, kv1, kv2, kv3,
    stats_ref, stats_pair_ref, probs_ref, dprobs_ref,
    dq_own_ref, dq_pair_ref, dkv0, dkv1, dkv2, dkv3,
):
    rows = q_own_ref.shape[0]
    keys = kv0.shape[0] // 2

    def swapped(row):
        return jnp.concatenate([row[:, rows:], row[:, :rows]], axis=1)

    for head in range(q_own_ref.shape[1] // HDIM):
        query = both_rows(q_own_ref, q_pair_ref, head)
        dattn = both_rows(d_own_ref, d_pair_ref, head)
        weight, weight_pair = merge_parts(
            stats_ref[head : head + 1], swapped(stats_pair_ref[head : head + 1])
        )
        delta = weight * stats_ref[8 + head : 9 + head]
        delta += weight_pair * swapped(stats_pair_ref[8 + head : 9 + head])
        features = slice(head * HDIM, (head + 1) * HDIM)
        dquery = None
        for step, (ref, out) in enumerate(zip((kv0, kv1, kv2, kv3), (dkv0, dkv1, dkv2, dkv3))):
            begin = (head * SQUARE + step) * keys
            probs = (probs_ref[begin : begin + keys].astype(F32) * weight).astype(BF16)
            dprobs = dprobs_ref[begin : begin + keys]
            dscores = (probs.astype(F32) * (dprobs - delta)).astype(BF16)
            out[:keys, features] = (contract(dscores, query, 1, 0) * SCALE).astype(out.dtype)
            out[keys:, features] = contract(probs, dattn, 1, 0).astype(out.dtype)
            part = contract(dscores, head_slice(ref[:keys], head), 0, 0)
            dquery = part if dquery is None else dquery + part
        dq_own_ref[:, features] = dquery[:rows] * SCALE
        dq_pair_ref[:, features] = (dquery[rows:] * SCALE).astype(BF16)


def add_grads_kernel(
    dq_ref, dq_pair_ref, dkv0, dkv1, dkv2, dkv3, q_out, k_out, v_out, hk_out, hv_out
):
    rows, capacity = k_out.shape[0], hk_out.shape[0]
    keys = rows + capacity
    q_out[...] = (dq_ref[...] + dq_pair_ref[...].astype(F32)).astype(BF16)

    def total(begin, size):
        part = slice(begin, begin + size)
        value = dkv0[part]
        for ref in (dkv1, dkv2, dkv3):
            value = value + ref[part].astype(F32)
        return value.astype(BF16)

    k_out[...] = total(0, rows)
    hk_out[...] = total(rows, capacity)
    v_out[...] = total(keys, rows)
    hv_out[...] = total(keys + rows, capacity)


def blocked(sec_q, sec_k, sec_v, hist_k, hist_v, frame_levels, frame_counts, w_out, grad_out):
    shape = jax.ShapeDtypeStruct
    rows, width = sec_q.shape
    heads = width // HDIM
    capacity = hist_k.shape[0]
    keys = rows + capacity
    share = grad_out.shape[1]
    work = 2 * SQUARE * keys * 2 * rows * width

    grad_core, grad_near, grad_far = (swap(grad_out, "head", step) for step in range(1, 4))
    kv0 = any_call(
        load_kernel, "load", [shape((2 * keys, width), BF16)], (sec_k, hist_k, sec_v, hist_v), copies=4
    )[0]
    kvs = [kv0] + [swap(kv0, "ctx", step) for step in range(1, SQUARE)]
    q_pair = swap(sec_q, "ctx", PAIR)
    d_own = local_call(
        dattn_kernel,
        "dattn",
        [shape((rows, width), BF16)],
        (grad_out, grad_core, grad_near, grad_far, w_out),
        flops=2 * rows * width * share * 4,
    )[0]
    d_pair = swap(d_own, "ctx", PAIR)
    limits = local_call(
        limits_kernel,
        "limits",
        [shape((8, 2 * rows), jnp.int32)],
        (frame_levels, frame_counts),
        tables=2,
    )[0]
    stats, attn_own, attn_pair, probs, dprobs = local_call(
        forward_kernel,
        "forward",
        [
            shape((16, 2 * rows), F32),
            shape((width, rows), F32),
            shape((width, rows), BF16),
            shape((heads * SQUARE * keys, 2 * rows), BF16),
            shape((heads * SQUARE * keys, 2 * rows), F32),
        ],
        (limits, sec_q, q_pair, d_own, d_pair, *kvs),
        flops=3 * work,
    )
    stats_pair = swap(stats, "ctx", PAIR)
    stats_pair, attn_pair = lax.optimization_barrier((stats_pair, attn_pair))
    attn_got = swap(attn_pair, "ctx", PAIR)
    dq_own, dq_pair, *dkvs = local_call(
        backward_kernel,
        "backward",
        [shape((rows, width), F32), shape((rows, width), BF16), shape((2 * keys, width), F32)]
        + [shape((2 * keys, width), BF16)] * 3,
        (sec_q, q_pair, d_own, d_pair, *kvs, stats, stats_pair, probs, dprobs),
        flops=3 * work,
    )
    dkv_got = [swap(dkvs[step], "ctx", step) for step in range(1, SQUARE)]
    dq_got = swap(dq_pair, "ctx", PAIR)
    attn_own, dq_own = lax.optimization_barrier((attn_own, dq_own))
    out_send, out_next, out_keep = local_call(
        project_kernel,
        "project",
        [shape((rows, 2 * share), BF16), shape((rows, share), F32), shape((rows, share), F32)],
        (attn_own, attn_got, stats, stats_pair, w_out),
        flops=2 * rows * width * share * 4,
    )
    out_core = swap(out_send, "head", 1)
    out_near = swap(
        local_call(add_near_kernel, "add_near", [shape((rows, share), BF16)], (out_next, out_core))[0],
        "head",
        2,
    )
    grad_q, grad_k, grad_v, grad_hk, grad_hv = local_call(
        add_grads_kernel,
        "add_grads",
        [shape((rows, width), BF16)] * 3 + [shape((capacity, width), BF16)] * 2,
        (dq_own, dq_got, dkvs[0], *dkv_got),
    )
    out = local_call(
        add_out_kernel, "add_out", [shape((rows, share), BF16)], (out_keep, out_core, out_near)
    )[0]
    grad_k, grad_v, grad_hk, grad_hv, grad_q, out = lax.optimization_barrier(
        (grad_k, grad_v, grad_hk, grad_hv, grad_q, out)
    )
    return out, grad_q, grad_k, grad_v, grad_hk, grad_hv


def gathered(sec_q, sec_k, sec_v, hist_k, hist_v, frame_levels, frame_counts, w_out, grad_out):
    rows = sec_q.shape[0]
    capacity = hist_k.shape[0]
    owners = lax.axis_size("ctx")
    me = lax.axis_index("ctx")
    frames = jnp.arange(FMAX, dtype=jnp.int32)[None, :]
    tokens = jnp.where(
        frames < frame_counts[:, None], jnp.right_shift(jnp.int32(FTOK), 2 * frame_levels), 0
    ).sum(axis=1)
    slots = jnp.arange(capacity, dtype=jnp.int32)
    all_valid = jnp.concatenate(
        [jnp.ones((owners * rows,), bool), (slots[None] < tokens[:, None]).reshape(-1)]
    )
    own_valid = jnp.concatenate(
        [jnp.ones((rows,), bool), slots < lax.dynamic_index_in_dim(tokens, me, keepdims=False)]
    )

    def everyone(block, axis=0):
        return lax.all_gather(block, "ctx", axis=axis, tiled=True)

    own_k, own_v = (jnp.concatenate(a, axis=0) for a in ((sec_k, hist_k), (sec_v, hist_v)))
    all_k = jnp.concatenate([everyone(sec_k), everyone(hist_k)], axis=0)
    all_v = jnp.concatenate([everyone(sec_v), everyone(hist_v)], axis=0)
    d_attn = contract(lax.all_gather(grad_out, "head", axis=1, tiled=True), w_out, 1, 1).astype(BF16)
    all_q, all_d = everyone(sec_q), everyone(d_attn)

    def probs_and_dscores(query, key, value, dattn, valid, lse, delta):
        scores = contract(query, key, 1, 1) * SCALE
        probs = jnp.where(valid[None, :], jnp.exp(scores - lse), 0.0).astype(BF16)
        dprobs = contract(dattn, value, 1, 1)
        return probs, (probs.astype(F32) * (dprobs - delta)).astype(BF16)

    attn_parts, q_parts, k_parts, v_parts = [], [], [], []
    for head in range(sec_q.shape[1] // HDIM):
        query, dattn, key, value = (head_slice(a, head) for a in (sec_q, d_attn, all_k, all_v))
        scores = jnp.where(all_valid[None, :], contract(query, key, 1, 1) * SCALE, NEG_FILL)
        lse = jax.nn.logsumexp(scores, axis=1, keepdims=True)
        probs = jnp.where(all_valid[None, :], jnp.exp(scores - lse), 0.0).astype(BF16)
        attn = contract(probs, value, 1, 0).astype(BF16)
        delta = jnp.sum(attn.astype(F32) * dattn.astype(F32), axis=1, keepdims=True)
        _, dscores = probs_and_dscores(query, key, value, dattn, all_valid, lse, delta)
        attn_parts.append(attn)
        q_parts.append(contract(dscores, key, 1, 0))
        query, dattn, key, value = (head_slice(a, head) for a in (all_q, all_d, own_k, own_v))
        probs, dscores = probs_and_dscores(
            query, key, value, dattn, own_valid, everyone(lse), everyone(delta)
        )
        k_parts.append(contract(dscores, query, 0, 0))
        v_parts.append(contract(probs, dattn, 0, 0))
    partial = contract(jnp.concatenate(attn_parts, axis=1), w_out, 1, 0).astype(BF16)
    out = lax.psum_scatter(partial, "head", scatter_dimension=1, tiled=True)
    grad_q, grad_k = (
        (jnp.concatenate(a, axis=1) * SCALE).astype(BF16) for a in (q_parts, k_parts)
    )
    grad_v = jnp.concatenate(v_parts, axis=1).astype(BF16)
    return out, grad_q, grad_k[:rows], grad_v[:rows], grad_k[rows:], grad_v[rows:]


def solution(mesh):
    split = P("ctx", "head")
    plan = blocked if (mesh.shape["ctx"], mesh.shape["head"]) == (2 * SQUARE, 4) else gathered
    return jax.shard_map(
        plan,
        mesh=mesh,
        in_specs=(split,) * 5 + (P(), P(), P("head", None), split),
        out_specs=(split,) * 6,
        check_vma=False,
    )
```

```python
import functools
import math

import jax
import jax.numpy as jnp
from jax import lax
from jax.experimental import pallas as pl
from jax.experimental.pallas import tpu as pltpu
from jax.sharding import PartitionSpec as P

HDIM = 128
FTOK = 16
FMAX = 2
NEG_FILL = -1e30
SCALE = 1.0 / math.sqrt(HDIM)
F32 = jnp.float32
BF16 = jnp.bfloat16
SQUARE = 4
PAIR = 4


def contract(left, right, left_dim, right_dim):
    return lax.dot_general(
        left, right, (((left_dim,), (right_dim,)), ((), ())), preferred_element_type=F32
    )


def head_slice(stacked, head):
    return stacked[:, head * HDIM : (head + 1) * HDIM]


def swap(block, axis, bit):
    count = lax.axis_size(axis)
    return lax.ppermute(block, axis, [(i, i ^ bit) for i in range(count)])


def local_call(body, name, out_shapes, args, tables=0, flops=0):
    spaces = [pltpu.SMEM] * tables + [pltpu.VMEM] * (len(args) - tables)
    moved = sum(a.size * a.dtype.itemsize for a in args)
    moved += sum(math.prod(o.shape) * o.dtype.itemsize for o in out_shapes)
    return pl.pallas_call(
        body,
        name=name,
        out_shape=out_shapes,
        in_specs=[pl.BlockSpec(memory_space=space) for space in spaces],
        out_specs=[pl.BlockSpec(memory_space=pltpu.VMEM)] * len(out_shapes),
        compiler_params=pltpu.CompilerParams(vmem_limit_bytes=40 * 2**20),
        cost_estimate=pl.CostEstimate(flops=flops, bytes_accessed=moved, transcendentals=0),
    )(*args)


def load_kernel(k_ref, hk_ref, v_ref, hv_ref, kv_out, kv_ref, sems):
    inward, outward, begin = [], [], 0
    for i, ref in enumerate((k_ref, hk_ref, v_ref, hv_ref)):
        part = pl.ds(begin, ref.shape[0])
        inward.append(pltpu.make_async_copy(ref, kv_ref.at[part], sems.at[0, i]))
        outward.append(pltpu.make_async_copy(kv_ref.at[part], kv_out.at[part], sems.at[1, i]))
        begin += ref.shape[0]
    for copy in inward:
        copy.start()
    for before, after in zip(inward, outward):
        before.wait()
        after.start()
    for copy in outward:
        copy.wait()


def load_keys(*arrays):
    rows = sum(a.shape[0] for a in arrays)
    width = arrays[0].shape[1]
    return pl.pallas_call(
        load_kernel,
        name="load",
        out_shape=jax.ShapeDtypeStruct((rows, width), BF16),
        in_specs=[pl.BlockSpec(memory_space=pl.ANY)] * len(arrays),
        out_specs=pl.BlockSpec(memory_space=pl.ANY),
        scratch_shapes=[pltpu.VMEM((rows, width), BF16), pltpu.SemaphoreType.DMA((2, len(arrays)))],
        compiler_params=pltpu.CompilerParams(vmem_limit_bytes=60 * 2**20),
        cost_estimate=pl.CostEstimate(
            flops=0, bytes_accessed=4 * rows * width * 2, transcendentals=0
        ),
    )(*arrays)


def limits_kernel(levels_ref, counts_ref, limits_ref):
    me = lax.axis_index("ctx")
    row = lax.broadcasted_iota(jnp.int32, limits_ref.shape, 0)
    limits = jnp.zeros(limits_ref.shape, jnp.int32)
    for step in range(SQUARE):
        total = jnp.int32(0)
        for frame in range(FMAX):
            tokens = lax.shift_right_logical(jnp.int32(FTOK), 2 * levels_ref[me ^ step, frame])
            total += jnp.where(frame < counts_ref[me ^ step], tokens, 0)
        limits = jnp.where(row == step, total, limits)
    limits_ref[...] = limits


def dattn_kernel(own_ref, core_ref, near_ref, far_ref, w_ref, out_ref):
    me = lax.axis_index("head")
    size = own_ref.shape[1]
    total = None
    for step, ref in enumerate((own_ref, core_ref, near_ref, far_ref)):
        columns = pl.ds(pl.multiple_of((me ^ step) * size, HDIM), size)
        part = contract(ref[...], w_ref[:, columns], 1, 1)
        total = part if total is None else total + part
    out_ref[...] = total.astype(BF16)


def both_rows(own_ref, pair_ref, head):
    return jnp.concatenate(
        [head_slice(own_ref[...], head), head_slice(pair_ref[...], head)], axis=0
    )


def forward_kernel(
    limits_ref, q_own_ref, q_pair_ref, d_own_ref, d_pair_ref, kv0, kv1, kv2, kv3,
    stats_ref, own_ref, pair_ref, probs_ref, dprobs_ref,
):
    rows = q_own_ref.shape[0]
    keys = kv0.shape[0] // 2
    blocks = (kv0, kv1, kv2, kv3)
    stats_ref[...] = jnp.zeros_like(stats_ref)
    for head in range(q_own_ref.shape[1] // HDIM):
        query = both_rows(q_own_ref, q_pair_ref, head)
        dattn = both_rows(d_own_ref, d_pair_ref, head)
        scores = []
        for step, ref in enumerate(blocks):
            block = contract(head_slice(ref[:keys], head), query, 1, 1) * SCALE
            slot = lax.broadcasted_iota(jnp.int32, block.shape, 0)
            valid = slot < rows + limits_ref[step : step + 1]
            scores.append(jnp.where(valid, block, NEG_FILL))
        top = functools.reduce(
            jnp.maximum, [jnp.max(block, axis=0, keepdims=True) for block in scores]
        )
        weights = [jnp.exp(block - top) for block in scores]
        total = sum(jnp.sum(block, axis=0, keepdims=True) for block in weights)
        inverse = 1.0 / total
        attn, delta = None, None
        for step, ref in enumerate(blocks):
            value = head_slice(ref[keys:], head)
            probs = weights[step] * inverse
            dprobs = contract(value, dattn, 1, 1)
            part = contract(value, probs.astype(BF16), 0, 0)
            delta_part = jnp.sum(probs * dprobs, axis=0, keepdims=True)
            attn = part if attn is None else attn + part
            delta = delta_part if delta is None else delta + delta_part
            begin = (head * SQUARE + step) * keys
            probs_ref[begin : begin + keys] = probs.astype(probs_ref.dtype)
            dprobs_ref[begin : begin + keys] = dprobs
        features = slice(head * HDIM, (head + 1) * HDIM)
        own_ref[features] = attn[:, :rows]
        pair_ref[features] = attn[:, rows:].astype(BF16)
        stats_ref[head : head + 1] = top + jnp.log(total)
        stats_ref[8 + head : 9 + head] = delta


def merge_parts(mine, theirs):
    top = jnp.maximum(mine, theirs)
    weight, weight_pair = jnp.exp(mine - top), jnp.exp(theirs - top)
    inverse = 1.0 / (weight + weight_pair)
    return weight * inverse, weight_pair * inverse


def project_kernel(own_ref, pair_ref, stats_ref, stats_pair_ref, w_ref, send_ref, next_ref, keep_ref):
    rows = own_ref.shape[1]
    parts = []
    for head in range(own_ref.shape[0] // HDIM):
        features = slice(head * HDIM, (head + 1) * HDIM)
        weight, weight_pair = merge_parts(
            stats_ref[head : head + 1, :rows], stats_pair_ref[head : head + 1, rows:]
        )
        parts.append(own_ref[features] * weight + pair_ref[features].astype(F32) * weight_pair)
    attn = jnp.concatenate(parts, axis=0).astype(BF16)
    me = lax.axis_index("head")
    size = keep_ref.shape[1]

    def columns_of(step):
        columns = pl.ds(pl.multiple_of((me ^ step) * size, HDIM), size)
        return contract(attn, w_ref[:, columns], 0, 0)

    send_ref[:, :size] = columns_of(1).astype(BF16)
    send_ref[:, size:] = columns_of(3).astype(BF16)
    next_ref[...] = columns_of(2)
    keep_ref[...] = columns_of(0)


def add_near_kernel(next_ref, core_ref, out_ref):
    size = next_ref.shape[1]
    out_ref[...] = (next_ref[...] + core_ref[:, size:].astype(F32)).astype(BF16)


def backward_kernel(
    q_own_ref, q_pair_ref, d_own_ref, d_pair_ref, kv0, kv1, kv2, kv3,
    stats_ref, stats_pair_ref, probs_ref, dprobs_ref,
    dq_own_ref, dq_pair_ref, dkv_ref,
):
    rows = q_own_ref.shape[0]
    keys = kv0.shape[0] // 2
    place = lax.rem(lax.axis_index("ctx"), SQUARE)

    def swapped(row):
        return jnp.concatenate([row[:, rows:], row[:, :rows]], axis=1)

    for head in range(q_own_ref.shape[1] // HDIM):
        query = both_rows(q_own_ref, q_pair_ref, head)
        dattn = both_rows(d_own_ref, d_pair_ref, head)
        weight, weight_pair = merge_parts(
            stats_ref[head : head + 1], swapped(stats_pair_ref[head : head + 1])
        )
        delta = weight * stats_ref[8 + head : 9 + head]
        delta += weight_pair * swapped(stats_pair_ref[8 + head : 9 + head])
        features = slice(head * HDIM, (head + 1) * HDIM)
        dquery = None
        for step, ref in enumerate((kv0, kv1, kv2, kv3)):
            first = pl.multiple_of((place ^ step) * 2 * keys, 2 * keys)
            begin = (head * SQUARE + step) * keys
            probs = (probs_ref[begin : begin + keys].astype(F32) * weight).astype(BF16)
            dprobs = dprobs_ref[begin : begin + keys]
            dscores = (probs.astype(F32) * (dprobs - delta)).astype(BF16)
            grad_key = (contract(dscores, query, 1, 0) * SCALE).astype(BF16)
            dkv_ref[pl.ds(first, keys), features] = grad_key
            grad_value = contract(probs, dattn, 1, 0).astype(BF16)
            dkv_ref[pl.ds(first + keys, keys), features] = grad_value
            part = contract(dscores, head_slice(ref[:keys], head), 0, 0)
            dquery = part if dquery is None else dquery + part
        dq_own_ref[:, features] = dquery[:rows] * SCALE
        dq_pair_ref[:, features] = (dquery[rows:] * SCALE).astype(BF16)


def finish_kernel(
    dq_ref, dq_pair_ref, dkv_ref, keep_ref, core_ref, near_ref,
    q_out, k_out, v_out, hk_out, hv_out, out_ref,
):
    rows, capacity = k_out.shape[0], hk_out.shape[0]
    keys = rows + capacity

    def total(begin, size):
        parts = (dkv_ref[pl.ds(step * 2 * keys + begin, size)] for step in range(SQUARE))
        return sum(part.astype(F32) for part in parts).astype(BF16)

    q_out[...] = (dq_ref[...] + dq_pair_ref[...].astype(F32)).astype(BF16)
    k_out[...] = total(0, rows)
    hk_out[...] = total(rows, capacity)
    v_out[...] = total(keys, rows)
    hv_out[...] = total(keys + rows, capacity)
    size = keep_ref.shape[1]
    out = keep_ref[...] + core_ref[:, :size].astype(F32) + near_ref[...].astype(F32)
    out_ref[...] = out.astype(BF16)


def blocked(sec_q, sec_k, sec_v, hist_k, hist_v, frame_levels, frame_counts, w_out, grad_out):
    shape = jax.ShapeDtypeStruct
    rows, width = sec_q.shape
    heads = width // HDIM
    capacity = hist_k.shape[0]
    keys = rows + capacity
    share = grad_out.shape[1]
    work = 2 * SQUARE * keys * 2 * rows * width

    grad_core, grad_near, grad_far = (swap(grad_out, "head", step) for step in range(1, 4))
    kv0 = load_keys(sec_k, hist_k, sec_v, hist_v)
    kvs = [kv0] + [swap(kv0, "ctx", step) for step in range(1, SQUARE)]
    q_pair = swap(sec_q, "ctx", PAIR)
    d_own = local_call(
        dattn_kernel,
        "dattn",
        [shape((rows, width), BF16)],
        (grad_out, grad_core, grad_near, grad_far, w_out),
        flops=2 * rows * width * share * 4,
    )[0]
    d_pair = swap(d_own, "ctx", PAIR)
    limits = local_call(
        limits_kernel,
        "limits",
        [shape((8, 2 * rows), jnp.int32)],
        (frame_levels, frame_counts),
        tables=2,
    )[0]
    stats, attn_own, attn_pair, probs, dprobs = local_call(
        forward_kernel,
        "forward",
        [
            shape((16, 2 * rows), F32),
            shape((width, rows), F32),
            shape((width, rows), BF16),
            shape((heads * SQUARE * keys, 2 * rows), BF16),
            shape((heads * SQUARE * keys, 2 * rows), F32),
        ],
        (limits, sec_q, q_pair, d_own, d_pair, *kvs),
        flops=3 * work,
    )
    stats_pair = swap(stats, "ctx", PAIR)
    stats_pair, attn_pair = lax.optimization_barrier((stats_pair, attn_pair))
    attn_got = swap(attn_pair, "ctx", PAIR)
    dq_own, dq_pair, dkv = local_call(
        backward_kernel,
        "backward",
        [
            shape((rows, width), F32),
            shape((rows, width), BF16),
            shape((SQUARE * 2 * keys, width), BF16),
        ],
        (sec_q, q_pair, d_own, d_pair, *kvs, stats, stats_pair, probs, dprobs),
        flops=3 * work,
    )
    squares = [list(range(i, i + SQUARE)) for i in range(0, lax.axis_size("ctx"), SQUARE)]
    dkv_got = lax.all_to_all(dkv, "ctx", 0, 0, axis_index_groups=squares, tiled=True)
    dq_got = swap(dq_pair, "ctx", PAIR)
    attn_own, dq_own = lax.optimization_barrier((attn_own, dq_own))
    out_send, out_next, out_keep = local_call(
        project_kernel,
        "project",
        [shape((rows, 2 * share), BF16), shape((rows, share), F32), shape((rows, share), F32)],
        (attn_own, attn_got, stats, stats_pair, w_out),
        flops=2 * rows * width * share * 4,
    )
    out_core = swap(out_send, "head", 1)
    out_near = swap(
        local_call(add_near_kernel, "add_near", [shape((rows, share), BF16)], (out_next, out_core))[0],
        "head",
        2,
    )
    grad_q, grad_k, grad_v, grad_hk, grad_hv, out = local_call(
        finish_kernel,
        "finish",
        [shape((rows, width), BF16)] * 3
        + [shape((capacity, width), BF16)] * 2
        + [shape((rows, share), BF16)],
        (dq_own, dq_got, dkv_got, out_keep, out_core, out_near),
    )
    return out, grad_q, grad_k, grad_v, grad_hk, grad_hv


def gathered(sec_q, sec_k, sec_v, hist_k, hist_v, frame_levels, frame_counts, w_out, grad_out):
    rows = sec_q.shape[0]
    capacity = hist_k.shape[0]
    owners = lax.axis_size("ctx")
    me = lax.axis_index("ctx")
    frames = jnp.arange(FMAX, dtype=jnp.int32)[None, :]
    tokens = jnp.where(
        frames < frame_counts[:, None], jnp.right_shift(jnp.int32(FTOK), 2 * frame_levels), 0
    ).sum(axis=1)
    slots = jnp.arange(capacity, dtype=jnp.int32)
    all_valid = jnp.concatenate(
        [jnp.ones((owners * rows,), bool), (slots[None] < tokens[:, None]).reshape(-1)]
    )
    own_valid = jnp.concatenate(
        [jnp.ones((rows,), bool), slots < lax.dynamic_index_in_dim(tokens, me, keepdims=False)]
    )

    def everyone(block, axis=0):
        return lax.all_gather(block, "ctx", axis=axis, tiled=True)

    own_k, own_v = (jnp.concatenate(a, axis=0) for a in ((sec_k, hist_k), (sec_v, hist_v)))
    all_k = jnp.concatenate([everyone(sec_k), everyone(hist_k)], axis=0)
    all_v = jnp.concatenate([everyone(sec_v), everyone(hist_v)], axis=0)
    d_attn = contract(lax.all_gather(grad_out, "head", axis=1, tiled=True), w_out, 1, 1).astype(BF16)
    all_q, all_d = everyone(sec_q), everyone(d_attn)

    def probs_and_dscores(query, key, value, dattn, valid, lse, delta):
        scores = contract(query, key, 1, 1) * SCALE
        probs = jnp.where(valid[None, :], jnp.exp(scores - lse), 0.0).astype(BF16)
        dprobs = contract(dattn, value, 1, 1)
        return probs, (probs.astype(F32) * (dprobs - delta)).astype(BF16)

    attn_parts, q_parts, k_parts, v_parts = [], [], [], []
    for head in range(sec_q.shape[1] // HDIM):
        query, dattn, key, value = (head_slice(a, head) for a in (sec_q, d_attn, all_k, all_v))
        scores = jnp.where(all_valid[None, :], contract(query, key, 1, 1) * SCALE, NEG_FILL)
        lse = jax.nn.logsumexp(scores, axis=1, keepdims=True)
        probs = jnp.where(all_valid[None, :], jnp.exp(scores - lse), 0.0).astype(BF16)
        attn = contract(probs, value, 1, 0).astype(BF16)
        delta = jnp.sum(attn.astype(F32) * dattn.astype(F32), axis=1, keepdims=True)
        _, dscores = probs_and_dscores(query, key, value, dattn, all_valid, lse, delta)
        attn_parts.append(attn)
        q_parts.append(contract(dscores, key, 1, 0))
        query, dattn, key, value = (head_slice(a, head) for a in (all_q, all_d, own_k, own_v))
        probs, dscores = probs_and_dscores(
            query, key, value, dattn, own_valid, everyone(lse), everyone(delta)
        )
        k_parts.append(contract(dscores, query, 0, 0))
        v_parts.append(contract(probs, dattn, 0, 0))
    partial = contract(jnp.concatenate(attn_parts, axis=1), w_out, 1, 0).astype(BF16)
    out = lax.psum_scatter(partial, "head", scatter_dimension=1, tiled=True)
    grad_q, grad_k = (
        (jnp.concatenate(a, axis=1) * SCALE).astype(BF16) for a in (q_parts, k_parts)
    )
    grad_v = jnp.concatenate(v_parts, axis=1).astype(BF16)
    return out, grad_q, grad_k[:rows], grad_v[:rows], grad_k[rows:], grad_v[rows:]


def solution(mesh):
    split = P("ctx", "head")
    plan = blocked if (mesh.shape["ctx"], mesh.shape["head"]) == (2 * SQUARE, 4) else gathered
    return jax.shard_map(
        plan,
        mesh=mesh,
        in_specs=(split,) * 5 + (P(), P(), P("head", None), split),
        out_specs=(split,) * 6,
        check_vma=False,
    )
```

```python
import functools
import math

import jax
import jax.numpy as jnp
from jax import lax
from jax.experimental import pallas as pl
from jax.experimental.pallas import tpu as pltpu
from jax.sharding import PartitionSpec as P

HDIM = 128
FTOK = 16
FMAX = 2
NEG_FILL = -1e30
SCALE = 1.0 / math.sqrt(HDIM)
F32 = jnp.float32
BF16 = jnp.bfloat16
SQUARE = 4
PAIR = 4


def contract(left, right, left_dim, right_dim):
    return lax.dot_general(
        left, right, (((left_dim,), (right_dim,)), ((), ())), preferred_element_type=F32
    )


def head_slice(stacked, head):
    return stacked[:, head * HDIM : (head + 1) * HDIM]


def swap(block, axis, bit):
    count = lax.axis_size(axis)
    return lax.ppermute(block, axis, [(i, i ^ bit) for i in range(count)])


def local_call(body, name, out_shapes, args, tables=0, flops=0):
    spaces = [pltpu.SMEM] * tables + [pltpu.VMEM] * (len(args) - tables)
    moved = sum(a.size * a.dtype.itemsize for a in args)
    moved += sum(math.prod(o.shape) * o.dtype.itemsize for o in out_shapes)
    return pl.pallas_call(
        body,
        name=name,
        out_shape=out_shapes,
        in_specs=[pl.BlockSpec(memory_space=space) for space in spaces],
        out_specs=[pl.BlockSpec(memory_space=pltpu.VMEM)] * len(out_shapes),
        compiler_params=pltpu.CompilerParams(vmem_limit_bytes=40 * 2**20),
        cost_estimate=pl.CostEstimate(flops=flops, bytes_accessed=moved, transcendentals=0),
    )(*args)


def load_kernel(k_ref, hk_ref, v_ref, hv_ref, kv_out, kv_ref, sems):
    inward, outward, begin = [], [], 0
    for i, ref in enumerate((k_ref, hk_ref, v_ref, hv_ref)):
        part = pl.ds(begin, ref.shape[0])
        inward.append(pltpu.make_async_copy(ref, kv_ref.at[part], sems.at[0, i]))
        outward.append(pltpu.make_async_copy(kv_ref.at[part], kv_out.at[part], sems.at[1, i]))
        begin += ref.shape[0]
    for copy in inward:
        copy.start()
    for before, after in zip(inward, outward):
        before.wait()
        after.start()
    for copy in outward:
        copy.wait()


def load_keys(*arrays):
    rows = sum(a.shape[0] for a in arrays)
    width = arrays[0].shape[1]
    return pl.pallas_call(
        load_kernel,
        name="load",
        out_shape=jax.ShapeDtypeStruct((rows, width), BF16),
        in_specs=[pl.BlockSpec(memory_space=pl.ANY)] * len(arrays),
        out_specs=pl.BlockSpec(memory_space=pl.ANY),
        scratch_shapes=[pltpu.VMEM((rows, width), BF16), pltpu.SemaphoreType.DMA((2, len(arrays)))],
        compiler_params=pltpu.CompilerParams(vmem_limit_bytes=60 * 2**20),
        cost_estimate=pl.CostEstimate(
            flops=0, bytes_accessed=4 * rows * width * 2, transcendentals=0
        ),
    )(*arrays)


def limits_kernel(levels_ref, counts_ref, limits_ref):
    me = lax.axis_index("ctx")
    row = lax.broadcasted_iota(jnp.int32, limits_ref.shape, 0)
    limits = jnp.zeros(limits_ref.shape, jnp.int32)
    for step in range(SQUARE):
        total = jnp.int32(0)
        for frame in range(FMAX):
            tokens = lax.shift_right_logical(jnp.int32(FTOK), 2 * levels_ref[me ^ step, frame])
            total += jnp.where(frame < counts_ref[me ^ step], tokens, 0)
        limits = jnp.where(row == step, total, limits)
    limits_ref[...] = limits


def dattn_kernel(own_ref, core_ref, near_ref, far_ref, w_ref, out_ref):
    me = lax.axis_index("head")
    size = own_ref.shape[1]
    total = None
    for step, ref in enumerate((own_ref, core_ref, near_ref, far_ref)):
        columns = pl.ds(pl.multiple_of((me ^ step) * size, HDIM), size)
        part = contract(ref[...], w_ref[:, columns], 1, 1)
        total = part if total is None else total + part
    out_ref[...] = total.astype(BF16)


def both_rows(own_ref, pair_ref, head):
    return jnp.concatenate(
        [head_slice(own_ref[...], head), head_slice(pair_ref[...], head)], axis=0
    )


def forward_kernel(
    limits_ref, q_own_ref, q_pair_ref, d_own_ref, d_pair_ref, kv0, kv1, kv2, kv3,
    stats_ref, own_ref, pair_ref, probs_ref, dprobs_ref,
):
    rows = q_own_ref.shape[0]
    keys = kv0.shape[0] // 2
    blocks = (kv0, kv1, kv2, kv3)
    stats_ref[...] = jnp.zeros_like(stats_ref)
    for head in range(q_own_ref.shape[1] // HDIM):
        query = both_rows(q_own_ref, q_pair_ref, head)
        dattn = both_rows(d_own_ref, d_pair_ref, head)
        scores = []
        for step, ref in enumerate(blocks):
            block = contract(head_slice(ref[:keys], head), query, 1, 1) * SCALE
            slot = lax.broadcasted_iota(jnp.int32, block.shape, 0)
            valid = slot < rows + limits_ref[step : step + 1]
            scores.append(jnp.where(valid, block, NEG_FILL))
        top = functools.reduce(
            jnp.maximum, [jnp.max(block, axis=0, keepdims=True) for block in scores]
        )
        weights = [jnp.exp(block - top) for block in scores]
        total = sum(jnp.sum(block, axis=0, keepdims=True) for block in weights)
        inverse = 1.0 / total
        attn, delta = None, None
        for step, ref in enumerate(blocks):
            value = head_slice(ref[keys:], head)
            probs = weights[step] * inverse
            dprobs = contract(value, dattn, 1, 1)
            part = contract(value, probs.astype(BF16), 0, 0)
            delta_part = jnp.sum(probs * dprobs, axis=0, keepdims=True)
            attn = part if attn is None else attn + part
            delta = delta_part if delta is None else delta + delta_part
            begin = (head * SQUARE + step) * keys
            probs_ref[begin : begin + keys] = probs.astype(probs_ref.dtype)
            dprobs_ref[begin : begin + keys] = dprobs
        features = slice(head * HDIM, (head + 1) * HDIM)
        own_ref[features] = attn[:, :rows]
        pair_ref[features] = attn[:, rows:].astype(BF16)
        stats_ref[head : head + 1] = top + jnp.log(total)
        stats_ref[8 + head : 9 + head] = delta


def merge_parts(mine, theirs):
    top = jnp.maximum(mine, theirs)
    weight, weight_pair = jnp.exp(mine - top), jnp.exp(theirs - top)
    inverse = 1.0 / (weight + weight_pair)
    return weight * inverse, weight_pair * inverse


def project_kernel(own_ref, pair_ref, stats_ref, stats_pair_ref, w_ref, keep_ref, *send_refs):
    rows = own_ref.shape[1]
    parts = []
    for head in range(own_ref.shape[0] // HDIM):
        features = slice(head * HDIM, (head + 1) * HDIM)
        weight, weight_pair = merge_parts(
            stats_ref[head : head + 1, :rows], stats_pair_ref[head : head + 1, rows:]
        )
        parts.append(own_ref[features] * weight + pair_ref[features].astype(F32) * weight_pair)
    attn = jnp.concatenate(parts, axis=0).astype(BF16)
    me = lax.axis_index("head")
    size = keep_ref.shape[1]
    for step, ref in enumerate((keep_ref, *send_refs)):
        columns = pl.ds(pl.multiple_of((me ^ step) * size, HDIM), size)
        ref[...] = contract(attn, w_ref[:, columns], 0, 0).astype(ref.dtype)


def backward_kernel(
    q_own_ref, q_pair_ref, d_own_ref, d_pair_ref, kv0, kv1, kv2, kv3,
    stats_ref, stats_pair_ref, probs_ref, dprobs_ref,
    dq_own_ref, dq_pair_ref, dkv_ref, send_k_ref, send_v_ref, near_k_ref, near_v_ref,
):
    rows = q_own_ref.shape[0]
    keys = kv0.shape[0] // 2
    key_parts = (dkv_ref.at[:keys], send_k_ref.at[:keys], near_k_ref, send_k_ref.at[keys:])
    value_parts = (dkv_ref.at[keys:], near_v_ref, send_v_ref.at[:keys], send_v_ref.at[keys:])

    def swapped(row):
        return jnp.concatenate([row[:, rows:], row[:, :rows]], axis=1)

    for head in range(q_own_ref.shape[1] // HDIM):
        query = both_rows(q_own_ref, q_pair_ref, head)
        dattn = both_rows(d_own_ref, d_pair_ref, head)
        weight, weight_pair = merge_parts(
            stats_ref[head : head + 1], swapped(stats_pair_ref[head : head + 1])
        )
        delta = weight * stats_ref[8 + head : 9 + head]
        delta += weight_pair * swapped(stats_pair_ref[8 + head : 9 + head])
        features = slice(head * HDIM, (head + 1) * HDIM)
        dquery = None
        for step, ref in enumerate((kv0, kv1, kv2, kv3)):
            begin = (head * SQUARE + step) * keys
            probs = (probs_ref[begin : begin + keys].astype(F32) * weight).astype(BF16)
            dprobs = dprobs_ref[begin : begin + keys]
            dscores = (probs.astype(F32) * (dprobs - delta)).astype(BF16)
            key_part, value_part = key_parts[step], value_parts[step]
            grad_key = contract(dscores, query, 1, 0) * SCALE
            key_part[:, features] = grad_key.astype(key_part.dtype)
            value_part[:, features] = contract(probs, dattn, 1, 0).astype(value_part.dtype)
            part = contract(dscores, head_slice(ref[:keys], head), 0, 0)
            dquery = part if dquery is None else dquery + part
        dq_own_ref[:, features] = dquery[:rows] * SCALE
        dq_pair_ref[:, features] = (dquery[rows:] * SCALE).astype(BF16)


def pass_on_kernel(near_k_ref, near_v_ref, got_k_ref, got_v_ref, k_ref, v_ref):
    keys = near_k_ref.shape[0]
    k_ref[...] = (near_k_ref[...] + got_k_ref[keys:].astype(F32)).astype(BF16)
    v_ref[...] = (near_v_ref[...] + got_v_ref[keys:].astype(F32)).astype(BF16)


def finish_kernel(
    dq_ref, dq_pair_ref, dkv_ref, got_k_ref, got_v_ref, rest_k_ref, rest_v_ref,
    keep_ref, core_ref, near_ref, far_ref,
    q_out, k_out, v_out, hk_out, hv_out, out_ref,
):
    rows, capacity = k_out.shape[0], hk_out.shape[0]
    keys = rows + capacity

    def total(first, *others):
        for other in others:
            first = first + other.astype(F32)
        return first.astype(BF16)

    q_out[...] = total(dq_ref[...], dq_pair_ref[...])
    k_out[...] = total(dkv_ref[:rows], got_k_ref[:rows], rest_k_ref[:rows])
    hk_out[...] = total(dkv_ref[rows:keys], got_k_ref[rows:keys], rest_k_ref[rows:])
    v_out[...] = total(dkv_ref[keys : keys + rows], got_v_ref[:rows], rest_v_ref[:rows])
    hv_out[...] = total(dkv_ref[keys + rows :], got_v_ref[rows:keys], rest_v_ref[rows:])
    out_ref[...] = total(keep_ref[...], core_ref[...], near_ref[...], far_ref[...])


def blocked(sec_q, sec_k, sec_v, hist_k, hist_v, frame_levels, frame_counts, w_out, grad_out):
    shape = jax.ShapeDtypeStruct
    rows, width = sec_q.shape
    heads = width // HDIM
    capacity = hist_k.shape[0]
    keys = rows + capacity
    share = grad_out.shape[1]
    work = 2 * SQUARE * keys * 2 * rows * width

    grad_core, grad_near, grad_far = (swap(grad_out, "head", step) for step in range(1, 4))
    kv0 = load_keys(sec_k, hist_k, sec_v, hist_v)
    kv2 = swap(kv0, "ctx", 2)
    kv1 = swap(kv0, "ctx", 1)
    kvs = [kv0, kv1, kv2, swap(kv2, "ctx", 1)]
    q_pair = swap(sec_q, "ctx", PAIR)
    d_own = local_call(
        dattn_kernel,
        "dattn",
        [shape((rows, width), BF16)],
        (grad_out, grad_core, grad_near, grad_far, w_out),
        flops=2 * rows * width * share * 4,
    )[0]
    d_pair = swap(d_own, "ctx", PAIR)
    limits = local_call(
        limits_kernel,
        "limits",
        [shape((8, 2 * rows), jnp.int32)],
        (frame_levels, frame_counts),
        tables=2,
    )[0]
    stats, attn_own, attn_pair, probs, dprobs = local_call(
        forward_kernel,
        "forward",
        [
            shape((16, 2 * rows), F32),
            shape((width, rows), F32),
            shape((width, rows), BF16),
            shape((heads * SQUARE * keys, 2 * rows), BF16),
            shape((heads * SQUARE * keys, 2 * rows), F32),
        ],
        (limits, sec_q, q_pair, d_own, d_pair, *kvs),
        flops=3 * work,
    )
    stats_pair = swap(stats, "ctx", PAIR)
    stats_pair, attn_pair = lax.optimization_barrier((stats_pair, attn_pair))
    attn_got = swap(attn_pair, "ctx", PAIR)
    dq_own, dq_pair, dkv_own, send_k, send_v, near_k, near_v = local_call(
        backward_kernel,
        "backward",
        [shape((rows, width), F32), shape((rows, width), BF16), shape((2 * keys, width), F32)]
        + [shape((2 * keys, width), BF16)] * 2
        + [shape((keys, width), F32)] * 2,
        (sec_q, q_pair, d_own, d_pair, *kvs, stats, stats_pair, probs, dprobs),
        flops=3 * work,
    )
    got_k = swap(send_k, "ctx", 1)
    got_v = swap(send_v, "ctx", 2)
    dq_got = swap(dq_pair, "ctx", PAIR)
    rest_k, rest_v = local_call(
        pass_on_kernel,
        "pass_on",
        [shape((keys, width), BF16)] * 2,
        (near_k, near_v, got_k, got_v),
    )
    rest_k = swap(rest_k, "ctx", 2)
    rest_v = swap(rest_v, "ctx", 1)
    attn_own, dq_own = lax.optimization_barrier((attn_own, dq_own))
    out_keep, *out_send = local_call(
        project_kernel,
        "project",
        [shape((rows, share), F32)] + [shape((rows, share), BF16)] * 3,
        (attn_own, attn_got, stats, stats_pair, w_out),
        flops=2 * rows * width * share * 4,
    )
    out_got = [swap(out_send[step - 1], "head", step) for step in (1, 2, 3)]
    grad_q, grad_k, grad_v, grad_hk, grad_hv, out = local_call(
        finish_kernel,
        "finish",
        [shape((rows, width), BF16)] * 3
        + [shape((capacity, width), BF16)] * 2
        + [shape((rows, share), BF16)],
        (dq_own, dq_got, dkv_own, got_k, got_v, rest_k, rest_v, out_keep, *out_got),
    )
    return out, grad_q, grad_k, grad_v, grad_hk, grad_hv


def gathered(sec_q, sec_k, sec_v, hist_k, hist_v, frame_levels, frame_counts, w_out, grad_out):
    rows = sec_q.shape[0]
    capacity = hist_k.shape[0]
    owners = lax.axis_size("ctx")
    me = lax.axis_index("ctx")
    frames = jnp.arange(FMAX, dtype=jnp.int32)[None, :]
    tokens = jnp.where(
        frames < frame_counts[:, None], jnp.right_shift(jnp.int32(FTOK), 2 * frame_levels), 0
    ).sum(axis=1)
    slots = jnp.arange(capacity, dtype=jnp.int32)
    all_valid = jnp.concatenate(
        [jnp.ones((owners * rows,), bool), (slots[None] < tokens[:, None]).reshape(-1)]
    )
    own_valid = jnp.concatenate(
        [jnp.ones((rows,), bool), slots < lax.dynamic_index_in_dim(tokens, me, keepdims=False)]
    )

    def everyone(block, axis=0):
        return lax.all_gather(block, "ctx", axis=axis, tiled=True)

    own_k, own_v = (jnp.concatenate(a, axis=0) for a in ((sec_k, hist_k), (sec_v, hist_v)))
    all_k = jnp.concatenate([everyone(sec_k), everyone(hist_k)], axis=0)
    all_v = jnp.concatenate([everyone(sec_v), everyone(hist_v)], axis=0)
    d_attn = contract(lax.all_gather(grad_out, "head", axis=1, tiled=True), w_out, 1, 1).astype(BF16)
    all_q, all_d = everyone(sec_q), everyone(d_attn)

    def probs_and_dscores(query, key, value, dattn, valid, lse, delta):
        scores = contract(query, key, 1, 1) * SCALE
        probs = jnp.where(valid[None, :], jnp.exp(scores - lse), 0.0).astype(BF16)
        dprobs = contract(dattn, value, 1, 1)
        return probs, (probs.astype(F32) * (dprobs - delta)).astype(BF16)

    attn_parts, q_parts, k_parts, v_parts = [], [], [], []
    for head in range(sec_q.shape[1] // HDIM):
        query, dattn, key, value = (head_slice(a, head) for a in (sec_q, d_attn, all_k, all_v))
        scores = jnp.where(all_valid[None, :], contract(query, key, 1, 1) * SCALE, NEG_FILL)
        lse = jax.nn.logsumexp(scores, axis=1, keepdims=True)
        probs = jnp.where(all_valid[None, :], jnp.exp(scores - lse), 0.0).astype(BF16)
        attn = contract(probs, value, 1, 0).astype(BF16)
        delta = jnp.sum(attn.astype(F32) * dattn.astype(F32), axis=1, keepdims=True)
        _, dscores = probs_and_dscores(query, key, value, dattn, all_valid, lse, delta)
        attn_parts.append(attn)
        q_parts.append(contract(dscores, key, 1, 0))
        query, dattn, key, value = (head_slice(a, head) for a in (all_q, all_d, own_k, own_v))
        probs, dscores = probs_and_dscores(
            query, key, value, dattn, own_valid, everyone(lse), everyone(delta)
        )
        k_parts.append(contract(dscores, query, 0, 0))
        v_parts.append(contract(probs, dattn, 0, 0))
    partial = contract(jnp.concatenate(attn_parts, axis=1), w_out, 1, 0).astype(BF16)
    out = lax.psum_scatter(partial, "head", scatter_dimension=1, tiled=True)
    grad_q, grad_k = (
        (jnp.concatenate(a, axis=1) * SCALE).astype(BF16) for a in (q_parts, k_parts)
    )
    grad_v = jnp.concatenate(v_parts, axis=1).astype(BF16)
    return out, grad_q, grad_k[:rows], grad_v[:rows], grad_k[rows:], grad_v[rows:]


def solution(mesh):
    split = P("ctx", "head")
    plan = blocked if (mesh.shape["ctx"], mesh.shape["head"]) == (2 * SQUARE, 4) else gathered
    return jax.shard_map(
        plan,
        mesh=mesh,
        in_specs=(split,) * 5 + (P(), P(), P("head", None), split),
        out_specs=(split,) * 6,
        check_vma=False,
    )
```

```python
import functools
import math

import jax
import jax.numpy as jnp
from jax import lax
from jax.experimental import pallas as pl
from jax.experimental.pallas import tpu as pltpu
from jax.sharding import PartitionSpec as P

HDIM = 128
FTOK = 16
FMAX = 2
NEG_FILL = -1e30
SCALE = 1.0 / math.sqrt(HDIM)
F32 = jnp.float32
BF16 = jnp.bfloat16
SQUARE = 4
HBM_BYTES = 3.69e6
PAIR = 4


def contract(left, right, left_dim, right_dim):
    return lax.dot_general(
        left, right, (((left_dim,), (right_dim,)), ((), ())), preferred_element_type=F32
    )


def head_slice(stacked, head):
    return stacked[:, head * HDIM : (head + 1) * HDIM]


def swap(block, axis, bit):
    count = lax.axis_size(axis)
    return lax.ppermute(block, axis, [(i, i ^ bit) for i in range(count)])


def cost_of(micros):
    return pl.CostEstimate(flops=0, bytes_accessed=int(micros * HBM_BYTES), transcendentals=0)


def local_call(body, name, micros, out_shapes, args, tables=0):
    spaces = [pltpu.SMEM] * tables + [pltpu.VMEM] * (len(args) - tables)
    return pl.pallas_call(
        body,
        name=name,
        out_shape=out_shapes,
        in_specs=[pl.BlockSpec(memory_space=space) for space in spaces],
        out_specs=[pl.BlockSpec(memory_space=pltpu.VMEM)] * len(out_shapes),
        compiler_params=pltpu.CompilerParams(vmem_limit_bytes=40 * 2**20),
        cost_estimate=cost_of(micros),
    )(*args)


def load_kernel(k_ref, hk_ref, v_ref, hv_ref, kv_out, kv_ref, sems):
    inward, outward, begin = [], [], 0
    for i, ref in enumerate((k_ref, hk_ref, v_ref, hv_ref)):
        part = pl.ds(begin, ref.shape[0])
        inward.append(pltpu.make_async_copy(ref, kv_ref.at[part], sems.at[0, i]))
        outward.append(pltpu.make_async_copy(kv_ref.at[part], kv_out.at[part], sems.at[1, i]))
        begin += ref.shape[0]
    for copy in inward:
        copy.start()
    for before, after in zip(inward, outward):
        before.wait()
        after.start()
    for copy in outward:
        copy.wait()


def load_keys(*arrays):
    rows = sum(a.shape[0] for a in arrays)
    width = arrays[0].shape[1]
    return pl.pallas_call(
        load_kernel,
        name="load",
        out_shape=jax.ShapeDtypeStruct((rows, width), BF16),
        in_specs=[pl.BlockSpec(memory_space=pl.ANY)] * len(arrays),
        out_specs=pl.BlockSpec(memory_space=pl.ANY),
        scratch_shapes=[pltpu.VMEM((rows, width), BF16), pltpu.SemaphoreType.DMA((2, len(arrays)))],
        compiler_params=pltpu.CompilerParams(vmem_limit_bytes=60 * 2**20),
        cost_estimate=cost_of(1.6),
    )(*arrays)


def limits_kernel(levels_ref, counts_ref, limits_ref):
    me = lax.axis_index("ctx")
    row = lax.broadcasted_iota(jnp.int32, limits_ref.shape, 0)
    limits = jnp.zeros(limits_ref.shape, jnp.int32)
    for step in range(SQUARE):
        total = jnp.int32(0)
        for frame in range(FMAX):
            tokens = lax.shift_right_logical(jnp.int32(FTOK), 2 * levels_ref[me ^ step, frame])
            total += jnp.where(frame < counts_ref[me ^ step], tokens, 0)
        limits = jnp.where(row == step, total, limits)
    limits_ref[...] = limits


def dattn_kernel(own_hbm, w_hbm, core_ref, near_ref, far_ref, out_ref, own_ref, w_ref, sems):
    me = lax.axis_index("head")
    size = core_ref.shape[1]
    copies = [pltpu.make_async_copy(own_hbm, own_ref, sems.at[4])]
    for step in range(4):
        columns = pl.ds(pl.multiple_of((me ^ step) * size, HDIM), size)
        copies.append(pltpu.make_async_copy(w_hbm.at[:, columns], w_ref.at[step], sems.at[step]))
    for copy in copies:
        copy.start()
    copies[0].wait()
    total = None
    for step, ref in enumerate((own_ref, core_ref, near_ref, far_ref)):
        copies[1 + step].wait()
        part = contract(ref[...], w_ref[step], 1, 1)
        total = part if total is None else total + part
    out_ref[...] = total.astype(BF16)


def dattn_call(grad_own, w_out, *blocks):
    rows, share = grad_own.shape
    width = w_out.shape[0]
    anywhere, inside = pl.BlockSpec(memory_space=pl.ANY), pl.BlockSpec(memory_space=pltpu.VMEM)
    return pl.pallas_call(
        dattn_kernel,
        name="dattn",
        out_shape=jax.ShapeDtypeStruct((rows, width), BF16),
        in_specs=[anywhere, anywhere, inside, inside, inside],
        out_specs=inside,
        scratch_shapes=[
            pltpu.VMEM((rows, share), BF16),
            pltpu.VMEM((4, width, share), BF16),
            pltpu.SemaphoreType.DMA((5,)),
        ],
        compiler_params=pltpu.CompilerParams(vmem_limit_bytes=52 * 2**20),
        cost_estimate=cost_of(1.5),
    )(grad_own, w_out, *blocks)


def both_rows(own_ref, pair_ref, head):
    return jnp.concatenate(
        [head_slice(own_ref[...], head), head_slice(pair_ref[...], head)], axis=0
    )


def forward_kernel(
    limits_ref, q_own_ref, q_pair_ref, d_own_ref, d_pair_ref, kv0, kv1, kv2, kv3,
    stats_ref, probs_ref, dprobs_ref,
):
    rows = q_own_ref.shape[0]
    keys = kv0.shape[0] // 2
    blocks = (kv0, kv1, kv2, kv3)
    stats_ref[...] = jnp.zeros_like(stats_ref)
    for head in range(q_own_ref.shape[1] // HDIM):
        query = both_rows(q_own_ref, q_pair_ref, head)
        dattn = both_rows(d_own_ref, d_pair_ref, head)
        scores = []
        for step, ref in enumerate(blocks):
            block = contract(head_slice(ref[:keys], head), query, 1, 1) * SCALE
            slot = lax.broadcasted_iota(jnp.int32, block.shape, 0)
            valid = slot < rows + limits_ref[step : step + 1]
            scores.append(jnp.where(valid, block, NEG_FILL))
        top = functools.reduce(
            jnp.maximum, [jnp.max(block, axis=0, keepdims=True) for block in scores]
        )
        weights = [jnp.exp(block - top) for block in scores]
        total = sum(jnp.sum(block, axis=0, keepdims=True) for block in weights)
        inverse = 1.0 / total
        delta = None
        for step, ref in enumerate(blocks):
            probs = weights[step] * inverse
            dprobs = contract(head_slice(ref[keys:], head), dattn, 1, 1)
            part = jnp.sum(probs * dprobs, axis=0, keepdims=True)
            delta = part if delta is None else delta + part
            begin = (head * SQUARE + step) * keys
            probs_ref[begin : begin + keys] = probs.astype(BF16)
            dprobs_ref[begin : begin + keys] = dprobs
        stats_ref[head : head + 1] = top + jnp.log(total)
        stats_ref[8 + head : 9 + head] = delta


def attn_kernel(kv0, kv1, kv2, kv3, probs_ref, own_ref, pair_ref):
    rows = own_ref.shape[1]
    keys = kv0.shape[0] // 2
    for head in range(own_ref.shape[0] // HDIM):
        attn = None
        for step, ref in enumerate((kv0, kv1, kv2, kv3)):
            begin = (head * SQUARE + step) * keys
            part = contract(head_slice(ref[keys:], head), probs_ref[begin : begin + keys], 0, 0)
            attn = part if attn is None else attn + part
        features = slice(head * HDIM, (head + 1) * HDIM)
        own_ref[features] = attn[:, :rows]
        pair_ref[features] = attn[:, rows:].astype(BF16)


def merge_parts(mine, theirs):
    top = jnp.maximum(mine, theirs)
    weight, weight_pair = jnp.exp(mine - top), jnp.exp(theirs - top)
    inverse = 1.0 / (weight + weight_pair)
    return weight * inverse, weight_pair * inverse


def project_kernel(own_ref, pair_ref, stats_ref, stats_pair_ref, w_ref, keep_ref, *send_refs):
    rows = own_ref.shape[1]
    parts = []
    for head in range(own_ref.shape[0] // HDIM):
        features = slice(head * HDIM, (head + 1) * HDIM)
        weight, weight_pair = merge_parts(
            stats_ref[head : head + 1, :rows], stats_pair_ref[head : head + 1, rows:]
        )
        parts.append(own_ref[features] * weight + pair_ref[features].astype(F32) * weight_pair)
    attn = jnp.concatenate(parts, axis=0).astype(BF16)
    me = lax.axis_index("head")
    size = keep_ref.shape[1]
    for step, ref in enumerate((keep_ref, *send_refs)):
        columns = pl.ds(pl.multiple_of((me ^ step) * size, HDIM), size)
        ref[...] = contract(attn, w_ref[:, columns], 0, 0).astype(ref.dtype)


def backward_kernel(
    q_own_ref, q_pair_ref, d_own_ref, d_pair_ref, kv0, kv1, kv2, kv3,
    stats_ref, stats_pair_ref, probs_ref, dprobs_ref,
    dq_own_ref, dq_pair_ref, dkv_ref, send_k_ref, send_v_ref, near_k_ref, near_v_ref,
):
    rows = q_own_ref.shape[0]
    keys = kv0.shape[0] // 2
    key_parts = (dkv_ref.at[:keys], send_k_ref.at[:keys], near_k_ref, send_k_ref.at[keys:])
    value_parts = (dkv_ref.at[keys:], near_v_ref, send_v_ref.at[:keys], send_v_ref.at[keys:])

    def swapped(row):
        return jnp.concatenate([row[:, rows:], row[:, :rows]], axis=1)

    for head in range(q_own_ref.shape[1] // HDIM):
        query = both_rows(q_own_ref, q_pair_ref, head)
        dattn = both_rows(d_own_ref, d_pair_ref, head)
        weight, weight_pair = merge_parts(
            stats_ref[head : head + 1], swapped(stats_pair_ref[head : head + 1])
        )
        delta = weight * stats_ref[8 + head : 9 + head]
        delta += weight_pair * swapped(stats_pair_ref[8 + head : 9 + head])
        features = slice(head * HDIM, (head + 1) * HDIM)
        dquery = None
        for step, ref in enumerate((kv0, kv1, kv2, kv3)):
            begin = (head * SQUARE + step) * keys
            probs = (probs_ref[begin : begin + keys].astype(F32) * weight).astype(BF16)
            dprobs = dprobs_ref[begin : begin + keys]
            dscores = (probs.astype(F32) * (dprobs - delta)).astype(BF16)
            key_part, value_part = key_parts[step], value_parts[step]
            grad_key = contract(dscores, query, 1, 0) * SCALE
            key_part[:, features] = grad_key.astype(key_part.dtype)
            value_part[:, features] = contract(probs, dattn, 1, 0).astype(value_part.dtype)
            part = contract(dscores, head_slice(ref[:keys], head), 0, 0)
            dquery = part if dquery is None else dquery + part
        dq_own_ref[:, features] = dquery[:rows] * SCALE
        dq_pair_ref[:, features] = (dquery[rows:] * SCALE).astype(BF16)


def pass_on_kernel(near_k_ref, near_v_ref, got_k_ref, got_v_ref, k_ref, v_ref):
    keys = near_k_ref.shape[0]
    k_ref[...] = (near_k_ref[...] + got_k_ref[keys:].astype(F32)).astype(BF16)
    v_ref[...] = (near_v_ref[...] + got_v_ref[keys:].astype(F32)).astype(BF16)


def finish_kernel(
    dq_ref, dq_pair_ref, dkv_ref, got_k_ref, got_v_ref, rest_k_ref, rest_v_ref,
    keep_ref, core_ref, near_ref, far_ref,
    q_out, k_out, v_out, hk_out, hv_out, out_ref,
):
    rows, capacity = k_out.shape[0], hk_out.shape[0]
    keys = rows + capacity

    def total(first, *others):
        for other in others:
            first = first + other.astype(F32)
        return first.astype(BF16)

    q_out[...] = total(dq_ref[...], dq_pair_ref[...])
    k_out[...] = total(dkv_ref[:rows], got_k_ref[:rows], rest_k_ref[:rows])
    hk_out[...] = total(dkv_ref[rows:keys], got_k_ref[rows:keys], rest_k_ref[rows:])
    v_out[...] = total(dkv_ref[keys : keys + rows], got_v_ref[:rows], rest_v_ref[:rows])
    hv_out[...] = total(dkv_ref[keys + rows :], got_v_ref[rows:keys], rest_v_ref[rows:])
    out_ref[...] = total(keep_ref[...], core_ref[...], near_ref[...], far_ref[...])


def blocked(sec_q, sec_k, sec_v, hist_k, hist_v, frame_levels, frame_counts, w_out, grad_out):
    shape = jax.ShapeDtypeStruct
    rows, width = sec_q.shape
    heads = width // HDIM
    capacity = hist_k.shape[0]
    keys = rows + capacity
    share = grad_out.shape[1]

    q_pair = swap(sec_q, "ctx", PAIR)
    grad_near = swap(grad_out, "head", 2)
    grad_near, q_pair = lax.optimization_barrier((grad_near, q_pair))
    grad_core = swap(grad_out, "head", 1)
    grad_far = swap(grad_near, "head", 1)
    kv0 = load_keys(sec_k, hist_k, sec_v, hist_v)
    kv2 = swap(kv0, "ctx", 2)
    kv1 = swap(kv0, "ctx", 1)
    kvs = [kv0, kv1, kv2, swap(kv2, "ctx", 1)]
    d_own = dattn_call(grad_out, w_out, grad_core, grad_near, grad_far)
    d_pair = swap(d_own, "ctx", PAIR)
    limits = local_call(
        limits_kernel,
        "limits",
        0.6,
        [shape((8, 2 * rows), jnp.int32)],
        (frame_levels, frame_counts),
        tables=2,
    )[0]
    stats, probs, dprobs = local_call(
        forward_kernel,
        "forward",
        1.5,
        [
            shape((16, 2 * rows), F32),
            shape((heads * SQUARE * keys, 2 * rows), BF16),
            shape((heads * SQUARE * keys, 2 * rows), F32),
        ],
        (limits, sec_q, q_pair, d_own, d_pair, *kvs),
    )
    stats_pair = swap(stats, "ctx", PAIR)
    attn_own, attn_pair = local_call(
        attn_kernel,
        "attn",
        0.5,
        [shape((width, rows), F32), shape((width, rows), BF16)],
        (*kvs, probs),
    )
    attn_own, probs = lax.optimization_barrier((attn_own, probs))
    dq_own, dq_pair, dkv_own, send_k, send_v, near_k, near_v = local_call(
        backward_kernel,
        "backward",
        1.1,
        [shape((rows, width), F32), shape((rows, width), BF16), shape((2 * keys, width), F32)]
        + [shape((2 * keys, width), BF16)] * 2
        + [shape((keys, width), F32)] * 2,
        (sec_q, q_pair, d_own, d_pair, *kvs, stats, stats_pair, probs, dprobs),
    )
    attn_got = swap(attn_pair, "ctx", PAIR)
    attn_got, send_k, send_v = lax.optimization_barrier((attn_got, send_k, send_v))
    got_k = swap(send_k, "ctx", 1)
    got_v = swap(send_v, "ctx", 2)
    dq_got = swap(dq_pair, "ctx", PAIR)
    rest_k, rest_v = local_call(
        pass_on_kernel,
        "pass_on",
        0.1,
        [shape((keys, width), BF16)] * 2,
        (near_k, near_v, got_k, got_v),
    )
    rest_k = swap(rest_k, "ctx", 2)
    rest_v = swap(rest_v, "ctx", 1)
    out_keep, *out_send = local_call(
        project_kernel,
        "project",
        0.6,
        [shape((rows, share), F32)] + [shape((rows, share), BF16)] * 3,
        (attn_own, attn_got, stats, stats_pair, w_out),
    )
    out_got = [swap(out_send[step - 1], "head", step) for step in (1, 2, 3)]
    grad_q, grad_k, grad_v, grad_hk, grad_hv, out = local_call(
        finish_kernel,
        "finish",
        0.9,
        [shape((rows, width), BF16)] * 3
        + [shape((capacity, width), BF16)] * 2
        + [shape((rows, share), BF16)],
        (dq_own, dq_got, dkv_own, got_k, got_v, rest_k, rest_v, out_keep, *out_got),
    )
    return out, grad_q, grad_k, grad_v, grad_hk, grad_hv


def gathered(sec_q, sec_k, sec_v, hist_k, hist_v, frame_levels, frame_counts, w_out, grad_out):
    rows = sec_q.shape[0]
    capacity = hist_k.shape[0]
    owners = lax.axis_size("ctx")
    me = lax.axis_index("ctx")
    frames = jnp.arange(FMAX, dtype=jnp.int32)[None, :]
    tokens = jnp.where(
        frames < frame_counts[:, None], jnp.right_shift(jnp.int32(FTOK), 2 * frame_levels), 0
    ).sum(axis=1)
    slots = jnp.arange(capacity, dtype=jnp.int32)
    all_valid = jnp.concatenate(
        [jnp.ones((owners * rows,), bool), (slots[None] < tokens[:, None]).reshape(-1)]
    )
    own_valid = jnp.concatenate(
        [jnp.ones((rows,), bool), slots < lax.dynamic_index_in_dim(tokens, me, keepdims=False)]
    )

    def everyone(block, axis=0):
        return lax.all_gather(block, "ctx", axis=axis, tiled=True)

    own_k, own_v = (jnp.concatenate(a, axis=0) for a in ((sec_k, hist_k), (sec_v, hist_v)))
    all_k = jnp.concatenate([everyone(sec_k), everyone(hist_k)], axis=0)
    all_v = jnp.concatenate([everyone(sec_v), everyone(hist_v)], axis=0)
    d_attn = contract(lax.all_gather(grad_out, "head", axis=1, tiled=True), w_out, 1, 1).astype(BF16)
    all_q, all_d = everyone(sec_q), everyone(d_attn)

    def probs_and_dscores(query, key, value, dattn, valid, lse, delta):
        scores = contract(query, key, 1, 1) * SCALE
        probs = jnp.where(valid[None, :], jnp.exp(scores - lse), 0.0).astype(BF16)
        dprobs = contract(dattn, value, 1, 1)
        return probs, (probs.astype(F32) * (dprobs - delta)).astype(BF16)

    attn_parts, q_parts, k_parts, v_parts = [], [], [], []
    for head in range(sec_q.shape[1] // HDIM):
        query, dattn, key, value = (head_slice(a, head) for a in (sec_q, d_attn, all_k, all_v))
        scores = jnp.where(all_valid[None, :], contract(query, key, 1, 1) * SCALE, NEG_FILL)
        lse = jax.nn.logsumexp(scores, axis=1, keepdims=True)
        probs = jnp.where(all_valid[None, :], jnp.exp(scores - lse), 0.0).astype(BF16)
        attn = contract(probs, value, 1, 0).astype(BF16)
        delta = jnp.sum(attn.astype(F32) * dattn.astype(F32), axis=1, keepdims=True)
        _, dscores = probs_and_dscores(query, key, value, dattn, all_valid, lse, delta)
        attn_parts.append(attn)
        q_parts.append(contract(dscores, key, 1, 0))
        query, dattn, key, value = (head_slice(a, head) for a in (all_q, all_d, own_k, own_v))
        probs, dscores = probs_and_dscores(
            query, key, value, dattn, own_valid, everyone(lse), everyone(delta)
        )
        k_parts.append(contract(dscores, query, 0, 0))
        v_parts.append(contract(probs, dattn, 0, 0))
    partial = contract(jnp.concatenate(attn_parts, axis=1), w_out, 1, 0).astype(BF16)
    out = lax.psum_scatter(partial, "head", scatter_dimension=1, tiled=True)
    grad_q, grad_k = (
        (jnp.concatenate(a, axis=1) * SCALE).astype(BF16) for a in (q_parts, k_parts)
    )
    grad_v = jnp.concatenate(v_parts, axis=1).astype(BF16)
    return out, grad_q, grad_k[:rows], grad_v[:rows], grad_k[rows:], grad_v[rows:]


def solution(mesh):
    split = P("ctx", "head")
    plan = blocked if (mesh.shape["ctx"], mesh.shape["head"]) == (2 * SQUARE, 4) else gathered
    return jax.shard_map(
        plan,
        mesh=mesh,
        in_specs=(split,) * 5 + (P(), P(), P("head", None), split),
        out_specs=(split,) * 6,
        check_vma=False,
    )
```

```python
import functools
import math

import jax
import jax.numpy as jnp
from jax import lax
from jax.experimental import pallas as pl
from jax.experimental.pallas import tpu as pltpu
from jax.sharding import PartitionSpec as P

HDIM = 128
FTOK = 16
FMAX = 2
NEG_FILL = -1e30
SCALE = 1.0 / math.sqrt(HDIM)
F32 = jnp.float32
BF16 = jnp.bfloat16
SQUARE = 4
HBM_BYTES = 3.69e6
PAIR = 4


def contract(left, right, left_dim, right_dim):
    return lax.dot_general(
        left, right, (((left_dim,), (right_dim,)), ((), ())), preferred_element_type=F32
    )


def head_slice(stacked, head):
    return stacked[:, head * HDIM : (head + 1) * HDIM]


def swap(block, axis, bit):
    count = lax.axis_size(axis)
    return lax.ppermute(block, axis, [(i, i ^ bit) for i in range(count)])


def cost_of(micros):
    return pl.CostEstimate(flops=0, bytes_accessed=int(micros * HBM_BYTES), transcendentals=0)


def local_call(body, name, micros, out_shapes, args, tables=0):
    spaces = [pltpu.SMEM] * tables + [pltpu.VMEM] * (len(args) - tables)
    return pl.pallas_call(
        body,
        name=name,
        out_shape=out_shapes,
        in_specs=[pl.BlockSpec(memory_space=space) for space in spaces],
        out_specs=[pl.BlockSpec(memory_space=pltpu.VMEM)] * len(out_shapes),
        compiler_params=pltpu.CompilerParams(vmem_limit_bytes=40 * 2**20),
        cost_estimate=cost_of(micros),
    )(*args)


def load_kernel(k_ref, hk_ref, v_ref, hv_ref, kv_out, kv_ref, sems):
    inward, outward, begin = [], [], 0
    for i, ref in enumerate((k_ref, hk_ref, v_ref, hv_ref)):
        part = pl.ds(begin, ref.shape[0])
        inward.append(pltpu.make_async_copy(ref, kv_ref.at[part], sems.at[0, i]))
        outward.append(pltpu.make_async_copy(kv_ref.at[part], kv_out.at[part], sems.at[1, i]))
        begin += ref.shape[0]
    for copy in inward:
        copy.start()
    for before, after in zip(inward, outward):
        before.wait()
        after.start()
    for copy in outward:
        copy.wait()


def load_keys(*arrays):
    rows = sum(a.shape[0] for a in arrays)
    width = arrays[0].shape[1]
    return pl.pallas_call(
        load_kernel,
        name="load",
        out_shape=jax.ShapeDtypeStruct((rows, width), BF16),
        in_specs=[pl.BlockSpec(memory_space=pl.ANY)] * len(arrays),
        out_specs=pl.BlockSpec(memory_space=pl.ANY),
        scratch_shapes=[pltpu.VMEM((rows, width), BF16), pltpu.SemaphoreType.DMA((2, len(arrays)))],
        compiler_params=pltpu.CompilerParams(vmem_limit_bytes=60 * 2**20),
        cost_estimate=cost_of(1.6),
    )(*arrays)


def pass_keys_kernel(kv1, kv2, key_ref, value_ref):
    keys = key_ref.shape[0]
    key_ref[...] = kv2[:keys]
    value_ref[...] = kv1[keys:]


def square_blocks(kv0, kv1, kv2, key3, value3):
    keys = key3.shape[0]
    pairs = [(ref.at[:keys], ref.at[keys:]) for ref in (kv0, kv1, kv2)]
    return pairs + [(key3, value3)]


def limits_kernel(levels_ref, counts_ref, limits_ref):
    me = lax.axis_index("ctx")
    row = lax.broadcasted_iota(jnp.int32, limits_ref.shape, 0)
    limits = jnp.zeros(limits_ref.shape, jnp.int32)
    for step in range(SQUARE):
        total = jnp.int32(0)
        for frame in range(FMAX):
            tokens = lax.shift_right_logical(jnp.int32(FTOK), 2 * levels_ref[me ^ step, frame])
            total += jnp.where(frame < counts_ref[me ^ step], tokens, 0)
        limits = jnp.where(row == step, total, limits)
    limits_ref[...] = limits


def dattn_kernel(own_hbm, w_hbm, core_ref, near_ref, far_ref, out_ref, own_ref, w_ref, sems):
    me = lax.axis_index("head")
    size = core_ref.shape[1]
    pieces = w_ref.shape[1] // HDIM
    own_copy = pltpu.make_async_copy(own_hbm, own_ref, sems.at[4, 0])
    own_copy.start()
    copies = []
    for step in range(4):
        columns = pl.ds(pl.multiple_of((me ^ step) * size, HDIM), size)
        for i in range(pieces):
            part = pl.ds(i * HDIM, HDIM)
            copies.append(
                pltpu.make_async_copy(
                    w_hbm.at[part, columns], w_ref.at[step, part], sems.at[step, i]
                )
            )
    for copy in copies:
        copy.start()
    own_copy.wait()
    total = None
    for step, ref in enumerate((own_ref, core_ref, near_ref, far_ref)):
        for copy in copies[step * pieces : (step + 1) * pieces]:
            copy.wait()
        part = contract(ref[...], w_ref[step], 1, 1)
        total = part if total is None else total + part
    out_ref[...] = total.astype(BF16)


def dattn_call(grad_own, w_out, *blocks):
    rows, share = grad_own.shape
    width = w_out.shape[0]
    anywhere, inside = pl.BlockSpec(memory_space=pl.ANY), pl.BlockSpec(memory_space=pltpu.VMEM)
    return pl.pallas_call(
        dattn_kernel,
        name="dattn",
        out_shape=jax.ShapeDtypeStruct((rows, width), BF16),
        in_specs=[anywhere, anywhere, inside, inside, inside],
        out_specs=inside,
        scratch_shapes=[
            pltpu.VMEM((rows, share), BF16),
            pltpu.VMEM((4, width, share), BF16),
            pltpu.SemaphoreType.DMA((5, width // HDIM)),
        ],
        compiler_params=pltpu.CompilerParams(vmem_limit_bytes=52 * 2**20),
        cost_estimate=cost_of(1.5),
    )(grad_own, w_out, *blocks)


def both_rows(own_ref, pair_ref, head):
    return jnp.concatenate(
        [head_slice(own_ref[...], head), head_slice(pair_ref[...], head)], axis=0
    )


def forward_kernel(
    limits_ref, q_own_ref, q_pair_ref, d_own_ref, d_pair_ref, kv0, kv1, kv2, key3, value3,
    stats_ref, probs_ref, dprobs_ref,
):
    rows = q_own_ref.shape[0]
    keys = key3.shape[0]
    blocks = square_blocks(kv0, kv1, kv2, key3, value3)
    stats_ref[...] = jnp.zeros_like(stats_ref)
    for head in range(q_own_ref.shape[1] // HDIM):
        query = both_rows(q_own_ref, q_pair_ref, head)
        dattn = both_rows(d_own_ref, d_pair_ref, head)
        scores = []
        for step, (key_ref, _) in enumerate(blocks):
            block = contract(head_slice(key_ref[...], head), query, 1, 1) * SCALE
            slot = lax.broadcasted_iota(jnp.int32, block.shape, 0)
            valid = slot < rows + limits_ref[step : step + 1]
            scores.append(jnp.where(valid, block, NEG_FILL))
        top = functools.reduce(
            jnp.maximum, [jnp.max(block, axis=0, keepdims=True) for block in scores]
        )
        weights = [jnp.exp(block - top) for block in scores]
        total = sum(jnp.sum(block, axis=0, keepdims=True) for block in weights)
        inverse = 1.0 / total
        delta = None
        for step, (_, value_ref) in enumerate(blocks):
            probs = weights[step] * inverse
            dprobs = contract(head_slice(value_ref[...], head), dattn, 1, 1)
            part = jnp.sum(probs * dprobs, axis=0, keepdims=True)
            delta = part if delta is None else delta + part
            begin = (head * SQUARE + step) * keys
            probs_ref[begin : begin + keys] = probs.astype(BF16)
            dprobs_ref[begin : begin + keys] = dprobs
        stats_ref[head : head + 1] = top + jnp.log(total)
        stats_ref[8 + head : 9 + head] = delta


def attn_kernel(kv0, kv1, kv2, key3, value3, probs_ref, own_ref, pair_ref):
    rows = own_ref.shape[1]
    keys = key3.shape[0]
    blocks = square_blocks(kv0, kv1, kv2, key3, value3)
    for head in range(own_ref.shape[0] // HDIM):
        attn = None
        for step, (_, value_ref) in enumerate(blocks):
            begin = (head * SQUARE + step) * keys
            part = contract(head_slice(value_ref[...], head), probs_ref[begin : begin + keys], 0, 0)
            attn = part if attn is None else attn + part
        features = slice(head * HDIM, (head + 1) * HDIM)
        own_ref[features] = attn[:, :rows]
        pair_ref[features] = attn[:, rows:].astype(BF16)


def merge_parts(mine, theirs):
    top = jnp.maximum(mine, theirs)
    weight, weight_pair = jnp.exp(mine - top), jnp.exp(theirs - top)
    inverse = 1.0 / (weight + weight_pair)
    return weight * inverse, weight_pair * inverse


def project_kernel(own_ref, pair_ref, stats_ref, stats_pair_ref, w_ref, keep_ref, *send_refs):
    rows = own_ref.shape[1]
    parts = []
    for head in range(own_ref.shape[0] // HDIM):
        features = slice(head * HDIM, (head + 1) * HDIM)
        weight, weight_pair = merge_parts(
            stats_ref[head : head + 1, :rows], stats_pair_ref[head : head + 1, rows:]
        )
        parts.append(own_ref[features] * weight + pair_ref[features].astype(F32) * weight_pair)
    attn = jnp.concatenate(parts, axis=0).astype(BF16)
    me = lax.axis_index("head")
    size = keep_ref.shape[1]
    for step, ref in enumerate((keep_ref, *send_refs)):
        columns = pl.ds(pl.multiple_of((me ^ step) * size, HDIM), size)
        ref[...] = contract(attn, w_ref[:, columns], 0, 0).astype(ref.dtype)


def backward_kernel(
    q_own_ref, q_pair_ref, d_own_ref, d_pair_ref, kv0, kv1, kv2, key3, value3,
    stats_ref, stats_pair_ref, probs_ref, dprobs_ref,
    dq_own_ref, dq_pair_ref, dkv_ref, send_k_ref, send_v_ref, near_k_ref, near_v_ref,
):
    rows = q_own_ref.shape[0]
    keys = key3.shape[0]
    blocks = square_blocks(kv0, kv1, kv2, key3, value3)
    key_parts = (dkv_ref.at[:keys], send_k_ref.at[:keys], near_k_ref, send_k_ref.at[keys:])
    value_parts = (dkv_ref.at[keys:], near_v_ref, send_v_ref.at[:keys], send_v_ref.at[keys:])

    def swapped(row):
        return jnp.concatenate([row[:, rows:], row[:, :rows]], axis=1)

    for head in range(q_own_ref.shape[1] // HDIM):
        query = both_rows(q_own_ref, q_pair_ref, head)
        dattn = both_rows(d_own_ref, d_pair_ref, head)
        weight, weight_pair = merge_parts(
            stats_ref[head : head + 1], swapped(stats_pair_ref[head : head + 1])
        )
        delta = weight * stats_ref[8 + head : 9 + head]
        delta += weight_pair * swapped(stats_pair_ref[8 + head : 9 + head])
        features = slice(head * HDIM, (head + 1) * HDIM)
        dquery = None
        for step, (key_ref, _) in enumerate(blocks):
            begin = (head * SQUARE + step) * keys
            probs = (probs_ref[begin : begin + keys].astype(F32) * weight).astype(BF16)
            dprobs = dprobs_ref[begin : begin + keys]
            dscores = (probs.astype(F32) * (dprobs - delta)).astype(BF16)
            key_part, value_part = key_parts[step], value_parts[step]
            grad_key = contract(dscores, query, 1, 0) * SCALE
            key_part[:, features] = grad_key.astype(key_part.dtype)
            value_part[:, features] = contract(probs, dattn, 1, 0).astype(value_part.dtype)
            part = contract(dscores, head_slice(key_ref[...], head), 0, 0)
            dquery = part if dquery is None else dquery + part
        dq_own_ref[:, features] = dquery[:rows] * SCALE
        dq_pair_ref[:, features] = (dquery[rows:] * SCALE).astype(BF16)


def pass_on_kernel(near_k_ref, near_v_ref, got_k_ref, got_v_ref, k_ref, v_ref):
    keys = near_k_ref.shape[0]
    k_ref[...] = (near_k_ref[...] + got_k_ref[keys:].astype(F32)).astype(BF16)
    v_ref[...] = (near_v_ref[...] + got_v_ref[keys:].astype(F32)).astype(BF16)


def finish_kernel(
    dq_ref, dq_pair_ref, dkv_ref, got_k_ref, got_v_ref, rest_k_ref, rest_v_ref,
    keep_ref, core_ref, near_ref, far_ref,
    q_out, k_out, v_out, hk_out, hv_out, out_ref,
):
    rows, capacity = k_out.shape[0], hk_out.shape[0]
    keys = rows + capacity

    def total(first, *others):
        for other in others:
            first = first + other.astype(F32)
        return first.astype(BF16)

    q_out[...] = total(dq_ref[...], dq_pair_ref[...])
    k_out[...] = total(dkv_ref[:rows], got_k_ref[:rows], rest_k_ref[:rows])
    hk_out[...] = total(dkv_ref[rows:keys], got_k_ref[rows:keys], rest_k_ref[rows:])
    v_out[...] = total(dkv_ref[keys : keys + rows], got_v_ref[:rows], rest_v_ref[:rows])
    hv_out[...] = total(dkv_ref[keys + rows :], got_v_ref[rows:keys], rest_v_ref[rows:])
    out_ref[...] = total(keep_ref[...], core_ref[...], near_ref[...], far_ref[...])


def blocked(sec_q, sec_k, sec_v, hist_k, hist_v, frame_levels, frame_counts, w_out, grad_out):
    shape = jax.ShapeDtypeStruct
    rows, width = sec_q.shape
    heads = width // HDIM
    capacity = hist_k.shape[0]
    keys = rows + capacity
    share = grad_out.shape[1]

    q_pair = swap(sec_q, "ctx", PAIR)
    grad_near = swap(grad_out, "head", 2)
    grad_core = swap(grad_out, "head", 1)
    grad_far = swap(grad_near, "head", 1)
    kv0 = load_keys(sec_k, hist_k, sec_v, hist_v)
    kv2 = swap(kv0, "ctx", 2)
    kv1 = swap(kv0, "ctx", 1)
    d_own = dattn_call(grad_out, w_out, grad_core, grad_near, grad_far)
    kv1, kv2, q_pair, d_own = lax.optimization_barrier((kv1, kv2, q_pair, d_own))
    key3, value3 = local_call(
        pass_keys_kernel, "pass_keys", 0.1, [shape((keys, width), BF16)] * 2, (kv1, kv2)
    )
    kvs = [kv0, kv1, kv2, swap(key3, "ctx", 1), swap(value3, "ctx", 2)]
    d_pair = swap(d_own, "ctx", PAIR)
    limits = local_call(
        limits_kernel,
        "limits",
        0.6,
        [shape((8, 2 * rows), jnp.int32)],
        (frame_levels, frame_counts),
        tables=2,
    )[0]
    stats, probs, dprobs = local_call(
        forward_kernel,
        "forward",
        1.5,
        [
            shape((16, 2 * rows), F32),
            shape((heads * SQUARE * keys, 2 * rows), BF16),
            shape((heads * SQUARE * keys, 2 * rows), F32),
        ],
        (limits, sec_q, q_pair, d_own, d_pair, *kvs),
    )
    stats_pair = swap(stats, "ctx", PAIR)
    attn_own, attn_pair = local_call(
        attn_kernel,
        "attn",
        0.5,
        [shape((width, rows), F32), shape((width, rows), BF16)],
        (*kvs, probs),
    )
    attn_own, probs = lax.optimization_barrier((attn_own, probs))
    dq_own, dq_pair, dkv_own, send_k, send_v, near_k, near_v = local_call(
        backward_kernel,
        "backward",
        1.1,
        [shape((rows, width), F32), shape((rows, width), BF16), shape((2 * keys, width), F32)]
        + [shape((2 * keys, width), BF16)] * 2
        + [shape((keys, width), F32)] * 2,
        (sec_q, q_pair, d_own, d_pair, *kvs, stats, stats_pair, probs, dprobs),
    )
    attn_got = swap(attn_pair, "ctx", PAIR)
    attn_got, send_k, send_v = lax.optimization_barrier((attn_got, send_k, send_v))
    got_k = swap(send_k, "ctx", 1)
    got_v = swap(send_v, "ctx", 2)
    dq_got = swap(dq_pair, "ctx", PAIR)
    rest_k, rest_v = local_call(
        pass_on_kernel,
        "pass_on",
        0.1,
        [shape((keys, width), BF16)] * 2,
        (near_k, near_v, got_k, got_v),
    )
    rest_k = swap(rest_k, "ctx", 2)
    rest_v = swap(rest_v, "ctx", 1)
    out_keep, *out_send = local_call(
        project_kernel,
        "project",
        0.6,
        [shape((rows, share), F32)] + [shape((rows, share), BF16)] * 3,
        (attn_own, attn_got, stats, stats_pair, w_out),
    )
    out_got = [swap(out_send[step - 1], "head", step) for step in (1, 2, 3)]
    grad_q, grad_k, grad_v, grad_hk, grad_hv, out = local_call(
        finish_kernel,
        "finish",
        0.9,
        [shape((rows, width), BF16)] * 3
        + [shape((capacity, width), BF16)] * 2
        + [shape((rows, share), BF16)],
        (dq_own, dq_got, dkv_own, got_k, got_v, rest_k, rest_v, out_keep, *out_got),
    )
    return out, grad_q, grad_k, grad_v, grad_hk, grad_hv


def gathered(sec_q, sec_k, sec_v, hist_k, hist_v, frame_levels, frame_counts, w_out, grad_out):
    rows = sec_q.shape[0]
    capacity = hist_k.shape[0]
    owners = lax.axis_size("ctx")
    me = lax.axis_index("ctx")
    frames = jnp.arange(FMAX, dtype=jnp.int32)[None, :]
    tokens = jnp.where(
        frames < frame_counts[:, None], jnp.right_shift(jnp.int32(FTOK), 2 * frame_levels), 0
    ).sum(axis=1)
    slots = jnp.arange(capacity, dtype=jnp.int32)
    all_valid = jnp.concatenate(
        [jnp.ones((owners * rows,), bool), (slots[None] < tokens[:, None]).reshape(-1)]
    )
    own_valid = jnp.concatenate(
        [jnp.ones((rows,), bool), slots < lax.dynamic_index_in_dim(tokens, me, keepdims=False)]
    )

    def everyone(block, axis=0):
        return lax.all_gather(block, "ctx", axis=axis, tiled=True)

    own_k, own_v = (jnp.concatenate(a, axis=0) for a in ((sec_k, hist_k), (sec_v, hist_v)))
    all_k = jnp.concatenate([everyone(sec_k), everyone(hist_k)], axis=0)
    all_v = jnp.concatenate([everyone(sec_v), everyone(hist_v)], axis=0)
    d_attn = contract(lax.all_gather(grad_out, "head", axis=1, tiled=True), w_out, 1, 1).astype(BF16)
    all_q, all_d = everyone(sec_q), everyone(d_attn)

    def probs_and_dscores(query, key, value, dattn, valid, lse, delta):
        scores = contract(query, key, 1, 1) * SCALE
        probs = jnp.where(valid[None, :], jnp.exp(scores - lse), 0.0).astype(BF16)
        dprobs = contract(dattn, value, 1, 1)
        return probs, (probs.astype(F32) * (dprobs - delta)).astype(BF16)

    attn_parts, q_parts, k_parts, v_parts = [], [], [], []
    for head in range(sec_q.shape[1] // HDIM):
        query, dattn, key, value = (head_slice(a, head) for a in (sec_q, d_attn, all_k, all_v))
        scores = jnp.where(all_valid[None, :], contract(query, key, 1, 1) * SCALE, NEG_FILL)
        lse = jax.nn.logsumexp(scores, axis=1, keepdims=True)
        probs = jnp.where(all_valid[None, :], jnp.exp(scores - lse), 0.0).astype(BF16)
        attn = contract(probs, value, 1, 0).astype(BF16)
        delta = jnp.sum(attn.astype(F32) * dattn.astype(F32), axis=1, keepdims=True)
        _, dscores = probs_and_dscores(query, key, value, dattn, all_valid, lse, delta)
        attn_parts.append(attn)
        q_parts.append(contract(dscores, key, 1, 0))
        query, dattn, key, value = (head_slice(a, head) for a in (all_q, all_d, own_k, own_v))
        probs, dscores = probs_and_dscores(
            query, key, value, dattn, own_valid, everyone(lse), everyone(delta)
        )
        k_parts.append(contract(dscores, query, 0, 0))
        v_parts.append(contract(probs, dattn, 0, 0))
    partial = contract(jnp.concatenate(attn_parts, axis=1), w_out, 1, 0).astype(BF16)
    out = lax.psum_scatter(partial, "head", scatter_dimension=1, tiled=True)
    grad_q, grad_k = (
        (jnp.concatenate(a, axis=1) * SCALE).astype(BF16) for a in (q_parts, k_parts)
    )
    grad_v = jnp.concatenate(v_parts, axis=1).astype(BF16)
    return out, grad_q, grad_k[:rows], grad_v[:rows], grad_k[rows:], grad_v[rows:]


def solution(mesh):
    split = P("ctx", "head")
    plan = blocked if (mesh.shape["ctx"], mesh.shape["head"]) == (2 * SQUARE, 4) else gathered
    return jax.shard_map(
        plan,
        mesh=mesh,
        in_specs=(split,) * 5 + (P(), P(), P("head", None), split),
        out_specs=(split,) * 6,
        check_vma=False,
    )
```

```python
import functools
import math

import jax
import jax.numpy as jnp
from jax import lax
from jax.experimental import pallas as pl
from jax.experimental.pallas import tpu as pltpu
from jax.sharding import PartitionSpec as P

HDIM = 128
FTOK = 16
FMAX = 2
NEG_FILL = -1e30
SCALE = 1.0 / math.sqrt(HDIM)
F32 = jnp.float32
BF16 = jnp.bfloat16
SQUARE = 4
HBM_BYTES = 3.69e6
PAIR = 4


def contract(left, right, left_dim, right_dim):
    return lax.dot_general(
        left, right, (((left_dim,), (right_dim,)), ((), ())), preferred_element_type=F32
    )


def head_slice(stacked, head):
    return stacked[:, head * HDIM : (head + 1) * HDIM]


def swap(block, axis, bit):
    count = lax.axis_size(axis)
    return lax.ppermute(block, axis, [(i, i ^ bit) for i in range(count)])


def cost_of(micros):
    return pl.CostEstimate(flops=0, bytes_accessed=int(micros * HBM_BYTES), transcendentals=0)


def local_call(body, name, micros, out_shapes, args, tables=0):
    spaces = [pltpu.SMEM] * tables + [pltpu.VMEM] * (len(args) - tables)
    return pl.pallas_call(
        body,
        name=name,
        out_shape=out_shapes,
        in_specs=[pl.BlockSpec(memory_space=space) for space in spaces],
        out_specs=[pl.BlockSpec(memory_space=pltpu.VMEM)] * len(out_shapes),
        compiler_params=pltpu.CompilerParams(vmem_limit_bytes=40 * 2**20),
        cost_estimate=cost_of(micros),
    )(*args)


def load_kernel(k_ref, hk_ref, v_ref, hv_ref, kv_out, kv_ref, sems):
    inward, outward, begin = [], [], 0
    for i, ref in enumerate((k_ref, hk_ref, v_ref, hv_ref)):
        part = pl.ds(begin, ref.shape[0])
        inward.append(pltpu.make_async_copy(ref, kv_ref.at[part], sems.at[0, i]))
        outward.append(pltpu.make_async_copy(kv_ref.at[part], kv_out.at[part], sems.at[1, i]))
        begin += ref.shape[0]
    for copy in inward:
        copy.start()
    for before, after in zip(inward, outward):
        before.wait()
        after.start()
    for copy in outward:
        copy.wait()


def load_keys(*arrays):
    rows = sum(a.shape[0] for a in arrays)
    width = arrays[0].shape[1]
    return pl.pallas_call(
        load_kernel,
        name="load",
        out_shape=jax.ShapeDtypeStruct((rows, width), BF16),
        in_specs=[pl.BlockSpec(memory_space=pl.ANY)] * len(arrays),
        out_specs=pl.BlockSpec(memory_space=pl.ANY),
        scratch_shapes=[pltpu.VMEM((rows, width), BF16), pltpu.SemaphoreType.DMA((2, len(arrays)))],
        compiler_params=pltpu.CompilerParams(vmem_limit_bytes=60 * 2**20),
        cost_estimate=cost_of(1.6),
    )(*arrays)


def pass_keys_kernel(kv1, kv2, key_ref, value_ref):
    keys = key_ref.shape[0]
    key_ref[...] = kv2[:keys]
    value_ref[...] = kv1[keys:]


def square_blocks(kv0, kv1, kv2, key3, value3):
    keys = key3.shape[0]
    pairs = [(ref.at[:keys], ref.at[keys:]) for ref in (kv0, kv1, kv2)]
    return pairs + [(key3, value3)]


def limits_kernel(levels_ref, counts_ref, limits_ref):
    me = lax.axis_index("ctx")
    row = lax.broadcasted_iota(jnp.int32, limits_ref.shape, 0)
    limits = jnp.zeros(limits_ref.shape, jnp.int32)
    for step in range(SQUARE):
        total = jnp.int32(0)
        for frame in range(FMAX):
            tokens = lax.shift_right_logical(jnp.int32(FTOK), 2 * levels_ref[me ^ step, frame])
            total += jnp.where(frame < counts_ref[me ^ step], tokens, 0)
        limits = jnp.where(row == step, total, limits)
    limits_ref[...] = limits


def dattn_kernel(own_hbm, w_hbm, core_ref, near_ref, far_ref, out_ref, own_ref, w_ref, sems):
    me = lax.axis_index("head")
    size = core_ref.shape[1]
    pieces = w_ref.shape[1] // HDIM
    own_copy = pltpu.make_async_copy(own_hbm, own_ref, sems.at[4, 0])
    own_copy.start()
    copies = []
    for step in range(4):
        columns = pl.ds(pl.multiple_of((me ^ step) * size, HDIM), size)
        for i in range(pieces):
            part = pl.ds(i * HDIM, HDIM)
            copies.append(
                pltpu.make_async_copy(
                    w_hbm.at[part, columns], w_ref.at[step, part], sems.at[step, i]
                )
            )
    for copy in copies:
        copy.start()
    own_copy.wait()
    total = None
    for step, ref in enumerate((own_ref, core_ref, near_ref, far_ref)):
        for copy in copies[step * pieces : (step + 1) * pieces]:
            copy.wait()
        part = contract(ref[...], w_ref[step], 1, 1)
        total = part if total is None else total + part
    out_ref[...] = total.astype(BF16)


def dattn_call(grad_own, w_out, *blocks):
    rows, share = grad_own.shape
    width = w_out.shape[0]
    anywhere, inside = pl.BlockSpec(memory_space=pl.ANY), pl.BlockSpec(memory_space=pltpu.VMEM)
    return pl.pallas_call(
        dattn_kernel,
        name="dattn",
        out_shape=jax.ShapeDtypeStruct((rows, width), BF16),
        in_specs=[anywhere, anywhere, inside, inside, inside],
        out_specs=inside,
        scratch_shapes=[
            pltpu.VMEM((rows, share), BF16),
            pltpu.VMEM((4, width, share), BF16),
            pltpu.SemaphoreType.DMA((5, width // HDIM)),
        ],
        compiler_params=pltpu.CompilerParams(vmem_limit_bytes=52 * 2**20),
        cost_estimate=cost_of(1.5),
    )(grad_own, w_out, *blocks)


def both_rows(own_ref, pair_ref, head):
    return jnp.concatenate(
        [head_slice(own_ref[...], head), head_slice(pair_ref[...], head)], axis=0
    )


def scores_kernel(
    limits_ref, q_own_ref, q_pair_ref, kv0, kv1, kv2, key3, value3, lse_ref, probs_ref
):
    rows = q_own_ref.shape[0]
    keys = key3.shape[0]
    blocks = square_blocks(kv0, kv1, kv2, key3, value3)
    lse_ref[...] = jnp.zeros_like(lse_ref)
    for head in range(q_own_ref.shape[1] // HDIM):
        query = both_rows(q_own_ref, q_pair_ref, head)
        scores = []
        for step, (key_ref, _) in enumerate(blocks):
            block = contract(head_slice(key_ref[...], head), query, 1, 1) * SCALE
            slot = lax.broadcasted_iota(jnp.int32, block.shape, 0)
            valid = slot < rows + limits_ref[step : step + 1]
            scores.append(jnp.where(valid, block, NEG_FILL))
        top = functools.reduce(
            jnp.maximum, [jnp.max(block, axis=0, keepdims=True) for block in scores]
        )
        weights = [jnp.exp(block - top) for block in scores]
        total = sum(jnp.sum(block, axis=0, keepdims=True) for block in weights)
        inverse = 1.0 / total
        for step, block in enumerate(weights):
            begin = (head * SQUARE + step) * keys
            probs_ref[begin : begin + keys] = (block * inverse).astype(BF16)
        lse_ref[head : head + 1] = top + jnp.log(total)


def delta_kernel(
    lse_ref, probs_ref, d_own_ref, d_pair_ref, kv0, kv1, kv2, key3, value3, stats_ref, dprobs_ref
):
    keys = key3.shape[0]
    blocks = square_blocks(kv0, kv1, kv2, key3, value3)
    stats_ref[...] = jnp.zeros_like(stats_ref)
    stats_ref[: lse_ref.shape[0]] = lse_ref[...]
    for head in range(d_own_ref.shape[1] // HDIM):
        dattn = both_rows(d_own_ref, d_pair_ref, head)
        delta = None
        for step, (_, value_ref) in enumerate(blocks):
            part = pl.ds((head * SQUARE + step) * keys, keys)
            dprobs = contract(head_slice(value_ref[...], head), dattn, 1, 1)
            dprobs_ref[part] = dprobs
            share = jnp.sum(probs_ref[part].astype(F32) * dprobs, axis=0, keepdims=True)
            delta = share if delta is None else delta + share
        stats_ref[8 + head : 9 + head] = delta


def attn_kernel(kv0, kv1, kv2, key3, value3, probs_ref, own_ref, pair_ref):
    rows = own_ref.shape[1]
    keys = key3.shape[0]
    blocks = square_blocks(kv0, kv1, kv2, key3, value3)
    for head in range(own_ref.shape[0] // HDIM):
        attn = None
        for step, (_, value_ref) in enumerate(blocks):
            begin = (head * SQUARE + step) * keys
            part = contract(head_slice(value_ref[...], head), probs_ref[begin : begin + keys], 0, 0)
            attn = part if attn is None else attn + part
        features = slice(head * HDIM, (head + 1) * HDIM)
        own_ref[features] = attn[:, :rows]
        pair_ref[features] = attn[:, rows:].astype(BF16)


def merge_parts(mine, theirs):
    top = jnp.maximum(mine, theirs)
    weight, weight_pair = jnp.exp(mine - top), jnp.exp(theirs - top)
    inverse = 1.0 / (weight + weight_pair)
    return weight * inverse, weight_pair * inverse


def project_kernel(own_ref, pair_ref, stats_ref, stats_pair_ref, w_ref, keep_ref, *send_refs):
    rows = own_ref.shape[1]
    parts = []
    for head in range(own_ref.shape[0] // HDIM):
        features = slice(head * HDIM, (head + 1) * HDIM)
        weight, weight_pair = merge_parts(
            stats_ref[head : head + 1, :rows], stats_pair_ref[head : head + 1, rows:]
        )
        parts.append(own_ref[features] * weight + pair_ref[features].astype(F32) * weight_pair)
    attn = jnp.concatenate(parts, axis=0).astype(BF16)
    me = lax.axis_index("head")
    size = keep_ref.shape[1]
    for step, ref in enumerate((keep_ref, *send_refs)):
        columns = pl.ds(pl.multiple_of((me ^ step) * size, HDIM), size)
        ref[...] = contract(attn, w_ref[:, columns], 0, 0).astype(ref.dtype)


def backward_kernel(
    q_own_ref, q_pair_ref, d_own_ref, d_pair_ref, kv0, kv1, kv2, key3, value3,
    stats_ref, stats_pair_ref, probs_ref, dprobs_ref,
    dq_own_ref, dq_pair_ref, dkv_ref, send_k_ref, send_v_ref, near_k_ref, near_v_ref,
):
    rows = q_own_ref.shape[0]
    keys = key3.shape[0]
    blocks = square_blocks(kv0, kv1, kv2, key3, value3)
    key_parts = (dkv_ref.at[:keys], send_k_ref.at[:keys], near_k_ref, send_k_ref.at[keys:])
    value_parts = (dkv_ref.at[keys:], near_v_ref, send_v_ref.at[:keys], send_v_ref.at[keys:])

    def swapped(row):
        return jnp.concatenate([row[:, rows:], row[:, :rows]], axis=1)

    for head in range(q_own_ref.shape[1] // HDIM):
        query = both_rows(q_own_ref, q_pair_ref, head)
        dattn = both_rows(d_own_ref, d_pair_ref, head)
        weight, weight_pair = merge_parts(
            stats_ref[head : head + 1], swapped(stats_pair_ref[head : head + 1])
        )
        delta = weight * stats_ref[8 + head : 9 + head]
        delta += weight_pair * swapped(stats_pair_ref[8 + head : 9 + head])
        features = slice(head * HDIM, (head + 1) * HDIM)
        dquery = None
        for step, (key_ref, _) in enumerate(blocks):
            begin = (head * SQUARE + step) * keys
            probs = (probs_ref[begin : begin + keys].astype(F32) * weight).astype(BF16)
            dprobs = dprobs_ref[begin : begin + keys]
            dscores = (probs.astype(F32) * (dprobs - delta)).astype(BF16)
            key_part, value_part = key_parts[step], value_parts[step]
            grad_key = contract(dscores, query, 1, 0) * SCALE
            key_part[:, features] = grad_key.astype(key_part.dtype)
            value_part[:, features] = contract(probs, dattn, 1, 0).astype(value_part.dtype)
            part = contract(dscores, head_slice(key_ref[...], head), 0, 0)
            dquery = part if dquery is None else dquery + part
        dq_own_ref[:, features] = dquery[:rows] * SCALE
        dq_pair_ref[:, features] = (dquery[rows:] * SCALE).astype(BF16)


def pass_on_kernel(near_k_ref, near_v_ref, got_k_ref, got_v_ref, k_ref, v_ref):
    keys = near_k_ref.shape[0]
    k_ref[...] = (near_k_ref[...] + got_k_ref[keys:].astype(F32)).astype(BF16)
    v_ref[...] = (near_v_ref[...] + got_v_ref[keys:].astype(F32)).astype(BF16)


def finish_kernel(
    keep_ref, near_ref, far_ref, dq_ref, dq_pair_ref, core_ref,
    dkv_ref, got_k_ref, got_v_ref, rest_k_ref, rest_v_ref,
    q_out, k_out, v_out, hk_out, hv_out, out_ref,
):
    rows, capacity = k_out.shape[0], hk_out.shape[0]
    keys = rows + capacity

    def total(first, *others):
        for other in others:
            first = first + other.astype(F32)
        return first.astype(BF16)

    q_out[...] = total(dq_ref[...], dq_pair_ref[...])
    k_out[...] = total(dkv_ref[:rows], got_k_ref[:rows], rest_k_ref[:rows])
    hk_out[...] = total(dkv_ref[rows:keys], got_k_ref[rows:keys], rest_k_ref[rows:])
    v_out[...] = total(dkv_ref[keys : keys + rows], got_v_ref[:rows], rest_v_ref[:rows])
    hv_out[...] = total(dkv_ref[keys + rows :], got_v_ref[rows:keys], rest_v_ref[rows:])
    out_ref[...] = total(keep_ref[...], core_ref[...], near_ref[...], far_ref[...])


def blocked(sec_q, sec_k, sec_v, hist_k, hist_v, frame_levels, frame_counts, w_out, grad_out):
    shape = jax.ShapeDtypeStruct
    rows, width = sec_q.shape
    heads = width // HDIM
    capacity = hist_k.shape[0]
    keys = rows + capacity
    share = grad_out.shape[1]

    q_pair = swap(sec_q, "ctx", PAIR)
    grad_near = swap(grad_out, "head", 2)
    grad_core = swap(grad_out, "head", 1)
    grad_far = swap(grad_near, "head", 1)
    kv0 = load_keys(sec_k, hist_k, sec_v, hist_v)
    kv2 = swap(kv0, "ctx", 2)
    kv1 = swap(kv0, "ctx", 1)
    d_own = dattn_call(grad_out, w_out, grad_core, grad_near, grad_far)
    kv1, kv2, q_pair, d_own = lax.optimization_barrier((kv1, kv2, q_pair, d_own))
    key3, value3 = local_call(
        pass_keys_kernel, "pass_keys", 0.1, [shape((keys, width), BF16)] * 2, (kv1, kv2)
    )
    kvs = [kv0, kv1, kv2, swap(key3, "ctx", 1), swap(value3, "ctx", 2)]
    d_pair = swap(d_own, "ctx", PAIR)
    limits = local_call(
        limits_kernel,
        "limits",
        0.6,
        [shape((8, 2 * rows), jnp.int32)],
        (frame_levels, frame_counts),
        tables=2,
    )[0]
    lse, probs = local_call(
        scores_kernel,
        "scores",
        0.9,
        [shape((8, 2 * rows), F32), shape((heads * SQUARE * keys, 2 * rows), BF16)],
        (limits, sec_q, q_pair, *kvs),
    )
    attn_own, attn_pair = local_call(
        attn_kernel,
        "attn",
        0.5,
        [shape((width, rows), F32), shape((width, rows), BF16)],
        (*kvs, probs),
    )
    lse, attn_own = lax.optimization_barrier((lse, attn_own))
    stats, dprobs = local_call(
        delta_kernel,
        "delta",
        0.7,
        [shape((16, 2 * rows), F32), shape((heads * SQUARE * keys, 2 * rows), F32)],
        (lse, probs, d_own, d_pair, *kvs),
    )
    stats_pair = swap(stats, "ctx", PAIR)
    dq_own, dq_pair, dkv_own, send_k, send_v, near_k, near_v = local_call(
        backward_kernel,
        "backward",
        1.1,
        [shape((rows, width), F32), shape((rows, width), BF16), shape((2 * keys, width), F32)]
        + [shape((2 * keys, width), BF16)] * 2
        + [shape((keys, width), F32)] * 2,
        (sec_q, q_pair, d_own, d_pair, *kvs, stats, stats_pair, probs, dprobs),
    )
    attn_got = swap(attn_pair, "ctx", PAIR)
    attn_got, send_k, send_v = lax.optimization_barrier((attn_got, send_k, send_v))
    got_k = swap(send_k, "ctx", 1)
    got_v = swap(send_v, "ctx", 2)
    rest_k, rest_v = local_call(
        pass_on_kernel,
        "pass_on",
        0.1,
        [shape((keys, width), BF16)] * 2,
        (near_k, near_v, got_k, got_v),
    )
    rest_k = swap(rest_k, "ctx", 2)
    rest_v = swap(rest_v, "ctx", 1)
    out_keep, *out_send = local_call(
        project_kernel,
        "project",
        0.6,
        [shape((rows, share), F32)] + [shape((rows, share), BF16)] * 3,
        (attn_own, attn_got, stats, stats_pair, w_out),
    )
    out_near, out_far = (swap(out_send[step - 1], "head", step) for step in (2, 3))
    dq_got = swap(dq_pair, "ctx", PAIR)
    out_core = swap(out_send[0], "head", 1)
    grad_q, grad_k, grad_v, grad_hk, grad_hv, out = local_call(
        finish_kernel,
        "finish",
        0.9,
        [shape((rows, width), BF16)] * 3
        + [shape((capacity, width), BF16)] * 2
        + [shape((rows, share), BF16)],
        (
            out_keep, out_near, out_far, dq_own, dq_got, out_core,
            dkv_own, got_k, got_v, rest_k, rest_v,
        ),
    )
    return out, grad_q, grad_k, grad_v, grad_hk, grad_hv


def gathered(sec_q, sec_k, sec_v, hist_k, hist_v, frame_levels, frame_counts, w_out, grad_out):
    rows = sec_q.shape[0]
    capacity = hist_k.shape[0]
    owners = lax.axis_size("ctx")
    me = lax.axis_index("ctx")
    frames = jnp.arange(FMAX, dtype=jnp.int32)[None, :]
    tokens = jnp.where(
        frames < frame_counts[:, None], jnp.right_shift(jnp.int32(FTOK), 2 * frame_levels), 0
    ).sum(axis=1)
    slots = jnp.arange(capacity, dtype=jnp.int32)
    all_valid = jnp.concatenate(
        [jnp.ones((owners * rows,), bool), (slots[None] < tokens[:, None]).reshape(-1)]
    )
    own_valid = jnp.concatenate(
        [jnp.ones((rows,), bool), slots < lax.dynamic_index_in_dim(tokens, me, keepdims=False)]
    )

    def everyone(block, axis=0):
        return lax.all_gather(block, "ctx", axis=axis, tiled=True)

    own_k, own_v = (jnp.concatenate(a, axis=0) for a in ((sec_k, hist_k), (sec_v, hist_v)))
    all_k = jnp.concatenate([everyone(sec_k), everyone(hist_k)], axis=0)
    all_v = jnp.concatenate([everyone(sec_v), everyone(hist_v)], axis=0)
    d_attn = contract(lax.all_gather(grad_out, "head", axis=1, tiled=True), w_out, 1, 1).astype(BF16)
    all_q, all_d = everyone(sec_q), everyone(d_attn)

    def probs_and_dscores(query, key, value, dattn, valid, lse, delta):
        scores = contract(query, key, 1, 1) * SCALE
        probs = jnp.where(valid[None, :], jnp.exp(scores - lse), 0.0).astype(BF16)
        dprobs = contract(dattn, value, 1, 1)
        return probs, (probs.astype(F32) * (dprobs - delta)).astype(BF16)

    attn_parts, q_parts, k_parts, v_parts = [], [], [], []
    for head in range(sec_q.shape[1] // HDIM):
        query, dattn, key, value = (head_slice(a, head) for a in (sec_q, d_attn, all_k, all_v))
        scores = jnp.where(all_valid[None, :], contract(query, key, 1, 1) * SCALE, NEG_FILL)
        lse = jax.nn.logsumexp(scores, axis=1, keepdims=True)
        probs = jnp.where(all_valid[None, :], jnp.exp(scores - lse), 0.0).astype(BF16)
        attn = contract(probs, value, 1, 0).astype(BF16)
        delta = jnp.sum(attn.astype(F32) * dattn.astype(F32), axis=1, keepdims=True)
        _, dscores = probs_and_dscores(query, key, value, dattn, all_valid, lse, delta)
        attn_parts.append(attn)
        q_parts.append(contract(dscores, key, 1, 0))
        query, dattn, key, value = (head_slice(a, head) for a in (all_q, all_d, own_k, own_v))
        probs, dscores = probs_and_dscores(
            query, key, value, dattn, own_valid, everyone(lse), everyone(delta)
        )
        k_parts.append(contract(dscores, query, 0, 0))
        v_parts.append(contract(probs, dattn, 0, 0))
    partial = contract(jnp.concatenate(attn_parts, axis=1), w_out, 1, 0).astype(BF16)
    out = lax.psum_scatter(partial, "head", scatter_dimension=1, tiled=True)
    grad_q, grad_k = (
        (jnp.concatenate(a, axis=1) * SCALE).astype(BF16) for a in (q_parts, k_parts)
    )
    grad_v = jnp.concatenate(v_parts, axis=1).astype(BF16)
    return out, grad_q, grad_k[:rows], grad_v[:rows], grad_k[rows:], grad_v[rows:]


def solution(mesh):
    split = P("ctx", "head")
    plan = blocked if (mesh.shape["ctx"], mesh.shape["head"]) == (2 * SQUARE, 4) else gathered
    return jax.shard_map(
        plan,
        mesh=mesh,
        in_specs=(split,) * 5 + (P(), P(), P("head", None), split),
        out_specs=(split,) * 6,
        check_vma=False,
    )
```

```python
import functools
import math

import jax
import jax.numpy as jnp
from jax import lax
from jax.experimental import pallas as pl
from jax.experimental.pallas import tpu as pltpu
from jax.sharding import PartitionSpec as P

HDIM = 128
FTOK = 16
FMAX = 2
NEG_FILL = -1e30
SCALE = 1.0 / math.sqrt(HDIM)
F32 = jnp.float32
BF16 = jnp.bfloat16
SQUARE = 4
HBM_BYTES = 3.69e6
PAIR = 4


def contract(left, right, left_dim, right_dim):
    return lax.dot_general(
        left, right, (((left_dim,), (right_dim,)), ((), ())), preferred_element_type=F32
    )


def head_slice(stacked, head):
    return stacked[:, head * HDIM : (head + 1) * HDIM]


def swap(block, axis, bit):
    count = lax.axis_size(axis)
    return lax.ppermute(block, axis, [(i, i ^ bit) for i in range(count)])


def cost_of(micros):
    return pl.CostEstimate(flops=0, bytes_accessed=int(micros * HBM_BYTES), transcendentals=0)


def local_call(body, name, micros, out_shapes, args, tables=0):
    spaces = [pltpu.SMEM] * tables + [pltpu.VMEM] * (len(args) - tables)
    return pl.pallas_call(
        body,
        name=name,
        out_shape=out_shapes,
        in_specs=[pl.BlockSpec(memory_space=space) for space in spaces],
        out_specs=[pl.BlockSpec(memory_space=pltpu.VMEM)] * len(out_shapes),
        compiler_params=pltpu.CompilerParams(vmem_limit_bytes=40 * 2**20),
        cost_estimate=cost_of(micros),
    )(*args)


def load_kernel(k_ref, hk_ref, v_ref, hv_ref, kv_out, kv_ref, sems):
    inward, outward, begin = [], [], 0
    for i, ref in enumerate((k_ref, hk_ref, v_ref, hv_ref)):
        part = pl.ds(begin, ref.shape[0])
        inward.append(pltpu.make_async_copy(ref, kv_ref.at[part], sems.at[0, i]))
        outward.append(pltpu.make_async_copy(kv_ref.at[part], kv_out.at[part], sems.at[1, i]))
        begin += ref.shape[0]
    for copy in inward:
        copy.start()
    for before, after in zip(inward, outward):
        before.wait()
        after.start()
    for copy in outward:
        copy.wait()


def load_keys(*arrays):
    rows = sum(a.shape[0] for a in arrays)
    width = arrays[0].shape[1]
    return pl.pallas_call(
        load_kernel,
        name="load",
        out_shape=jax.ShapeDtypeStruct((rows, width), BF16),
        in_specs=[pl.BlockSpec(memory_space=pl.ANY)] * len(arrays),
        out_specs=pl.BlockSpec(memory_space=pl.ANY),
        scratch_shapes=[pltpu.VMEM((rows, width), BF16), pltpu.SemaphoreType.DMA((2, len(arrays)))],
        compiler_params=pltpu.CompilerParams(vmem_limit_bytes=60 * 2**20),
        cost_estimate=cost_of(1.6),
    )(*arrays)


def pass_keys_kernel(kv1, kv2, key_ref, value_ref):
    keys = key_ref.shape[0]
    key_ref[...] = kv2[:keys]
    value_ref[...] = kv1[keys:]


def square_blocks(kv0, kv1, kv2, key3, value3):
    keys = key3.shape[0]
    pairs = [(ref.at[:keys], ref.at[keys:]) for ref in (kv0, kv1, kv2)]
    return pairs + [(key3, value3)]


def limits_kernel(levels_ref, counts_ref, limits_ref):
    me = lax.axis_index("ctx")
    row = lax.broadcasted_iota(jnp.int32, limits_ref.shape, 0)
    limits = jnp.zeros(limits_ref.shape, jnp.int32)
    for step in range(SQUARE):
        total = jnp.int32(0)
        for frame in range(FMAX):
            tokens = lax.shift_right_logical(jnp.int32(FTOK), 2 * levels_ref[me ^ step, frame])
            total += jnp.where(frame < counts_ref[me ^ step], tokens, 0)
        limits = jnp.where(row == step, total, limits)
    limits_ref[...] = limits


def dattn_kernel(own_ref, core_ref, near_ref, far_ref, w_ref, out_ref):
    me = lax.axis_index("head")
    size = own_ref.shape[1]
    total = None
    for step, ref in enumerate((own_ref, core_ref, near_ref, far_ref)):
        columns = pl.ds(pl.multiple_of((me ^ step) * size, HDIM), size)
        part = contract(ref[...], w_ref[:, columns], 1, 1)
        total = part if total is None else total + part
    out_ref[...] = total.astype(BF16)


def both_rows(own_ref, pair_ref, head):
    return jnp.concatenate(
        [head_slice(own_ref[...], head), head_slice(pair_ref[...], head)], axis=0
    )


def scores_kernel(
    limits_ref, q_own_ref, q_pair_ref, kv0, kv1, kv2, key3, value3, lse_ref, probs_ref
):
    rows = q_own_ref.shape[0]
    keys = key3.shape[0]
    blocks = square_blocks(kv0, kv1, kv2, key3, value3)
    lse_ref[...] = jnp.zeros_like(lse_ref)
    for head in range(q_own_ref.shape[1] // HDIM):
        query = both_rows(q_own_ref, q_pair_ref, head)
        scores = []
        for step, (key_ref, _) in enumerate(blocks):
            block = contract(head_slice(key_ref[...], head), query, 1, 1) * SCALE
            slot = lax.broadcasted_iota(jnp.int32, block.shape, 0)
            valid = slot < rows + limits_ref[step : step + 1]
            scores.append(jnp.where(valid, block, NEG_FILL))
        top = functools.reduce(
            jnp.maximum, [jnp.max(block, axis=0, keepdims=True) for block in scores]
        )
        weights = [jnp.exp(block - top) for block in scores]
        total = sum(jnp.sum(block, axis=0, keepdims=True) for block in weights)
        inverse = 1.0 / total
        for step, block in enumerate(weights):
            begin = (head * SQUARE + step) * keys
            probs_ref[begin : begin + keys] = (block * inverse).astype(BF16)
        lse_ref[head : head + 1] = top + jnp.log(total)


def delta_kernel(
    lse_ref, probs_ref, d_own_ref, d_pair_ref, kv0, kv1, kv2, key3, value3, stats_ref, dprobs_ref
):
    keys = key3.shape[0]
    blocks = square_blocks(kv0, kv1, kv2, key3, value3)
    stats_ref[...] = jnp.zeros_like(stats_ref)
    stats_ref[: lse_ref.shape[0]] = lse_ref[...]
    for head in range(d_own_ref.shape[1] // HDIM):
        dattn = both_rows(d_own_ref, d_pair_ref, head)
        delta = None
        for step, (_, value_ref) in enumerate(blocks):
            part = pl.ds((head * SQUARE + step) * keys, keys)
            dprobs = contract(head_slice(value_ref[...], head), dattn, 1, 1)
            dprobs_ref[part] = dprobs
            share = jnp.sum(probs_ref[part].astype(F32) * dprobs, axis=0, keepdims=True)
            delta = share if delta is None else delta + share
        stats_ref[8 + head : 9 + head] = delta


def attn_kernel(kv0, kv1, kv2, key3, value3, probs_ref, own_ref, pair_ref):
    rows = own_ref.shape[1]
    keys = key3.shape[0]
    blocks = square_blocks(kv0, kv1, kv2, key3, value3)
    for head in range(own_ref.shape[0] // HDIM):
        attn = None
        for step, (_, value_ref) in enumerate(blocks):
            begin = (head * SQUARE + step) * keys
            part = contract(head_slice(value_ref[...], head), probs_ref[begin : begin + keys], 0, 0)
            attn = part if attn is None else attn + part
        features = slice(head * HDIM, (head + 1) * HDIM)
        own_ref[features] = attn[:, :rows]
        pair_ref[features] = attn[:, rows:].astype(BF16)


def merge_parts(mine, theirs):
    top = jnp.maximum(mine, theirs)
    weight, weight_pair = jnp.exp(mine - top), jnp.exp(theirs - top)
    inverse = 1.0 / (weight + weight_pair)
    return weight * inverse, weight_pair * inverse


def project_kernel(own_ref, pair_ref, stats_ref, stats_pair_ref, w_ref, keep_ref, *send_refs):
    rows = own_ref.shape[1]
    parts = []
    for head in range(own_ref.shape[0] // HDIM):
        features = slice(head * HDIM, (head + 1) * HDIM)
        weight, weight_pair = merge_parts(
            stats_ref[head : head + 1, :rows], stats_pair_ref[head : head + 1, rows:]
        )
        parts.append(own_ref[features] * weight + pair_ref[features].astype(F32) * weight_pair)
    attn = jnp.concatenate(parts, axis=0).astype(BF16)
    me = lax.axis_index("head")
    size = keep_ref.shape[1]
    for step, ref in enumerate((keep_ref, *send_refs)):
        columns = pl.ds(pl.multiple_of((me ^ step) * size, HDIM), size)
        ref[...] = contract(attn, w_ref[:, columns], 0, 0).astype(ref.dtype)


def backward_kernel(
    q_own_ref, q_pair_ref, d_own_ref, d_pair_ref, kv0, kv1, kv2, key3, value3,
    stats_ref, stats_pair_ref, probs_ref, dprobs_ref,
    dq_own_ref, dq_pair_ref, dkv_ref, send_k_ref, send_v_ref, near_k_ref, near_v_ref,
):
    rows = q_own_ref.shape[0]
    keys = key3.shape[0]
    blocks = square_blocks(kv0, kv1, kv2, key3, value3)
    key_parts = (dkv_ref.at[:keys], send_k_ref.at[:keys], near_k_ref, send_k_ref.at[keys:])
    value_parts = (dkv_ref.at[keys:], near_v_ref, send_v_ref.at[:keys], send_v_ref.at[keys:])

    def swapped(row):
        return jnp.concatenate([row[:, rows:], row[:, :rows]], axis=1)

    for head in range(q_own_ref.shape[1] // HDIM):
        query = both_rows(q_own_ref, q_pair_ref, head)
        dattn = both_rows(d_own_ref, d_pair_ref, head)
        weight, weight_pair = merge_parts(
            stats_ref[head : head + 1], swapped(stats_pair_ref[head : head + 1])
        )
        delta = weight * stats_ref[8 + head : 9 + head]
        delta += weight_pair * swapped(stats_pair_ref[8 + head : 9 + head])
        features = slice(head * HDIM, (head + 1) * HDIM)
        dquery = None
        for step, (key_ref, _) in enumerate(blocks):
            begin = (head * SQUARE + step) * keys
            probs = (probs_ref[begin : begin + keys].astype(F32) * weight).astype(BF16)
            dprobs = dprobs_ref[begin : begin + keys]
            dscores = (probs.astype(F32) * (dprobs - delta)).astype(BF16)
            key_part, value_part = key_parts[step], value_parts[step]
            grad_key = contract(dscores, query, 1, 0) * SCALE
            key_part[:, features] = grad_key.astype(key_part.dtype)
            value_part[:, features] = contract(probs, dattn, 1, 0).astype(value_part.dtype)
            part = contract(dscores, head_slice(key_ref[...], head), 0, 0)
            dquery = part if dquery is None else dquery + part
        dq_own_ref[:, features] = dquery[:rows] * SCALE
        dq_pair_ref[:, features] = (dquery[rows:] * SCALE).astype(BF16)


def pass_on_kernel(near_k_ref, near_v_ref, got_k_ref, got_v_ref, k_ref, v_ref):
    keys = near_k_ref.shape[0]
    k_ref[...] = (near_k_ref[...] + got_k_ref[keys:].astype(F32)).astype(BF16)
    v_ref[...] = (near_v_ref[...] + got_v_ref[keys:].astype(F32)).astype(BF16)


def finish_kernel(
    keep_ref, near_ref, far_ref, dq_ref, dq_pair_ref, core_ref,
    dkv_ref, got_k_ref, got_v_ref, rest_k_ref, rest_v_ref,
    q_out, k_out, v_out, hk_out, hv_out, out_ref,
):
    rows, capacity = k_out.shape[0], hk_out.shape[0]
    keys = rows + capacity

    def total(first, *others):
        for other in others:
            first = first + other.astype(F32)
        return first.astype(BF16)

    q_out[...] = total(dq_ref[...], dq_pair_ref[...])
    k_out[...] = total(dkv_ref[:rows], got_k_ref[:rows], rest_k_ref[:rows])
    hk_out[...] = total(dkv_ref[rows:keys], got_k_ref[rows:keys], rest_k_ref[rows:])
    v_out[...] = total(dkv_ref[keys : keys + rows], got_v_ref[:rows], rest_v_ref[:rows])
    hv_out[...] = total(dkv_ref[keys + rows :], got_v_ref[rows:keys], rest_v_ref[rows:])
    out_ref[...] = total(keep_ref[...], core_ref[...], near_ref[...], far_ref[...])


def blocked(sec_q, sec_k, sec_v, hist_k, hist_v, frame_levels, frame_counts, w_out, grad_out):
    shape = jax.ShapeDtypeStruct
    rows, width = sec_q.shape
    heads = width // HDIM
    capacity = hist_k.shape[0]
    keys = rows + capacity
    share = grad_out.shape[1]

    grad_near = swap(grad_out, "head", 2)
    grad_core = swap(grad_out, "head", 1)
    grad_far = swap(grad_near, "head", 1)
    kv0 = load_keys(sec_k, hist_k, sec_v, hist_v)
    kv2 = swap(kv0, "ctx", 2)
    kv1 = swap(kv0, "ctx", 1)
    d_own = local_call(
        dattn_kernel,
        "dattn",
        0.8,
        [shape((rows, width), BF16)],
        (grad_out, grad_core, grad_near, grad_far, w_out),
    )[0]
    kv1, kv2, d_own, sec_q = lax.optimization_barrier((kv1, kv2, d_own, sec_q))
    key3, value3 = local_call(
        pass_keys_kernel, "pass_keys", 0.1, [shape((keys, width), BF16)] * 2, (kv1, kv2)
    )
    kvs = [kv0, kv1, kv2, swap(key3, "ctx", 1), swap(value3, "ctx", 2)]
    q_pair = swap(sec_q, "ctx", PAIR)
    d_pair = swap(d_own, "ctx", PAIR)
    limits = local_call(
        limits_kernel,
        "limits",
        0.6,
        [shape((8, 2 * rows), jnp.int32)],
        (frame_levels, frame_counts),
        tables=2,
    )[0]
    lse, probs = local_call(
        scores_kernel,
        "scores",
        0.9,
        [shape((8, 2 * rows), F32), shape((heads * SQUARE * keys, 2 * rows), BF16)],
        (limits, sec_q, q_pair, *kvs),
    )
    attn_own, attn_pair = local_call(
        attn_kernel,
        "attn",
        0.5,
        [shape((width, rows), F32), shape((width, rows), BF16)],
        (*kvs, probs),
    )
    lse, attn_own = lax.optimization_barrier((lse, attn_own))
    stats, dprobs = local_call(
        delta_kernel,
        "delta",
        0.7,
        [shape((16, 2 * rows), F32), shape((heads * SQUARE * keys, 2 * rows), F32)],
        (lse, probs, d_own, d_pair, *kvs),
    )
    stats_pair = swap(stats, "ctx", PAIR)
    dq_own, dq_pair, dkv_own, send_k, send_v, near_k, near_v = local_call(
        backward_kernel,
        "backward",
        1.1,
        [shape((rows, width), F32), shape((rows, width), BF16), shape((2 * keys, width), F32)]
        + [shape((2 * keys, width), BF16)] * 2
        + [shape((keys, width), F32)] * 2,
        (sec_q, q_pair, d_own, d_pair, *kvs, stats, stats_pair, probs, dprobs),
    )
    attn_got = swap(attn_pair, "ctx", PAIR)
    attn_got, send_k, send_v = lax.optimization_barrier((attn_got, send_k, send_v))
    got_k = swap(send_k, "ctx", 1)
    got_v = swap(send_v, "ctx", 2)
    rest_k, rest_v = local_call(
        pass_on_kernel,
        "pass_on",
        0.1,
        [shape((keys, width), BF16)] * 2,
        (near_k, near_v, got_k, got_v),
    )
    rest_k = swap(rest_k, "ctx", 2)
    rest_v = swap(rest_v, "ctx", 1)
    out_keep, *out_send = local_call(
        project_kernel,
        "project",
        0.6,
        [shape((rows, share), F32)] + [shape((rows, share), BF16)] * 3,
        (attn_own, attn_got, stats, stats_pair, w_out),
    )
    out_near, out_far = (swap(out_send[step - 1], "head", step) for step in (2, 3))
    dq_got = swap(dq_pair, "ctx", PAIR)
    out_core = swap(out_send[0], "head", 1)
    grad_q, grad_k, grad_v, grad_hk, grad_hv, out = local_call(
        finish_kernel,
        "finish",
        0.9,
        [shape((rows, width), BF16)] * 3
        + [shape((capacity, width), BF16)] * 2
        + [shape((rows, share), BF16)],
        (
            out_keep, out_near, out_far, dq_own, dq_got, out_core,
            dkv_own, got_k, got_v, rest_k, rest_v,
        ),
    )
    return out, grad_q, grad_k, grad_v, grad_hk, grad_hv


def gathered(sec_q, sec_k, sec_v, hist_k, hist_v, frame_levels, frame_counts, w_out, grad_out):
    rows = sec_q.shape[0]
    capacity = hist_k.shape[0]
    owners = lax.axis_size("ctx")
    me = lax.axis_index("ctx")
    frames = jnp.arange(FMAX, dtype=jnp.int32)[None, :]
    tokens = jnp.where(
        frames < frame_counts[:, None], jnp.right_shift(jnp.int32(FTOK), 2 * frame_levels), 0
    ).sum(axis=1)
    slots = jnp.arange(capacity, dtype=jnp.int32)
    all_valid = jnp.concatenate(
        [jnp.ones((owners * rows,), bool), (slots[None] < tokens[:, None]).reshape(-1)]
    )
    own_valid = jnp.concatenate(
        [jnp.ones((rows,), bool), slots < lax.dynamic_index_in_dim(tokens, me, keepdims=False)]
    )

    def everyone(block, axis=0):
        return lax.all_gather(block, "ctx", axis=axis, tiled=True)

    own_k, own_v = (jnp.concatenate(a, axis=0) for a in ((sec_k, hist_k), (sec_v, hist_v)))
    all_k = jnp.concatenate([everyone(sec_k), everyone(hist_k)], axis=0)
    all_v = jnp.concatenate([everyone(sec_v), everyone(hist_v)], axis=0)
    d_attn = contract(lax.all_gather(grad_out, "head", axis=1, tiled=True), w_out, 1, 1).astype(BF16)
    all_q, all_d = everyone(sec_q), everyone(d_attn)

    def probs_and_dscores(query, key, value, dattn, valid, lse, delta):
        scores = contract(query, key, 1, 1) * SCALE
        probs = jnp.where(valid[None, :], jnp.exp(scores - lse), 0.0).astype(BF16)
        dprobs = contract(dattn, value, 1, 1)
        return probs, (probs.astype(F32) * (dprobs - delta)).astype(BF16)

    attn_parts, q_parts, k_parts, v_parts = [], [], [], []
    for head in range(sec_q.shape[1] // HDIM):
        query, dattn, key, value = (head_slice(a, head) for a in (sec_q, d_attn, all_k, all_v))
        scores = jnp.where(all_valid[None, :], contract(query, key, 1, 1) * SCALE, NEG_FILL)
        lse = jax.nn.logsumexp(scores, axis=1, keepdims=True)
        probs = jnp.where(all_valid[None, :], jnp.exp(scores - lse), 0.0).astype(BF16)
        attn = contract(probs, value, 1, 0).astype(BF16)
        delta = jnp.sum(attn.astype(F32) * dattn.astype(F32), axis=1, keepdims=True)
        _, dscores = probs_and_dscores(query, key, value, dattn, all_valid, lse, delta)
        attn_parts.append(attn)
        q_parts.append(contract(dscores, key, 1, 0))
        query, dattn, key, value = (head_slice(a, head) for a in (all_q, all_d, own_k, own_v))
        probs, dscores = probs_and_dscores(
            query, key, value, dattn, own_valid, everyone(lse), everyone(delta)
        )
        k_parts.append(contract(dscores, query, 0, 0))
        v_parts.append(contract(probs, dattn, 0, 0))
    partial = contract(jnp.concatenate(attn_parts, axis=1), w_out, 1, 0).astype(BF16)
    out = lax.psum_scatter(partial, "head", scatter_dimension=1, tiled=True)
    grad_q, grad_k = (
        (jnp.concatenate(a, axis=1) * SCALE).astype(BF16) for a in (q_parts, k_parts)
    )
    grad_v = jnp.concatenate(v_parts, axis=1).astype(BF16)
    return out, grad_q, grad_k[:rows], grad_v[:rows], grad_k[rows:], grad_v[rows:]


def solution(mesh):
    split = P("ctx", "head")
    plan = blocked if (mesh.shape["ctx"], mesh.shape["head"]) == (2 * SQUARE, 4) else gathered
    return jax.shard_map(
        plan,
        mesh=mesh,
        in_specs=(split,) * 5 + (P(), P(), P("head", None), split),
        out_specs=(split,) * 6,
        check_vma=False,
    )
```

```python
import functools
import math

import jax
import jax.numpy as jnp
from jax import lax
from jax.experimental import pallas as pl
from jax.experimental.pallas import tpu as pltpu
from jax.sharding import PartitionSpec as P

HDIM = 128
FTOK = 16
FMAX = 2
NEG_FILL = -1e30
SCALE = 1.0 / math.sqrt(HDIM)
F32 = jnp.float32
BF16 = jnp.bfloat16
SQUARE = 4
HBM_BYTES = 3.69e6
PAIR = 4


def contract(left, right, left_dim, right_dim):
    return lax.dot_general(
        left, right, (((left_dim,), (right_dim,)), ((), ())), preferred_element_type=F32
    )


def head_slice(stacked, head):
    return stacked[:, head * HDIM : (head + 1) * HDIM]


def swap(block, axis, bit):
    count = lax.axis_size(axis)
    return lax.ppermute(block, axis, [(i, i ^ bit) for i in range(count)])


def cost_of(micros):
    return pl.CostEstimate(flops=0, bytes_accessed=int(micros * HBM_BYTES), transcendentals=0)


def local_call(body, name, micros, out_shapes, args, tables=0):
    spaces = [pltpu.SMEM] * tables + [pltpu.VMEM] * (len(args) - tables)
    return pl.pallas_call(
        body,
        name=name,
        out_shape=out_shapes,
        in_specs=[pl.BlockSpec(memory_space=space) for space in spaces],
        out_specs=[pl.BlockSpec(memory_space=pltpu.VMEM)] * len(out_shapes),
        compiler_params=pltpu.CompilerParams(vmem_limit_bytes=40 * 2**20),
        cost_estimate=cost_of(micros),
    )(*args)


def load_kernel(k_ref, hk_ref, v_ref, hv_ref, kv_out, kv_ref, sems):
    inward, outward, begin = [], [], 0
    for i, ref in enumerate((k_ref, hk_ref, v_ref, hv_ref)):
        part = pl.ds(begin, ref.shape[0])
        inward.append(pltpu.make_async_copy(ref, kv_ref.at[part], sems.at[0, i]))
        outward.append(pltpu.make_async_copy(kv_ref.at[part], kv_out.at[part], sems.at[1, i]))
        begin += ref.shape[0]
    for copy in inward:
        copy.start()
    for before, after in zip(inward, outward):
        before.wait()
        after.start()
    for copy in outward:
        copy.wait()


def load_keys(*arrays):
    rows = sum(a.shape[0] for a in arrays)
    width = arrays[0].shape[1]
    return pl.pallas_call(
        load_kernel,
        name="load",
        out_shape=jax.ShapeDtypeStruct((rows, width), BF16),
        in_specs=[pl.BlockSpec(memory_space=pl.ANY)] * len(arrays),
        out_specs=pl.BlockSpec(memory_space=pl.ANY),
        scratch_shapes=[pltpu.VMEM((rows, width), BF16), pltpu.SemaphoreType.DMA((2, len(arrays)))],
        compiler_params=pltpu.CompilerParams(vmem_limit_bytes=60 * 2**20),
        cost_estimate=cost_of(1.6),
    )(*arrays)


def pass_keys_kernel(kv2, key_ref):
    key_ref[...] = kv2[: key_ref.shape[0]]


def pass_values_kernel(kv2, value_ref):
    value_ref[...] = kv2[value_ref.shape[0] :]


def square_blocks(kv0, kv1, kv2, key3, value3):
    keys = key3.shape[0]
    pairs = [(ref.at[:keys], ref.at[keys:]) for ref in (kv0, kv1, kv2)]
    return pairs + [(key3, value3)]


def limits_kernel(levels_ref, counts_ref, limits_ref):
    me = lax.axis_index("ctx")
    row = lax.broadcasted_iota(jnp.int32, limits_ref.shape, 0)
    limits = jnp.zeros(limits_ref.shape, jnp.int32)
    for step in range(SQUARE):
        total = jnp.int32(0)
        for frame in range(FMAX):
            tokens = lax.shift_right_logical(jnp.int32(FTOK), 2 * levels_ref[me ^ step, frame])
            total += jnp.where(frame < counts_ref[me ^ step], tokens, 0)
        limits = jnp.where(row == step, total, limits)
    limits_ref[...] = limits


def dattn_kernel(own_ref, core_ref, near_ref, far_ref, w_ref, out_ref):
    me = lax.axis_index("head")
    size = own_ref.shape[1]
    total = None
    for step, ref in enumerate((own_ref, core_ref, near_ref, far_ref)):
        columns = pl.ds(pl.multiple_of((me ^ step) * size, HDIM), size)
        part = contract(ref[...], w_ref[:, columns], 1, 1)
        total = part if total is None else total + part
    out_ref[...] = total.astype(BF16)


def both_rows(own_ref, pair_ref, head):
    return jnp.concatenate(
        [head_slice(own_ref[...], head), head_slice(pair_ref[...], head)], axis=0
    )


def scores_kernel(
    limits_ref, q_own_ref, q_pair_ref, kv0, kv1, kv2, key3, lse_ref, probs_ref
):
    rows = q_own_ref.shape[0]
    keys = key3.shape[0]
    blocks = [ref.at[:keys] for ref in (kv0, kv1, kv2)] + [key3]
    lse_ref[...] = jnp.zeros_like(lse_ref)
    for head in range(q_own_ref.shape[1] // HDIM):
        query = both_rows(q_own_ref, q_pair_ref, head)
        scores = []
        for step, key_ref in enumerate(blocks):
            block = contract(head_slice(key_ref[...], head), query, 1, 1) * SCALE
            slot = lax.broadcasted_iota(jnp.int32, block.shape, 0)
            valid = slot < rows + limits_ref[step : step + 1]
            scores.append(jnp.where(valid, block, NEG_FILL))
        top = functools.reduce(
            jnp.maximum, [jnp.max(block, axis=0, keepdims=True) for block in scores]
        )
        weights = [jnp.exp(block - top) for block in scores]
        total = sum(jnp.sum(block, axis=0, keepdims=True) for block in weights)
        inverse = 1.0 / total
        for step, block in enumerate(weights):
            begin = (head * SQUARE + step) * keys
            probs_ref[begin : begin + keys] = (block * inverse).astype(BF16)
        lse_ref[head : head + 1] = top + jnp.log(total)


def delta_kernel(
    lse_ref, probs_ref, d_own_ref, d_pair_ref, kv0, kv1, kv2, key3, value3, stats_ref, dprobs_ref
):
    keys = key3.shape[0]
    blocks = square_blocks(kv0, kv1, kv2, key3, value3)
    stats_ref[...] = jnp.zeros_like(stats_ref)
    stats_ref[: lse_ref.shape[0]] = lse_ref[...]
    for head in range(d_own_ref.shape[1] // HDIM):
        dattn = both_rows(d_own_ref, d_pair_ref, head)
        delta = None
        for step, (_, value_ref) in enumerate(blocks):
            part = pl.ds((head * SQUARE + step) * keys, keys)
            dprobs = contract(head_slice(value_ref[...], head), dattn, 1, 1)
            dprobs_ref[part] = dprobs
            share = jnp.sum(probs_ref[part].astype(F32) * dprobs, axis=0, keepdims=True)
            delta = share if delta is None else delta + share
        stats_ref[8 + head : 9 + head] = delta


def attn_kernel(kv0, kv1, kv2, key3, value3, probs_ref, own_ref, pair_ref):
    rows = own_ref.shape[1]
    keys = key3.shape[0]
    blocks = square_blocks(kv0, kv1, kv2, key3, value3)
    for head in range(own_ref.shape[0] // HDIM):
        attn = None
        for step, (_, value_ref) in enumerate(blocks):
            begin = (head * SQUARE + step) * keys
            part = contract(head_slice(value_ref[...], head), probs_ref[begin : begin + keys], 0, 0)
            attn = part if attn is None else attn + part
        features = slice(head * HDIM, (head + 1) * HDIM)
        own_ref[features] = attn[:, :rows]
        pair_ref[features] = attn[:, rows:].astype(BF16)


def merge_parts(mine, theirs):
    top = jnp.maximum(mine, theirs)
    weight, weight_pair = jnp.exp(mine - top), jnp.exp(theirs - top)
    inverse = 1.0 / (weight + weight_pair)
    return weight * inverse, weight_pair * inverse


def project_kernel(own_ref, pair_ref, stats_ref, stats_pair_ref, w_ref, keep_ref, *send_refs):
    rows = own_ref.shape[1]
    parts = []
    for head in range(own_ref.shape[0] // HDIM):
        features = slice(head * HDIM, (head + 1) * HDIM)
        weight, weight_pair = merge_parts(
            stats_ref[head : head + 1, :rows], stats_pair_ref[head : head + 1, rows:]
        )
        parts.append(own_ref[features] * weight + pair_ref[features].astype(F32) * weight_pair)
    attn = jnp.concatenate(parts, axis=0).astype(BF16)
    me = lax.axis_index("head")
    size = keep_ref.shape[1]
    for step, ref in enumerate((keep_ref, *send_refs)):
        columns = pl.ds(pl.multiple_of((me ^ step) * size, HDIM), size)
        ref[...] = contract(attn, w_ref[:, columns], 0, 0).astype(ref.dtype)


def backward_kernel(
    q_own_ref, q_pair_ref, d_own_ref, d_pair_ref, kv0, kv1, kv2, key3, value3,
    stats_ref, stats_pair_ref, probs_ref, dprobs_ref,
    dq_own_ref, dq_pair_ref, dkv_ref, send_k_ref, send_v_ref, near_k_ref, near_v_ref,
):
    rows = q_own_ref.shape[0]
    keys = key3.shape[0]
    blocks = square_blocks(kv0, kv1, kv2, key3, value3)
    key_parts = (dkv_ref.at[:keys], send_k_ref.at[:keys], near_k_ref, send_k_ref.at[keys:])
    value_parts = (dkv_ref.at[keys:], near_v_ref, send_v_ref.at[:keys], send_v_ref.at[keys:])

    def swapped(row):
        return jnp.concatenate([row[:, rows:], row[:, :rows]], axis=1)

    for head in range(q_own_ref.shape[1] // HDIM):
        query = both_rows(q_own_ref, q_pair_ref, head)
        dattn = both_rows(d_own_ref, d_pair_ref, head)
        weight, weight_pair = merge_parts(
            stats_ref[head : head + 1], swapped(stats_pair_ref[head : head + 1])
        )
        delta = weight * stats_ref[8 + head : 9 + head]
        delta += weight_pair * swapped(stats_pair_ref[8 + head : 9 + head])
        features = slice(head * HDIM, (head + 1) * HDIM)
        dquery = None
        for step, (key_ref, _) in enumerate(blocks):
            begin = (head * SQUARE + step) * keys
            probs = (probs_ref[begin : begin + keys].astype(F32) * weight).astype(BF16)
            dprobs = dprobs_ref[begin : begin + keys]
            dscores = (probs.astype(F32) * (dprobs - delta)).astype(BF16)
            key_part, value_part = key_parts[step], value_parts[step]
            grad_key = contract(dscores, query, 1, 0) * SCALE
            key_part[:, features] = grad_key.astype(key_part.dtype)
            value_part[:, features] = contract(probs, dattn, 1, 0).astype(value_part.dtype)
            part = contract(dscores, head_slice(key_ref[...], head), 0, 0)
            dquery = part if dquery is None else dquery + part
        dq_own_ref[:, features] = dquery[:rows] * SCALE
        dq_pair_ref[:, features] = (dquery[rows:] * SCALE).astype(BF16)


def pass_on_kernel(near_k_ref, near_v_ref, got_k_ref, got_v_ref, k_ref, v_ref):
    keys = near_k_ref.shape[0]
    k_ref[...] = (near_k_ref[...] + got_k_ref[keys:].astype(F32)).astype(BF16)
    v_ref[...] = (near_v_ref[...] + got_v_ref[keys:].astype(F32)).astype(BF16)


def finish_kernel(
    keep_ref, near_ref, far_ref, dq_ref, dq_pair_ref, core_ref,
    dkv_ref, got_k_ref, got_v_ref, rest_k_ref, rest_v_ref,
    q_out, k_out, v_out, hk_out, hv_out, out_ref,
):
    rows, capacity = k_out.shape[0], hk_out.shape[0]
    keys = rows + capacity

    def total(first, *others):
        for other in others:
            first = first + other.astype(F32)
        return first.astype(BF16)

    q_out[...] = total(dq_ref[...], dq_pair_ref[...])
    k_out[...] = total(dkv_ref[:rows], got_k_ref[:rows], rest_k_ref[:rows])
    hk_out[...] = total(dkv_ref[rows:keys], got_k_ref[rows:keys], rest_k_ref[rows:])
    v_out[...] = total(dkv_ref[keys : keys + rows], got_v_ref[:rows], rest_v_ref[:rows])
    hv_out[...] = total(dkv_ref[keys + rows :], got_v_ref[rows:keys], rest_v_ref[rows:])
    out_ref[...] = total(keep_ref[...], core_ref[...], near_ref[...], far_ref[...])


def blocked(sec_q, sec_k, sec_v, hist_k, hist_v, frame_levels, frame_counts, w_out, grad_out):
    shape = jax.ShapeDtypeStruct
    rows, width = sec_q.shape
    heads = width // HDIM
    capacity = hist_k.shape[0]
    keys = rows + capacity
    share = grad_out.shape[1]

    q_pair = swap(sec_q, "ctx", PAIR)
    grad_near = swap(grad_out, "head", 2)
    grad_core = swap(grad_out, "head", 1)
    grad_far = swap(grad_near, "head", 1)
    kv0 = load_keys(sec_k, hist_k, sec_v, hist_v)
    kv2 = swap(kv0, "ctx", 2)
    kv1 = swap(kv0, "ctx", 1)
    d_own = local_call(
        dattn_kernel,
        "dattn",
        0.8,
        [shape((rows, width), BF16)],
        (grad_out, grad_core, grad_near, grad_far, w_out),
    )[0]
    kv2, d_own = lax.optimization_barrier((kv2, d_own))
    key3 = local_call(pass_keys_kernel, "pass_keys", 0.1, [shape((keys, width), BF16)], (kv2,))[0]
    kv2_kept, q_pair, _ = lax.optimization_barrier((kv2, q_pair, key3))
    value3 = local_call(
        pass_values_kernel, "pass_values", 1.0, [shape((keys, width), BF16)], (kv2_kept,)
    )[0]
    kvs = [kv0, kv1, kv2, swap(key3, "ctx", 1), swap(value3, "ctx", 1)]
    d_pair = swap(d_own, "ctx", PAIR)
    limits = local_call(
        limits_kernel,
        "limits",
        0.6,
        [shape((8, 2 * rows), jnp.int32)],
        (frame_levels, frame_counts),
        tables=2,
    )[0]
    lse, probs = local_call(
        scores_kernel,
        "scores",
        0.9,
        [shape((8, 2 * rows), F32), shape((heads * SQUARE * keys, 2 * rows), BF16)],
        (limits, sec_q, q_pair, *kvs[:4]),
    )
    attn_own, attn_pair = local_call(
        attn_kernel,
        "attn",
        0.5,
        [shape((width, rows), F32), shape((width, rows), BF16)],
        (*kvs, probs),
    )
    lse, attn_own = lax.optimization_barrier((lse, attn_own))
    stats, dprobs = local_call(
        delta_kernel,
        "delta",
        0.7,
        [shape((16, 2 * rows), F32), shape((heads * SQUARE * keys, 2 * rows), F32)],
        (lse, probs, d_own, d_pair, *kvs),
    )
    stats_pair = swap(stats, "ctx", PAIR)
    dq_own, dq_pair, dkv_own, send_k, send_v, near_k, near_v = local_call(
        backward_kernel,
        "backward",
        1.1,
        [shape((rows, width), F32), shape((rows, width), BF16), shape((2 * keys, width), F32)]
        + [shape((2 * keys, width), BF16)] * 2
        + [shape((keys, width), F32)] * 2,
        (sec_q, q_pair, d_own, d_pair, *kvs, stats, stats_pair, probs, dprobs),
    )
    attn_got = swap(attn_pair, "ctx", PAIR)
    attn_got, send_k, send_v = lax.optimization_barrier((attn_got, send_k, send_v))
    got_k = swap(send_k, "ctx", 1)
    got_v = swap(send_v, "ctx", 2)
    rest_k, rest_v = local_call(
        pass_on_kernel,
        "pass_on",
        0.1,
        [shape((keys, width), BF16)] * 2,
        (near_k, near_v, got_k, got_v),
    )
    rest_k = swap(rest_k, "ctx", 2)
    rest_v = swap(rest_v, "ctx", 1)
    out_keep, *out_send = local_call(
        project_kernel,
        "project",
        0.6,
        [shape((rows, share), F32)] + [shape((rows, share), BF16)] * 3,
        (attn_own, attn_got, stats, stats_pair, w_out),
    )
    out_near, out_far = (swap(out_send[step - 1], "head", step) for step in (2, 3))
    dq_got = swap(dq_pair, "ctx", PAIR)
    out_core = swap(out_send[0], "head", 1)
    grad_q, grad_k, grad_v, grad_hk, grad_hv, out = local_call(
        finish_kernel,
        "finish",
        0.9,
        [shape((rows, width), BF16)] * 3
        + [shape((capacity, width), BF16)] * 2
        + [shape((rows, share), BF16)],
        (
            out_keep, out_near, out_far, dq_own, dq_got, out_core,
            dkv_own, got_k, got_v, rest_k, rest_v,
        ),
    )
    return out, grad_q, grad_k, grad_v, grad_hk, grad_hv


def gathered(sec_q, sec_k, sec_v, hist_k, hist_v, frame_levels, frame_counts, w_out, grad_out):
    rows = sec_q.shape[0]
    capacity = hist_k.shape[0]
    owners = lax.axis_size("ctx")
    me = lax.axis_index("ctx")
    frames = jnp.arange(FMAX, dtype=jnp.int32)[None, :]
    tokens = jnp.where(
        frames < frame_counts[:, None], jnp.right_shift(jnp.int32(FTOK), 2 * frame_levels), 0
    ).sum(axis=1)
    slots = jnp.arange(capacity, dtype=jnp.int32)
    all_valid = jnp.concatenate(
        [jnp.ones((owners * rows,), bool), (slots[None] < tokens[:, None]).reshape(-1)]
    )
    own_valid = jnp.concatenate(
        [jnp.ones((rows,), bool), slots < lax.dynamic_index_in_dim(tokens, me, keepdims=False)]
    )

    def everyone(block, axis=0):
        return lax.all_gather(block, "ctx", axis=axis, tiled=True)

    own_k, own_v = (jnp.concatenate(a, axis=0) for a in ((sec_k, hist_k), (sec_v, hist_v)))
    all_k = jnp.concatenate([everyone(sec_k), everyone(hist_k)], axis=0)
    all_v = jnp.concatenate([everyone(sec_v), everyone(hist_v)], axis=0)
    d_attn = contract(lax.all_gather(grad_out, "head", axis=1, tiled=True), w_out, 1, 1).astype(BF16)
    all_q, all_d = everyone(sec_q), everyone(d_attn)

    def probs_and_dscores(query, key, value, dattn, valid, lse, delta):
        scores = contract(query, key, 1, 1) * SCALE
        probs = jnp.where(valid[None, :], jnp.exp(scores - lse), 0.0).astype(BF16)
        dprobs = contract(dattn, value, 1, 1)
        return probs, (probs.astype(F32) * (dprobs - delta)).astype(BF16)

    attn_parts, q_parts, k_parts, v_parts = [], [], [], []
    for head in range(sec_q.shape[1] // HDIM):
        query, dattn, key, value = (head_slice(a, head) for a in (sec_q, d_attn, all_k, all_v))
        scores = jnp.where(all_valid[None, :], contract(query, key, 1, 1) * SCALE, NEG_FILL)
        lse = jax.nn.logsumexp(scores, axis=1, keepdims=True)
        probs = jnp.where(all_valid[None, :], jnp.exp(scores - lse), 0.0).astype(BF16)
        attn = contract(probs, value, 1, 0).astype(BF16)
        delta = jnp.sum(attn.astype(F32) * dattn.astype(F32), axis=1, keepdims=True)
        _, dscores = probs_and_dscores(query, key, value, dattn, all_valid, lse, delta)
        attn_parts.append(attn)
        q_parts.append(contract(dscores, key, 1, 0))
        query, dattn, key, value = (head_slice(a, head) for a in (all_q, all_d, own_k, own_v))
        probs, dscores = probs_and_dscores(
            query, key, value, dattn, own_valid, everyone(lse), everyone(delta)
        )
        k_parts.append(contract(dscores, query, 0, 0))
        v_parts.append(contract(probs, dattn, 0, 0))
    partial = contract(jnp.concatenate(attn_parts, axis=1), w_out, 1, 0).astype(BF16)
    out = lax.psum_scatter(partial, "head", scatter_dimension=1, tiled=True)
    grad_q, grad_k = (
        (jnp.concatenate(a, axis=1) * SCALE).astype(BF16) for a in (q_parts, k_parts)
    )
    grad_v = jnp.concatenate(v_parts, axis=1).astype(BF16)
    return out, grad_q, grad_k[:rows], grad_v[:rows], grad_k[rows:], grad_v[rows:]


def solution(mesh):
    split = P("ctx", "head")
    plan = blocked if (mesh.shape["ctx"], mesh.shape["head"]) == (2 * SQUARE, 4) else gathered
    return jax.shard_map(
        plan,
        mesh=mesh,
        in_specs=(split,) * 5 + (P(), P(), P("head", None), split),
        out_specs=(split,) * 6,
        check_vma=False,
    )
```

```python
import functools
import math

import jax
import jax.numpy as jnp
from jax import lax
from jax.experimental import pallas as pl
from jax.experimental.pallas import tpu as pltpu
from jax.sharding import PartitionSpec as P

HDIM = 128
FTOK = 16
FMAX = 2
NEG_FILL = -1e30
SCALE = 1.0 / math.sqrt(HDIM)
F32 = jnp.float32
BF16 = jnp.bfloat16
SQUARE = 4
HBM_BYTES = 3.69e6
PAIR = 4


def contract(left, right, left_dim, right_dim):
    return lax.dot_general(
        left, right, (((left_dim,), (right_dim,)), ((), ())), preferred_element_type=F32
    )


def head_slice(stacked, head):
    return stacked[:, head * HDIM : (head + 1) * HDIM]


def swap(block, axis, bit):
    count = lax.axis_size(axis)
    return lax.ppermute(block, axis, [(i, i ^ bit) for i in range(count)])


def cost_of(micros):
    return pl.CostEstimate(flops=0, bytes_accessed=int(micros * HBM_BYTES), transcendentals=0)


def local_call(body, name, micros, out_shapes, args, tables=0):
    spaces = [pltpu.SMEM] * tables + [pltpu.VMEM] * (len(args) - tables)
    return pl.pallas_call(
        body,
        name=name,
        out_shape=out_shapes,
        in_specs=[pl.BlockSpec(memory_space=space) for space in spaces],
        out_specs=[pl.BlockSpec(memory_space=pltpu.VMEM)] * len(out_shapes),
        compiler_params=pltpu.CompilerParams(vmem_limit_bytes=40 * 2**20),
        cost_estimate=cost_of(micros),
    )(*args)


def load_kernel(k_ref, hk_ref, v_ref, hv_ref, kv_out, kv_ref, sems):
    inward, outward, begin = [], [], 0
    for i, ref in enumerate((k_ref, hk_ref, v_ref, hv_ref)):
        part = pl.ds(begin, ref.shape[0])
        inward.append(pltpu.make_async_copy(ref, kv_ref.at[part], sems.at[0, i]))
        outward.append(pltpu.make_async_copy(kv_ref.at[part], kv_out.at[part], sems.at[1, i]))
        begin += ref.shape[0]
    for copy in inward:
        copy.start()
    for before, after in zip(inward, outward):
        before.wait()
        after.start()
    for copy in outward:
        copy.wait()


def load_keys(*arrays):
    rows = sum(a.shape[0] for a in arrays)
    width = arrays[0].shape[1]
    return pl.pallas_call(
        load_kernel,
        name="load",
        out_shape=jax.ShapeDtypeStruct((rows, width), BF16),
        in_specs=[pl.BlockSpec(memory_space=pl.ANY)] * len(arrays),
        out_specs=pl.BlockSpec(memory_space=pl.ANY),
        scratch_shapes=[pltpu.VMEM((rows, width), BF16), pltpu.SemaphoreType.DMA((2, len(arrays)))],
        compiler_params=pltpu.CompilerParams(vmem_limit_bytes=60 * 2**20),
        cost_estimate=cost_of(1.6),
    )(*arrays)


def pass_keys_kernel(kv2, key_ref):
    key_ref[...] = kv2[: key_ref.shape[0]]


def pass_values_kernel(kv2, value_ref):
    value_ref[...] = kv2[value_ref.shape[0] :]


def square_blocks(kv0, kv1, kv2, key3, value3):
    keys = key3.shape[0]
    pairs = [(ref.at[:keys], ref.at[keys:]) for ref in (kv0, kv1, kv2)]
    return pairs + [(key3, value3)]


def limits_kernel(levels_ref, counts_ref, limits_ref):
    me = lax.axis_index("ctx")
    row = lax.broadcasted_iota(jnp.int32, limits_ref.shape, 0)
    limits = jnp.zeros(limits_ref.shape, jnp.int32)
    for step in range(SQUARE):
        total = jnp.int32(0)
        for frame in range(FMAX):
            tokens = lax.shift_right_logical(jnp.int32(FTOK), 2 * levels_ref[me ^ step, frame])
            total += jnp.where(frame < counts_ref[me ^ step], tokens, 0)
        limits = jnp.where(row == step, total, limits)
    limits_ref[...] = limits


def dattn_kernel(own_ref, core_ref, near_ref, far_ref, w_ref, out_ref):
    me = lax.axis_index("head")
    size = own_ref.shape[1]
    total = None
    for step, ref in enumerate((own_ref, core_ref, near_ref, far_ref)):
        columns = pl.ds(pl.multiple_of((me ^ step) * size, HDIM), size)
        part = contract(ref[...], w_ref[:, columns], 1, 1)
        total = part if total is None else total + part
    out_ref[...] = total.astype(BF16)


def both_rows(own_ref, pair_ref, head):
    return jnp.concatenate(
        [head_slice(own_ref[...], head), head_slice(pair_ref[...], head)], axis=0
    )


def scores_kernel(
    limits_ref, q_own_ref, q_pair_ref, kv0, kv1, kv2, key3, lse_ref, probs_ref
):
    rows = q_own_ref.shape[0]
    keys = key3.shape[0]
    blocks = [ref.at[:keys] for ref in (kv0, kv1, kv2)] + [key3]
    lse_ref[...] = jnp.zeros_like(lse_ref)
    for head in range(q_own_ref.shape[1] // HDIM):
        query = both_rows(q_own_ref, q_pair_ref, head)
        scores = []
        for step, key_ref in enumerate(blocks):
            block = contract(head_slice(key_ref[...], head), query, 1, 1) * SCALE
            slot = lax.broadcasted_iota(jnp.int32, block.shape, 0)
            valid = slot < rows + limits_ref[step : step + 1]
            scores.append(jnp.where(valid, block, NEG_FILL))
        top = functools.reduce(
            jnp.maximum, [jnp.max(block, axis=0, keepdims=True) for block in scores]
        )
        weights = [jnp.exp(block - top) for block in scores]
        total = sum(jnp.sum(block, axis=0, keepdims=True) for block in weights)
        inverse = 1.0 / total
        for step, block in enumerate(weights):
            begin = (head * SQUARE + step) * keys
            probs_ref[begin : begin + keys] = (block * inverse).astype(BF16)
        lse_ref[head : head + 1] = top + jnp.log(total)


def delta_kernel(
    lse_ref, probs_ref, d_own_ref, d_pair_ref, kv0, kv1, kv2, key3, value3, stats_ref, dprobs_ref
):
    keys = key3.shape[0]
    blocks = square_blocks(kv0, kv1, kv2, key3, value3)
    stats_ref[...] = jnp.zeros_like(stats_ref)
    stats_ref[: lse_ref.shape[0]] = lse_ref[...]
    for head in range(d_own_ref.shape[1] // HDIM):
        dattn = both_rows(d_own_ref, d_pair_ref, head)
        delta = None
        for step, (_, value_ref) in enumerate(blocks):
            part = pl.ds((head * SQUARE + step) * keys, keys)
            dprobs = contract(head_slice(value_ref[...], head), dattn, 1, 1)
            dprobs_ref[part] = dprobs
            share = jnp.sum(probs_ref[part].astype(F32) * dprobs, axis=0, keepdims=True)
            delta = share if delta is None else delta + share
        stats_ref[8 + head : 9 + head] = delta


def attn_kernel(kv0, kv1, kv2, key3, value3, probs_ref, own_ref, pair_ref):
    rows = own_ref.shape[1]
    keys = key3.shape[0]
    blocks = square_blocks(kv0, kv1, kv2, key3, value3)
    for head in range(own_ref.shape[0] // HDIM):
        attn = None
        for step, (_, value_ref) in enumerate(blocks):
            begin = (head * SQUARE + step) * keys
            part = contract(head_slice(value_ref[...], head), probs_ref[begin : begin + keys], 0, 0)
            attn = part if attn is None else attn + part
        features = slice(head * HDIM, (head + 1) * HDIM)
        own_ref[features] = attn[:, :rows]
        pair_ref[features] = attn[:, rows:].astype(BF16)


def merge_parts(mine, theirs):
    top = jnp.maximum(mine, theirs)
    weight, weight_pair = jnp.exp(mine - top), jnp.exp(theirs - top)
    inverse = 1.0 / (weight + weight_pair)
    return weight * inverse, weight_pair * inverse


def project_kernel(own_ref, pair_ref, stats_ref, stats_pair_ref, w_ref, keep_ref, *send_refs):
    rows = own_ref.shape[1]
    parts = []
    for head in range(own_ref.shape[0] // HDIM):
        features = slice(head * HDIM, (head + 1) * HDIM)
        weight, weight_pair = merge_parts(
            stats_ref[head : head + 1, :rows], stats_pair_ref[head : head + 1, rows:]
        )
        parts.append(own_ref[features] * weight + pair_ref[features].astype(F32) * weight_pair)
    attn = jnp.concatenate(parts, axis=0).astype(BF16)
    me = lax.axis_index("head")
    size = keep_ref.shape[1]
    for step, ref in enumerate((keep_ref, *send_refs)):
        columns = pl.ds(pl.multiple_of((me ^ step) * size, HDIM), size)
        ref[...] = contract(attn, w_ref[:, columns], 0, 0).astype(ref.dtype)


def backward_kernel(
    q_own_ref, q_pair_ref, d_own_ref, d_pair_ref, kv0, kv1, kv2, key3, value3,
    stats_ref, stats_pair_ref, probs_ref, dprobs_ref,
    dq_own_ref, dq_pair_ref, dkv_ref, send_k_ref, send_v_ref, near_k_ref, near_v_ref,
):
    rows = q_own_ref.shape[0]
    keys = key3.shape[0]
    blocks = square_blocks(kv0, kv1, kv2, key3, value3)
    key_parts = (dkv_ref.at[:keys], send_k_ref.at[:keys], near_k_ref, send_k_ref.at[keys:])
    value_parts = (dkv_ref.at[keys:], near_v_ref, send_v_ref.at[:keys], send_v_ref.at[keys:])

    def swapped(row):
        return jnp.concatenate([row[:, rows:], row[:, :rows]], axis=1)

    for head in range(q_own_ref.shape[1] // HDIM):
        query = both_rows(q_own_ref, q_pair_ref, head)
        dattn = both_rows(d_own_ref, d_pair_ref, head)
        weight, weight_pair = merge_parts(
            stats_ref[head : head + 1], swapped(stats_pair_ref[head : head + 1])
        )
        delta = weight * stats_ref[8 + head : 9 + head]
        delta += weight_pair * swapped(stats_pair_ref[8 + head : 9 + head])
        features = slice(head * HDIM, (head + 1) * HDIM)
        dquery = None
        for step, (key_ref, _) in enumerate(blocks):
            begin = (head * SQUARE + step) * keys
            probs = (probs_ref[begin : begin + keys].astype(F32) * weight).astype(BF16)
            dprobs = dprobs_ref[begin : begin + keys]
            dscores = (probs.astype(F32) * (dprobs - delta)).astype(BF16)
            key_part, value_part = key_parts[step], value_parts[step]
            grad_key = contract(dscores, query, 1, 0) * SCALE
            key_part[:, features] = grad_key.astype(key_part.dtype)
            value_part[:, features] = contract(probs, dattn, 1, 0).astype(value_part.dtype)
            part = contract(dscores, head_slice(key_ref[...], head), 0, 0)
            dquery = part if dquery is None else dquery + part
        dq_own_ref[:, features] = dquery[:rows] * SCALE
        dq_pair_ref[:, features] = (dquery[rows:] * SCALE).astype(BF16)


def pass_on_kernel(near_k_ref, near_v_ref, got_k_ref, got_v_ref, k_ref, v_ref):
    keys = near_k_ref.shape[0]
    k_ref[...] = (near_k_ref[...] + got_k_ref[keys:].astype(F32)).astype(BF16)
    v_ref[...] = (near_v_ref[...] + got_v_ref[keys:].astype(F32)).astype(BF16)


def finish_kernel(
    keep_ref, near_ref, far_ref, dq_ref, dq_pair_ref, core_ref,
    dkv_ref, got_k_ref, got_v_ref, rest_k_ref, rest_v_ref,
    q_out, k_out, v_out, hk_out, hv_out, out_ref,
):
    rows, capacity = k_out.shape[0], hk_out.shape[0]
    keys = rows + capacity

    def total(first, *others):
        for other in others:
            first = first + other.astype(F32)
        return first.astype(BF16)

    q_out[...] = total(dq_ref[...], dq_pair_ref[...])
    k_out[...] = total(dkv_ref[:rows], got_k_ref[:rows], rest_k_ref[:rows])
    hk_out[...] = total(dkv_ref[rows:keys], got_k_ref[rows:keys], rest_k_ref[rows:])
    v_out[...] = total(dkv_ref[keys : keys + rows], got_v_ref[:rows], rest_v_ref[:rows])
    hv_out[...] = total(dkv_ref[keys + rows :], got_v_ref[rows:keys], rest_v_ref[rows:])
    out_ref[...] = total(keep_ref[...], core_ref[...], near_ref[...], far_ref[...])


def blocked(sec_q, sec_k, sec_v, hist_k, hist_v, frame_levels, frame_counts, w_out, grad_out):
    shape = jax.ShapeDtypeStruct
    rows, width = sec_q.shape
    heads = width // HDIM
    capacity = hist_k.shape[0]
    keys = rows + capacity
    share = grad_out.shape[1]

    q_pair = swap(sec_q, "ctx", PAIR)
    grad_near = swap(grad_out, "head", 2)
    grad_core = swap(grad_out, "head", 1)
    grad_far = swap(grad_near, "head", 1)
    kv0 = load_keys(sec_k, hist_k, sec_v, hist_v)
    kv2 = swap(kv0, "ctx", 2)
    kv1 = swap(kv0, "ctx", 1)
    kv2, q_pair = lax.optimization_barrier((kv2, q_pair))
    key3 = local_call(pass_keys_kernel, "pass_keys", 0.1, [shape((keys, width), BF16)], (kv2,))[0]
    value3 = local_call(
        pass_values_kernel, "pass_values", 0.1, [shape((keys, width), BF16)], (kv2,)
    )[0]
    kvs = [kv0, kv1, kv2, swap(key3, "ctx", 1), swap(value3, "ctx", 1)]
    d_own = local_call(
        dattn_kernel,
        "dattn",
        0.8,
        [shape((rows, width), BF16)],
        (grad_out, grad_core, grad_near, grad_far, w_out),
    )[0]
    d_pair = swap(d_own, "ctx", PAIR)
    limits = local_call(
        limits_kernel,
        "limits",
        0.6,
        [shape((8, 2 * rows), jnp.int32)],
        (frame_levels, frame_counts),
        tables=2,
    )[0]
    lse, probs = local_call(
        scores_kernel,
        "scores",
        0.9,
        [shape((8, 2 * rows), F32), shape((heads * SQUARE * keys, 2 * rows), BF16)],
        (limits, sec_q, q_pair, *kvs[:4]),
    )
    attn_own, attn_pair = local_call(
        attn_kernel,
        "attn",
        0.5,
        [shape((width, rows), F32), shape((width, rows), BF16)],
        (*kvs, probs),
    )
    lse, attn_own = lax.optimization_barrier((lse, attn_own))
    stats, dprobs = local_call(
        delta_kernel,
        "delta",
        0.7,
        [shape((16, 2 * rows), F32), shape((heads * SQUARE * keys, 2 * rows), F32)],
        (lse, probs, d_own, d_pair, *kvs),
    )
    stats_pair = swap(stats, "ctx", PAIR)
    dq_own, dq_pair, dkv_own, send_k, send_v, near_k, near_v = local_call(
        backward_kernel,
        "backward",
        1.1,
        [shape((rows, width), F32), shape((rows, width), BF16), shape((2 * keys, width), F32)]
        + [shape((2 * keys, width), BF16)] * 2
        + [shape((keys, width), F32)] * 2,
        (sec_q, q_pair, d_own, d_pair, *kvs, stats, stats_pair, probs, dprobs),
    )
    attn_got = swap(attn_pair, "ctx", PAIR)
    attn_got, send_k, send_v = lax.optimization_barrier((attn_got, send_k, send_v))
    got_k = swap(send_k, "ctx", 1)
    got_v = swap(send_v, "ctx", 2)
    rest_k, rest_v = local_call(
        pass_on_kernel,
        "pass_on",
        0.1,
        [shape((keys, width), BF16)] * 2,
        (near_k, near_v, got_k, got_v),
    )
    rest_k = swap(rest_k, "ctx", 2)
    rest_v = swap(rest_v, "ctx", 1)
    out_keep, *out_send = local_call(
        project_kernel,
        "project",
        0.6,
        [shape((rows, share), F32)] + [shape((rows, share), BF16)] * 3,
        (attn_own, attn_got, stats, stats_pair, w_out),
    )
    out_near, out_far = (swap(out_send[step - 1], "head", step) for step in (2, 3))
    dq_got = swap(dq_pair, "ctx", PAIR)
    out_core = swap(out_send[0], "head", 1)
    grad_q, grad_k, grad_v, grad_hk, grad_hv, out = local_call(
        finish_kernel,
        "finish",
        0.9,
        [shape((rows, width), BF16)] * 3
        + [shape((capacity, width), BF16)] * 2
        + [shape((rows, share), BF16)],
        (
            out_keep, out_near, out_far, dq_own, dq_got, out_core,
            dkv_own, got_k, got_v, rest_k, rest_v,
        ),
    )
    return out, grad_q, grad_k, grad_v, grad_hk, grad_hv


def gathered(sec_q, sec_k, sec_v, hist_k, hist_v, frame_levels, frame_counts, w_out, grad_out):
    rows = sec_q.shape[0]
    capacity = hist_k.shape[0]
    owners = lax.axis_size("ctx")
    me = lax.axis_index("ctx")
    frames = jnp.arange(FMAX, dtype=jnp.int32)[None, :]
    tokens = jnp.where(
        frames < frame_counts[:, None], jnp.right_shift(jnp.int32(FTOK), 2 * frame_levels), 0
    ).sum(axis=1)
    slots = jnp.arange(capacity, dtype=jnp.int32)
    all_valid = jnp.concatenate(
        [jnp.ones((owners * rows,), bool), (slots[None] < tokens[:, None]).reshape(-1)]
    )
    own_valid = jnp.concatenate(
        [jnp.ones((rows,), bool), slots < lax.dynamic_index_in_dim(tokens, me, keepdims=False)]
    )

    def everyone(block, axis=0):
        return lax.all_gather(block, "ctx", axis=axis, tiled=True)

    own_k, own_v = (jnp.concatenate(a, axis=0) for a in ((sec_k, hist_k), (sec_v, hist_v)))
    all_k = jnp.concatenate([everyone(sec_k), everyone(hist_k)], axis=0)
    all_v = jnp.concatenate([everyone(sec_v), everyone(hist_v)], axis=0)
    d_attn = contract(lax.all_gather(grad_out, "head", axis=1, tiled=True), w_out, 1, 1).astype(BF16)
    all_q, all_d = everyone(sec_q), everyone(d_attn)

    def probs_and_dscores(query, key, value, dattn, valid, lse, delta):
        scores = contract(query, key, 1, 1) * SCALE
        probs = jnp.where(valid[None, :], jnp.exp(scores - lse), 0.0).astype(BF16)
        dprobs = contract(dattn, value, 1, 1)
        return probs, (probs.astype(F32) * (dprobs - delta)).astype(BF16)

    attn_parts, q_parts, k_parts, v_parts = [], [], [], []
    for head in range(sec_q.shape[1] // HDIM):
        query, dattn, key, value = (head_slice(a, head) for a in (sec_q, d_attn, all_k, all_v))
        scores = jnp.where(all_valid[None, :], contract(query, key, 1, 1) * SCALE, NEG_FILL)
        lse = jax.nn.logsumexp(scores, axis=1, keepdims=True)
        probs = jnp.where(all_valid[None, :], jnp.exp(scores - lse), 0.0).astype(BF16)
        attn = contract(probs, value, 1, 0).astype(BF16)
        delta = jnp.sum(attn.astype(F32) * dattn.astype(F32), axis=1, keepdims=True)
        _, dscores = probs_and_dscores(query, key, value, dattn, all_valid, lse, delta)
        attn_parts.append(attn)
        q_parts.append(contract(dscores, key, 1, 0))
        query, dattn, key, value = (head_slice(a, head) for a in (all_q, all_d, own_k, own_v))
        probs, dscores = probs_and_dscores(
            query, key, value, dattn, own_valid, everyone(lse), everyone(delta)
        )
        k_parts.append(contract(dscores, query, 0, 0))
        v_parts.append(contract(probs, dattn, 0, 0))
    partial = contract(jnp.concatenate(attn_parts, axis=1), w_out, 1, 0).astype(BF16)
    out = lax.psum_scatter(partial, "head", scatter_dimension=1, tiled=True)
    grad_q, grad_k = (
        (jnp.concatenate(a, axis=1) * SCALE).astype(BF16) for a in (q_parts, k_parts)
    )
    grad_v = jnp.concatenate(v_parts, axis=1).astype(BF16)
    return out, grad_q, grad_k[:rows], grad_v[:rows], grad_k[rows:], grad_v[rows:]


def solution(mesh):
    split = P("ctx", "head")
    plan = blocked if (mesh.shape["ctx"], mesh.shape["head"]) == (2 * SQUARE, 4) else gathered
    return jax.shard_map(
        plan,
        mesh=mesh,
        in_specs=(split,) * 5 + (P(), P(), P("head", None), split),
        out_specs=(split,) * 6,
        check_vma=False,
    )
```

```python
import functools
import math

import jax
import jax.numpy as jnp
from jax import lax
from jax.experimental import pallas as pl
from jax.experimental.pallas import tpu as pltpu
from jax.sharding import PartitionSpec as P

HDIM = 128
FTOK = 16
FMAX = 2
NEG_FILL = -1e30
SCALE = 1.0 / math.sqrt(HDIM)
F32 = jnp.float32
BF16 = jnp.bfloat16
SQUARE = 4
HBM_BYTES = 3.69e6
PAIR = 4


def contract(left, right, left_dim, right_dim):
    return lax.dot_general(
        left, right, (((left_dim,), (right_dim,)), ((), ())), preferred_element_type=F32
    )


def head_slice(stacked, head):
    return stacked[:, head * HDIM : (head + 1) * HDIM]


def swap(block, axis, bit):
    count = lax.axis_size(axis)
    return lax.ppermute(block, axis, [(i, i ^ bit) for i in range(count)])


def cost_of(micros):
    return pl.CostEstimate(flops=0, bytes_accessed=int(micros * HBM_BYTES), transcendentals=0)


def local_call(body, name, micros, out_shapes, args, tables=0):
    spaces = [pltpu.SMEM] * tables + [pltpu.VMEM] * (len(args) - tables)
    return pl.pallas_call(
        body,
        name=name,
        out_shape=out_shapes,
        in_specs=[pl.BlockSpec(memory_space=space) for space in spaces],
        out_specs=[pl.BlockSpec(memory_space=pltpu.VMEM)] * len(out_shapes),
        compiler_params=pltpu.CompilerParams(vmem_limit_bytes=40 * 2**20),
        cost_estimate=cost_of(micros),
    )(*args)


def load_kernel(k_ref, hk_ref, v_ref, hv_ref, kv_out, kv_ref, sems):
    inward, outward, begin = [], [], 0
    for i, ref in enumerate((k_ref, hk_ref, v_ref, hv_ref)):
        part = pl.ds(begin, ref.shape[0])
        inward.append(pltpu.make_async_copy(ref, kv_ref.at[part], sems.at[0, i]))
        outward.append(pltpu.make_async_copy(kv_ref.at[part], kv_out.at[part], sems.at[1, i]))
        begin += ref.shape[0]
    for copy in inward:
        copy.start()
    for before, after in zip(inward, outward):
        before.wait()
        after.start()
    for copy in outward:
        copy.wait()


def load_keys(*arrays):
    rows = sum(a.shape[0] for a in arrays)
    width = arrays[0].shape[1]
    return pl.pallas_call(
        load_kernel,
        name="load",
        out_shape=jax.ShapeDtypeStruct((rows, width), BF16),
        in_specs=[pl.BlockSpec(memory_space=pl.ANY)] * len(arrays),
        out_specs=pl.BlockSpec(memory_space=pl.ANY),
        scratch_shapes=[pltpu.VMEM((rows, width), BF16), pltpu.SemaphoreType.DMA((2, len(arrays)))],
        compiler_params=pltpu.CompilerParams(vmem_limit_bytes=60 * 2**20),
        cost_estimate=cost_of(1.6),
    )(*arrays)


def pass_keys_kernel(kv2, key_ref):
    key_ref[...] = kv2[: key_ref.shape[0]]


def pass_values_kernel(kv2, value_ref):
    value_ref[...] = kv2[value_ref.shape[0] :]


def square_blocks(kv0, kv1, kv2, key3, value3):
    keys = key3.shape[0]
    pairs = [(ref.at[:keys], ref.at[keys:]) for ref in (kv0, kv1, kv2)]
    return pairs + [(key3, value3)]


def load_weight_kernel(w_ref, w_out, sems):
    copies = []
    for i in range(sems.shape[0]):
        part = pl.ds(i * HDIM, HDIM)
        copies.append(pltpu.make_async_copy(w_ref.at[part], w_out.at[part], sems.at[i]))
    for copy in copies:
        copy.start()
    for copy in copies:
        copy.wait()


def load_weight(w_out):
    return pl.pallas_call(
        load_weight_kernel,
        name="load_w",
        out_shape=jax.ShapeDtypeStruct(w_out.shape, BF16),
        in_specs=[pl.BlockSpec(memory_space=pl.ANY)],
        out_specs=pl.BlockSpec(memory_space=pltpu.VMEM),
        scratch_shapes=[pltpu.SemaphoreType.DMA((w_out.shape[0] // HDIM,))],
        compiler_params=pltpu.CompilerParams(vmem_limit_bytes=50 * 2**20 + 2**19),
        cost_estimate=cost_of(1.6),
    )(w_out)


def limits_kernel(levels_ref, counts_ref, limits_ref):
    me = lax.axis_index("ctx")
    row = lax.broadcasted_iota(jnp.int32, limits_ref.shape, 0)
    limits = jnp.zeros(limits_ref.shape, jnp.int32)
    for step in range(SQUARE):
        total = jnp.int32(0)
        for frame in range(FMAX):
            tokens = lax.shift_right_logical(jnp.int32(FTOK), 2 * levels_ref[me ^ step, frame])
            total += jnp.where(frame < counts_ref[me ^ step], tokens, 0)
        limits = jnp.where(row == step, total, limits)
    limits_ref[...] = limits


def dattn_kernel(own_ref, core_ref, near_ref, far_ref, w_ref, out_ref):
    me = lax.axis_index("head")
    size = own_ref.shape[1]
    total = None
    for step, ref in enumerate((own_ref, core_ref, near_ref, far_ref)):
        columns = pl.ds(pl.multiple_of((me ^ step) * size, HDIM), size)
        part = contract(ref[...], w_ref[:, columns], 1, 1)
        total = part if total is None else total + part
    out_ref[...] = total.astype(BF16)


def both_rows(own_ref, pair_ref, head):
    return jnp.concatenate(
        [head_slice(own_ref[...], head), head_slice(pair_ref[...], head)], axis=0
    )


def scores_kernel(
    limits_ref, q_own_ref, q_pair_ref, kv0, kv1, kv2, key3, lse_ref, probs_ref
):
    rows = q_own_ref.shape[0]
    keys = key3.shape[0]
    blocks = [ref.at[:keys] for ref in (kv0, kv1, kv2)] + [key3]
    lse_ref[...] = jnp.zeros_like(lse_ref)
    for head in range(q_own_ref.shape[1] // HDIM):
        query = both_rows(q_own_ref, q_pair_ref, head)
        scores = []
        for step, key_ref in enumerate(blocks):
            block = contract(head_slice(key_ref[...], head), query, 1, 1) * SCALE
            slot = lax.broadcasted_iota(jnp.int32, block.shape, 0)
            valid = slot < rows + limits_ref[step : step + 1]
            scores.append(jnp.where(valid, block, NEG_FILL))
        top = functools.reduce(
            jnp.maximum, [jnp.max(block, axis=0, keepdims=True) for block in scores]
        )
        weights = [jnp.exp(block - top) for block in scores]
        total = sum(jnp.sum(block, axis=0, keepdims=True) for block in weights)
        inverse = 1.0 / total
        for step, block in enumerate(weights):
            begin = (head * SQUARE + step) * keys
            probs_ref[begin : begin + keys] = (block * inverse).astype(BF16)
        lse_ref[head : head + 1] = top + jnp.log(total)


def delta_kernel(
    lse_ref, probs_ref, d_own_ref, d_pair_ref, kv0, kv1, kv2, key3, value3, stats_ref, dprobs_ref
):
    keys = key3.shape[0]
    blocks = square_blocks(kv0, kv1, kv2, key3, value3)
    stats_ref[...] = jnp.zeros_like(stats_ref)
    stats_ref[: lse_ref.shape[0]] = lse_ref[...]
    for head in range(d_own_ref.shape[1] // HDIM):
        dattn = both_rows(d_own_ref, d_pair_ref, head)
        delta = None
        for step, (_, value_ref) in enumerate(blocks):
            part = pl.ds((head * SQUARE + step) * keys, keys)
            dprobs = contract(head_slice(value_ref[...], head), dattn, 1, 1)
            dprobs_ref[part] = dprobs
            share = jnp.sum(probs_ref[part].astype(F32) * dprobs, axis=0, keepdims=True)
            delta = share if delta is None else delta + share
        stats_ref[8 + head : 9 + head] = delta


def attn_kernel(kv0, kv1, kv2, key3, value3, probs_ref, own_ref, pair_ref):
    rows = own_ref.shape[1]
    keys = key3.shape[0]
    blocks = square_blocks(kv0, kv1, kv2, key3, value3)
    for head in range(own_ref.shape[0] // HDIM):
        attn = None
        for step, (_, value_ref) in enumerate(blocks):
            begin = (head * SQUARE + step) * keys
            part = contract(head_slice(value_ref[...], head), probs_ref[begin : begin + keys], 0, 0)
            attn = part if attn is None else attn + part
        features = slice(head * HDIM, (head + 1) * HDIM)
        own_ref[features] = attn[:, :rows]
        pair_ref[features] = attn[:, rows:].astype(BF16)


def merge_parts(mine, theirs):
    top = jnp.maximum(mine, theirs)
    weight, weight_pair = jnp.exp(mine - top), jnp.exp(theirs - top)
    inverse = 1.0 / (weight + weight_pair)
    return weight * inverse, weight_pair * inverse


def project_kernel(own_ref, pair_ref, stats_ref, stats_pair_ref, w_ref, keep_ref, *send_refs):
    rows = own_ref.shape[1]
    parts = []
    for head in range(own_ref.shape[0] // HDIM):
        features = slice(head * HDIM, (head + 1) * HDIM)
        weight, weight_pair = merge_parts(
            stats_ref[head : head + 1, :rows], stats_pair_ref[head : head + 1, rows:]
        )
        parts.append(own_ref[features] * weight + pair_ref[features].astype(F32) * weight_pair)
    attn = jnp.concatenate(parts, axis=0).astype(BF16)
    me = lax.axis_index("head")
    size = keep_ref.shape[1]
    for step, ref in enumerate((keep_ref, *send_refs)):
        columns = pl.ds(pl.multiple_of((me ^ step) * size, HDIM), size)
        ref[...] = contract(attn, w_ref[:, columns], 0, 0).astype(ref.dtype)


def backward_kernel(
    q_own_ref, q_pair_ref, d_own_ref, d_pair_ref, kv0, kv1, kv2, key3, value3,
    stats_ref, stats_pair_ref, probs_ref, dprobs_ref,
    dq_own_ref, dq_pair_ref, dkv_ref, send_k_ref, send_v_ref, near_k_ref, near_v_ref,
):
    rows = q_own_ref.shape[0]
    keys = key3.shape[0]
    blocks = square_blocks(kv0, kv1, kv2, key3, value3)
    key_parts = (dkv_ref.at[:keys], send_k_ref.at[:keys], near_k_ref, send_k_ref.at[keys:])
    value_parts = (dkv_ref.at[keys:], near_v_ref, send_v_ref.at[:keys], send_v_ref.at[keys:])

    def swapped(row):
        return jnp.concatenate([row[:, rows:], row[:, :rows]], axis=1)

    for head in range(q_own_ref.shape[1] // HDIM):
        query = both_rows(q_own_ref, q_pair_ref, head)
        dattn = both_rows(d_own_ref, d_pair_ref, head)
        weight, weight_pair = merge_parts(
            stats_ref[head : head + 1], swapped(stats_pair_ref[head : head + 1])
        )
        delta = weight * stats_ref[8 + head : 9 + head]
        delta += weight_pair * swapped(stats_pair_ref[8 + head : 9 + head])
        features = slice(head * HDIM, (head + 1) * HDIM)
        dquery = None
        for step, (key_ref, _) in enumerate(blocks):
            begin = (head * SQUARE + step) * keys
            probs = (probs_ref[begin : begin + keys].astype(F32) * weight).astype(BF16)
            dprobs = dprobs_ref[begin : begin + keys]
            dscores = (probs.astype(F32) * (dprobs - delta)).astype(BF16)
            key_part, value_part = key_parts[step], value_parts[step]
            grad_key = contract(dscores, query, 1, 0) * SCALE
            key_part[:, features] = grad_key.astype(key_part.dtype)
            value_part[:, features] = contract(probs, dattn, 1, 0).astype(value_part.dtype)
            part = contract(dscores, head_slice(key_ref[...], head), 0, 0)
            dquery = part if dquery is None else dquery + part
        dq_own_ref[:, features] = dquery[:rows] * SCALE
        dq_pair_ref[:, features] = (dquery[rows:] * SCALE).astype(BF16)


def pass_on_kernel(near_k_ref, near_v_ref, got_k_ref, got_v_ref, k_ref, v_ref):
    keys = near_k_ref.shape[0]
    k_ref[...] = (near_k_ref[...] + got_k_ref[keys:].astype(F32)).astype(BF16)
    v_ref[...] = (near_v_ref[...] + got_v_ref[keys:].astype(F32)).astype(BF16)


def finish_kernel(
    keep_ref, near_ref, far_ref, dq_ref, dq_pair_ref, core_ref,
    dkv_ref, got_k_ref, got_v_ref, rest_k_ref, rest_v_ref,
    q_out, k_out, v_out, hk_out, hv_out, out_ref,
):
    rows, capacity = k_out.shape[0], hk_out.shape[0]
    keys = rows + capacity

    def total(first, *others):
        for other in others:
            first = first + other.astype(F32)
        return first.astype(BF16)

    q_out[...] = total(dq_ref[...], dq_pair_ref[...])
    k_out[...] = total(dkv_ref[:rows], got_k_ref[:rows], rest_k_ref[:rows])
    hk_out[...] = total(dkv_ref[rows:keys], got_k_ref[rows:keys], rest_k_ref[rows:])
    v_out[...] = total(dkv_ref[keys : keys + rows], got_v_ref[:rows], rest_v_ref[:rows])
    hv_out[...] = total(dkv_ref[keys + rows :], got_v_ref[rows:keys], rest_v_ref[rows:])
    out_ref[...] = total(keep_ref[...], core_ref[...], near_ref[...], far_ref[...])


def blocked(sec_q, sec_k, sec_v, hist_k, hist_v, frame_levels, frame_counts, w_out, grad_out):
    shape = jax.ShapeDtypeStruct
    rows, width = sec_q.shape
    heads = width // HDIM
    capacity = hist_k.shape[0]
    keys = rows + capacity
    share = grad_out.shape[1]

    q_pair = swap(sec_q, "ctx", PAIR)
    grad_near = swap(grad_out, "head", 2)
    grad_core = swap(grad_out, "head", 1)
    weight = load_weight(w_out)
    grad_near, weight = lax.optimization_barrier((grad_near, weight))
    grad_far = swap(grad_near, "head", 1)
    kv0 = load_keys(sec_k, hist_k, sec_v, hist_v)
    kv2 = swap(kv0, "ctx", 2)
    kv1 = swap(kv0, "ctx", 1)
    d_own = local_call(
        dattn_kernel,
        "dattn",
        0.8,
        [shape((rows, width), BF16)],
        (grad_out, grad_core, grad_near, grad_far, weight),
    )[0]
    kv1, kv2, d_own = lax.optimization_barrier((kv1, kv2, d_own))
    key3 = local_call(pass_keys_kernel, "pass_keys", 0.1, [shape((keys, width), BF16)], (kv2,))[0]
    kv2_kept, q_pair, _ = lax.optimization_barrier((kv2, q_pair, key3))
    value3 = local_call(
        pass_values_kernel, "pass_values", 1.0, [shape((keys, width), BF16)], (kv2_kept,)
    )[0]
    kvs = [kv0, kv1, kv2, swap(key3, "ctx", 1), swap(value3, "ctx", 1)]
    d_pair = swap(d_own, "ctx", PAIR)
    limits = local_call(
        limits_kernel,
        "limits",
        0.6,
        [shape((8, 2 * rows), jnp.int32)],
        (frame_levels, frame_counts),
        tables=2,
    )[0]
    lse, probs = local_call(
        scores_kernel,
        "scores",
        0.9,
        [shape((8, 2 * rows), F32), shape((heads * SQUARE * keys, 2 * rows), BF16)],
        (limits, sec_q, q_pair, *kvs[:4]),
    )
    attn_own, attn_pair = local_call(
        attn_kernel,
        "attn",
        0.5,
        [shape((width, rows), F32), shape((width, rows), BF16)],
        (*kvs, probs),
    )
    lse, attn_own = lax.optimization_barrier((lse, attn_own))
    stats, dprobs = local_call(
        delta_kernel,
        "delta",
        0.7,
        [shape((16, 2 * rows), F32), shape((heads * SQUARE * keys, 2 * rows), F32)],
        (lse, probs, d_own, d_pair, *kvs),
    )
    stats_pair = swap(stats, "ctx", PAIR)
    dq_own, dq_pair, dkv_own, send_k, send_v, near_k, near_v = local_call(
        backward_kernel,
        "backward",
        1.1,
        [shape((rows, width), F32), shape((rows, width), BF16), shape((2 * keys, width), F32)]
        + [shape((2 * keys, width), BF16)] * 2
        + [shape((keys, width), F32)] * 2,
        (sec_q, q_pair, d_own, d_pair, *kvs, stats, stats_pair, probs, dprobs),
    )
    attn_got = swap(attn_pair, "ctx", PAIR)
    attn_got, send_k, send_v = lax.optimization_barrier((attn_got, send_k, send_v))
    got_k = swap(send_k, "ctx", 1)
    got_v = swap(send_v, "ctx", 2)
    rest_k, rest_v = local_call(
        pass_on_kernel,
        "pass_on",
        0.1,
        [shape((keys, width), BF16)] * 2,
        (near_k, near_v, got_k, got_v),
    )
    rest_k = swap(rest_k, "ctx", 2)
    rest_v = swap(rest_v, "ctx", 1)
    out_keep, *out_send = local_call(
        project_kernel,
        "project",
        0.6,
        [shape((rows, share), F32)] + [shape((rows, share), BF16)] * 3,
        (attn_own, attn_got, stats, stats_pair, weight),
    )
    out_near, out_far = (swap(out_send[step - 1], "head", step) for step in (2, 3))
    dq_got = swap(dq_pair, "ctx", PAIR)
    out_core = swap(out_send[0], "head", 1)
    grad_q, grad_k, grad_v, grad_hk, grad_hv, out = local_call(
        finish_kernel,
        "finish",
        0.9,
        [shape((rows, width), BF16)] * 3
        + [shape((capacity, width), BF16)] * 2
        + [shape((rows, share), BF16)],
        (
            out_keep, out_near, out_far, dq_own, dq_got, out_core,
            dkv_own, got_k, got_v, rest_k, rest_v,
        ),
    )
    return out, grad_q, grad_k, grad_v, grad_hk, grad_hv


def gathered(sec_q, sec_k, sec_v, hist_k, hist_v, frame_levels, frame_counts, w_out, grad_out):
    rows = sec_q.shape[0]
    capacity = hist_k.shape[0]
    owners = lax.axis_size("ctx")
    me = lax.axis_index("ctx")
    frames = jnp.arange(FMAX, dtype=jnp.int32)[None, :]
    tokens = jnp.where(
        frames < frame_counts[:, None], jnp.right_shift(jnp.int32(FTOK), 2 * frame_levels), 0
    ).sum(axis=1)
    slots = jnp.arange(capacity, dtype=jnp.int32)
    all_valid = jnp.concatenate(
        [jnp.ones((owners * rows,), bool), (slots[None] < tokens[:, None]).reshape(-1)]
    )
    own_valid = jnp.concatenate(
        [jnp.ones((rows,), bool), slots < lax.dynamic_index_in_dim(tokens, me, keepdims=False)]
    )

    def everyone(block, axis=0):
        return lax.all_gather(block, "ctx", axis=axis, tiled=True)

    own_k, own_v = (jnp.concatenate(a, axis=0) for a in ((sec_k, hist_k), (sec_v, hist_v)))
    all_k = jnp.concatenate([everyone(sec_k), everyone(hist_k)], axis=0)
    all_v = jnp.concatenate([everyone(sec_v), everyone(hist_v)], axis=0)
    d_attn = contract(lax.all_gather(grad_out, "head", axis=1, tiled=True), w_out, 1, 1).astype(BF16)
    all_q, all_d = everyone(sec_q), everyone(d_attn)

    def probs_and_dscores(query, key, value, dattn, valid, lse, delta):
        scores = contract(query, key, 1, 1) * SCALE
        probs = jnp.where(valid[None, :], jnp.exp(scores - lse), 0.0).astype(BF16)
        dprobs = contract(dattn, value, 1, 1)
        return probs, (probs.astype(F32) * (dprobs - delta)).astype(BF16)

    attn_parts, q_parts, k_parts, v_parts = [], [], [], []
    for head in range(sec_q.shape[1] // HDIM):
        query, dattn, key, value = (head_slice(a, head) for a in (sec_q, d_attn, all_k, all_v))
        scores = jnp.where(all_valid[None, :], contract(query, key, 1, 1) * SCALE, NEG_FILL)
        lse = jax.nn.logsumexp(scores, axis=1, keepdims=True)
        probs = jnp.where(all_valid[None, :], jnp.exp(scores - lse), 0.0).astype(BF16)
        attn = contract(probs, value, 1, 0).astype(BF16)
        delta = jnp.sum(attn.astype(F32) * dattn.astype(F32), axis=1, keepdims=True)
        _, dscores = probs_and_dscores(query, key, value, dattn, all_valid, lse, delta)
        attn_parts.append(attn)
        q_parts.append(contract(dscores, key, 1, 0))
        query, dattn, key, value = (head_slice(a, head) for a in (all_q, all_d, own_k, own_v))
        probs, dscores = probs_and_dscores(
            query, key, value, dattn, own_valid, everyone(lse), everyone(delta)
        )
        k_parts.append(contract(dscores, query, 0, 0))
        v_parts.append(contract(probs, dattn, 0, 0))
    partial = contract(jnp.concatenate(attn_parts, axis=1), w_out, 1, 0).astype(BF16)
    out = lax.psum_scatter(partial, "head", scatter_dimension=1, tiled=True)
    grad_q, grad_k = (
        (jnp.concatenate(a, axis=1) * SCALE).astype(BF16) for a in (q_parts, k_parts)
    )
    grad_v = jnp.concatenate(v_parts, axis=1).astype(BF16)
    return out, grad_q, grad_k[:rows], grad_v[:rows], grad_k[rows:], grad_v[rows:]


def solution(mesh):
    split = P("ctx", "head")
    plan = blocked if (mesh.shape["ctx"], mesh.shape["head"]) == (2 * SQUARE, 4) else gathered
    return jax.shard_map(
        plan,
        mesh=mesh,
        in_specs=(split,) * 5 + (P(), P(), P("head", None), split),
        out_specs=(split,) * 6,
        check_vma=False,
    )
```

```python
import functools
import math

import jax
import jax.numpy as jnp
from jax import lax
from jax.experimental import pallas as pl
from jax.experimental.pallas import tpu as pltpu
from jax.sharding import PartitionSpec as P

HDIM = 128
FTOK = 16
FMAX = 2
NEG_FILL = -1e30
SCALE = 1.0 / math.sqrt(HDIM)
F32 = jnp.float32
BF16 = jnp.bfloat16
SQUARE = 4
HBM_BYTES = 3.69e6
PAIR = 4


def contract(left, right, left_dim, right_dim):
    return lax.dot_general(
        left, right, (((left_dim,), (right_dim,)), ((), ())), preferred_element_type=F32
    )


def head_slice(stacked, head):
    return stacked[:, head * HDIM : (head + 1) * HDIM]


def swap(block, axis, bit):
    count = lax.axis_size(axis)
    return lax.ppermute(block, axis, [(i, i ^ bit) for i in range(count)])


def cost_of(micros):
    return pl.CostEstimate(flops=0, bytes_accessed=int(micros * HBM_BYTES), transcendentals=0)


def local_call(body, name, micros, out_shapes, args, tables=0):
    spaces = [pltpu.SMEM] * tables + [pltpu.VMEM] * (len(args) - tables)
    return pl.pallas_call(
        body,
        name=name,
        out_shape=out_shapes,
        in_specs=[pl.BlockSpec(memory_space=space) for space in spaces],
        out_specs=[pl.BlockSpec(memory_space=pltpu.VMEM)] * len(out_shapes),
        compiler_params=pltpu.CompilerParams(vmem_limit_bytes=20 * 2**20),
        cost_estimate=cost_of(micros),
    )(*args)


def load_kernel(k_ref, hk_ref, v_ref, hv_ref, kv_out, kv_ref, sems):
    inward, outward, begin = [], [], 0
    for i, ref in enumerate((k_ref, hk_ref, v_ref, hv_ref)):
        part = pl.ds(begin, ref.shape[0])
        inward.append(pltpu.make_async_copy(ref, kv_ref.at[part], sems.at[0, i]))
        outward.append(pltpu.make_async_copy(kv_ref.at[part], kv_out.at[part], sems.at[1, i]))
        begin += ref.shape[0]
    for copy in inward:
        copy.start()
    for before, after in zip(inward, outward):
        before.wait()
        after.start()
    for copy in outward:
        copy.wait()


def load_keys(*arrays):
    rows = sum(a.shape[0] for a in arrays)
    width = arrays[0].shape[1]
    return pl.pallas_call(
        load_kernel,
        name="load",
        out_shape=jax.ShapeDtypeStruct((rows, width), BF16),
        in_specs=[pl.BlockSpec(memory_space=pl.ANY)] * len(arrays),
        out_specs=pl.BlockSpec(memory_space=pl.ANY),
        scratch_shapes=[pltpu.VMEM((rows, width), BF16), pltpu.SemaphoreType.DMA((2, len(arrays)))],
        compiler_params=pltpu.CompilerParams(vmem_limit_bytes=60 * 2**20),
        cost_estimate=cost_of(1.6),
    )(*arrays)


def pass_keys_kernel(kv2, key_ref):
    key_ref[...] = kv2[: key_ref.shape[0]]


def pass_values_kernel(kv2, value_ref):
    value_ref[...] = kv2[value_ref.shape[0] :]


def square_blocks(kv0, kv1, kv2, key3, value3):
    keys = key3.shape[0]
    pairs = [(ref.at[:keys], ref.at[keys:]) for ref in (kv0, kv1, kv2)]
    return pairs + [(key3, value3)]


def load_weight_kernel(w_ref, w_out, sems):
    copies = []
    for i in range(sems.shape[0]):
        part = pl.ds(i * HDIM, HDIM)
        copies.append(pltpu.make_async_copy(w_ref.at[part], w_out.at[part], sems.at[i]))
    for copy in copies:
        copy.start()
    for copy in copies:
        copy.wait()


def load_weight(w_out):
    return pl.pallas_call(
        load_weight_kernel,
        name="load_w",
        out_shape=jax.ShapeDtypeStruct(w_out.shape, BF16),
        in_specs=[pl.BlockSpec(memory_space=pl.ANY)],
        out_specs=pl.BlockSpec(memory_space=pltpu.VMEM),
        scratch_shapes=[pltpu.SemaphoreType.DMA((w_out.shape[0] // HDIM,))],
        compiler_params=pltpu.CompilerParams(vmem_limit_bytes=50 * 2**20 + 2**19),
        cost_estimate=cost_of(1.6),
    )(w_out)


def limits_kernel(levels_ref, counts_ref, limits_ref):
    me = lax.axis_index("ctx")
    row = lax.broadcasted_iota(jnp.int32, limits_ref.shape, 0)
    limits = jnp.zeros(limits_ref.shape, jnp.int32)
    for step in range(SQUARE):
        total = jnp.int32(0)
        for frame in range(FMAX):
            tokens = lax.shift_right_logical(jnp.int32(FTOK), 2 * levels_ref[me ^ step, frame])
            total += jnp.where(frame < counts_ref[me ^ step], tokens, 0)
        limits = jnp.where(row == step, total, limits)
    limits_ref[...] = limits


def dattn_kernel(own_ref, core_ref, near_ref, far_ref, w_ref, out_ref):
    me = lax.axis_index("head")
    size = own_ref.shape[1]
    total = None
    for step, ref in enumerate((own_ref, core_ref, near_ref, far_ref)):
        columns = pl.ds(pl.multiple_of((me ^ step) * size, HDIM), size)
        part = contract(ref[...], w_ref[:, columns], 1, 1)
        total = part if total is None else total + part
    out_ref[...] = total.astype(BF16)


def both_rows(own_ref, pair_ref, head):
    return jnp.concatenate(
        [head_slice(own_ref[...], head), head_slice(pair_ref[...], head)], axis=0
    )


def scores_kernel(
    limits_ref, q_own_ref, q_pair_ref, kv0, kv1, kv2, key3, lse_ref, probs_ref
):
    rows = q_own_ref.shape[0]
    keys = key3.shape[0]
    blocks = [ref.at[:keys] for ref in (kv0, kv1, kv2)] + [key3]
    lse_ref[...] = jnp.zeros_like(lse_ref)
    for head in range(q_own_ref.shape[1] // HDIM):
        query = both_rows(q_own_ref, q_pair_ref, head)
        scores = []
        for step, key_ref in enumerate(blocks):
            block = contract(head_slice(key_ref[...], head), query, 1, 1) * SCALE
            slot = lax.broadcasted_iota(jnp.int32, block.shape, 0)
            valid = slot < rows + limits_ref[step : step + 1]
            scores.append(jnp.where(valid, block, NEG_FILL))
        top = functools.reduce(
            jnp.maximum, [jnp.max(block, axis=0, keepdims=True) for block in scores]
        )
        weights = [jnp.exp(block - top) for block in scores]
        total = sum(jnp.sum(block, axis=0, keepdims=True) for block in weights)
        inverse = 1.0 / total
        for step, block in enumerate(weights):
            begin = (head * SQUARE + step) * keys
            probs_ref[begin : begin + keys] = (block * inverse).astype(BF16)
        lse_ref[head : head + 1] = top + jnp.log(total)


def delta_kernel(
    lse_ref, probs_ref, d_own_ref, d_pair_ref, kv0, kv1, kv2, key3, value3, stats_ref, dprobs_ref
):
    keys = key3.shape[0]
    blocks = square_blocks(kv0, kv1, kv2, key3, value3)
    stats_ref[...] = jnp.zeros_like(stats_ref)
    stats_ref[: lse_ref.shape[0]] = lse_ref[...]
    for head in range(d_own_ref.shape[1] // HDIM):
        dattn = both_rows(d_own_ref, d_pair_ref, head)
        delta = None
        for step, (_, value_ref) in enumerate(blocks):
            part = pl.ds((head * SQUARE + step) * keys, keys)
            dprobs = contract(head_slice(value_ref[...], head), dattn, 1, 1)
            dprobs_ref[part] = dprobs
            share = jnp.sum(probs_ref[part].astype(F32) * dprobs, axis=0, keepdims=True)
            delta = share if delta is None else delta + share
        stats_ref[8 + head : 9 + head] = delta


def attn_kernel(kv0, kv1, kv2, key3, value3, probs_ref, own_ref, pair_ref):
    rows = own_ref.shape[1]
    keys = key3.shape[0]
    blocks = square_blocks(kv0, kv1, kv2, key3, value3)
    for head in range(own_ref.shape[0] // HDIM):
        attn = None
        for step, (_, value_ref) in enumerate(blocks):
            begin = (head * SQUARE + step) * keys
            part = contract(head_slice(value_ref[...], head), probs_ref[begin : begin + keys], 0, 0)
            attn = part if attn is None else attn + part
        features = slice(head * HDIM, (head + 1) * HDIM)
        own_ref[features] = attn[:, :rows]
        pair_ref[features] = attn[:, rows:].astype(BF16)


def merge_parts(mine, theirs):
    top = jnp.maximum(mine, theirs)
    weight, weight_pair = jnp.exp(mine - top), jnp.exp(theirs - top)
    inverse = 1.0 / (weight + weight_pair)
    return weight * inverse, weight_pair * inverse


def project_kernel(own_ref, pair_ref, stats_ref, stats_pair_ref, w_ref, keep_ref, *send_refs):
    rows = own_ref.shape[1]
    parts = []
    for head in range(own_ref.shape[0] // HDIM):
        features = slice(head * HDIM, (head + 1) * HDIM)
        weight, weight_pair = merge_parts(
            stats_ref[head : head + 1, :rows], stats_pair_ref[head : head + 1, rows:]
        )
        parts.append(own_ref[features] * weight + pair_ref[features].astype(F32) * weight_pair)
    attn = jnp.concatenate(parts, axis=0).astype(BF16)
    me = lax.axis_index("head")
    size = keep_ref.shape[1]
    for step, ref in enumerate((keep_ref, *send_refs)):
        columns = pl.ds(pl.multiple_of((me ^ step) * size, HDIM), size)
        ref[...] = contract(attn, w_ref[:, columns], 0, 0).astype(ref.dtype)


def backward_kernel(
    q_own_ref, q_pair_ref, d_own_ref, d_pair_ref, kv0, kv1, kv2, key3, value3,
    stats_ref, stats_pair_ref, probs_ref, dprobs_ref,
    dq_own_ref, dq_pair_ref, dkv_ref, send_k_ref, send_v_ref, near_k_ref, near_v_ref,
):
    rows = q_own_ref.shape[0]
    keys = key3.shape[0]
    blocks = square_blocks(kv0, kv1, kv2, key3, value3)
    key_parts = (dkv_ref.at[:keys], send_k_ref.at[:keys], near_k_ref, send_k_ref.at[keys:])
    value_parts = (dkv_ref.at[keys:], near_v_ref, send_v_ref.at[:keys], send_v_ref.at[keys:])

    def swapped(row):
        return jnp.concatenate([row[:, rows:], row[:, :rows]], axis=1)

    for head in range(q_own_ref.shape[1] // HDIM):
        query = both_rows(q_own_ref, q_pair_ref, head)
        dattn = both_rows(d_own_ref, d_pair_ref, head)
        weight, weight_pair = merge_parts(
            stats_ref[head : head + 1], swapped(stats_pair_ref[head : head + 1])
        )
        delta = weight * stats_ref[8 + head : 9 + head]
        delta += weight_pair * swapped(stats_pair_ref[8 + head : 9 + head])
        features = slice(head * HDIM, (head + 1) * HDIM)
        dquery = None
        for step, (key_ref, _) in enumerate(blocks):
            begin = (head * SQUARE + step) * keys
            probs = (probs_ref[begin : begin + keys].astype(F32) * weight).astype(BF16)
            dprobs = dprobs_ref[begin : begin + keys]
            dscores = (probs.astype(F32) * (dprobs - delta)).astype(BF16)
            key_part, value_part = key_parts[step], value_parts[step]
            grad_key = contract(dscores, query, 1, 0) * SCALE
            key_part[:, features] = grad_key.astype(key_part.dtype)
            value_part[:, features] = contract(probs, dattn, 1, 0).astype(value_part.dtype)
            part = contract(dscores, head_slice(key_ref[...], head), 0, 0)
            dquery = part if dquery is None else dquery + part
        dq_own_ref[:, features] = dquery[:rows] * SCALE
        dq_pair_ref[:, features] = (dquery[rows:] * SCALE).astype(BF16)


def pass_on_kernel(near_k_ref, near_v_ref, got_k_ref, got_v_ref, k_ref, v_ref):
    keys = near_k_ref.shape[0]
    k_ref[...] = (near_k_ref[...] + got_k_ref[keys:].astype(F32)).astype(BF16)
    v_ref[...] = (near_v_ref[...] + got_v_ref[keys:].astype(F32)).astype(BF16)


def finish_kernel(
    keep_ref, near_ref, far_ref, dq_ref, dq_pair_ref, core_ref,
    dkv_ref, got_k_ref, got_v_ref, rest_k_ref, rest_v_ref,
    q_out, k_out, v_out, hk_out, hv_out, out_ref,
):
    rows, capacity = k_out.shape[0], hk_out.shape[0]
    keys = rows + capacity

    def total(first, *others):
        for other in others:
            first = first + other.astype(F32)
        return first.astype(BF16)

    q_out[...] = total(dq_ref[...], dq_pair_ref[...])
    k_out[...] = total(dkv_ref[:rows], got_k_ref[:rows], rest_k_ref[:rows])
    hk_out[...] = total(dkv_ref[rows:keys], got_k_ref[rows:keys], rest_k_ref[rows:])
    v_out[...] = total(dkv_ref[keys : keys + rows], got_v_ref[:rows], rest_v_ref[:rows])
    hv_out[...] = total(dkv_ref[keys + rows :], got_v_ref[rows:keys], rest_v_ref[rows:])
    out_ref[...] = total(keep_ref[...], core_ref[...], near_ref[...], far_ref[...])


def blocked(sec_q, sec_k, sec_v, hist_k, hist_v, frame_levels, frame_counts, w_out, grad_out):
    shape = jax.ShapeDtypeStruct
    rows, width = sec_q.shape
    heads = width // HDIM
    capacity = hist_k.shape[0]
    keys = rows + capacity
    share = grad_out.shape[1]

    q_pair = swap(sec_q, "ctx", PAIR)
    grad_near = swap(grad_out, "head", 2)
    grad_core = swap(grad_out, "head", 1)
    weight = load_weight(w_out)
    grad_near, weight = lax.optimization_barrier((grad_near, weight))
    grad_far = swap(grad_near, "head", 1)
    kv0 = load_keys(sec_k, hist_k, sec_v, hist_v)
    kv2 = swap(kv0, "ctx", 2)
    kv1 = swap(kv0, "ctx", 1)
    d_own = local_call(
        dattn_kernel,
        "dattn",
        0.8,
        [shape((rows, width), BF16)],
        (grad_out, grad_core, grad_near, grad_far, weight),
    )[0]
    kv1, kv2, d_own = lax.optimization_barrier((kv1, kv2, d_own))
    key3 = local_call(pass_keys_kernel, "pass_keys", 0.1, [shape((keys, width), BF16)], (kv2,))[0]
    limits = local_call(
        limits_kernel,
        "limits",
        0.6,
        [shape((8, 2 * rows), jnp.int32)],
        (frame_levels, frame_counts),
        tables=2,
    )[0]
    kv2_kept, q_pair, limits, _ = lax.optimization_barrier((kv2, q_pair, limits, key3))
    value3 = local_call(
        pass_values_kernel, "pass_values", 1.0, [shape((keys, width), BF16)], (kv2_kept,)
    )[0]
    kvs = [kv0, kv1, kv2, swap(key3, "ctx", 1), swap(value3, "ctx", 1)]
    d_pair = swap(d_own, "ctx", PAIR)
    lse, probs = local_call(
        scores_kernel,
        "scores",
        0.9,
        [shape((8, 2 * rows), F32), shape((heads * SQUARE * keys, 2 * rows), BF16)],
        (limits, sec_q, q_pair, *kvs[:4]),
    )
    attn_own, attn_pair = local_call(
        attn_kernel,
        "attn",
        0.5,
        [shape((width, rows), F32), shape((width, rows), BF16)],
        (*kvs, probs),
    )
    lse, attn_own = lax.optimization_barrier((lse, attn_own))
    stats, dprobs = local_call(
        delta_kernel,
        "delta",
        0.7,
        [shape((16, 2 * rows), F32), shape((heads * SQUARE * keys, 2 * rows), F32)],
        (lse, probs, d_own, d_pair, *kvs),
    )
    stats_pair = swap(stats, "ctx", PAIR)
    dq_own, dq_pair, dkv_own, send_k, send_v, near_k, near_v = local_call(
        backward_kernel,
        "backward",
        1.1,
        [shape((rows, width), F32), shape((rows, width), BF16), shape((2 * keys, width), F32)]
        + [shape((2 * keys, width), BF16)] * 2
        + [shape((keys, width), F32)] * 2,
        (sec_q, q_pair, d_own, d_pair, *kvs, stats, stats_pair, probs, dprobs),
    )
    attn_got = swap(attn_pair, "ctx", PAIR)
    attn_got, send_k, send_v = lax.optimization_barrier((attn_got, send_k, send_v))
    got_k = swap(send_k, "ctx", 1)
    got_v = swap(send_v, "ctx", 2)
    rest_k, rest_v = local_call(
        pass_on_kernel,
        "pass_on",
        0.1,
        [shape((keys, width), BF16)] * 2,
        (near_k, near_v, got_k, got_v),
    )
    rest_k = swap(rest_k, "ctx", 2)
    rest_v = swap(rest_v, "ctx", 1)
    out_keep, *out_send = local_call(
        project_kernel,
        "project",
        0.6,
        [shape((rows, share), F32)] + [shape((rows, share), BF16)] * 3,
        (attn_own, attn_got, stats, stats_pair, weight),
    )
    out_near, out_far = (swap(out_send[step - 1], "head", step) for step in (2, 3))
    dq_got = swap(dq_pair, "ctx", PAIR)
    out_core = swap(out_send[0], "head", 1)
    grad_q, grad_k, grad_v, grad_hk, grad_hv, out = local_call(
        finish_kernel,
        "finish",
        0.9,
        [shape((rows, width), BF16)] * 3
        + [shape((capacity, width), BF16)] * 2
        + [shape((rows, share), BF16)],
        (
            out_keep, out_near, out_far, dq_own, dq_got, out_core,
            dkv_own, got_k, got_v, rest_k, rest_v,
        ),
    )
    return out, grad_q, grad_k, grad_v, grad_hk, grad_hv


def gathered(sec_q, sec_k, sec_v, hist_k, hist_v, frame_levels, frame_counts, w_out, grad_out):
    rows = sec_q.shape[0]
    capacity = hist_k.shape[0]
    owners = lax.axis_size("ctx")
    me = lax.axis_index("ctx")
    frames = jnp.arange(FMAX, dtype=jnp.int32)[None, :]
    tokens = jnp.where(
        frames < frame_counts[:, None], jnp.right_shift(jnp.int32(FTOK), 2 * frame_levels), 0
    ).sum(axis=1)
    slots = jnp.arange(capacity, dtype=jnp.int32)
    all_valid = jnp.concatenate(
        [jnp.ones((owners * rows,), bool), (slots[None] < tokens[:, None]).reshape(-1)]
    )
    own_valid = jnp.concatenate(
        [jnp.ones((rows,), bool), slots < lax.dynamic_index_in_dim(tokens, me, keepdims=False)]
    )

    def everyone(block, axis=0):
        return lax.all_gather(block, "ctx", axis=axis, tiled=True)

    own_k, own_v = (jnp.concatenate(a, axis=0) for a in ((sec_k, hist_k), (sec_v, hist_v)))
    all_k = jnp.concatenate([everyone(sec_k), everyone(hist_k)], axis=0)
    all_v = jnp.concatenate([everyone(sec_v), everyone(hist_v)], axis=0)
    d_attn = contract(lax.all_gather(grad_out, "head", axis=1, tiled=True), w_out, 1, 1).astype(BF16)
    all_q, all_d = everyone(sec_q), everyone(d_attn)

    def probs_and_dscores(query, key, value, dattn, valid, lse, delta):
        scores = contract(query, key, 1, 1) * SCALE
        probs = jnp.where(valid[None, :], jnp.exp(scores - lse), 0.0).astype(BF16)
        dprobs = contract(dattn, value, 1, 1)
        return probs, (probs.astype(F32) * (dprobs - delta)).astype(BF16)

    attn_parts, q_parts, k_parts, v_parts = [], [], [], []
    for head in range(sec_q.shape[1] // HDIM):
        query, dattn, key, value = (head_slice(a, head) for a in (sec_q, d_attn, all_k, all_v))
        scores = jnp.where(all_valid[None, :], contract(query, key, 1, 1) * SCALE, NEG_FILL)
        lse = jax.nn.logsumexp(scores, axis=1, keepdims=True)
        probs = jnp.where(all_valid[None, :], jnp.exp(scores - lse), 0.0).astype(BF16)
        attn = contract(probs, value, 1, 0).astype(BF16)
        delta = jnp.sum(attn.astype(F32) * dattn.astype(F32), axis=1, keepdims=True)
        _, dscores = probs_and_dscores(query, key, value, dattn, all_valid, lse, delta)
        attn_parts.append(attn)
        q_parts.append(contract(dscores, key, 1, 0))
        query, dattn, key, value = (head_slice(a, head) for a in (all_q, all_d, own_k, own_v))
        probs, dscores = probs_and_dscores(
            query, key, value, dattn, own_valid, everyone(lse), everyone(delta)
        )
        k_parts.append(contract(dscores, query, 0, 0))
        v_parts.append(contract(probs, dattn, 0, 0))
    partial = contract(jnp.concatenate(attn_parts, axis=1), w_out, 1, 0).astype(BF16)
    out = lax.psum_scatter(partial, "head", scatter_dimension=1, tiled=True)
    grad_q, grad_k = (
        (jnp.concatenate(a, axis=1) * SCALE).astype(BF16) for a in (q_parts, k_parts)
    )
    grad_v = jnp.concatenate(v_parts, axis=1).astype(BF16)
    return out, grad_q, grad_k[:rows], grad_v[:rows], grad_k[rows:], grad_v[rows:]


def solution(mesh):
    split = P("ctx", "head")
    plan = blocked if (mesh.shape["ctx"], mesh.shape["head"]) == (2 * SQUARE, 4) else gathered
    return jax.shard_map(
        plan,
        mesh=mesh,
        in_specs=(split,) * 5 + (P(), P(), P("head", None), split),
        out_specs=(split,) * 6,
        check_vma=False,
    )
```

```python
import functools
import math

import jax
import jax.numpy as jnp
from jax import lax
from jax.experimental import pallas as pl
from jax.experimental.pallas import tpu as pltpu
from jax.sharding import PartitionSpec as P

HDIM = 128
FTOK = 16
FMAX = 2
NEG_FILL = -1e30
SCALE = 1.0 / math.sqrt(HDIM)
F32 = jnp.float32
BF16 = jnp.bfloat16
SQUARE = 4
HBM_BYTES = 3.69e6
PAIR = 4


def contract(left, right, left_dim, right_dim):
    return lax.dot_general(
        left, right, (((left_dim,), (right_dim,)), ((), ())), preferred_element_type=F32
    )


def head_slice(stacked, head):
    return stacked[:, head * HDIM : (head + 1) * HDIM]


def swap(block, axis, bit):
    count = lax.axis_size(axis)
    return lax.ppermute(block, axis, [(i, i ^ bit) for i in range(count)])


def cost_of(micros):
    return pl.CostEstimate(flops=0, bytes_accessed=int(micros * HBM_BYTES), transcendentals=0)


def local_call(body, name, micros, out_shapes, args, tables=0, vmem=20):
    spaces = [pltpu.SMEM] * tables + [pltpu.VMEM] * (len(args) - tables)
    return pl.pallas_call(
        body,
        name=name,
        out_shape=out_shapes,
        in_specs=[pl.BlockSpec(memory_space=space) for space in spaces],
        out_specs=[pl.BlockSpec(memory_space=pltpu.VMEM)] * len(out_shapes),
        compiler_params=pltpu.CompilerParams(vmem_limit_bytes=vmem * 2**20),
        cost_estimate=cost_of(micros),
    )(*args)


def load_kernel(k_ref, hk_ref, v_ref, hv_ref, kv_out, kv_ref, sems):
    inward, outward, begin = [], [], 0
    for i, ref in enumerate((k_ref, hk_ref, v_ref, hv_ref)):
        part = pl.ds(begin, ref.shape[0])
        inward.append(pltpu.make_async_copy(ref, kv_ref.at[part], sems.at[0, i]))
        outward.append(pltpu.make_async_copy(kv_ref.at[part], kv_out.at[part], sems.at[1, i]))
        begin += ref.shape[0]
    for copy in inward:
        copy.start()
    for before, after in zip(inward, outward):
        before.wait()
        after.start()
    for copy in outward:
        copy.wait()


def load_keys(*arrays):
    rows = sum(a.shape[0] for a in arrays)
    width = arrays[0].shape[1]
    return pl.pallas_call(
        load_kernel,
        name="load",
        out_shape=jax.ShapeDtypeStruct((rows, width), BF16),
        in_specs=[pl.BlockSpec(memory_space=pl.ANY)] * len(arrays),
        out_specs=pl.BlockSpec(memory_space=pl.ANY),
        scratch_shapes=[pltpu.VMEM((rows, width), BF16), pltpu.SemaphoreType.DMA((2, len(arrays)))],
        compiler_params=pltpu.CompilerParams(vmem_limit_bytes=60 * 2**20),
        cost_estimate=cost_of(1.6),
    )(*arrays)


def split_heads_kernel(kv_ref, *out_refs):
    for head, ref in enumerate(out_refs):
        ref[...] = head_slice(kv_ref[...], head)


def square_keys(head, near, far):
    keys = near[0].shape[0] // 2
    return [head_slice(ref[:keys], head) for ref in near] + [far[head][:keys]]


def square_values(head, near, far):
    keys = near[0].shape[0] // 2
    return [head_slice(ref[keys:], head) for ref in near] + [far[head][keys:]]


def load_weight_kernel(w_ref, w_out, sems):
    copies = []
    for i in range(sems.shape[0]):
        part = pl.ds(i * HDIM, HDIM)
        copies.append(pltpu.make_async_copy(w_ref.at[part], w_out.at[part], sems.at[i]))
    for copy in copies:
        copy.start()
    for copy in copies:
        copy.wait()


def load_weight(w_out):
    return pl.pallas_call(
        load_weight_kernel,
        name="load_w",
        out_shape=jax.ShapeDtypeStruct(w_out.shape, BF16),
        in_specs=[pl.BlockSpec(memory_space=pl.ANY)],
        out_specs=pl.BlockSpec(memory_space=pltpu.VMEM),
        scratch_shapes=[pltpu.SemaphoreType.DMA((w_out.shape[0] // HDIM,))],
        compiler_params=pltpu.CompilerParams(vmem_limit_bytes=50 * 2**20 + 2**19),
        cost_estimate=cost_of(1.6),
    )(w_out)


def limits_kernel(levels_ref, counts_ref, limits_ref):
    me = lax.axis_index("ctx")
    row = lax.broadcasted_iota(jnp.int32, limits_ref.shape, 0)
    limits = jnp.zeros(limits_ref.shape, jnp.int32)
    for step in range(SQUARE):
        total = jnp.int32(0)
        for frame in range(FMAX):
            tokens = lax.shift_right_logical(jnp.int32(FTOK), 2 * levels_ref[me ^ step, frame])
            total += jnp.where(frame < counts_ref[me ^ step], tokens, 0)
        limits = jnp.where(row == step, total, limits)
    limits_ref[...] = limits


def dattn_kernel(own_ref, core_ref, near_ref, far_ref, w_ref, out_ref):
    me = lax.axis_index("head")
    size = own_ref.shape[1]
    total = None
    for step, ref in enumerate((own_ref, core_ref, near_ref, far_ref)):
        columns = pl.ds(pl.multiple_of((me ^ step) * size, HDIM), size)
        part = contract(ref[...], w_ref[:, columns], 1, 1)
        total = part if total is None else total + part
    out_ref[...] = total.astype(BF16)


def both_rows(own_ref, pair_ref, head):
    return jnp.concatenate(
        [head_slice(own_ref[...], head), head_slice(pair_ref[...], head)], axis=0
    )


def scores_kernel(
    limits_ref, q_own_ref, q_pair_ref, kv0, kv1, kv2, *refs
):
    rows = q_own_ref.shape[0]
    *far, lse_ref, probs_ref = refs
    keys = kv0.shape[0] // 2
    lse_ref[...] = jnp.zeros_like(lse_ref)
    for head in range(q_own_ref.shape[1] // HDIM):
        query = both_rows(q_own_ref, q_pair_ref, head)
        scores = []
        for step, key in enumerate(square_keys(head, (kv0, kv1, kv2), far)):
            block = contract(key, query, 1, 1) * SCALE
            slot = lax.broadcasted_iota(jnp.int32, block.shape, 0)
            valid = slot < rows + limits_ref[step : step + 1]
            scores.append(jnp.where(valid, block, NEG_FILL))
        top = functools.reduce(
            jnp.maximum, [jnp.max(block, axis=0, keepdims=True) for block in scores]
        )
        weights = [jnp.exp(block - top) for block in scores]
        total = sum(jnp.sum(block, axis=0, keepdims=True) for block in weights)
        inverse = 1.0 / total
        for step, block in enumerate(weights):
            begin = (head * SQUARE + step) * keys
            probs_ref[begin : begin + keys] = (block * inverse).astype(BF16)
        lse_ref[head : head + 1] = top + jnp.log(total)


def delta_kernel(lse_ref, probs_ref, d_own_ref, d_pair_ref, kv0, kv1, kv2, *refs):
    *far, stats_ref, dprobs_ref = refs
    keys = kv0.shape[0] // 2
    stats_ref[...] = jnp.zeros_like(stats_ref)
    stats_ref[: lse_ref.shape[0]] = lse_ref[...]
    for head in range(d_own_ref.shape[1] // HDIM):
        dattn = both_rows(d_own_ref, d_pair_ref, head)
        delta = None
        for step, value in enumerate(square_values(head, (kv0, kv1, kv2), far)):
            part = pl.ds((head * SQUARE + step) * keys, keys)
            dprobs = contract(value, dattn, 1, 1)
            dprobs_ref[part] = dprobs
            share = jnp.sum(probs_ref[part].astype(F32) * dprobs, axis=0, keepdims=True)
            delta = share if delta is None else delta + share
        stats_ref[8 + head : 9 + head] = delta


def attn_kernel(probs_ref, kv0, kv1, kv2, *refs):
    *far, own_ref, pair_ref = refs
    rows = own_ref.shape[1]
    keys = kv0.shape[0] // 2
    for head in range(own_ref.shape[0] // HDIM):
        attn = None
        for step, value in enumerate(square_values(head, (kv0, kv1, kv2), far)):
            begin = (head * SQUARE + step) * keys
            part = contract(value, probs_ref[begin : begin + keys], 0, 0)
            attn = part if attn is None else attn + part
        features = slice(head * HDIM, (head + 1) * HDIM)
        own_ref[features] = attn[:, :rows]
        pair_ref[features] = attn[:, rows:].astype(BF16)


def merge_parts(mine, theirs):
    top = jnp.maximum(mine, theirs)
    weight, weight_pair = jnp.exp(mine - top), jnp.exp(theirs - top)
    inverse = 1.0 / (weight + weight_pair)
    return weight * inverse, weight_pair * inverse


def project_kernel(own_ref, pair_ref, stats_ref, stats_pair_ref, w_ref, keep_ref, *send_refs):
    rows = own_ref.shape[1]
    parts = []
    for head in range(own_ref.shape[0] // HDIM):
        features = slice(head * HDIM, (head + 1) * HDIM)
        weight, weight_pair = merge_parts(
            stats_ref[head : head + 1, :rows], stats_pair_ref[head : head + 1, rows:]
        )
        parts.append(own_ref[features] * weight + pair_ref[features].astype(F32) * weight_pair)
    attn = jnp.concatenate(parts, axis=0).astype(BF16)
    me = lax.axis_index("head")
    size = keep_ref.shape[1]
    for step, ref in enumerate((keep_ref, *send_refs)):
        columns = pl.ds(pl.multiple_of((me ^ step) * size, HDIM), size)
        ref[...] = contract(attn, w_ref[:, columns], 0, 0).astype(ref.dtype)


def backward_kernel(
    q_own_ref, q_pair_ref, d_own_ref, d_pair_ref, stats_ref, stats_pair_ref, probs_ref, dprobs_ref,
    kv0, kv1, kv2, *refs,
):
    rows = q_own_ref.shape[0]
    *far, dq_own_ref, dq_pair_ref, dkv_ref, send_k_ref, send_v_ref, near_k_ref, near_v_ref = refs
    keys = kv0.shape[0] // 2
    key_parts = (dkv_ref.at[:keys], send_k_ref.at[:keys], near_k_ref, send_k_ref.at[keys:])
    value_parts = (dkv_ref.at[keys:], near_v_ref, send_v_ref.at[:keys], send_v_ref.at[keys:])

    def swapped(row):
        return jnp.concatenate([row[:, rows:], row[:, :rows]], axis=1)

    for head in range(q_own_ref.shape[1] // HDIM):
        query = both_rows(q_own_ref, q_pair_ref, head)
        dattn = both_rows(d_own_ref, d_pair_ref, head)
        weight, weight_pair = merge_parts(
            stats_ref[head : head + 1], swapped(stats_pair_ref[head : head + 1])
        )
        delta = weight * stats_ref[8 + head : 9 + head]
        delta += weight_pair * swapped(stats_pair_ref[8 + head : 9 + head])
        features = slice(head * HDIM, (head + 1) * HDIM)
        dquery = None
        for step, key in enumerate(square_keys(head, (kv0, kv1, kv2), far)):
            begin = (head * SQUARE + step) * keys
            probs = (probs_ref[begin : begin + keys].astype(F32) * weight).astype(BF16)
            dprobs = dprobs_ref[begin : begin + keys]
            dscores = (probs.astype(F32) * (dprobs - delta)).astype(BF16)
            key_part, value_part = key_parts[step], value_parts[step]
            grad_key = contract(dscores, query, 1, 0) * SCALE
            key_part[:, features] = grad_key.astype(key_part.dtype)
            value_part[:, features] = contract(probs, dattn, 1, 0).astype(value_part.dtype)
            part = contract(dscores, key, 0, 0)
            dquery = part if dquery is None else dquery + part
        dq_own_ref[:, features] = dquery[:rows] * SCALE
        dq_pair_ref[:, features] = (dquery[rows:] * SCALE).astype(BF16)


def pass_on_kernel(near_k_ref, near_v_ref, got_k_ref, got_v_ref, k_ref, v_ref):
    keys = near_k_ref.shape[0]
    k_ref[...] = (near_k_ref[...] + got_k_ref[keys:].astype(F32)).astype(BF16)
    v_ref[...] = (near_v_ref[...] + got_v_ref[keys:].astype(F32)).astype(BF16)


def finish_kernel(
    keep_ref, near_ref, far_ref, dq_ref, dq_pair_ref, core_ref,
    dkv_ref, got_k_ref, got_v_ref, rest_k_ref, rest_v_ref,
    q_out, k_out, v_out, hk_out, hv_out, out_ref,
):
    rows, capacity = k_out.shape[0], hk_out.shape[0]
    keys = rows + capacity

    def total(first, *others):
        for other in others:
            first = first + other.astype(F32)
        return first.astype(BF16)

    q_out[...] = total(dq_ref[...], dq_pair_ref[...])
    k_out[...] = total(dkv_ref[:rows], got_k_ref[:rows], rest_k_ref[:rows])
    hk_out[...] = total(dkv_ref[rows:keys], got_k_ref[rows:keys], rest_k_ref[rows:])
    v_out[...] = total(dkv_ref[keys : keys + rows], got_v_ref[:rows], rest_v_ref[:rows])
    hv_out[...] = total(dkv_ref[keys + rows :], got_v_ref[rows:keys], rest_v_ref[rows:])
    out_ref[...] = total(keep_ref[...], core_ref[...], near_ref[...], far_ref[...])


def blocked(sec_q, sec_k, sec_v, hist_k, hist_v, frame_levels, frame_counts, w_out, grad_out):
    shape = jax.ShapeDtypeStruct
    rows, width = sec_q.shape
    heads = width // HDIM
    capacity = hist_k.shape[0]
    keys = rows + capacity
    share = grad_out.shape[1]

    q_pair = swap(sec_q, "ctx", PAIR)
    grad_near = swap(grad_out, "head", 2)
    grad_core = swap(grad_out, "head", 1)
    weight = load_weight(w_out)
    grad_near, weight = lax.optimization_barrier((grad_near, weight))
    grad_far = swap(grad_near, "head", 1)
    kv0 = load_keys(sec_k, hist_k, sec_v, hist_v)
    kv2 = swap(kv0, "ctx", 2)
    kv1 = swap(kv0, "ctx", 1)
    d_own = local_call(
        dattn_kernel,
        "dattn",
        0.8,
        [shape((rows, width), BF16)],
        (grad_out, grad_core, grad_near, grad_far, weight),
        vmem=40,
    )[0]
    limits = local_call(
        limits_kernel,
        "limits",
        0.6,
        [shape((8, 2 * rows), jnp.int32)],
        (frame_levels, frame_counts),
        tables=2,
    )[0]
    kv1, kv2, d_own, limits = lax.optimization_barrier((kv1, kv2, d_own, limits))
    pieces = local_call(
        split_heads_kernel, "split_heads", 0.1, [shape((2 * keys, HDIM), BF16)] * heads, (kv2,)
    )
    kvs = (kv0, kv1, kv2, *(swap(piece, "ctx", 1) for piece in pieces))
    d_pair = swap(d_own, "ctx", PAIR)
    lse, probs = local_call(
        scores_kernel,
        "scores",
        0.9,
        [shape((8, 2 * rows), F32), shape((heads * SQUARE * keys, 2 * rows), BF16)],
        (limits, sec_q, q_pair, *kvs),
    )
    attn_own, attn_pair = local_call(
        attn_kernel,
        "attn",
        0.5,
        [shape((width, rows), F32), shape((width, rows), BF16)],
        (probs, *kvs),
    )
    lse, attn_own = lax.optimization_barrier((lse, attn_own))
    stats, dprobs = local_call(
        delta_kernel,
        "delta",
        0.7,
        [shape((16, 2 * rows), F32), shape((heads * SQUARE * keys, 2 * rows), F32)],
        (lse, probs, d_own, d_pair, *kvs),
    )
    stats_pair = swap(stats, "ctx", PAIR)
    dq_own, dq_pair, dkv_own, send_k, send_v, near_k, near_v = local_call(
        backward_kernel,
        "backward",
        1.1,
        [shape((rows, width), F32), shape((rows, width), BF16), shape((2 * keys, width), F32)]
        + [shape((2 * keys, width), BF16)] * 2
        + [shape((keys, width), F32)] * 2,
        (sec_q, q_pair, d_own, d_pair, stats, stats_pair, probs, dprobs, *kvs),
    )
    attn_got = swap(attn_pair, "ctx", PAIR)
    attn_got, send_k, send_v = lax.optimization_barrier((attn_got, send_k, send_v))
    got_k = swap(send_k, "ctx", 1)
    got_v = swap(send_v, "ctx", 2)
    rest_k, rest_v = local_call(
        pass_on_kernel,
        "pass_on",
        0.1,
        [shape((keys, width), BF16)] * 2,
        (near_k, near_v, got_k, got_v),
    )
    rest_k = swap(rest_k, "ctx", 2)
    rest_v = swap(rest_v, "ctx", 1)
    out_keep, *out_send = local_call(
        project_kernel,
        "project",
        0.6,
        [shape((rows, share), F32)] + [shape((rows, share), BF16)] * 3,
        (attn_own, attn_got, stats, stats_pair, weight),
    )
    out_near, out_far = (swap(out_send[step - 1], "head", step) for step in (2, 3))
    dq_got = swap(dq_pair, "ctx", PAIR)
    out_core = swap(out_send[0], "head", 1)
    grad_q, grad_k, grad_v, grad_hk, grad_hv, out = local_call(
        finish_kernel,
        "finish",
        0.9,
        [shape((rows, width), BF16)] * 3
        + [shape((capacity, width), BF16)] * 2
        + [shape((rows, share), BF16)],
        (
            out_keep, out_near, out_far, dq_own, dq_got, out_core,
            dkv_own, got_k, got_v, rest_k, rest_v,
        ),
    )
    return out, grad_q, grad_k, grad_v, grad_hk, grad_hv


def gathered(sec_q, sec_k, sec_v, hist_k, hist_v, frame_levels, frame_counts, w_out, grad_out):
    rows = sec_q.shape[0]
    capacity = hist_k.shape[0]
    owners = lax.axis_size("ctx")
    me = lax.axis_index("ctx")
    frames = jnp.arange(FMAX, dtype=jnp.int32)[None, :]
    tokens = jnp.where(
        frames < frame_counts[:, None], jnp.right_shift(jnp.int32(FTOK), 2 * frame_levels), 0
    ).sum(axis=1)
    slots = jnp.arange(capacity, dtype=jnp.int32)
    all_valid = jnp.concatenate(
        [jnp.ones((owners * rows,), bool), (slots[None] < tokens[:, None]).reshape(-1)]
    )
    own_valid = jnp.concatenate(
        [jnp.ones((rows,), bool), slots < lax.dynamic_index_in_dim(tokens, me, keepdims=False)]
    )

    def everyone(block, axis=0):
        return lax.all_gather(block, "ctx", axis=axis, tiled=True)

    own_k, own_v = (jnp.concatenate(a, axis=0) for a in ((sec_k, hist_k), (sec_v, hist_v)))
    all_k = jnp.concatenate([everyone(sec_k), everyone(hist_k)], axis=0)
    all_v = jnp.concatenate([everyone(sec_v), everyone(hist_v)], axis=0)
    d_attn = contract(lax.all_gather(grad_out, "head", axis=1, tiled=True), w_out, 1, 1).astype(BF16)
    all_q, all_d = everyone(sec_q), everyone(d_attn)

    def probs_and_dscores(query, key, value, dattn, valid, lse, delta):
        scores = contract(query, key, 1, 1) * SCALE
        probs = jnp.where(valid[None, :], jnp.exp(scores - lse), 0.0).astype(BF16)
        dprobs = contract(dattn, value, 1, 1)
        return probs, (probs.astype(F32) * (dprobs - delta)).astype(BF16)

    attn_parts, q_parts, k_parts, v_parts = [], [], [], []
    for head in range(sec_q.shape[1] // HDIM):
        query, dattn, key, value = (head_slice(a, head) for a in (sec_q, d_attn, all_k, all_v))
        scores = jnp.where(all_valid[None, :], contract(query, key, 1, 1) * SCALE, NEG_FILL)
        lse = jax.nn.logsumexp(scores, axis=1, keepdims=True)
        probs = jnp.where(all_valid[None, :], jnp.exp(scores - lse), 0.0).astype(BF16)
        attn = contract(probs, value, 1, 0).astype(BF16)
        delta = jnp.sum(attn.astype(F32) * dattn.astype(F32), axis=1, keepdims=True)
        _, dscores = probs_and_dscores(query, key, value, dattn, all_valid, lse, delta)
        attn_parts.append(attn)
        q_parts.append(contract(dscores, key, 1, 0))
        query, dattn, key, value = (head_slice(a, head) for a in (all_q, all_d, own_k, own_v))
        probs, dscores = probs_and_dscores(
            query, key, value, dattn, own_valid, everyone(lse), everyone(delta)
        )
        k_parts.append(contract(dscores, query, 0, 0))
        v_parts.append(contract(probs, dattn, 0, 0))
    partial = contract(jnp.concatenate(attn_parts, axis=1), w_out, 1, 0).astype(BF16)
    out = lax.psum_scatter(partial, "head", scatter_dimension=1, tiled=True)
    grad_q, grad_k = (
        (jnp.concatenate(a, axis=1) * SCALE).astype(BF16) for a in (q_parts, k_parts)
    )
    grad_v = jnp.concatenate(v_parts, axis=1).astype(BF16)
    return out, grad_q, grad_k[:rows], grad_v[:rows], grad_k[rows:], grad_v[rows:]


def solution(mesh):
    split = P("ctx", "head")
    plan = blocked if (mesh.shape["ctx"], mesh.shape["head"]) == (2 * SQUARE, 4) else gathered
    return jax.shard_map(
        plan,
        mesh=mesh,
        in_specs=(split,) * 5 + (P(), P(), P("head", None), split),
        out_specs=(split,) * 6,
        check_vma=False,
    )
```

```python
import functools
import math

import jax
import jax.numpy as jnp
from jax import lax
from jax.experimental import pallas as pl
from jax.experimental.pallas import tpu as pltpu
from jax.sharding import PartitionSpec as P

HDIM = 128
FTOK = 16
FMAX = 2
NEG_FILL = -1e30
SCALE = 1.0 / math.sqrt(HDIM)
F32 = jnp.float32
BF16 = jnp.bfloat16
SQUARE = 4
HBM_BYTES = 3.69e6
PAIR = 4


def contract(left, right, left_dim, right_dim):
    return lax.dot_general(
        left, right, (((left_dim,), (right_dim,)), ((), ())), preferred_element_type=F32
    )


def head_slice(stacked, head):
    return stacked[:, head * HDIM : (head + 1) * HDIM]


def swap(block, axis, bit):
    count = lax.axis_size(axis)
    return lax.ppermute(block, axis, [(i, i ^ bit) for i in range(count)])


def cost_of(micros):
    return pl.CostEstimate(flops=0, bytes_accessed=int(micros * HBM_BYTES), transcendentals=0)


def local_call(body, name, micros, out_shapes, args, tables=0, vmem=20):
    spaces = [pltpu.SMEM] * tables + [pltpu.VMEM] * (len(args) - tables)
    return pl.pallas_call(
        body,
        name=name,
        out_shape=out_shapes,
        in_specs=[pl.BlockSpec(memory_space=space) for space in spaces],
        out_specs=[pl.BlockSpec(memory_space=pltpu.VMEM)] * len(out_shapes),
        compiler_params=pltpu.CompilerParams(vmem_limit_bytes=vmem * 2**20),
        cost_estimate=cost_of(micros),
    )(*args)


def load_kernel(k_ref, hk_ref, v_ref, hv_ref, kv_out, kv_ref, sems):
    inward, outward, begin = [], [], 0
    for i, ref in enumerate((k_ref, hk_ref, v_ref, hv_ref)):
        part = pl.ds(begin, ref.shape[0])
        inward.append(pltpu.make_async_copy(ref, kv_ref.at[part], sems.at[0, i]))
        outward.append(pltpu.make_async_copy(kv_ref.at[part], kv_out.at[part], sems.at[1, i]))
        begin += ref.shape[0]
    for copy in inward:
        copy.start()
    for before, after in zip(inward, outward):
        before.wait()
        after.start()
    for copy in outward:
        copy.wait()


def load_keys(*arrays):
    rows = sum(a.shape[0] for a in arrays)
    width = arrays[0].shape[1]
    return pl.pallas_call(
        load_kernel,
        name="load",
        out_shape=jax.ShapeDtypeStruct((rows, width), BF16),
        in_specs=[pl.BlockSpec(memory_space=pl.ANY)] * len(arrays),
        out_specs=pl.BlockSpec(memory_space=pl.ANY),
        scratch_shapes=[pltpu.VMEM((rows, width), BF16), pltpu.SemaphoreType.DMA((2, len(arrays)))],
        compiler_params=pltpu.CompilerParams(vmem_limit_bytes=60 * 2**20),
        cost_estimate=cost_of(1.6),
    )(*arrays)


def split_heads_kernel(kv_ref, *out_refs):
    for head, ref in enumerate(out_refs):
        ref[...] = head_slice(kv_ref[...], head)


def square_keys(head, near, far):
    keys = near[0].shape[0] // 2
    return [head_slice(ref[:keys], head) for ref in near] + [far[head][:keys]]


def square_values(head, near, far):
    keys = near[0].shape[0] // 2
    return [head_slice(ref[keys:], head) for ref in near] + [far[head][keys:]]


def load_weight_kernel(w_ref, w_out, sems):
    copies = []
    for i in range(sems.shape[0]):
        part = pl.ds(i * HDIM, HDIM)
        copies.append(pltpu.make_async_copy(w_ref.at[part], w_out.at[part], sems.at[i]))
    for copy in copies:
        copy.start()
    for copy in copies:
        copy.wait()


def load_weight(w_out):
    return pl.pallas_call(
        load_weight_kernel,
        name="load_w",
        out_shape=jax.ShapeDtypeStruct(w_out.shape, BF16),
        in_specs=[pl.BlockSpec(memory_space=pl.ANY)],
        out_specs=pl.BlockSpec(memory_space=pltpu.VMEM),
        scratch_shapes=[pltpu.SemaphoreType.DMA((w_out.shape[0] // HDIM,))],
        compiler_params=pltpu.CompilerParams(vmem_limit_bytes=50 * 2**20 + 2**19),
        cost_estimate=cost_of(1.6),
    )(w_out)


def limits_kernel(levels_ref, counts_ref, limits_ref):
    me = lax.axis_index("ctx")
    row = lax.broadcasted_iota(jnp.int32, limits_ref.shape, 0)
    limits = jnp.zeros(limits_ref.shape, jnp.int32)
    for step in range(SQUARE):
        total = jnp.int32(0)
        for frame in range(FMAX):
            tokens = lax.shift_right_logical(jnp.int32(FTOK), 2 * levels_ref[me ^ step, frame])
            total += jnp.where(frame < counts_ref[me ^ step], tokens, 0)
        limits = jnp.where(row == step, total, limits)
    limits_ref[...] = limits


def dattn_kernel(own_ref, core_ref, near_ref, far_ref, w_ref, out_ref):
    me = lax.axis_index("head")
    size = own_ref.shape[1]
    total = None
    for step, ref in enumerate((own_ref, core_ref, near_ref, far_ref)):
        columns = pl.ds(pl.multiple_of((me ^ step) * size, HDIM), size)
        part = contract(ref[...], w_ref[:, columns], 1, 1)
        total = part if total is None else total + part
    out_ref[...] = total.astype(BF16)


def both_rows(own_ref, pair_ref, head):
    return jnp.concatenate(
        [head_slice(own_ref[...], head), head_slice(pair_ref[...], head)], axis=0
    )


def scores_kernel(
    limits_ref, q_own_ref, q_pair_ref, kv0, kv1, kv2, *refs
):
    rows = q_own_ref.shape[0]
    *far, lse_ref, probs_ref = refs
    keys = kv0.shape[0] // 2
    lse_ref[...] = jnp.zeros_like(lse_ref)
    for head in range(q_own_ref.shape[1] // HDIM):
        query = both_rows(q_own_ref, q_pair_ref, head)
        scores = []
        for step, key in enumerate(square_keys(head, (kv0, kv1, kv2), far)):
            block = contract(key, query, 1, 1) * SCALE
            slot = lax.broadcasted_iota(jnp.int32, block.shape, 0)
            valid = slot < rows + limits_ref[step : step + 1]
            scores.append(jnp.where(valid, block, NEG_FILL))
        top = functools.reduce(
            jnp.maximum, [jnp.max(block, axis=0, keepdims=True) for block in scores]
        )
        weights = [jnp.exp(block - top) for block in scores]
        total = sum(jnp.sum(block, axis=0, keepdims=True) for block in weights)
        inverse = 1.0 / total
        for step, block in enumerate(weights):
            begin = (head * SQUARE + step) * keys
            probs_ref[begin : begin + keys] = (block * inverse).astype(BF16)
        lse_ref[head : head + 1] = top + jnp.log(total)


def delta_kernel(lse_ref, probs_ref, d_own_ref, d_pair_ref, kv0, kv1, kv2, *refs):
    *far, stats_ref, dprobs_ref = refs
    keys = kv0.shape[0] // 2
    stats_ref[...] = jnp.zeros_like(stats_ref)
    stats_ref[: lse_ref.shape[0]] = lse_ref[...]
    for head in range(d_own_ref.shape[1] // HDIM):
        dattn = both_rows(d_own_ref, d_pair_ref, head)
        delta = None
        for step, value in enumerate(square_values(head, (kv0, kv1, kv2), far)):
            part = pl.ds((head * SQUARE + step) * keys, keys)
            dprobs = contract(value, dattn, 1, 1)
            dprobs_ref[part] = dprobs
            share = jnp.sum(probs_ref[part].astype(F32) * dprobs, axis=0, keepdims=True)
            delta = share if delta is None else delta + share
        stats_ref[8 + head : 9 + head] = delta


def attn_kernel(probs_ref, kv0, kv1, kv2, *refs):
    *far, own_ref, pair_ref = refs
    rows = own_ref.shape[1]
    keys = kv0.shape[0] // 2
    for head in range(own_ref.shape[0] // HDIM):
        attn = None
        for step, value in enumerate(square_values(head, (kv0, kv1, kv2), far)):
            begin = (head * SQUARE + step) * keys
            part = contract(value, probs_ref[begin : begin + keys], 0, 0)
            attn = part if attn is None else attn + part
        features = slice(head * HDIM, (head + 1) * HDIM)
        own_ref[features] = attn[:, :rows]
        pair_ref[features] = attn[:, rows:].astype(BF16)


def merge_parts(mine, theirs):
    top = jnp.maximum(mine, theirs)
    weight, weight_pair = jnp.exp(mine - top), jnp.exp(theirs - top)
    inverse = 1.0 / (weight + weight_pair)
    return weight * inverse, weight_pair * inverse


def project_kernel(
    own_ref, pair_ref, stats_ref, stats_pair_ref, w_ref,
    keep_ref, next_ref, core_ref, far_left_ref, far_right_ref,
):
    rows = own_ref.shape[1]
    parts = []
    for head in range(own_ref.shape[0] // HDIM):
        features = slice(head * HDIM, (head + 1) * HDIM)
        weight, weight_pair = merge_parts(
            stats_ref[head : head + 1, :rows], stats_pair_ref[head : head + 1, rows:]
        )
        parts.append(own_ref[features] * weight + pair_ref[features].astype(F32) * weight_pair)
    attn = jnp.concatenate(parts, axis=0).astype(BF16)
    me = lax.axis_index("head")
    size = keep_ref.shape[1]
    half = size // 2

    def columns_of(step):
        columns = pl.ds(pl.multiple_of((me ^ step) * size, HDIM), size)
        return contract(attn, w_ref[:, columns], 0, 0)

    far = columns_of(3).astype(BF16)
    far_left_ref[...] = far[:, :half]
    far_right_ref[...] = far[:, half:]
    next_ref[...] = columns_of(2)
    core_ref[...] = columns_of(1).astype(BF16)
    keep_ref[...] = columns_of(0)


def add_near_kernel(next_ref, left_ref, right_ref, out_ref):
    half = left_ref.shape[1]
    out_ref[:, :half] = (next_ref[:, :half] + left_ref[...].astype(F32)).astype(BF16)
    out_ref[:, half:] = (next_ref[:, half:] + right_ref[...].astype(F32)).astype(BF16)


def backward_kernel(
    q_own_ref, q_pair_ref, d_own_ref, d_pair_ref, stats_ref, stats_pair_ref, probs_ref, dprobs_ref,
    kv0, kv1, kv2, *refs,
):
    rows = q_own_ref.shape[0]
    *far, dq_own_ref, dq_pair_ref, dkv_ref, send_k_ref, send_v_ref, near_k_ref, near_v_ref = refs
    keys = kv0.shape[0] // 2
    dq_pair_ref[rows:] = jnp.zeros((dq_pair_ref.shape[0] - rows, dq_pair_ref.shape[1]), BF16)
    key_parts = (dkv_ref.at[:keys], send_k_ref.at[:keys], near_k_ref, send_k_ref.at[keys:])
    value_parts = (dkv_ref.at[keys:], near_v_ref, send_v_ref.at[:keys], send_v_ref.at[keys:])

    def swapped(row):
        return jnp.concatenate([row[:, rows:], row[:, :rows]], axis=1)

    for head in range(q_own_ref.shape[1] // HDIM):
        query = both_rows(q_own_ref, q_pair_ref, head)
        dattn = both_rows(d_own_ref, d_pair_ref, head)
        weight, weight_pair = merge_parts(
            stats_ref[head : head + 1], swapped(stats_pair_ref[head : head + 1])
        )
        delta = weight * stats_ref[8 + head : 9 + head]
        delta += weight_pair * swapped(stats_pair_ref[8 + head : 9 + head])
        features = slice(head * HDIM, (head + 1) * HDIM)
        dquery = None
        for step, key in enumerate(square_keys(head, (kv0, kv1, kv2), far)):
            begin = (head * SQUARE + step) * keys
            probs = (probs_ref[begin : begin + keys].astype(F32) * weight).astype(BF16)
            dprobs = dprobs_ref[begin : begin + keys]
            dscores = (probs.astype(F32) * (dprobs - delta)).astype(BF16)
            key_part, value_part = key_parts[step], value_parts[step]
            grad_key = contract(dscores, query, 1, 0) * SCALE
            key_part[:, features] = grad_key.astype(key_part.dtype)
            value_part[:, features] = contract(probs, dattn, 1, 0).astype(value_part.dtype)
            part = contract(dscores, key, 0, 0)
            dquery = part if dquery is None else dquery + part
        dq_own_ref[:, features] = dquery[:rows] * SCALE
        dq_pair_ref[:rows, features] = (dquery[rows:] * SCALE).astype(BF16)


def pass_on_kernel(near_k_ref, near_v_ref, got_k_ref, got_v_ref, k_ref, v_ref):
    keys = near_k_ref.shape[0]
    k_ref[...] = (near_k_ref[...] + got_k_ref[keys:].astype(F32)).astype(BF16)
    v_ref[...] = (near_v_ref[...] + got_v_ref[keys:].astype(F32)).astype(BF16)


def finish_kernel(
    keep_ref, core_ref, near_ref, dq_ref, dq_pair_ref,
    dkv_ref, got_k_ref, got_v_ref, rest_k_ref, rest_v_ref,
    q_out, k_out, v_out, hk_out, hv_out, out_ref,
):
    rows, capacity = k_out.shape[0], hk_out.shape[0]
    keys = rows + capacity

    def total(first, *others):
        for other in others:
            first = first + other.astype(F32)
        return first.astype(BF16)

    q_out[...] = total(dq_ref[...], dq_pair_ref[:rows])
    k_out[...] = total(dkv_ref[:rows], got_k_ref[:rows], rest_k_ref[:rows])
    hk_out[...] = total(dkv_ref[rows:keys], got_k_ref[rows:keys], rest_k_ref[rows:])
    v_out[...] = total(dkv_ref[keys : keys + rows], got_v_ref[:rows], rest_v_ref[:rows])
    hv_out[...] = total(dkv_ref[keys + rows :], got_v_ref[rows:keys], rest_v_ref[rows:])
    out_ref[...] = total(keep_ref[...], core_ref[...], near_ref[...])


def blocked(sec_q, sec_k, sec_v, hist_k, hist_v, frame_levels, frame_counts, w_out, grad_out):
    shape = jax.ShapeDtypeStruct
    rows, width = sec_q.shape
    heads = width // HDIM
    capacity = hist_k.shape[0]
    keys = rows + capacity
    share = grad_out.shape[1]

    q_pair = swap(sec_q, "ctx", PAIR)
    grad_near = swap(grad_out, "head", 2)
    grad_core = swap(grad_out, "head", 1)
    weight = load_weight(w_out)
    grad_near, weight = lax.optimization_barrier((grad_near, weight))
    grad_far = swap(grad_near, "head", 1)
    kv0 = load_keys(sec_k, hist_k, sec_v, hist_v)
    kv2 = swap(kv0, "ctx", 2)
    kv1 = swap(kv0, "ctx", 1)
    kv1, kv2 = lax.optimization_barrier((kv1, kv2))
    pieces = local_call(
        split_heads_kernel, "split_heads", 0.1, [shape((2 * keys, HDIM), BF16)] * heads, (kv2,)
    )
    kvs = (kv0, kv1, kv2, *(swap(piece, "ctx", 1) for piece in pieces))
    d_own = local_call(
        dattn_kernel,
        "dattn",
        0.8,
        [shape((rows, width), BF16)],
        (grad_out, grad_core, grad_near, grad_far, weight),
        vmem=40,
    )[0]
    d_pair = swap(d_own, "ctx", PAIR)
    limits = local_call(
        limits_kernel,
        "limits",
        0.6,
        [shape((8, 2 * rows), jnp.int32)],
        (frame_levels, frame_counts),
        tables=2,
    )[0]
    lse, probs = local_call(
        scores_kernel,
        "scores",
        0.9,
        [shape((8, 2 * rows), F32), shape((heads * SQUARE * keys, 2 * rows), BF16)],
        (limits, sec_q, q_pair, *kvs),
    )
    attn_own, attn_pair = local_call(
        attn_kernel,
        "attn",
        0.5,
        [shape((width, rows), F32), shape((width, rows), BF16)],
        (probs, *kvs),
    )
    lse, attn_own = lax.optimization_barrier((lse, attn_own))
    stats, dprobs = local_call(
        delta_kernel,
        "delta",
        0.7,
        [shape((16, 2 * rows), F32), shape((heads * SQUARE * keys, 2 * rows), F32)],
        (lse, probs, d_own, d_pair, *kvs),
    )
    stats_pair = swap(stats, "ctx", PAIR)
    dq_own, dq_pair, dkv_own, send_k, send_v, near_k, near_v = local_call(
        backward_kernel,
        "backward",
        1.1,
        [shape((rows, width), F32), shape((keys + 16, width), BF16), shape((2 * keys, width), F32)]
        + [shape((2 * keys, width), BF16)] * 2
        + [shape((keys, width), F32)] * 2,
        (sec_q, q_pair, d_own, d_pair, stats, stats_pair, probs, dprobs, *kvs),
    )
    attn_got = swap(attn_pair, "ctx", PAIR)
    attn_got, send_k, send_v = lax.optimization_barrier((attn_got, send_k, send_v))
    got_k = swap(send_k, "ctx", 1)
    got_v = swap(send_v, "ctx", 2)
    rest_k, rest_v = local_call(
        pass_on_kernel,
        "pass_on",
        0.1,
        [shape((keys, width), BF16)] * 2,
        (near_k, near_v, got_k, got_v),
    )
    rest_k = swap(rest_k, "ctx", 2)
    rest_v = swap(rest_v, "ctx", 1)
    half = share // 2
    out_keep, out_next, out_core, far_left, far_right = local_call(
        project_kernel,
        "project",
        0.6,
        [shape((rows, share), F32)] * 2
        + [shape((rows, share), BF16)]
        + [shape((rows, half), BF16)] * 2,
        (attn_own, attn_got, stats, stats_pair, weight),
    )
    far_left, far_right = (swap(part, "head", 1) for part in (far_left, far_right))
    out_near = swap(
        local_call(
            add_near_kernel,
            "add_near",
            0.1,
            [shape((rows, share), BF16)],
            (out_next, far_left, far_right),
        )[0],
        "head",
        2,
    )
    dq_got = swap(dq_pair, "ctx", PAIR)
    out_core = swap(out_core, "head", 1)
    grad_q, grad_k, grad_v, grad_hk, grad_hv, out = local_call(
        finish_kernel,
        "finish",
        0.9,
        [shape((rows, width), BF16)] * 3
        + [shape((capacity, width), BF16)] * 2
        + [shape((rows, share), BF16)],
        (
            out_keep, out_core, out_near, dq_own, dq_got,
            dkv_own, got_k, got_v, rest_k, rest_v,
        ),
    )
    return out, grad_q, grad_k, grad_v, grad_hk, grad_hv


def gathered(sec_q, sec_k, sec_v, hist_k, hist_v, frame_levels, frame_counts, w_out, grad_out):
    rows = sec_q.shape[0]
    capacity = hist_k.shape[0]
    owners = lax.axis_size("ctx")
    me = lax.axis_index("ctx")
    frames = jnp.arange(FMAX, dtype=jnp.int32)[None, :]
    tokens = jnp.where(
        frames < frame_counts[:, None], jnp.right_shift(jnp.int32(FTOK), 2 * frame_levels), 0
    ).sum(axis=1)
    slots = jnp.arange(capacity, dtype=jnp.int32)
    all_valid = jnp.concatenate(
        [jnp.ones((owners * rows,), bool), (slots[None] < tokens[:, None]).reshape(-1)]
    )
    own_valid = jnp.concatenate(
        [jnp.ones((rows,), bool), slots < lax.dynamic_index_in_dim(tokens, me, keepdims=False)]
    )

    def everyone(block, axis=0):
        return lax.all_gather(block, "ctx", axis=axis, tiled=True)

    own_k, own_v = (jnp.concatenate(a, axis=0) for a in ((sec_k, hist_k), (sec_v, hist_v)))
    all_k = jnp.concatenate([everyone(sec_k), everyone(hist_k)], axis=0)
    all_v = jnp.concatenate([everyone(sec_v), everyone(hist_v)], axis=0)
    d_attn = contract(lax.all_gather(grad_out, "head", axis=1, tiled=True), w_out, 1, 1).astype(BF16)
    all_q, all_d = everyone(sec_q), everyone(d_attn)

    def probs_and_dscores(query, key, value, dattn, valid, lse, delta):
        scores = contract(query, key, 1, 1) * SCALE
        probs = jnp.where(valid[None, :], jnp.exp(scores - lse), 0.0).astype(BF16)
        dprobs = contract(dattn, value, 1, 1)
        return probs, (probs.astype(F32) * (dprobs - delta)).astype(BF16)

    attn_parts, q_parts, k_parts, v_parts = [], [], [], []
    for head in range(sec_q.shape[1] // HDIM):
        query, dattn, key, value = (head_slice(a, head) for a in (sec_q, d_attn, all_k, all_v))
        scores = jnp.where(all_valid[None, :], contract(query, key, 1, 1) * SCALE, NEG_FILL)
        lse = jax.nn.logsumexp(scores, axis=1, keepdims=True)
        probs = jnp.where(all_valid[None, :], jnp.exp(scores - lse), 0.0).astype(BF16)
        attn = contract(probs, value, 1, 0).astype(BF16)
        delta = jnp.sum(attn.astype(F32) * dattn.astype(F32), axis=1, keepdims=True)
        _, dscores = probs_and_dscores(query, key, value, dattn, all_valid, lse, delta)
        attn_parts.append(attn)
        q_parts.append(contract(dscores, key, 1, 0))
        query, dattn, key, value = (head_slice(a, head) for a in (all_q, all_d, own_k, own_v))
        probs, dscores = probs_and_dscores(
            query, key, value, dattn, own_valid, everyone(lse), everyone(delta)
        )
        k_parts.append(contract(dscores, query, 0, 0))
        v_parts.append(contract(probs, dattn, 0, 0))
    partial = contract(jnp.concatenate(attn_parts, axis=1), w_out, 1, 0).astype(BF16)
    out = lax.psum_scatter(partial, "head", scatter_dimension=1, tiled=True)
    grad_q, grad_k = (
        (jnp.concatenate(a, axis=1) * SCALE).astype(BF16) for a in (q_parts, k_parts)
    )
    grad_v = jnp.concatenate(v_parts, axis=1).astype(BF16)
    return out, grad_q, grad_k[:rows], grad_v[:rows], grad_k[rows:], grad_v[rows:]


def solution(mesh):
    split = P("ctx", "head")
    plan = blocked if (mesh.shape["ctx"], mesh.shape["head"]) == (2 * SQUARE, 4) else gathered
    return jax.shard_map(
        plan,
        mesh=mesh,
        in_specs=(split,) * 5 + (P(), P(), P("head", None), split),
        out_specs=(split,) * 6,
        check_vma=False,
    )
```

```python
import functools
import math

import jax
import jax.numpy as jnp
from jax import lax
from jax.experimental import pallas as pl
from jax.experimental.pallas import tpu as pltpu
from jax.sharding import PartitionSpec as P

HDIM = 128
FTOK = 16
FMAX = 2
NEG_FILL = -1e30
SCALE = 1.0 / math.sqrt(HDIM)
F32 = jnp.float32
BF16 = jnp.bfloat16
SQUARE = 4
HBM_BYTES = 3.69e6
PAIR = 4


def contract(left, right, left_dim, right_dim):
    return lax.dot_general(
        left, right, (((left_dim,), (right_dim,)), ((), ())), preferred_element_type=F32
    )


def head_slice(stacked, head):
    return stacked[:, head * HDIM : (head + 1) * HDIM]


def swap(block, axis, bit):
    count = lax.axis_size(axis)
    return lax.ppermute(block, axis, [(i, i ^ bit) for i in range(count)])


def cost_of(micros):
    return pl.CostEstimate(flops=0, bytes_accessed=int(micros * HBM_BYTES), transcendentals=0)


def local_call(body, name, micros, out_shapes, args, tables=0):
    spaces = [pltpu.SMEM] * tables + [pltpu.VMEM] * (len(args) - tables)
    return pl.pallas_call(
        body,
        name=name,
        out_shape=out_shapes,
        in_specs=[pl.BlockSpec(memory_space=space) for space in spaces],
        out_specs=[pl.BlockSpec(memory_space=pltpu.VMEM)] * len(out_shapes),
        compiler_params=pltpu.CompilerParams(vmem_limit_bytes=16 * 2**20),
        cost_estimate=cost_of(micros),
    )(*args)


def load_kernel(k_ref, hk_ref, v_ref, hv_ref, kv_out, kv_ref, sems):
    inward, outward, begin = [], [], 0
    for i, ref in enumerate((k_ref, hk_ref, v_ref, hv_ref)):
        part = pl.ds(begin, ref.shape[0])
        inward.append(pltpu.make_async_copy(ref, kv_ref.at[part], sems.at[0, i]))
        outward.append(pltpu.make_async_copy(kv_ref.at[part], kv_out.at[part], sems.at[1, i]))
        begin += ref.shape[0]
    for copy in inward:
        copy.start()
    for before, after in zip(inward, outward):
        before.wait()
        after.start()
    for copy in outward:
        copy.wait()


def load_keys(*arrays):
    rows = sum(a.shape[0] for a in arrays)
    width = arrays[0].shape[1]
    return pl.pallas_call(
        load_kernel,
        name="load",
        out_shape=jax.ShapeDtypeStruct((rows, width), BF16),
        in_specs=[pl.BlockSpec(memory_space=pl.ANY)] * len(arrays),
        out_specs=pl.BlockSpec(memory_space=pl.ANY),
        scratch_shapes=[pltpu.VMEM((rows, width), BF16), pltpu.SemaphoreType.DMA((2, len(arrays)))],
        compiler_params=pltpu.CompilerParams(vmem_limit_bytes=60 * 2**20),
        cost_estimate=cost_of(1.6),
    )(*arrays)


def split_heads_kernel(kv_ref, *out_refs):
    for head, ref in enumerate(out_refs):
        ref[...] = head_slice(kv_ref[...], head)


def square_keys(head, near, far):
    keys = near[0].shape[0] // 2
    return [head_slice(ref[:keys], head) for ref in near] + [far[head][:keys]]


def square_values(head, near, far):
    keys = near[0].shape[0] // 2
    return [head_slice(ref[keys:], head) for ref in near] + [far[head][keys:]]


def load_weight_kernel(w_ref, w_out, sems):
    copies = []
    for i in range(sems.shape[0]):
        part = pl.ds(i * HDIM, HDIM)
        copies.append(pltpu.make_async_copy(w_ref.at[part], w_out.at[part], sems.at[i]))
    for copy in copies:
        copy.start()
    for copy in copies:
        copy.wait()


def load_weight(w_out):
    return pl.pallas_call(
        load_weight_kernel,
        name="load_w",
        out_shape=jax.ShapeDtypeStruct(w_out.shape, BF16),
        in_specs=[pl.BlockSpec(memory_space=pl.ANY)],
        out_specs=pl.BlockSpec(memory_space=pltpu.VMEM),
        scratch_shapes=[pltpu.SemaphoreType.DMA((w_out.shape[0] // HDIM,))],
        compiler_params=pltpu.CompilerParams(vmem_limit_bytes=50 * 2**20 + 2**19),
        cost_estimate=cost_of(1.6),
    )(w_out)


def limits_kernel(levels_ref, counts_ref, limits_ref):
    me = lax.axis_index("ctx")
    row = lax.broadcasted_iota(jnp.int32, limits_ref.shape, 0)
    limits = jnp.zeros(limits_ref.shape, jnp.int32)
    for step in range(SQUARE):
        total = jnp.int32(0)
        for frame in range(FMAX):
            tokens = lax.shift_right_logical(jnp.int32(FTOK), 2 * levels_ref[me ^ step, frame])
            total += jnp.where(frame < counts_ref[me ^ step], tokens, 0)
        limits = jnp.where(row == step, total, limits)
    limits_ref[...] = limits


def dattn_kernel(own_ref, core_ref, near_ref, far_ref, w_ref, out_ref):
    me = lax.axis_index("head")
    size = own_ref.shape[1]
    total = None
    for step, ref in enumerate((own_ref, core_ref, near_ref, far_ref)):
        columns = pl.ds(pl.multiple_of((me ^ step) * size, HDIM), size)
        part = contract(ref[...], w_ref[:, columns], 1, 1)
        total = part if total is None else total + part
    out_ref[...] = total.astype(BF16)


def both_rows(own_ref, pair_ref, head):
    return jnp.concatenate(
        [head_slice(own_ref[...], head), head_slice(pair_ref[...], head)], axis=0
    )


def scores_kernel(
    limits_ref, q_own_ref, q_pair_ref, kv0, kv1, kv2, *refs
):
    rows = q_own_ref.shape[0]
    *far, lse_ref, probs_ref = refs
    keys = kv0.shape[0] // 2
    lse_ref[...] = jnp.zeros_like(lse_ref)
    for head in range(q_own_ref.shape[1] // HDIM):
        query = both_rows(q_own_ref, q_pair_ref, head)
        scores = []
        for step, key in enumerate(square_keys(head, (kv0, kv1, kv2), far)):
            block = contract(key, query, 1, 1) * SCALE
            slot = lax.broadcasted_iota(jnp.int32, block.shape, 0)
            valid = slot < rows + limits_ref[step : step + 1]
            scores.append(jnp.where(valid, block, NEG_FILL))
        top = functools.reduce(
            jnp.maximum, [jnp.max(block, axis=0, keepdims=True) for block in scores]
        )
        weights = [jnp.exp(block - top) for block in scores]
        total = sum(jnp.sum(block, axis=0, keepdims=True) for block in weights)
        inverse = 1.0 / total
        for step, block in enumerate(weights):
            begin = (head * SQUARE + step) * keys
            probs_ref[begin : begin + keys] = (block * inverse).astype(BF16)
        lse_ref[head : head + 1] = top + jnp.log(total)


def delta_kernel(lse_ref, probs_ref, d_own_ref, d_pair_ref, kv0, kv1, kv2, *refs):
    *far, stats_ref, dprobs_ref = refs
    keys = kv0.shape[0] // 2
    stats_ref[...] = jnp.zeros_like(stats_ref)
    stats_ref[: lse_ref.shape[0]] = lse_ref[...]
    for head in range(d_own_ref.shape[1] // HDIM):
        dattn = both_rows(d_own_ref, d_pair_ref, head)
        delta = None
        for step, value in enumerate(square_values(head, (kv0, kv1, kv2), far)):
            part = pl.ds((head * SQUARE + step) * keys, keys)
            dprobs = contract(value, dattn, 1, 1)
            dprobs_ref[part] = dprobs
            share = jnp.sum(probs_ref[part].astype(F32) * dprobs, axis=0, keepdims=True)
            delta = share if delta is None else delta + share
        stats_ref[8 + head : 9 + head] = delta


def attn_kernel(probs_ref, kv0, kv1, kv2, *refs):
    *far, own_ref, pair_ref = refs
    rows = own_ref.shape[1]
    keys = kv0.shape[0] // 2
    for head in range(own_ref.shape[0] // HDIM):
        attn = None
        for step, value in enumerate(square_values(head, (kv0, kv1, kv2), far)):
            begin = (head * SQUARE + step) * keys
            part = contract(value, probs_ref[begin : begin + keys], 0, 0)
            attn = part if attn is None else attn + part
        features = slice(head * HDIM, (head + 1) * HDIM)
        own_ref[features] = attn[:, :rows]
        pair_ref[features] = attn[:, rows:].astype(BF16)


def merge_parts(mine, theirs):
    top = jnp.maximum(mine, theirs)
    weight, weight_pair = jnp.exp(mine - top), jnp.exp(theirs - top)
    inverse = 1.0 / (weight + weight_pair)
    return weight * inverse, weight_pair * inverse


def project_kernel(
    own_ref, pair_ref, stats_ref, stats_pair_ref, w_ref,
    keep_ref, next_ref, core_ref, far_left_ref, far_right_ref,
):
    rows = own_ref.shape[1]
    parts = []
    for head in range(own_ref.shape[0] // HDIM):
        features = slice(head * HDIM, (head + 1) * HDIM)
        weight, weight_pair = merge_parts(
            stats_ref[head : head + 1, :rows], stats_pair_ref[head : head + 1, rows:]
        )
        parts.append(own_ref[features] * weight + pair_ref[features].astype(F32) * weight_pair)
    attn = jnp.concatenate(parts, axis=0).astype(BF16)
    me = lax.axis_index("head")
    size = keep_ref.shape[1]
    half = size // 2

    def columns_of(step):
        columns = pl.ds(pl.multiple_of((me ^ step) * size, HDIM), size)
        return contract(attn, w_ref[:, columns], 0, 0)

    far = columns_of(3).astype(BF16)
    far_left_ref[...] = far[:, :half]
    far_right_ref[...] = far[:, half:]
    next_ref[...] = columns_of(2)
    core_ref[...] = columns_of(1).astype(BF16)
    keep_ref[...] = columns_of(0)


def add_near_kernel(next_ref, left_ref, right_ref, out_ref):
    half = left_ref.shape[1]
    out_ref[:, :half] = (next_ref[:, :half] + left_ref[...].astype(F32)).astype(BF16)
    out_ref[:, half:] = (next_ref[:, half:] + right_ref[...].astype(F32)).astype(BF16)


def backward_kernel(
    q_own_ref, q_pair_ref, d_own_ref, d_pair_ref, stats_ref, stats_pair_ref, probs_ref, dprobs_ref,
    kv0, kv1, kv2, *refs,
):
    rows = q_own_ref.shape[0]
    *far, dq_own_ref, dq_pair_ref, dkv_ref, send_k_ref, send_v_ref, near_k_ref, near_v_ref = refs
    keys = kv0.shape[0] // 2
    dq_pair_ref[rows:] = jnp.zeros((dq_pair_ref.shape[0] - rows, dq_pair_ref.shape[1]), BF16)
    key_parts = (dkv_ref.at[:keys], send_k_ref.at[:keys], near_k_ref, send_k_ref.at[keys:])
    value_parts = (dkv_ref.at[keys:], near_v_ref, send_v_ref.at[:keys], send_v_ref.at[keys:])

    def swapped(row):
        return jnp.concatenate([row[:, rows:], row[:, :rows]], axis=1)

    for head in range(q_own_ref.shape[1] // HDIM):
        query = both_rows(q_own_ref, q_pair_ref, head)
        dattn = both_rows(d_own_ref, d_pair_ref, head)
        weight, weight_pair = merge_parts(
            stats_ref[head : head + 1], swapped(stats_pair_ref[head : head + 1])
        )
        delta = weight * stats_ref[8 + head : 9 + head]
        delta += weight_pair * swapped(stats_pair_ref[8 + head : 9 + head])
        features = slice(head * HDIM, (head + 1) * HDIM)
        dquery = None
        for step, key in enumerate(square_keys(head, (kv0, kv1, kv2), far)):
            begin = (head * SQUARE + step) * keys
            probs = (probs_ref[begin : begin + keys].astype(F32) * weight).astype(BF16)
            dprobs = dprobs_ref[begin : begin + keys]
            dscores = (probs.astype(F32) * (dprobs - delta)).astype(BF16)
            key_part, value_part = key_parts[step], value_parts[step]
            grad_key = contract(dscores, query, 1, 0) * SCALE
            key_part[:, features] = grad_key.astype(key_part.dtype)
            value_part[:, features] = contract(probs, dattn, 1, 0).astype(value_part.dtype)
            part = contract(dscores, key, 0, 0)
            dquery = part if dquery is None else dquery + part
        dq_own_ref[:, features] = dquery[:rows] * SCALE
        dq_pair_ref[:rows, features] = (dquery[rows:] * SCALE).astype(BF16)


def pass_on_kernel(near_k_ref, near_v_ref, got_k_ref, got_v_ref, k_ref, v_ref):
    keys = near_k_ref.shape[0]
    k_ref[...] = (near_k_ref[...] + got_k_ref[keys:].astype(F32)).astype(BF16)
    v_ref[...] = (near_v_ref[...] + got_v_ref[keys:].astype(F32)).astype(BF16)


def finish_kernel(
    keep_ref, core_ref, near_ref, dq_ref, dq_pair_ref,
    dkv_ref, got_k_ref, got_v_ref, rest_k_ref, rest_v_ref,
    q_out, k_out, v_out, hk_out, hv_out, out_ref,
):
    rows, capacity = k_out.shape[0], hk_out.shape[0]
    keys = rows + capacity

    def total(first, *others):
        for other in others:
            first = first + other.astype(F32)
        return first.astype(BF16)

    q_out[...] = total(dq_ref[...], dq_pair_ref[:rows])
    k_out[...] = total(dkv_ref[:rows], got_k_ref[:rows], rest_k_ref[:rows])
    hk_out[...] = total(dkv_ref[rows:keys], got_k_ref[rows:keys], rest_k_ref[rows:])
    v_out[...] = total(dkv_ref[keys : keys + rows], got_v_ref[:rows], rest_v_ref[:rows])
    hv_out[...] = total(dkv_ref[keys + rows :], got_v_ref[rows:keys], rest_v_ref[rows:])
    out_ref[...] = total(keep_ref[...], core_ref[...], near_ref[...])


def blocked(sec_q, sec_k, sec_v, hist_k, hist_v, frame_levels, frame_counts, w_out, grad_out):
    shape = jax.ShapeDtypeStruct
    rows, width = sec_q.shape
    heads = width // HDIM
    capacity = hist_k.shape[0]
    keys = rows + capacity
    share = grad_out.shape[1]

    q_pair = swap(sec_q, "ctx", PAIR)
    grad_near = swap(grad_out, "head", 2)
    grad_core = swap(grad_out, "head", 1)
    weight = load_weight(w_out)
    grad_near, weight = lax.optimization_barrier((grad_near, weight))
    grad_far = swap(grad_near, "head", 1)
    kv0 = load_keys(sec_k, hist_k, sec_v, hist_v)
    kv2 = swap(kv0, "ctx", 2)
    kv1 = swap(kv0, "ctx", 1)
    kv1, kv2 = lax.optimization_barrier((kv1, kv2))
    pieces = local_call(
        split_heads_kernel, "split_heads", 0.1, [shape((2 * keys, HDIM), BF16)] * heads, (kv2,)
    )
    kvs = (kv0, kv1, kv2, *(swap(piece, "ctx", 1) for piece in pieces))
    d_own = local_call(
        dattn_kernel,
        "dattn",
        0.8,
        [shape((rows, width), BF16)],
        (grad_out, grad_core, grad_near, grad_far, weight),
    )[0]
    d_pair = swap(d_own, "ctx", PAIR)
    limits = local_call(
        limits_kernel,
        "limits",
        0.6,
        [shape((8, 2 * rows), jnp.int32)],
        (frame_levels, frame_counts),
        tables=2,
    )[0]
    lse, probs = local_call(
        scores_kernel,
        "scores",
        0.9,
        [shape((8, 2 * rows), F32), shape((heads * SQUARE * keys, 2 * rows), BF16)],
        (limits, sec_q, q_pair, *kvs),
    )
    attn_own, attn_pair = local_call(
        attn_kernel,
        "attn",
        0.5,
        [shape((width, rows), F32), shape((width, rows), BF16)],
        (probs, *kvs),
    )
    lse, attn_own = lax.optimization_barrier((lse, attn_own))
    stats, dprobs = local_call(
        delta_kernel,
        "delta",
        0.7,
        [shape((16, 2 * rows), F32), shape((heads * SQUARE * keys, 2 * rows), F32)],
        (lse, probs, d_own, d_pair, *kvs),
    )
    stats_pair = swap(stats, "ctx", PAIR)
    dq_own, dq_pair, dkv_own, send_k, send_v, near_k, near_v = local_call(
        backward_kernel,
        "backward",
        1.1,
        [shape((rows, width), F32), shape((keys + 16, width), BF16), shape((2 * keys, width), F32)]
        + [shape((2 * keys, width), BF16)] * 2
        + [shape((keys, width), F32)] * 2,
        (sec_q, q_pair, d_own, d_pair, stats, stats_pair, probs, dprobs, *kvs),
    )
    attn_got = swap(attn_pair, "ctx", PAIR)
    attn_got, send_k, send_v = lax.optimization_barrier((attn_got, send_k, send_v))
    got_k = swap(send_k, "ctx", 1)
    got_v = swap(send_v, "ctx", 2)
    rest_k, rest_v = local_call(
        pass_on_kernel,
        "pass_on",
        0.1,
        [shape((keys, width), BF16)] * 2,
        (near_k, near_v, got_k, got_v),
    )
    rest_k = swap(rest_k, "ctx", 2)
    rest_v = swap(rest_v, "ctx", 1)
    half = share // 2
    out_keep, out_next, out_core, far_left, far_right = local_call(
        project_kernel,
        "project",
        0.6,
        [shape((rows, share), F32)] * 2
        + [shape((rows, share), BF16)]
        + [shape((rows, half), BF16)] * 2,
        (attn_own, attn_got, stats, stats_pair, w_out),
    )
    far_left, far_right = (swap(part, "head", 1) for part in (far_left, far_right))
    out_near = swap(
        local_call(
            add_near_kernel,
            "add_near",
            0.1,
            [shape((rows, share), BF16)],
            (out_next, far_left, far_right),
        )[0],
        "head",
        2,
    )
    dq_got = swap(dq_pair, "ctx", PAIR)
    out_core = swap(out_core, "head", 1)
    grad_q, grad_k, grad_v, grad_hk, grad_hv, out = local_call(
        finish_kernel,
        "finish",
        0.9,
        [shape((rows, width), BF16)] * 3
        + [shape((capacity, width), BF16)] * 2
        + [shape((rows, share), BF16)],
        (
            out_keep, out_core, out_near, dq_own, dq_got,
            dkv_own, got_k, got_v, rest_k, rest_v,
        ),
    )
    return out, grad_q, grad_k, grad_v, grad_hk, grad_hv


def gathered(sec_q, sec_k, sec_v, hist_k, hist_v, frame_levels, frame_counts, w_out, grad_out):
    rows = sec_q.shape[0]
    capacity = hist_k.shape[0]
    owners = lax.axis_size("ctx")
    me = lax.axis_index("ctx")
    frames = jnp.arange(FMAX, dtype=jnp.int32)[None, :]
    tokens = jnp.where(
        frames < frame_counts[:, None], jnp.right_shift(jnp.int32(FTOK), 2 * frame_levels), 0
    ).sum(axis=1)
    slots = jnp.arange(capacity, dtype=jnp.int32)
    all_valid = jnp.concatenate(
        [jnp.ones((owners * rows,), bool), (slots[None] < tokens[:, None]).reshape(-1)]
    )
    own_valid = jnp.concatenate(
        [jnp.ones((rows,), bool), slots < lax.dynamic_index_in_dim(tokens, me, keepdims=False)]
    )

    def everyone(block, axis=0):
        return lax.all_gather(block, "ctx", axis=axis, tiled=True)

    own_k, own_v = (jnp.concatenate(a, axis=0) for a in ((sec_k, hist_k), (sec_v, hist_v)))
    all_k = jnp.concatenate([everyone(sec_k), everyone(hist_k)], axis=0)
    all_v = jnp.concatenate([everyone(sec_v), everyone(hist_v)], axis=0)
    d_attn = contract(lax.all_gather(grad_out, "head", axis=1, tiled=True), w_out, 1, 1).astype(BF16)
    all_q, all_d = everyone(sec_q), everyone(d_attn)

    def probs_and_dscores(query, key, value, dattn, valid, lse, delta):
        scores = contract(query, key, 1, 1) * SCALE
        probs = jnp.where(valid[None, :], jnp.exp(scores - lse), 0.0).astype(BF16)
        dprobs = contract(dattn, value, 1, 1)
        return probs, (probs.astype(F32) * (dprobs - delta)).astype(BF16)

    attn_parts, q_parts, k_parts, v_parts = [], [], [], []
    for head in range(sec_q.shape[1] // HDIM):
        query, dattn, key, value = (head_slice(a, head) for a in (sec_q, d_attn, all_k, all_v))
        scores = jnp.where(all_valid[None, :], contract(query, key, 1, 1) * SCALE, NEG_FILL)
        lse = jax.nn.logsumexp(scores, axis=1, keepdims=True)
        probs = jnp.where(all_valid[None, :], jnp.exp(scores - lse), 0.0).astype(BF16)
        attn = contract(probs, value, 1, 0).astype(BF16)
        delta = jnp.sum(attn.astype(F32) * dattn.astype(F32), axis=1, keepdims=True)
        _, dscores = probs_and_dscores(query, key, value, dattn, all_valid, lse, delta)
        attn_parts.append(attn)
        q_parts.append(contract(dscores, key, 1, 0))
        query, dattn, key, value = (head_slice(a, head) for a in (all_q, all_d, own_k, own_v))
        probs, dscores = probs_and_dscores(
            query, key, value, dattn, own_valid, everyone(lse), everyone(delta)
        )
        k_parts.append(contract(dscores, query, 0, 0))
        v_parts.append(contract(probs, dattn, 0, 0))
    partial = contract(jnp.concatenate(attn_parts, axis=1), w_out, 1, 0).astype(BF16)
    out = lax.psum_scatter(partial, "head", scatter_dimension=1, tiled=True)
    grad_q, grad_k = (
        (jnp.concatenate(a, axis=1) * SCALE).astype(BF16) for a in (q_parts, k_parts)
    )
    grad_v = jnp.concatenate(v_parts, axis=1).astype(BF16)
    return out, grad_q, grad_k[:rows], grad_v[:rows], grad_k[rows:], grad_v[rows:]


def solution(mesh):
    split = P("ctx", "head")
    plan = blocked if (mesh.shape["ctx"], mesh.shape["head"]) == (2 * SQUARE, 4) else gathered
    return jax.shard_map(
        plan,
        mesh=mesh,
        in_specs=(split,) * 5 + (P(), P(), P("head", None), split),
        out_specs=(split,) * 6,
        check_vma=False,
    )
```

```python
import functools
import math

import jax
import jax.numpy as jnp
from jax import lax
from jax.experimental import pallas as pl
from jax.experimental.pallas import tpu as pltpu
from jax.sharding import PartitionSpec as P

HDIM = 128
FTOK = 16
FMAX = 2
NEG_FILL = -1e30
SCALE = 1.0 / math.sqrt(HDIM)
F32 = jnp.float32
BF16 = jnp.bfloat16
SQUARE = 4
HBM_BYTES = 3.69e6
PAIR = 4


def contract(left, right, left_dim, right_dim):
    return lax.dot_general(
        left, right, (((left_dim,), (right_dim,)), ((), ())), preferred_element_type=F32
    )


def head_slice(stacked, head):
    return stacked[:, head * HDIM : (head + 1) * HDIM]


def swap(block, axis, bit):
    count = lax.axis_size(axis)
    return lax.ppermute(block, axis, [(i, i ^ bit) for i in range(count)])


def cost_of(micros):
    return pl.CostEstimate(flops=0, bytes_accessed=int(micros * HBM_BYTES), transcendentals=0)


def local_call(body, name, micros, out_shapes, args, tables=0):
    spaces = [pltpu.SMEM] * tables + [pltpu.VMEM] * (len(args) - tables)
    return pl.pallas_call(
        body,
        name=name,
        out_shape=out_shapes,
        in_specs=[pl.BlockSpec(memory_space=space) for space in spaces],
        out_specs=[pl.BlockSpec(memory_space=pltpu.VMEM)] * len(out_shapes),
        compiler_params=pltpu.CompilerParams(vmem_limit_bytes=16 * 2**20),
        cost_estimate=cost_of(micros),
    )(*args)


def load_kernel(k_ref, hk_ref, v_ref, hv_ref, kv_out, kv_ref, sems):
    inward, outward, begin = [], [], 0
    for i, ref in enumerate((k_ref, hk_ref, v_ref, hv_ref)):
        part = pl.ds(begin, ref.shape[0])
        inward.append(pltpu.make_async_copy(ref, kv_ref.at[part], sems.at[0, i]))
        outward.append(pltpu.make_async_copy(kv_ref.at[part], kv_out.at[part], sems.at[1, i]))
        begin += ref.shape[0]
    for copy in inward:
        copy.start()
    for before, after in zip(inward, outward):
        before.wait()
        after.start()
    for copy in outward:
        copy.wait()


def load_keys(*arrays):
    rows = sum(a.shape[0] for a in arrays)
    width = arrays[0].shape[1]
    return pl.pallas_call(
        load_kernel,
        name="load",
        out_shape=jax.ShapeDtypeStruct((rows, width), BF16),
        in_specs=[pl.BlockSpec(memory_space=pl.ANY)] * len(arrays),
        out_specs=pl.BlockSpec(memory_space=pl.ANY),
        scratch_shapes=[pltpu.VMEM((rows, width), BF16), pltpu.SemaphoreType.DMA((2, len(arrays)))],
        compiler_params=pltpu.CompilerParams(vmem_limit_bytes=60 * 2**20),
        cost_estimate=cost_of(1.6),
    )(*arrays)


def split_heads_kernel(kv_ref, *out_refs):
    for head, ref in enumerate(out_refs):
        ref[...] = head_slice(kv_ref[...], head)


def square_keys(head, near, far):
    keys = near[0].shape[0] // 2
    return [head_slice(ref[:keys], head) for ref in near] + [far[head][:keys]]


def square_values(head, near, far):
    keys = near[0].shape[0] // 2
    return [head_slice(ref[keys:], head) for ref in near] + [far[head][keys:]]


def load_weight_kernel(w_ref, w_out, sems):
    copies = []
    for i in range(sems.shape[0]):
        part = pl.ds(i * HDIM, HDIM)
        copies.append(pltpu.make_async_copy(w_ref.at[part], w_out.at[part], sems.at[i]))
    for copy in copies:
        copy.start()
    for copy in copies:
        copy.wait()


def load_weight(w_out):
    return pl.pallas_call(
        load_weight_kernel,
        name="load_w",
        out_shape=jax.ShapeDtypeStruct(w_out.shape, BF16),
        in_specs=[pl.BlockSpec(memory_space=pl.ANY)],
        out_specs=pl.BlockSpec(memory_space=pltpu.VMEM),
        scratch_shapes=[pltpu.SemaphoreType.DMA((w_out.shape[0] // HDIM,))],
        compiler_params=pltpu.CompilerParams(vmem_limit_bytes=50 * 2**20 + 2**19),
        cost_estimate=cost_of(1.6),
    )(w_out)


def limits_kernel(levels_ref, counts_ref, limits_ref):
    me = lax.axis_index("ctx")
    row = lax.broadcasted_iota(jnp.int32, limits_ref.shape, 0)
    limits = jnp.zeros(limits_ref.shape, jnp.int32)
    for step in range(SQUARE):
        total = jnp.int32(0)
        for frame in range(FMAX):
            tokens = lax.shift_right_logical(jnp.int32(FTOK), 2 * levels_ref[me ^ step, frame])
            total += jnp.where(frame < counts_ref[me ^ step], tokens, 0)
        limits = jnp.where(row == step, total, limits)
    limits_ref[...] = limits


def dattn_kernel(own_ref, core_ref, near_ref, far_ref, w_ref, out_ref):
    me = lax.axis_index("head")
    size = own_ref.shape[1]
    total = None
    for step, ref in enumerate((own_ref, core_ref, near_ref, far_ref)):
        columns = pl.ds(pl.multiple_of((me ^ step) * size, HDIM), size)
        part = contract(ref[...], w_ref[:, columns], 1, 1)
        total = part if total is None else total + part
    out_ref[...] = total.astype(BF16)


def both_rows(own_ref, pair_ref, head):
    return jnp.concatenate(
        [head_slice(own_ref[...], head), head_slice(pair_ref[...], head)], axis=0
    )


def scores_kernel(
    limits_ref, q_own_ref, q_pair_ref, kv0, kv1, kv2, *refs
):
    rows = q_own_ref.shape[0]
    *far, lse_ref, probs_ref = refs
    keys = kv0.shape[0] // 2
    lse_ref[...] = jnp.zeros_like(lse_ref)
    for head in range(q_own_ref.shape[1] // HDIM):
        query = both_rows(q_own_ref, q_pair_ref, head)
        scores = []
        for step, key in enumerate(square_keys(head, (kv0, kv1, kv2), far)):
            block = contract(key, query, 1, 1) * SCALE
            slot = lax.broadcasted_iota(jnp.int32, block.shape, 0)
            valid = slot < rows + limits_ref[step : step + 1]
            scores.append(jnp.where(valid, block, NEG_FILL))
        top = functools.reduce(
            jnp.maximum, [jnp.max(block, axis=0, keepdims=True) for block in scores]
        )
        weights = [jnp.exp(block - top) for block in scores]
        total = sum(jnp.sum(block, axis=0, keepdims=True) for block in weights)
        inverse = 1.0 / total
        for step, block in enumerate(weights):
            begin = (head * SQUARE + step) * keys
            probs_ref[begin : begin + keys] = (block * inverse).astype(BF16)
        lse_ref[head : head + 1] = top + jnp.log(total)


def delta_kernel(lse_ref, probs_ref, d_own_ref, d_pair_ref, kv0, kv1, kv2, *refs):
    *far, stats_ref, dprobs_ref = refs
    keys = kv0.shape[0] // 2
    stats_ref[...] = jnp.zeros_like(stats_ref)
    stats_ref[: lse_ref.shape[0]] = lse_ref[...]
    for head in range(d_own_ref.shape[1] // HDIM):
        dattn = both_rows(d_own_ref, d_pair_ref, head)
        delta = None
        for step, value in enumerate(square_values(head, (kv0, kv1, kv2), far)):
            part = pl.ds((head * SQUARE + step) * keys, keys)
            dprobs = contract(value, dattn, 1, 1)
            dprobs_ref[part] = dprobs
            share = jnp.sum(probs_ref[part].astype(F32) * dprobs, axis=0, keepdims=True)
            delta = share if delta is None else delta + share
        stats_ref[8 + head : 9 + head] = delta


def attn_kernel(probs_ref, kv0, kv1, kv2, *refs):
    *far, own_ref, pair_ref = refs
    rows = own_ref.shape[1]
    keys = kv0.shape[0] // 2
    for head in range(own_ref.shape[0] // HDIM):
        attn = None
        for step, value in enumerate(square_values(head, (kv0, kv1, kv2), far)):
            begin = (head * SQUARE + step) * keys
            part = contract(value, probs_ref[begin : begin + keys], 0, 0)
            attn = part if attn is None else attn + part
        features = slice(head * HDIM, (head + 1) * HDIM)
        own_ref[features] = attn[:, :rows]
        pair_ref[features] = attn[:, rows:].astype(BF16)


def merge_parts(mine, theirs):
    top = jnp.maximum(mine, theirs)
    weight, weight_pair = jnp.exp(mine - top), jnp.exp(theirs - top)
    inverse = 1.0 / (weight + weight_pair)
    return weight * inverse, weight_pair * inverse


def project_kernel(
    own_ref, pair_ref, stats_ref, stats_pair_ref, w_ref,
    keep_ref, next_ref, core_ref, far_left_ref, far_right_ref,
):
    rows = own_ref.shape[1]
    parts = []
    for head in range(own_ref.shape[0] // HDIM):
        features = slice(head * HDIM, (head + 1) * HDIM)
        weight, weight_pair = merge_parts(
            stats_ref[head : head + 1, :rows], stats_pair_ref[head : head + 1, rows:]
        )
        parts.append(own_ref[features] * weight + pair_ref[features].astype(F32) * weight_pair)
    attn = jnp.concatenate(parts, axis=0).astype(BF16)
    me = lax.axis_index("head")
    size = keep_ref.shape[1]
    half = size // 2

    def columns_of(step):
        columns = pl.ds(pl.multiple_of((me ^ step) * size, HDIM), size)
        return contract(attn, w_ref[:, columns], 0, 0)

    far = columns_of(3).astype(BF16)
    far_left_ref[...] = far[:, :half]
    far_right_ref[...] = far[:, half:]
    next_ref[...] = columns_of(2)
    core_ref[...] = columns_of(1).astype(BF16)
    keep_ref[...] = columns_of(0)


def add_near_kernel(next_ref, left_ref, right_ref, out_ref):
    half = left_ref.shape[1]
    out_ref[:, :half] = (next_ref[:, :half] + left_ref[...].astype(F32)).astype(BF16)
    out_ref[:, half:] = (next_ref[:, half:] + right_ref[...].astype(F32)).astype(BF16)


def backward_kernel(
    q_own_ref, q_pair_ref, d_own_ref, d_pair_ref, stats_ref, stats_pair_ref, probs_ref, dprobs_ref,
    kv0, kv1, kv2, *refs,
):
    rows = q_own_ref.shape[0]
    *far, dq_own_ref, dq_pair_ref, dkv_ref, send_k_ref, send_v_ref, near_k_ref, near_v_ref = refs
    keys = kv0.shape[0] // 2
    dq_pair_ref[rows:] = jnp.zeros((dq_pair_ref.shape[0] - rows, dq_pair_ref.shape[1]), BF16)
    key_parts = (dkv_ref.at[:keys], send_k_ref.at[:keys], near_k_ref, send_k_ref.at[keys:])
    value_parts = (dkv_ref.at[keys:], near_v_ref, send_v_ref.at[:keys], send_v_ref.at[keys:])

    def swapped(row):
        return jnp.concatenate([row[:, rows:], row[:, :rows]], axis=1)

    for head in range(q_own_ref.shape[1] // HDIM):
        query = both_rows(q_own_ref, q_pair_ref, head)
        dattn = both_rows(d_own_ref, d_pair_ref, head)
        weight, weight_pair = merge_parts(
            stats_ref[head : head + 1], swapped(stats_pair_ref[head : head + 1])
        )
        delta = weight * stats_ref[8 + head : 9 + head]
        delta += weight_pair * swapped(stats_pair_ref[8 + head : 9 + head])
        features = slice(head * HDIM, (head + 1) * HDIM)
        dquery = None
        for step, key in enumerate(square_keys(head, (kv0, kv1, kv2), far)):
            begin = (head * SQUARE + step) * keys
            probs = (probs_ref[begin : begin + keys].astype(F32) * weight).astype(BF16)
            dprobs = dprobs_ref[begin : begin + keys]
            dscores = (probs.astype(F32) * (dprobs - delta)).astype(BF16)
            key_part, value_part = key_parts[step], value_parts[step]
            grad_key = contract(dscores, query, 1, 0) * SCALE
            key_part[:, features] = grad_key.astype(key_part.dtype)
            value_part[:, features] = contract(probs, dattn, 1, 0).astype(value_part.dtype)
            part = contract(dscores, key, 0, 0)
            dquery = part if dquery is None else dquery + part
        dq_own_ref[:, features] = dquery[:rows] * SCALE
        dq_pair_ref[:rows, features] = (dquery[rows:] * SCALE).astype(BF16)


def pass_on_kernel(near_k_ref, near_v_ref, got_k_ref, got_v_ref, k_ref, v_ref):
    keys = near_k_ref.shape[0]
    k_ref[...] = (near_k_ref[...] + got_k_ref[keys:].astype(F32)).astype(BF16)
    v_ref[...] = (near_v_ref[...] + got_v_ref[keys:].astype(F32)).astype(BF16)


def finish_kernel(
    keep_ref, core_ref, near_ref, dq_ref, dq_pair_ref,
    dkv_ref, got_k_ref, got_v_ref, rest_k_ref, rest_v_ref,
    q_out, k_out, v_out, hk_out, hv_out, out_ref,
):
    rows, capacity = k_out.shape[0], hk_out.shape[0]
    keys = rows + capacity

    def total(first, *others):
        for other in others:
            first = first + other.astype(F32)
        return first.astype(BF16)

    q_out[...] = total(dq_ref[...], dq_pair_ref[:rows])
    k_out[...] = total(dkv_ref[:rows], got_k_ref[:rows], rest_k_ref[:rows])
    hk_out[...] = total(dkv_ref[rows:keys], got_k_ref[rows:keys], rest_k_ref[rows:])
    v_out[...] = total(dkv_ref[keys : keys + rows], got_v_ref[:rows], rest_v_ref[:rows])
    hv_out[...] = total(dkv_ref[keys + rows :], got_v_ref[rows:keys], rest_v_ref[rows:])
    out_ref[...] = total(keep_ref[...], core_ref[...], near_ref[...])


def blocked(sec_q, sec_k, sec_v, hist_k, hist_v, frame_levels, frame_counts, w_out, grad_out):
    shape = jax.ShapeDtypeStruct
    rows, width = sec_q.shape
    heads = width // HDIM
    capacity = hist_k.shape[0]
    keys = rows + capacity
    share = grad_out.shape[1]

    q_pair = swap(sec_q, "ctx", PAIR)
    grad_near = swap(grad_out, "head", 2)
    grad_core = swap(grad_out, "head", 1)
    weight = load_weight(w_out)
    grad_near, weight = lax.optimization_barrier((grad_near, weight))
    grad_far = swap(grad_near, "head", 1)
    kv0 = load_keys(sec_k, hist_k, sec_v, hist_v)
    kv2 = swap(kv0, "ctx", 2)
    kv1 = swap(kv0, "ctx", 1)
    d_own = local_call(
        dattn_kernel,
        "dattn",
        0.8,
        [shape((rows, width), BF16)],
        (grad_out, grad_core, grad_near, grad_far, weight),
    )[0]
    kv1, kv2, d_own = lax.optimization_barrier((kv1, kv2, d_own))
    pieces = local_call(
        split_heads_kernel, "split_heads", 0.1, [shape((2 * keys, HDIM), BF16)] * heads, (kv2,)
    )
    kvs = (kv0, kv1, kv2, *(swap(piece, "ctx", 1) for piece in pieces))
    d_pair = swap(d_own, "ctx", PAIR)
    limits = local_call(
        limits_kernel,
        "limits",
        0.6,
        [shape((8, 2 * rows), jnp.int32)],
        (frame_levels, frame_counts),
        tables=2,
    )[0]
    lse, probs = local_call(
        scores_kernel,
        "scores",
        0.9,
        [shape((8, 2 * rows), F32), shape((heads * SQUARE * keys, 2 * rows), BF16)],
        (limits, sec_q, q_pair, *kvs),
    )
    attn_own, attn_pair = local_call(
        attn_kernel,
        "attn",
        0.5,
        [shape((width, rows), F32), shape((width, rows), BF16)],
        (probs, *kvs),
    )
    lse, attn_own = lax.optimization_barrier((lse, attn_own))
    stats, dprobs = local_call(
        delta_kernel,
        "delta",
        0.7,
        [shape((16, 2 * rows), F32), shape((heads * SQUARE * keys, 2 * rows), F32)],
        (lse, probs, d_own, d_pair, *kvs),
    )
    stats_pair = swap(stats, "ctx", PAIR)
    dq_own, dq_pair, dkv_own, send_k, send_v, near_k, near_v = local_call(
        backward_kernel,
        "backward",
        1.1,
        [shape((rows, width), F32), shape((keys + 16, width), BF16), shape((2 * keys, width), F32)]
        + [shape((2 * keys, width), BF16)] * 2
        + [shape((keys, width), F32)] * 2,
        (sec_q, q_pair, d_own, d_pair, stats, stats_pair, probs, dprobs, *kvs),
    )
    attn_got = swap(attn_pair, "ctx", PAIR)
    attn_got, send_k, send_v = lax.optimization_barrier((attn_got, send_k, send_v))
    got_k = swap(send_k, "ctx", 1)
    got_v = swap(send_v, "ctx", 2)
    rest_k, rest_v = local_call(
        pass_on_kernel,
        "pass_on",
        0.1,
        [shape((keys, width), BF16)] * 2,
        (near_k, near_v, got_k, got_v),
    )
    rest_k = swap(rest_k, "ctx", 2)
    rest_v = swap(rest_v, "ctx", 1)
    half = share // 2
    out_keep, out_next, out_core, far_left, far_right = local_call(
        project_kernel,
        "project",
        0.6,
        [shape((rows, share), F32)] * 2
        + [shape((rows, share), BF16)]
        + [shape((rows, half), BF16)] * 2,
        (attn_own, attn_got, stats, stats_pair, w_out),
    )
    far_left, far_right = (swap(part, "head", 1) for part in (far_left, far_right))
    out_near = swap(
        local_call(
            add_near_kernel,
            "add_near",
            0.1,
            [shape((rows, share), BF16)],
            (out_next, far_left, far_right),
        )[0],
        "head",
        2,
    )
    dq_got = swap(dq_pair, "ctx", PAIR)
    out_core = swap(out_core, "head", 1)
    grad_q, grad_k, grad_v, grad_hk, grad_hv, out = local_call(
        finish_kernel,
        "finish",
        0.9,
        [shape((rows, width), BF16)] * 3
        + [shape((capacity, width), BF16)] * 2
        + [shape((rows, share), BF16)],
        (
            out_keep, out_core, out_near, dq_own, dq_got,
            dkv_own, got_k, got_v, rest_k, rest_v,
        ),
    )
    return out, grad_q, grad_k, grad_v, grad_hk, grad_hv


def gathered(sec_q, sec_k, sec_v, hist_k, hist_v, frame_levels, frame_counts, w_out, grad_out):
    rows = sec_q.shape[0]
    capacity = hist_k.shape[0]
    owners = lax.axis_size("ctx")
    me = lax.axis_index("ctx")
    frames = jnp.arange(FMAX, dtype=jnp.int32)[None, :]
    tokens = jnp.where(
        frames < frame_counts[:, None], jnp.right_shift(jnp.int32(FTOK), 2 * frame_levels), 0
    ).sum(axis=1)
    slots = jnp.arange(capacity, dtype=jnp.int32)
    all_valid = jnp.concatenate(
        [jnp.ones((owners * rows,), bool), (slots[None] < tokens[:, None]).reshape(-1)]
    )
    own_valid = jnp.concatenate(
        [jnp.ones((rows,), bool), slots < lax.dynamic_index_in_dim(tokens, me, keepdims=False)]
    )

    def everyone(block, axis=0):
        return lax.all_gather(block, "ctx", axis=axis, tiled=True)

    own_k, own_v = (jnp.concatenate(a, axis=0) for a in ((sec_k, hist_k), (sec_v, hist_v)))
    all_k = jnp.concatenate([everyone(sec_k), everyone(hist_k)], axis=0)
    all_v = jnp.concatenate([everyone(sec_v), everyone(hist_v)], axis=0)
    d_attn = contract(lax.all_gather(grad_out, "head", axis=1, tiled=True), w_out, 1, 1).astype(BF16)
    all_q, all_d = everyone(sec_q), everyone(d_attn)

    def probs_and_dscores(query, key, value, dattn, valid, lse, delta):
        scores = contract(query, key, 1, 1) * SCALE
        probs = jnp.where(valid[None, :], jnp.exp(scores - lse), 0.0).astype(BF16)
        dprobs = contract(dattn, value, 1, 1)
        return probs, (probs.astype(F32) * (dprobs - delta)).astype(BF16)

    attn_parts, q_parts, k_parts, v_parts = [], [], [], []
    for head in range(sec_q.shape[1] // HDIM):
        query, dattn, key, value = (head_slice(a, head) for a in (sec_q, d_attn, all_k, all_v))
        scores = jnp.where(all_valid[None, :], contract(query, key, 1, 1) * SCALE, NEG_FILL)
        lse = jax.nn.logsumexp(scores, axis=1, keepdims=True)
        probs = jnp.where(all_valid[None, :], jnp.exp(scores - lse), 0.0).astype(BF16)
        attn = contract(probs, value, 1, 0).astype(BF16)
        delta = jnp.sum(attn.astype(F32) * dattn.astype(F32), axis=1, keepdims=True)
        _, dscores = probs_and_dscores(query, key, value, dattn, all_valid, lse, delta)
        attn_parts.append(attn)
        q_parts.append(contract(dscores, key, 1, 0))
        query, dattn, key, value = (head_slice(a, head) for a in (all_q, all_d, own_k, own_v))
        probs, dscores = probs_and_dscores(
            query, key, value, dattn, own_valid, everyone(lse), everyone(delta)
        )
        k_parts.append(contract(dscores, query, 0, 0))
        v_parts.append(contract(probs, dattn, 0, 0))
    partial = contract(jnp.concatenate(attn_parts, axis=1), w_out, 1, 0).astype(BF16)
    out = lax.psum_scatter(partial, "head", scatter_dimension=1, tiled=True)
    grad_q, grad_k = (
        (jnp.concatenate(a, axis=1) * SCALE).astype(BF16) for a in (q_parts, k_parts)
    )
    grad_v = jnp.concatenate(v_parts, axis=1).astype(BF16)
    return out, grad_q, grad_k[:rows], grad_v[:rows], grad_k[rows:], grad_v[rows:]


def solution(mesh):
    split = P("ctx", "head")
    plan = blocked if (mesh.shape["ctx"], mesh.shape["head"]) == (2 * SQUARE, 4) else gathered
    return jax.shard_map(
        plan,
        mesh=mesh,
        in_specs=(split,) * 5 + (P(), P(), P("head", None), split),
        out_specs=(split,) * 6,
        check_vma=False,
    )
```

```python
import functools
import math

import jax
import jax.numpy as jnp
from jax import lax
from jax.experimental import pallas as pl
from jax.experimental.pallas import tpu as pltpu
from jax.sharding import PartitionSpec as P

HDIM = 128
FTOK = 16
FMAX = 2
NEG_FILL = -1e30
SCALE = 1.0 / math.sqrt(HDIM)
F32 = jnp.float32
BF16 = jnp.bfloat16
SQUARE = 4
HBM_BYTES = 3.69e6
PAIR = 4


def contract(left, right, left_dim, right_dim):
    return lax.dot_general(
        left, right, (((left_dim,), (right_dim,)), ((), ())), preferred_element_type=F32
    )


def head_slice(stacked, head):
    return stacked[:, head * HDIM : (head + 1) * HDIM]


def swap(block, axis, bit):
    count = lax.axis_size(axis)
    return lax.ppermute(block, axis, [(i, i ^ bit) for i in range(count)])


def cost_of(micros):
    return pl.CostEstimate(flops=0, bytes_accessed=int(micros * HBM_BYTES), transcendentals=0)


def local_call(body, name, micros, out_shapes, args, tables=0):
    spaces = [pltpu.SMEM] * tables + [pltpu.VMEM] * (len(args) - tables)
    return pl.pallas_call(
        body,
        name=name,
        out_shape=out_shapes,
        in_specs=[pl.BlockSpec(memory_space=space) for space in spaces],
        out_specs=[pl.BlockSpec(memory_space=pltpu.VMEM)] * len(out_shapes),
        compiler_params=pltpu.CompilerParams(vmem_limit_bytes=16 * 2**20),
        cost_estimate=cost_of(micros),
    )(*args)


def load_kernel(k_ref, hk_ref, v_ref, hv_ref, kv_out, kv_ref, sems):
    inward, outward, begin = [], [], 0
    for i, ref in enumerate((k_ref, hk_ref, v_ref, hv_ref)):
        part = pl.ds(begin, ref.shape[0])
        inward.append(pltpu.make_async_copy(ref, kv_ref.at[part], sems.at[0, i]))
        outward.append(pltpu.make_async_copy(kv_ref.at[part], kv_out.at[part], sems.at[1, i]))
        begin += ref.shape[0]
    for copy in inward:
        copy.start()
    for before, after in zip(inward, outward):
        before.wait()
        after.start()
    for copy in outward:
        copy.wait()


def load_keys(*arrays):
    rows = sum(a.shape[0] for a in arrays)
    width = arrays[0].shape[1]
    return pl.pallas_call(
        load_kernel,
        name="load",
        out_shape=jax.ShapeDtypeStruct((rows, width), BF16),
        in_specs=[pl.BlockSpec(memory_space=pl.ANY)] * len(arrays),
        out_specs=pl.BlockSpec(memory_space=pl.ANY),
        scratch_shapes=[pltpu.VMEM((rows, width), BF16), pltpu.SemaphoreType.DMA((2, len(arrays)))],
        compiler_params=pltpu.CompilerParams(vmem_limit_bytes=60 * 2**20),
        cost_estimate=cost_of(1.6),
    )(*arrays)


def split_heads_kernel(kv_ref, *out_refs):
    for head, ref in enumerate(out_refs):
        ref[...] = head_slice(kv_ref[...], head)


def square_keys(head, near, far):
    keys = near[0].shape[0] // 2
    return [head_slice(ref[:keys], head) for ref in near] + [far[head][:keys]]


def square_values(head, near, far):
    keys = near[0].shape[0] // 2
    return [head_slice(ref[keys:], head) for ref in near] + [far[head][keys:]]


def load_weight_kernel(w_ref, w_out, sems):
    copies = []
    for i in range(sems.shape[0]):
        part = pl.ds(i * HDIM, HDIM)
        copies.append(pltpu.make_async_copy(w_ref.at[part], w_out.at[part], sems.at[i]))
    for copy in copies:
        copy.start()
    for copy in copies:
        copy.wait()


def load_weight(w_out):
    return pl.pallas_call(
        load_weight_kernel,
        name="load_w",
        out_shape=jax.ShapeDtypeStruct(w_out.shape, BF16),
        in_specs=[pl.BlockSpec(memory_space=pl.ANY)],
        out_specs=pl.BlockSpec(memory_space=pltpu.VMEM),
        scratch_shapes=[pltpu.SemaphoreType.DMA((w_out.shape[0] // HDIM,))],
        compiler_params=pltpu.CompilerParams(vmem_limit_bytes=50 * 2**20 + 2**19),
        cost_estimate=cost_of(1.6),
    )(w_out)


def limits_kernel(levels_ref, counts_ref, limits_ref):
    me = lax.axis_index("ctx")
    row = lax.broadcasted_iota(jnp.int32, limits_ref.shape, 0)
    limits = jnp.zeros(limits_ref.shape, jnp.int32)
    for step in range(SQUARE):
        total = jnp.int32(0)
        for frame in range(FMAX):
            tokens = lax.shift_right_logical(jnp.int32(FTOK), 2 * levels_ref[me ^ step, frame])
            total += jnp.where(frame < counts_ref[me ^ step], tokens, 0)
        limits = jnp.where(row == step, total, limits)
    limits_ref[...] = limits


def dattn_kernel(own_ref, core_ref, near_ref, far_ref, w_ref, out_ref):
    me = lax.axis_index("head")
    size = own_ref.shape[1]
    total = None
    for step, ref in enumerate((own_ref, core_ref, near_ref, far_ref)):
        columns = pl.ds(pl.multiple_of((me ^ step) * size, HDIM), size)
        part = contract(ref[...], w_ref[:, columns], 1, 1)
        total = part if total is None else total + part
    out_ref[...] = total.astype(BF16)


def both_rows(own_ref, pair_ref, head):
    return jnp.concatenate(
        [head_slice(own_ref[...], head), head_slice(pair_ref[...], head)], axis=0
    )


def scores_kernel(
    limits_ref, q_own_ref, q_pair_ref, kv0, kv1, kv2, *refs
):
    rows = q_own_ref.shape[0]
    *far, lse_ref, probs_ref = refs
    keys = kv0.shape[0] // 2
    lse_ref[...] = jnp.zeros_like(lse_ref)
    for head in range(q_own_ref.shape[1] // HDIM):
        query = both_rows(q_own_ref, q_pair_ref, head)
        scores = []
        for step, key in enumerate(square_keys(head, (kv0, kv1, kv2), far)):
            block = contract(key, query, 1, 1) * SCALE
            slot = lax.broadcasted_iota(jnp.int32, block.shape, 0)
            valid = slot < rows + limits_ref[step : step + 1]
            scores.append(jnp.where(valid, block, NEG_FILL))
        top = functools.reduce(
            jnp.maximum, [jnp.max(block, axis=0, keepdims=True) for block in scores]
        )
        weights = [jnp.exp(block - top) for block in scores]
        total = sum(jnp.sum(block, axis=0, keepdims=True) for block in weights)
        inverse = 1.0 / total
        for step, block in enumerate(weights):
            begin = (head * SQUARE + step) * keys
            probs_ref[begin : begin + keys] = (block * inverse).astype(BF16)
        lse_ref[head : head + 1] = top + jnp.log(total)


def delta_kernel(lse_ref, probs_ref, d_own_ref, d_pair_ref, kv0, kv1, kv2, *refs):
    *far, stats_ref, dprobs_ref = refs
    keys = kv0.shape[0] // 2
    stats_ref[...] = jnp.zeros_like(stats_ref)
    stats_ref[: lse_ref.shape[0]] = lse_ref[...]
    for head in range(d_own_ref.shape[1] // HDIM):
        dattn = both_rows(d_own_ref, d_pair_ref, head)
        delta = None
        for step, value in enumerate(square_values(head, (kv0, kv1, kv2), far)):
            part = pl.ds((head * SQUARE + step) * keys, keys)
            dprobs = contract(value, dattn, 1, 1)
            dprobs_ref[part] = dprobs
            share = jnp.sum(probs_ref[part].astype(F32) * dprobs, axis=0, keepdims=True)
            delta = share if delta is None else delta + share
        stats_ref[8 + head : 9 + head] = delta


def attn_kernel(probs_ref, kv0, kv1, kv2, *refs):
    *far, own_ref, pair_ref = refs
    rows = own_ref.shape[1]
    keys = kv0.shape[0] // 2
    for head in range(own_ref.shape[0] // HDIM):
        attn = None
        for step, value in enumerate(square_values(head, (kv0, kv1, kv2), far)):
            begin = (head * SQUARE + step) * keys
            part = contract(value, probs_ref[begin : begin + keys], 0, 0)
            attn = part if attn is None else attn + part
        features = slice(head * HDIM, (head + 1) * HDIM)
        own_ref[features] = attn[:, :rows]
        pair_ref[features] = attn[:, rows:].astype(BF16)


def merge_parts(mine, theirs):
    top = jnp.maximum(mine, theirs)
    weight, weight_pair = jnp.exp(mine - top), jnp.exp(theirs - top)
    inverse = 1.0 / (weight + weight_pair)
    return weight * inverse, weight_pair * inverse


def project_kernel(
    own_ref, pair_ref, stats_ref, stats_pair_ref, w_ref,
    keep_ref, next_ref, core_ref, far_left_ref, far_right_ref,
):
    rows = own_ref.shape[1]
    parts = []
    for head in range(own_ref.shape[0] // HDIM):
        features = slice(head * HDIM, (head + 1) * HDIM)
        weight, weight_pair = merge_parts(
            stats_ref[head : head + 1, :rows], stats_pair_ref[head : head + 1, rows:]
        )
        parts.append(own_ref[features] * weight + pair_ref[features].astype(F32) * weight_pair)
    attn = jnp.concatenate(parts, axis=0).astype(BF16)
    me = lax.axis_index("head")
    size = keep_ref.shape[1]
    half = size // 2

    def columns_of(step):
        columns = pl.ds(pl.multiple_of((me ^ step) * size, HDIM), size)
        return contract(attn, w_ref[:, columns], 0, 0)

    far = columns_of(3).astype(BF16)
    far_left_ref[...] = far[:, :half]
    far_right_ref[...] = far[:, half:]
    next_ref[...] = columns_of(2)
    core_ref[...] = columns_of(1).astype(BF16)
    keep_ref[...] = columns_of(0)


def add_near_kernel(next_ref, left_ref, right_ref, out_ref):
    half = left_ref.shape[1]
    out_ref[:, :half] = (next_ref[:, :half] + left_ref[...].astype(F32)).astype(BF16)
    out_ref[:, half:] = (next_ref[:, half:] + right_ref[...].astype(F32)).astype(BF16)


def backward_kernel(
    q_own_ref, q_pair_ref, d_own_ref, d_pair_ref, stats_ref, stats_pair_ref, probs_ref, dprobs_ref,
    kv0, kv1, kv2, *refs,
):
    rows = q_own_ref.shape[0]
    *far, dq_own_ref, dq_pair_ref, dkv_ref, send_y_ref, send_z_ref, near_y_ref, near_z_ref = refs
    keys = kv0.shape[0] // 2
    wide = near_y_ref.shape[0]
    key_parts = (
        dkv_ref.at[:keys], send_y_ref.at[:keys], near_y_ref.at[:keys], send_y_ref.at[wide : wide + keys]
    )
    value_parts = (
        dkv_ref.at[keys : keys + rows], near_z_ref, send_z_ref.at[:rows], send_z_ref.at[rows:]
    )
    hist_parts = (
        dkv_ref.at[keys + rows :], send_y_ref.at[keys:wide], near_y_ref.at[keys:], send_y_ref.at[wide + keys :]
    )

    def swapped(row):
        return jnp.concatenate([row[:, rows:], row[:, :rows]], axis=1)

    for head in range(q_own_ref.shape[1] // HDIM):
        query = both_rows(q_own_ref, q_pair_ref, head)
        dattn = both_rows(d_own_ref, d_pair_ref, head)
        weight, weight_pair = merge_parts(
            stats_ref[head : head + 1], swapped(stats_pair_ref[head : head + 1])
        )
        delta = weight * stats_ref[8 + head : 9 + head]
        delta += weight_pair * swapped(stats_pair_ref[8 + head : 9 + head])
        features = slice(head * HDIM, (head + 1) * HDIM)
        dquery = None
        for step, key in enumerate(square_keys(head, (kv0, kv1, kv2), far)):
            begin = (head * SQUARE + step) * keys
            probs = (probs_ref[begin : begin + keys].astype(F32) * weight).astype(BF16)
            dprobs = dprobs_ref[begin : begin + keys]
            dscores = (probs.astype(F32) * (dprobs - delta)).astype(BF16)
            grad_key = contract(dscores, query, 1, 0) * SCALE
            grad_value = contract(probs, dattn, 1, 0)
            parts = (grad_key, grad_value[:rows], grad_value[rows:])
            for part, targets in zip(parts, (key_parts, value_parts, hist_parts)):
                targets[step][:, features] = part.astype(targets[step].dtype)
            grad_query = contract(dscores, key, 0, 0)
            dquery = grad_query if dquery is None else dquery + grad_query
        dq_own_ref[:, features] = dquery[:rows] * SCALE
        dq_pair_ref[:, features] = (dquery[rows:] * SCALE).astype(BF16)


def pass_on_kernel(
    near_y_ref, near_z_ref, got_y_ref, got_z_ref, keep_ref, core_ref,
    key_ref, hist_ref, value_ref, sum_ref,
):
    rows = key_ref.shape[0]
    wide = near_y_ref.shape[0]
    total_y = near_y_ref[...] + got_y_ref[wide:].astype(F32)
    key_ref[...] = total_y[:rows].astype(BF16)
    hist_ref[...] = total_y[rows:].astype(BF16)
    value_ref[...] = (near_z_ref[...] + got_z_ref[rows:].astype(F32)).astype(BF16)
    sum_ref[...] = keep_ref[...] + core_ref[...].astype(F32)


def finish_kernel(
    keep_ref, near_ref, dq_ref, dq_pair_ref,
    dkv_ref, got_y_ref, got_z_ref, rest_k_ref, rest_h_ref, rest_v_ref,
    q_out, k_out, v_out, hk_out, hv_out, out_ref,
):
    rows, capacity = k_out.shape[0], hk_out.shape[0]
    keys = rows + capacity

    def total(first, *others):
        for other in others:
            first = first + other.astype(F32)
        return first.astype(BF16)

    q_out[...] = total(dq_ref[...], dq_pair_ref[...])
    k_out[...] = total(dkv_ref[:rows], got_y_ref[:rows], rest_k_ref[...])
    hk_out[...] = total(dkv_ref[rows:keys], got_y_ref[rows:keys], rest_h_ref[:capacity])
    v_out[...] = total(dkv_ref[keys : keys + rows], got_z_ref[:rows], rest_v_ref[...])
    hv_out[...] = total(
        dkv_ref[keys + rows :], got_y_ref[keys : keys + capacity], rest_h_ref[capacity:]
    )
    out_ref[...] = total(keep_ref[...], near_ref[...])


def blocked(sec_q, sec_k, sec_v, hist_k, hist_v, frame_levels, frame_counts, w_out, grad_out):
    shape = jax.ShapeDtypeStruct
    rows, width = sec_q.shape
    heads = width // HDIM
    capacity = hist_k.shape[0]
    keys = rows + capacity
    share = grad_out.shape[1]

    q_pair = swap(sec_q, "ctx", PAIR)
    grad_near = swap(grad_out, "head", 2)
    grad_core = swap(grad_out, "head", 1)
    weight = load_weight(w_out)
    grad_near, weight = lax.optimization_barrier((grad_near, weight))
    grad_far = swap(grad_near, "head", 1)
    kv0 = load_keys(sec_k, hist_k, sec_v, hist_v)
    kv2 = swap(kv0, "ctx", 2)
    kv1 = swap(kv0, "ctx", 1)
    d_own = local_call(
        dattn_kernel,
        "dattn",
        0.8,
        [shape((rows, width), BF16)],
        (grad_out, grad_core, grad_near, grad_far, weight),
    )[0]
    kv1, kv2, d_own = lax.optimization_barrier((kv1, kv2, d_own))
    pieces = local_call(
        split_heads_kernel, "split_heads", 0.1, [shape((2 * keys, HDIM), BF16)] * heads, (kv2,)
    )
    kvs = (kv0, kv1, kv2, *(swap(piece, "ctx", 1) for piece in pieces))
    d_pair = swap(d_own, "ctx", PAIR)
    limits = local_call(
        limits_kernel,
        "limits",
        0.6,
        [shape((8, 2 * rows), jnp.int32)],
        (frame_levels, frame_counts),
        tables=2,
    )[0]
    lse, probs = local_call(
        scores_kernel,
        "scores",
        0.9,
        [shape((8, 2 * rows), F32), shape((heads * SQUARE * keys, 2 * rows), BF16)],
        (limits, sec_q, q_pair, *kvs),
    )
    attn_own, attn_pair = local_call(
        attn_kernel,
        "attn",
        0.5,
        [shape((width, rows), F32), shape((width, rows), BF16)],
        (probs, *kvs),
    )
    lse, attn_own = lax.optimization_barrier((lse, attn_own))
    stats, dprobs = local_call(
        delta_kernel,
        "delta",
        0.7,
        [shape((16, 2 * rows), F32), shape((heads * SQUARE * keys, 2 * rows), F32)],
        (lse, probs, d_own, d_pair, *kvs),
    )
    stats_pair = swap(stats, "ctx", PAIR)
    wide = keys + capacity
    dq_own, dq_pair, dkv_own, send_y, send_z, near_y, near_z = local_call(
        backward_kernel,
        "backward",
        1.1,
        [shape((rows, width), F32), shape((rows, width), BF16), shape((2 * keys, width), F32)]
        + [shape((2 * wide, width), BF16), shape((2 * rows, width), BF16)]
        + [shape((wide, width), F32), shape((rows, width), F32)],
        (sec_q, q_pair, d_own, d_pair, stats, stats_pair, probs, dprobs, *kvs),
    )
    attn_got = swap(attn_pair, "ctx", PAIR)
    attn_got, send_y, send_z = lax.optimization_barrier((attn_got, send_y, send_z))
    got_y = swap(send_y, "ctx", 1)
    got_z = swap(send_z, "ctx", 2)
    half = share // 2
    out_keep, out_next, out_core, far_left, far_right = local_call(
        project_kernel,
        "project",
        0.6,
        [shape((rows, share), F32)] * 2
        + [shape((rows, share), BF16)]
        + [shape((rows, half), BF16)] * 2,
        (attn_own, attn_got, stats, stats_pair, w_out),
    )
    far_left, far_right = (swap(part, "head", 1) for part in (far_left, far_right))
    out_near = swap(
        local_call(
            add_near_kernel,
            "add_near",
            0.1,
            [shape((rows, share), BF16)],
            (out_next, far_left, far_right),
        )[0],
        "head",
        2,
    )
    dq_got = swap(dq_pair, "ctx", PAIR)
    out_core = swap(out_core, "head", 1)
    rest_k, rest_h, rest_v, out_keep = local_call(
        pass_on_kernel,
        "pass_on",
        0.1,
        [shape((size, width), BF16) for size in (rows, 2 * capacity, rows)]
        + [shape((rows, share), F32)],
        (near_y, near_z, got_y, got_z, out_keep, out_core),
    )
    rest_k = swap(rest_k, "ctx", 2)
    rest_h = swap(rest_h, "ctx", 2)
    rest_v = swap(rest_v, "ctx", 1)
    grad_q, grad_k, grad_v, grad_hk, grad_hv, out = local_call(
        finish_kernel,
        "finish",
        0.9,
        [shape((rows, width), BF16)] * 3
        + [shape((capacity, width), BF16)] * 2
        + [shape((rows, share), BF16)],
        (
            out_keep, out_near, dq_own, dq_got,
            dkv_own, got_y, got_z, rest_k, rest_h, rest_v,
        ),
    )
    return out, grad_q, grad_k, grad_v, grad_hk, grad_hv


def gathered(sec_q, sec_k, sec_v, hist_k, hist_v, frame_levels, frame_counts, w_out, grad_out):
    rows = sec_q.shape[0]
    capacity = hist_k.shape[0]
    owners = lax.axis_size("ctx")
    me = lax.axis_index("ctx")
    frames = jnp.arange(FMAX, dtype=jnp.int32)[None, :]
    tokens = jnp.where(
        frames < frame_counts[:, None], jnp.right_shift(jnp.int32(FTOK), 2 * frame_levels), 0
    ).sum(axis=1)
    slots = jnp.arange(capacity, dtype=jnp.int32)
    all_valid = jnp.concatenate(
        [jnp.ones((owners * rows,), bool), (slots[None] < tokens[:, None]).reshape(-1)]
    )
    own_valid = jnp.concatenate(
        [jnp.ones((rows,), bool), slots < lax.dynamic_index_in_dim(tokens, me, keepdims=False)]
    )

    def everyone(block, axis=0):
        return lax.all_gather(block, "ctx", axis=axis, tiled=True)

    own_k, own_v = (jnp.concatenate(a, axis=0) for a in ((sec_k, hist_k), (sec_v, hist_v)))
    all_k = jnp.concatenate([everyone(sec_k), everyone(hist_k)], axis=0)
    all_v = jnp.concatenate([everyone(sec_v), everyone(hist_v)], axis=0)
    d_attn = contract(lax.all_gather(grad_out, "head", axis=1, tiled=True), w_out, 1, 1).astype(BF16)
    all_q, all_d = everyone(sec_q), everyone(d_attn)

    def probs_and_dscores(query, key, value, dattn, valid, lse, delta):
        scores = contract(query, key, 1, 1) * SCALE
        probs = jnp.where(valid[None, :], jnp.exp(scores - lse), 0.0).astype(BF16)
        dprobs = contract(dattn, value, 1, 1)
        return probs, (probs.astype(F32) * (dprobs - delta)).astype(BF16)

    attn_parts, q_parts, k_parts, v_parts = [], [], [], []
    for head in range(sec_q.shape[1] // HDIM):
        query, dattn, key, value = (head_slice(a, head) for a in (sec_q, d_attn, all_k, all_v))
        scores = jnp.where(all_valid[None, :], contract(query, key, 1, 1) * SCALE, NEG_FILL)
        lse = jax.nn.logsumexp(scores, axis=1, keepdims=True)
        probs = jnp.where(all_valid[None, :], jnp.exp(scores - lse), 0.0).astype(BF16)
        attn = contract(probs, value, 1, 0).astype(BF16)
        delta = jnp.sum(attn.astype(F32) * dattn.astype(F32), axis=1, keepdims=True)
        _, dscores = probs_and_dscores(query, key, value, dattn, all_valid, lse, delta)
        attn_parts.append(attn)
        q_parts.append(contract(dscores, key, 1, 0))
        query, dattn, key, value = (head_slice(a, head) for a in (all_q, all_d, own_k, own_v))
        probs, dscores = probs_and_dscores(
            query, key, value, dattn, own_valid, everyone(lse), everyone(delta)
        )
        k_parts.append(contract(dscores, query, 0, 0))
        v_parts.append(contract(probs, dattn, 0, 0))
    partial = contract(jnp.concatenate(attn_parts, axis=1), w_out, 1, 0).astype(BF16)
    out = lax.psum_scatter(partial, "head", scatter_dimension=1, tiled=True)
    grad_q, grad_k = (
        (jnp.concatenate(a, axis=1) * SCALE).astype(BF16) for a in (q_parts, k_parts)
    )
    grad_v = jnp.concatenate(v_parts, axis=1).astype(BF16)
    return out, grad_q, grad_k[:rows], grad_v[:rows], grad_k[rows:], grad_v[rows:]


def solution(mesh):
    split = P("ctx", "head")
    plan = blocked if (mesh.shape["ctx"], mesh.shape["head"]) == (2 * SQUARE, 4) else gathered
    return jax.shard_map(
        plan,
        mesh=mesh,
        in_specs=(split,) * 5 + (P(), P(), P("head", None), split),
        out_specs=(split,) * 6,
        check_vma=False,
    )
```

```python
import functools
import math

import jax
import jax.numpy as jnp
from jax import lax
from jax.experimental import pallas as pl
from jax.experimental.pallas import tpu as pltpu
from jax.sharding import PartitionSpec as P

HDIM = 128
FTOK = 16
FMAX = 2
NEG_FILL = -1e30
SCALE = 1.0 / math.sqrt(HDIM)
F32 = jnp.float32
BF16 = jnp.bfloat16
SQUARE = 4
HBM_BYTES = 3.69e6
PAIR = 4


def contract(left, right, left_dim, right_dim):
    return lax.dot_general(
        left, right, (((left_dim,), (right_dim,)), ((), ())), preferred_element_type=F32
    )


def head_slice(stacked, head):
    return stacked[:, head * HDIM : (head + 1) * HDIM]


def swap(block, axis, bit):
    count = lax.axis_size(axis)
    return lax.ppermute(block, axis, [(i, i ^ bit) for i in range(count)])


def cost_of(micros):
    return pl.CostEstimate(flops=0, bytes_accessed=int(micros * HBM_BYTES), transcendentals=0)


def local_call(body, name, micros, out_shapes, args, tables=0):
    spaces = [pltpu.SMEM] * tables + [pltpu.VMEM] * (len(args) - tables)
    return pl.pallas_call(
        body,
        name=name,
        out_shape=out_shapes,
        in_specs=[pl.BlockSpec(memory_space=space) for space in spaces],
        out_specs=[pl.BlockSpec(memory_space=pltpu.VMEM)] * len(out_shapes),
        compiler_params=pltpu.CompilerParams(vmem_limit_bytes=16 * 2**20),
        cost_estimate=cost_of(micros),
    )(*args)


def load_kernel(k_ref, hk_ref, v_ref, hv_ref, kv_out, kv_ref, sems):
    inward, outward, begin = [], [], 0
    for i, ref in enumerate((k_ref, hk_ref, v_ref, hv_ref)):
        part = pl.ds(begin, ref.shape[0])
        inward.append(pltpu.make_async_copy(ref, kv_ref.at[part], sems.at[0, i]))
        outward.append(pltpu.make_async_copy(kv_ref.at[part], kv_out.at[part], sems.at[1, i]))
        begin += ref.shape[0]
    for copy in inward:
        copy.start()
    for before, after in zip(inward, outward):
        before.wait()
        after.start()
    for copy in outward:
        copy.wait()


def load_keys(*arrays):
    rows = sum(a.shape[0] for a in arrays)
    width = arrays[0].shape[1]
    return pl.pallas_call(
        load_kernel,
        name="load",
        out_shape=jax.ShapeDtypeStruct((rows, width), BF16),
        in_specs=[pl.BlockSpec(memory_space=pl.ANY)] * len(arrays),
        out_specs=pl.BlockSpec(memory_space=pl.ANY),
        scratch_shapes=[pltpu.VMEM((rows, width), BF16), pltpu.SemaphoreType.DMA((2, len(arrays)))],
        compiler_params=pltpu.CompilerParams(vmem_limit_bytes=60 * 2**20),
        cost_estimate=cost_of(1.6),
    )(*arrays)


def split_heads_kernel(kv_ref, *out_refs):
    for head, ref in enumerate(out_refs):
        ref[...] = head_slice(kv_ref[...], head)


def square_keys(head, near, far):
    keys = near[0].shape[0] // 2
    return [head_slice(ref[:keys], head) for ref in near] + [far[head][:keys]]


def square_values(head, near, far):
    keys = near[0].shape[0] // 2
    return [head_slice(ref[keys:], head) for ref in near] + [far[head][keys:]]


def load_weight_kernel(w_ref, w_out, sems):
    copies = []
    for i in range(sems.shape[0]):
        part = pl.ds(i * HDIM, HDIM)
        copies.append(pltpu.make_async_copy(w_ref.at[part], w_out.at[part], sems.at[i]))
    for copy in copies:
        copy.start()
    for copy in copies:
        copy.wait()


def load_weight(w_out):
    return pl.pallas_call(
        load_weight_kernel,
        name="load_w",
        out_shape=jax.ShapeDtypeStruct(w_out.shape, BF16),
        in_specs=[pl.BlockSpec(memory_space=pl.ANY)],
        out_specs=pl.BlockSpec(memory_space=pltpu.VMEM),
        scratch_shapes=[pltpu.SemaphoreType.DMA((w_out.shape[0] // HDIM,))],
        compiler_params=pltpu.CompilerParams(vmem_limit_bytes=50 * 2**20 + 2**19),
        cost_estimate=cost_of(1.6),
    )(w_out)


def limits_kernel(levels_ref, counts_ref, limits_ref):
    me = lax.axis_index("ctx")
    row = lax.broadcasted_iota(jnp.int32, limits_ref.shape, 0)
    limits = jnp.zeros(limits_ref.shape, jnp.int32)
    for step in range(SQUARE):
        total = jnp.int32(0)
        for frame in range(FMAX):
            tokens = lax.shift_right_logical(jnp.int32(FTOK), 2 * levels_ref[me ^ step, frame])
            total += jnp.where(frame < counts_ref[me ^ step], tokens, 0)
        limits = jnp.where(row == step, total, limits)
    limits_ref[...] = limits


def dattn_kernel(own_ref, core_ref, near_ref, far_ref, w_ref, out_ref):
    me = lax.axis_index("head")
    size = own_ref.shape[1]
    total = None
    for step, ref in enumerate((own_ref, core_ref, near_ref, far_ref)):
        columns = pl.ds(pl.multiple_of((me ^ step) * size, HDIM), size)
        part = contract(ref[...], w_ref[:, columns], 1, 1)
        total = part if total is None else total + part
    out_ref[...] = total.astype(BF16)


def both_rows(own_ref, pair_ref, head):
    return jnp.concatenate(
        [head_slice(own_ref[...], head), head_slice(pair_ref[...], head)], axis=0
    )


def scores_kernel(
    limits_ref, q_own_ref, q_pair_ref, kv0, kv1, kv2, *refs
):
    rows = q_own_ref.shape[0]
    *far, lse_ref, probs_ref = refs
    keys = kv0.shape[0] // 2
    lse_ref[...] = jnp.zeros_like(lse_ref)
    for head in range(q_own_ref.shape[1] // HDIM):
        query = both_rows(q_own_ref, q_pair_ref, head)
        scores = []
        for step, key in enumerate(square_keys(head, (kv0, kv1, kv2), far)):
            block = contract(key, query, 1, 1) * SCALE
            slot = lax.broadcasted_iota(jnp.int32, block.shape, 0)
            valid = slot < rows + limits_ref[step : step + 1]
            scores.append(jnp.where(valid, block, NEG_FILL))
        top = functools.reduce(
            jnp.maximum, [jnp.max(block, axis=0, keepdims=True) for block in scores]
        )
        weights = [jnp.exp(block - top) for block in scores]
        total = sum(jnp.sum(block, axis=0, keepdims=True) for block in weights)
        inverse = 1.0 / total
        for step, block in enumerate(weights):
            begin = (head * SQUARE + step) * keys
            probs_ref[begin : begin + keys] = (block * inverse).astype(BF16)
        lse_ref[head : head + 1] = top + jnp.log(total)


def delta_kernel(lse_ref, probs_ref, d_own_ref, d_pair_ref, kv0, kv1, kv2, *refs):
    *far, stats_ref, dprobs_ref = refs
    keys = kv0.shape[0] // 2
    stats_ref[...] = jnp.zeros_like(stats_ref)
    stats_ref[: lse_ref.shape[0]] = lse_ref[...]
    for head in range(d_own_ref.shape[1] // HDIM):
        dattn = both_rows(d_own_ref, d_pair_ref, head)
        delta = None
        for step, value in enumerate(square_values(head, (kv0, kv1, kv2), far)):
            part = pl.ds((head * SQUARE + step) * keys, keys)
            dprobs = contract(value, dattn, 1, 1)
            dprobs_ref[part] = dprobs
            share = jnp.sum(probs_ref[part].astype(F32) * dprobs, axis=0, keepdims=True)
            delta = share if delta is None else delta + share
        stats_ref[8 + head : 9 + head] = delta


def attn_kernel(probs_ref, kv0, kv1, kv2, *refs):
    *far, own_ref, pair_ref = refs
    rows = own_ref.shape[1]
    keys = kv0.shape[0] // 2
    for head in range(own_ref.shape[0] // HDIM):
        attn = None
        for step, value in enumerate(square_values(head, (kv0, kv1, kv2), far)):
            begin = (head * SQUARE + step) * keys
            part = contract(value, probs_ref[begin : begin + keys], 0, 0)
            attn = part if attn is None else attn + part
        features = slice(head * HDIM, (head + 1) * HDIM)
        own_ref[features] = attn[:, :rows]
        pair_ref[features] = attn[:, rows:].astype(BF16)


def merge_parts(mine, theirs):
    top = jnp.maximum(mine, theirs)
    weight, weight_pair = jnp.exp(mine - top), jnp.exp(theirs - top)
    inverse = 1.0 / (weight + weight_pair)
    return weight * inverse, weight_pair * inverse


def project_kernel(
    own_ref, pair_ref, stats_ref, stats_pair_ref, w_ref,
    keep_ref, next_ref, core_ref, far_left_ref, far_right_ref,
):
    rows = own_ref.shape[1]
    parts = []
    for head in range(own_ref.shape[0] // HDIM):
        features = slice(head * HDIM, (head + 1) * HDIM)
        weight, weight_pair = merge_parts(
            stats_ref[head : head + 1, :rows], stats_pair_ref[head : head + 1, rows:]
        )
        parts.append(own_ref[features] * weight + pair_ref[features].astype(F32) * weight_pair)
    attn = jnp.concatenate(parts, axis=0).astype(BF16)
    me = lax.axis_index("head")
    size = keep_ref.shape[1]
    half = size // 2

    def columns_of(step):
        columns = pl.ds(pl.multiple_of((me ^ step) * size, HDIM), size)
        return contract(attn, w_ref[:, columns], 0, 0)

    far = columns_of(3).astype(BF16)
    far_left_ref[...] = far[:, :half]
    far_right_ref[...] = far[:, half:]
    next_ref[...] = columns_of(2)
    core_ref[...] = columns_of(1).astype(BF16)
    keep_ref[...] = columns_of(0)


def add_near_kernel(next_ref, left_ref, right_ref, out_ref):
    half = left_ref.shape[1]
    out_ref[:, :half] = (next_ref[:, :half] + left_ref[...].astype(F32)).astype(BF16)
    out_ref[:, half:] = (next_ref[:, half:] + right_ref[...].astype(F32)).astype(BF16)


def backward_kernel(
    q_own_ref, q_pair_ref, d_own_ref, d_pair_ref, stats_ref, stats_pair_ref, probs_ref, dprobs_ref,
    kv0, kv1, kv2, *refs,
):
    rows = q_own_ref.shape[0]
    *far, dq_own_ref, dq_pair_ref, dkv_ref, send_y_ref, send_z_ref, near_y_ref, near_z_ref = refs
    keys = kv0.shape[0] // 2
    wide = near_y_ref.shape[0]
    key_parts = (
        dkv_ref.at[:keys], send_y_ref.at[:keys], near_y_ref.at[:keys], send_y_ref.at[wide : wide + keys]
    )
    value_parts = (
        dkv_ref.at[keys : keys + rows], near_z_ref, send_z_ref.at[:rows], send_z_ref.at[rows:]
    )
    hist_parts = (
        dkv_ref.at[keys + rows :], send_y_ref.at[keys:wide], near_y_ref.at[keys:], send_y_ref.at[wide + keys :]
    )

    def swapped(row):
        return jnp.concatenate([row[:, rows:], row[:, :rows]], axis=1)

    for head in range(q_own_ref.shape[1] // HDIM):
        query = both_rows(q_own_ref, q_pair_ref, head)
        dattn = both_rows(d_own_ref, d_pair_ref, head)
        weight, weight_pair = merge_parts(
            stats_ref[head : head + 1], swapped(stats_pair_ref[head : head + 1])
        )
        delta = weight * stats_ref[8 + head : 9 + head]
        delta += weight_pair * swapped(stats_pair_ref[8 + head : 9 + head])
        features = slice(head * HDIM, (head + 1) * HDIM)
        dquery = None
        for step, key in enumerate(square_keys(head, (kv0, kv1, kv2), far)):
            begin = (head * SQUARE + step) * keys
            probs = (probs_ref[begin : begin + keys].astype(F32) * weight).astype(BF16)
            dprobs = dprobs_ref[begin : begin + keys]
            dscores = (probs.astype(F32) * (dprobs - delta)).astype(BF16)
            grad_key = contract(dscores, query, 1, 0) * SCALE
            grad_value = contract(probs, dattn, 1, 0)
            parts = (grad_key, grad_value[:rows], grad_value[rows:])
            for part, targets in zip(parts, (key_parts, value_parts, hist_parts)):
                targets[step][:, features] = part.astype(targets[step].dtype)
            grad_query = contract(dscores, key, 0, 0)
            dquery = grad_query if dquery is None else dquery + grad_query
        dq_own_ref[:, features] = dquery[:rows] * SCALE
        dq_pair_ref[:, features] = (dquery[rows:] * SCALE).astype(BF16)


def pass_on_kernel(
    near_y_ref, near_z_ref, got_y_ref, got_z_ref, keep_ref, core_ref,
    key_ref, hist_ref, value_ref, sum_ref,
):
    rows = key_ref.shape[0]
    wide = near_y_ref.shape[0]
    total_y = near_y_ref[...] + got_y_ref[wide:].astype(F32)
    key_ref[...] = total_y[:rows].astype(BF16)
    hist_ref[...] = total_y[rows:].astype(BF16)
    value_ref[...] = (near_z_ref[...] + got_z_ref[rows:].astype(F32)).astype(BF16)
    sum_ref[...] = keep_ref[...] + core_ref[...].astype(F32)


def finish_kernel(
    keep_ref, near_ref, dq_ref, dq_pair_ref,
    dkv_ref, got_y_ref, got_z_ref, rest_k_ref, rest_h_ref, rest_v_ref,
    q_out, k_out, v_out, hk_out, hv_out, out_ref,
):
    rows, capacity = k_out.shape[0], hk_out.shape[0]
    keys = rows + capacity

    def total(first, *others):
        for other in others:
            first = first + other.astype(F32)
        return first.astype(BF16)

    q_out[...] = total(dq_ref[...], dq_pair_ref[...])
    k_out[...] = total(dkv_ref[:rows], got_y_ref[:rows], rest_k_ref[...])
    hk_out[...] = total(dkv_ref[rows:keys], got_y_ref[rows:keys], rest_h_ref[:capacity])
    v_out[...] = total(dkv_ref[keys : keys + rows], got_z_ref[:rows], rest_v_ref[...])
    hv_out[...] = total(
        dkv_ref[keys + rows :], got_y_ref[keys : keys + capacity], rest_h_ref[capacity:]
    )
    out_ref[...] = total(keep_ref[...], near_ref[...])


def blocked(sec_q, sec_k, sec_v, hist_k, hist_v, frame_levels, frame_counts, w_out, grad_out):
    shape = jax.ShapeDtypeStruct
    rows, width = sec_q.shape
    heads = width // HDIM
    capacity = hist_k.shape[0]
    keys = rows + capacity
    share = grad_out.shape[1]

    q_pair = swap(sec_q, "ctx", PAIR)
    grad_near = swap(grad_out, "head", 2)
    grad_core = swap(grad_out, "head", 1)
    weight = load_weight(w_out)
    grad_near, weight = lax.optimization_barrier((grad_near, weight))
    grad_far = swap(grad_near, "head", 1)
    kv0 = load_keys(sec_k, hist_k, sec_v, hist_v)
    kv2 = swap(kv0, "ctx", 2)
    kv1 = swap(kv0, "ctx", 1)
    d_own = local_call(
        dattn_kernel,
        "dattn",
        0.8,
        [shape((rows, width), BF16)],
        (grad_out, grad_core, grad_near, grad_far, weight),
    )[0]
    kv1, kv2, d_own = lax.optimization_barrier((kv1, kv2, d_own))
    pieces = local_call(
        split_heads_kernel, "split_heads", 0.1, [shape((2 * keys, HDIM), BF16)] * heads, (kv2,)
    )
    kvs = (kv0, kv1, kv2, *(swap(piece, "ctx", 1) for piece in pieces))
    d_pair = swap(d_own, "ctx", PAIR)
    limits = local_call(
        limits_kernel,
        "limits",
        0.6,
        [shape((8, 2 * rows), jnp.int32)],
        (frame_levels, frame_counts),
        tables=2,
    )[0]
    lse, probs = local_call(
        scores_kernel,
        "scores",
        0.9,
        [shape((8, 2 * rows), F32), shape((heads * SQUARE * keys, 2 * rows), BF16)],
        (limits, sec_q, q_pair, *kvs),
    )
    stats, dprobs = local_call(
        delta_kernel,
        "delta",
        0.7,
        [shape((16, 2 * rows), F32), shape((heads * SQUARE * keys, 2 * rows), F32)],
        (lse, probs, d_own, d_pair, *kvs),
    )
    stats_pair = swap(stats, "ctx", PAIR)
    probs, stats_pair = lax.optimization_barrier((probs, stats_pair))
    attn_own, attn_pair = local_call(
        attn_kernel,
        "attn",
        0.5,
        [shape((width, rows), F32), shape((width, rows), BF16)],
        (probs, *kvs),
    )
    wide = keys + capacity
    dq_own, dq_pair, dkv_own, send_y, send_z, near_y, near_z = local_call(
        backward_kernel,
        "backward",
        1.1,
        [shape((rows, width), F32), shape((rows, width), BF16), shape((2 * keys, width), F32)]
        + [shape((2 * wide, width), BF16), shape((2 * rows, width), BF16)]
        + [shape((wide, width), F32), shape((rows, width), F32)],
        (sec_q, q_pair, d_own, d_pair, stats, stats_pair, probs, dprobs, *kvs),
    )
    attn_got = swap(attn_pair, "ctx", PAIR)
    got_y = swap(send_y, "ctx", 1)
    got_z = swap(send_z, "ctx", 2)
    half = share // 2
    out_keep, out_next, out_core, far_left, far_right = local_call(
        project_kernel,
        "project",
        0.6,
        [shape((rows, share), F32)] * 2
        + [shape((rows, share), BF16)]
        + [shape((rows, half), BF16)] * 2,
        (attn_own, attn_got, stats, stats_pair, w_out),
    )
    far_left, far_right = (swap(part, "head", 1) for part in (far_left, far_right))
    out_near = swap(
        local_call(
            add_near_kernel,
            "add_near",
            0.1,
            [shape((rows, share), BF16)],
            (out_next, far_left, far_right),
        )[0],
        "head",
        2,
    )
    dq_got = swap(dq_pair, "ctx", PAIR)
    out_core = swap(out_core, "head", 1)
    rest_k, rest_h, rest_v, out_keep = local_call(
        pass_on_kernel,
        "pass_on",
        0.1,
        [shape((size, width), BF16) for size in (rows, 2 * capacity, rows)]
        + [shape((rows, share), F32)],
        (near_y, near_z, got_y, got_z, out_keep, out_core),
    )
    rest_k = swap(rest_k, "ctx", 2)
    rest_h = swap(rest_h, "ctx", 2)
    rest_v = swap(rest_v, "ctx", 1)
    grad_q, grad_k, grad_v, grad_hk, grad_hv, out = local_call(
        finish_kernel,
        "finish",
        0.9,
        [shape((rows, width), BF16)] * 3
        + [shape((capacity, width), BF16)] * 2
        + [shape((rows, share), BF16)],
        (
            out_keep, out_near, dq_own, dq_got,
            dkv_own, got_y, got_z, rest_k, rest_h, rest_v,
        ),
    )
    return out, grad_q, grad_k, grad_v, grad_hk, grad_hv


def gathered(sec_q, sec_k, sec_v, hist_k, hist_v, frame_levels, frame_counts, w_out, grad_out):
    rows = sec_q.shape[0]
    capacity = hist_k.shape[0]
    owners = lax.axis_size("ctx")
    me = lax.axis_index("ctx")
    frames = jnp.arange(FMAX, dtype=jnp.int32)[None, :]
    tokens = jnp.where(
        frames < frame_counts[:, None], jnp.right_shift(jnp.int32(FTOK), 2 * frame_levels), 0
    ).sum(axis=1)
    slots = jnp.arange(capacity, dtype=jnp.int32)
    all_valid = jnp.concatenate(
        [jnp.ones((owners * rows,), bool), (slots[None] < tokens[:, None]).reshape(-1)]
    )
    own_valid = jnp.concatenate(
        [jnp.ones((rows,), bool), slots < lax.dynamic_index_in_dim(tokens, me, keepdims=False)]
    )

    def everyone(block, axis=0):
        return lax.all_gather(block, "ctx", axis=axis, tiled=True)

    own_k, own_v = (jnp.concatenate(a, axis=0) for a in ((sec_k, hist_k), (sec_v, hist_v)))
    all_k = jnp.concatenate([everyone(sec_k), everyone(hist_k)], axis=0)
    all_v = jnp.concatenate([everyone(sec_v), everyone(hist_v)], axis=0)
    d_attn = contract(lax.all_gather(grad_out, "head", axis=1, tiled=True), w_out, 1, 1).astype(BF16)
    all_q, all_d = everyone(sec_q), everyone(d_attn)

    def probs_and_dscores(query, key, value, dattn, valid, lse, delta):
        scores = contract(query, key, 1, 1) * SCALE
        probs = jnp.where(valid[None, :], jnp.exp(scores - lse), 0.0).astype(BF16)
        dprobs = contract(dattn, value, 1, 1)
        return probs, (probs.astype(F32) * (dprobs - delta)).astype(BF16)

    attn_parts, q_parts, k_parts, v_parts = [], [], [], []
    for head in range(sec_q.shape[1] // HDIM):
        query, dattn, key, value = (head_slice(a, head) for a in (sec_q, d_attn, all_k, all_v))
        scores = jnp.where(all_valid[None, :], contract(query, key, 1, 1) * SCALE, NEG_FILL)
        lse = jax.nn.logsumexp(scores, axis=1, keepdims=True)
        probs = jnp.where(all_valid[None, :], jnp.exp(scores - lse), 0.0).astype(BF16)
        attn = contract(probs, value, 1, 0).astype(BF16)
        delta = jnp.sum(attn.astype(F32) * dattn.astype(F32), axis=1, keepdims=True)
        _, dscores = probs_and_dscores(query, key, value, dattn, all_valid, lse, delta)
        attn_parts.append(attn)
        q_parts.append(contract(dscores, key, 1, 0))
        query, dattn, key, value = (head_slice(a, head) for a in (all_q, all_d, own_k, own_v))
        probs, dscores = probs_and_dscores(
            query, key, value, dattn, own_valid, everyone(lse), everyone(delta)
        )
        k_parts.append(contract(dscores, query, 0, 0))
        v_parts.append(contract(probs, dattn, 0, 0))
    partial = contract(jnp.concatenate(attn_parts, axis=1), w_out, 1, 0).astype(BF16)
    out = lax.psum_scatter(partial, "head", scatter_dimension=1, tiled=True)
    grad_q, grad_k = (
        (jnp.concatenate(a, axis=1) * SCALE).astype(BF16) for a in (q_parts, k_parts)
    )
    grad_v = jnp.concatenate(v_parts, axis=1).astype(BF16)
    return out, grad_q, grad_k[:rows], grad_v[:rows], grad_k[rows:], grad_v[rows:]


def solution(mesh):
    split = P("ctx", "head")
    plan = blocked if (mesh.shape["ctx"], mesh.shape["head"]) == (2 * SQUARE, 4) else gathered
    return jax.shard_map(
        plan,
        mesh=mesh,
        in_specs=(split,) * 5 + (P(), P(), P("head", None), split),
        out_specs=(split,) * 6,
        check_vma=False,
    )
```

```python
import functools
import math

import jax
import jax.numpy as jnp
from jax import lax
from jax.experimental import pallas as pl
from jax.experimental.pallas import tpu as pltpu
from jax.sharding import PartitionSpec as P

HDIM = 128
FTOK = 16
FMAX = 2
NEG_FILL = -1e30
SCALE = 1.0 / math.sqrt(HDIM)
F32 = jnp.float32
BF16 = jnp.bfloat16
SQUARE = 4
HBM_BYTES = 3.69e6
PAIR = 4


def contract(left, right, left_dim, right_dim):
    return lax.dot_general(
        left, right, (((left_dim,), (right_dim,)), ((), ())), preferred_element_type=F32
    )


def head_slice(stacked, head):
    return stacked[:, head * HDIM : (head + 1) * HDIM]


def swap(block, axis, bit):
    count = lax.axis_size(axis)
    return lax.ppermute(block, axis, [(i, i ^ bit) for i in range(count)])


def cost_of(micros):
    return pl.CostEstimate(flops=0, bytes_accessed=int(micros * HBM_BYTES), transcendentals=0)


def local_call(body, name, micros, out_shapes, args, tables=0):
    spaces = [pltpu.SMEM] * tables + [pltpu.VMEM] * (len(args) - tables)
    return pl.pallas_call(
        body,
        name=name,
        out_shape=out_shapes,
        in_specs=[pl.BlockSpec(memory_space=space) for space in spaces],
        out_specs=[pl.BlockSpec(memory_space=pltpu.VMEM)] * len(out_shapes),
        compiler_params=pltpu.CompilerParams(vmem_limit_bytes=16 * 2**20),
        cost_estimate=cost_of(micros),
    )(*args)


def load_kernel(k_ref, hk_ref, v_ref, hv_ref, kv_out, kv_ref, sems):
    inward, outward, begin = [], [], 0
    for i, ref in enumerate((k_ref, hk_ref, v_ref, hv_ref)):
        part = pl.ds(begin, ref.shape[0])
        inward.append(pltpu.make_async_copy(ref, kv_ref.at[part], sems.at[0, i]))
        outward.append(pltpu.make_async_copy(kv_ref.at[part], kv_out.at[part], sems.at[1, i]))
        begin += ref.shape[0]
    for copy in inward:
        copy.start()
    for before, after in zip(inward, outward):
        before.wait()
        after.start()
    for copy in outward:
        copy.wait()


def load_keys(*arrays):
    rows = sum(a.shape[0] for a in arrays)
    width = arrays[0].shape[1]
    return pl.pallas_call(
        load_kernel,
        name="load",
        out_shape=jax.ShapeDtypeStruct((rows, width), BF16),
        in_specs=[pl.BlockSpec(memory_space=pl.ANY)] * len(arrays),
        out_specs=pl.BlockSpec(memory_space=pl.ANY),
        scratch_shapes=[pltpu.VMEM((rows, width), BF16), pltpu.SemaphoreType.DMA((2, len(arrays)))],
        compiler_params=pltpu.CompilerParams(vmem_limit_bytes=60 * 2**20),
        cost_estimate=cost_of(1.6),
    )(*arrays)


def split_heads_kernel(kv_ref, *out_refs):
    for head, ref in enumerate(out_refs):
        ref[...] = head_slice(kv_ref[...], head)


def square_keys(head, near, far):
    keys = near[0].shape[0] // 2
    return [head_slice(ref[:keys], head) for ref in near] + [far[head][:keys]]


def square_values(head, near, far):
    keys = near[0].shape[0] // 2
    return [head_slice(ref[keys:], head) for ref in near] + [far[head][keys:]]


def load_weight_kernel(w_ref, w_out, sems):
    copies = []
    for i in range(sems.shape[0]):
        part = pl.ds(i * HDIM, HDIM)
        copies.append(pltpu.make_async_copy(w_ref.at[part], w_out.at[part], sems.at[i]))
    for copy in copies:
        copy.start()
    for copy in copies:
        copy.wait()


def load_weight(w_out):
    return pl.pallas_call(
        load_weight_kernel,
        name="load_w",
        out_shape=jax.ShapeDtypeStruct(w_out.shape, BF16),
        in_specs=[pl.BlockSpec(memory_space=pl.ANY)],
        out_specs=pl.BlockSpec(memory_space=pltpu.VMEM),
        scratch_shapes=[pltpu.SemaphoreType.DMA((w_out.shape[0] // HDIM,))],
        compiler_params=pltpu.CompilerParams(vmem_limit_bytes=50 * 2**20 + 2**19),
        cost_estimate=cost_of(1.6),
    )(w_out)


def limits_kernel(levels_ref, counts_ref, limits_ref):
    me = lax.axis_index("ctx")
    row = lax.broadcasted_iota(jnp.int32, limits_ref.shape, 0)
    limits = jnp.zeros(limits_ref.shape, jnp.int32)
    for step in range(SQUARE):
        total = jnp.int32(0)
        for frame in range(FMAX):
            tokens = lax.shift_right_logical(jnp.int32(FTOK), 2 * levels_ref[me ^ step, frame])
            total += jnp.where(frame < counts_ref[me ^ step], tokens, 0)
        limits = jnp.where(row == step, total, limits)
    limits_ref[...] = limits


def dattn_kernel(own_ref, core_ref, near_ref, far_ref, w_ref, out_ref):
    me = lax.axis_index("head")
    size = own_ref.shape[1]
    total = None
    for step, ref in enumerate((own_ref, core_ref, near_ref, far_ref)):
        columns = pl.ds(pl.multiple_of((me ^ step) * size, HDIM), size)
        part = contract(ref[...], w_ref[:, columns], 1, 1)
        total = part if total is None else total + part
    out_ref[...] = total.astype(BF16)


def both_rows(own_ref, pair_ref, head):
    return jnp.concatenate(
        [head_slice(own_ref[...], head), head_slice(pair_ref[...], head)], axis=0
    )


def scores_kernel(
    limits_ref, q_own_ref, q_pair_ref, kv0, kv1, kv2, *refs
):
    rows = q_own_ref.shape[0]
    *far, lse_ref, probs_ref = refs
    keys = kv0.shape[0] // 2
    lse_ref[...] = jnp.zeros_like(lse_ref)
    for head in range(q_own_ref.shape[1] // HDIM):
        query = both_rows(q_own_ref, q_pair_ref, head)
        scores = []
        for step, key in enumerate(square_keys(head, (kv0, kv1, kv2), far)):
            block = contract(key, query, 1, 1) * SCALE
            slot = lax.broadcasted_iota(jnp.int32, block.shape, 0)
            valid = slot < rows + limits_ref[step : step + 1]
            scores.append(jnp.where(valid, block, NEG_FILL))
        top = functools.reduce(
            jnp.maximum, [jnp.max(block, axis=0, keepdims=True) for block in scores]
        )
        weights = [jnp.exp(block - top) for block in scores]
        total = sum(jnp.sum(block, axis=0, keepdims=True) for block in weights)
        inverse = 1.0 / total
        for step, block in enumerate(weights):
            begin = (head * SQUARE + step) * keys
            probs_ref[begin : begin + keys] = (block * inverse).astype(BF16)
        lse_ref[head : head + 1] = top + jnp.log(total)


def delta_kernel(lse_ref, probs_ref, d_own_ref, d_pair_ref, kv0, kv1, kv2, *refs):
    *far, stats_ref, dprobs_ref = refs
    keys = kv0.shape[0] // 2
    stats_ref[...] = jnp.zeros_like(stats_ref)
    stats_ref[: lse_ref.shape[0]] = lse_ref[...]
    for head in range(d_own_ref.shape[1] // HDIM):
        dattn = both_rows(d_own_ref, d_pair_ref, head)
        delta = None
        for step, value in enumerate(square_values(head, (kv0, kv1, kv2), far)):
            part = pl.ds((head * SQUARE + step) * keys, keys)
            dprobs = contract(value, dattn, 1, 1)
            dprobs_ref[part] = dprobs
            share = jnp.sum(probs_ref[part].astype(F32) * dprobs, axis=0, keepdims=True)
            delta = share if delta is None else delta + share
        stats_ref[8 + head : 9 + head] = delta


def attn_kernel(probs_ref, kv0, kv1, kv2, *refs):
    *far, own_ref, pair_ref = refs
    rows = own_ref.shape[1]
    keys = kv0.shape[0] // 2
    for head in range(own_ref.shape[0] // HDIM):
        attn = None
        for step, value in enumerate(square_values(head, (kv0, kv1, kv2), far)):
            begin = (head * SQUARE + step) * keys
            part = contract(value, probs_ref[begin : begin + keys], 0, 0)
            attn = part if attn is None else attn + part
        features = slice(head * HDIM, (head + 1) * HDIM)
        own_ref[features] = attn[:, :rows]
        pair_ref[features] = attn[:, rows:].astype(BF16)


def merge_parts(mine, theirs):
    top = jnp.maximum(mine, theirs)
    weight, weight_pair = jnp.exp(mine - top), jnp.exp(theirs - top)
    inverse = 1.0 / (weight + weight_pair)
    return weight * inverse, weight_pair * inverse


def project_kernel(
    own_ref, pair_ref, stats_ref, stats_pair_ref, w_ref,
    keep_ref, next_ref, core_ref, far_left_ref, far_right_ref,
):
    rows = own_ref.shape[1]
    parts = []
    for head in range(own_ref.shape[0] // HDIM):
        features = slice(head * HDIM, (head + 1) * HDIM)
        weight, weight_pair = merge_parts(
            stats_ref[head : head + 1, :rows], stats_pair_ref[head : head + 1, rows:]
        )
        parts.append(own_ref[features] * weight + pair_ref[features].astype(F32) * weight_pair)
    attn = jnp.concatenate(parts, axis=0).astype(BF16)
    me = lax.axis_index("head")
    size = keep_ref.shape[1]
    half = size // 2

    def columns_of(step):
        columns = pl.ds(pl.multiple_of((me ^ step) * size, HDIM), size)
        return contract(attn, w_ref[:, columns], 0, 0)

    far = columns_of(3).astype(BF16)
    far_left_ref[...] = far[:, :half]
    far_right_ref[...] = far[:, half:]
    next_ref[...] = columns_of(2)
    core_ref[...] = columns_of(1).astype(BF16)
    keep_ref[...] = columns_of(0)


def add_near_kernel(next_ref, left_ref, right_ref, out_ref):
    half = left_ref.shape[1]
    out_ref[:, :half] = (next_ref[:, :half] + left_ref[...].astype(F32)).astype(BF16)
    out_ref[:, half:] = (next_ref[:, half:] + right_ref[...].astype(F32)).astype(BF16)


def backward_kernel(
    q_own_ref, q_pair_ref, d_own_ref, d_pair_ref, stats_ref, stats_pair_ref, probs_ref, dprobs_ref,
    kv0, kv1, kv2, *refs,
):
    rows = q_own_ref.shape[0]
    *far, dq_own_ref, dq_pair_ref, dkv_ref, send_y_ref, send_z_ref, near_y_ref, near_z_ref = refs
    keys = kv0.shape[0] // 2
    wide = near_y_ref.shape[0]
    key_parts = (
        dkv_ref.at[:keys], send_y_ref.at[:keys], near_y_ref.at[:keys], send_y_ref.at[wide : wide + keys]
    )
    value_parts = (
        dkv_ref.at[keys : keys + rows], near_z_ref, send_z_ref.at[:rows], send_z_ref.at[rows:]
    )
    hist_parts = (
        dkv_ref.at[keys + rows :], send_y_ref.at[keys:wide], near_y_ref.at[keys:], send_y_ref.at[wide + keys :]
    )

    def swapped(row):
        return jnp.concatenate([row[:, rows:], row[:, :rows]], axis=1)

    for head in range(q_own_ref.shape[1] // HDIM):
        query = both_rows(q_own_ref, q_pair_ref, head)
        dattn = both_rows(d_own_ref, d_pair_ref, head)
        weight, weight_pair = merge_parts(
            stats_ref[head : head + 1], swapped(stats_pair_ref[head : head + 1])
        )
        delta = weight * stats_ref[8 + head : 9 + head]
        delta += weight_pair * swapped(stats_pair_ref[8 + head : 9 + head])
        features = slice(head * HDIM, (head + 1) * HDIM)
        dquery = None
        for step, key in enumerate(square_keys(head, (kv0, kv1, kv2), far)):
            begin = (head * SQUARE + step) * keys
            probs = (probs_ref[begin : begin + keys].astype(F32) * weight).astype(BF16)
            dprobs = dprobs_ref[begin : begin + keys]
            dscores = (probs.astype(F32) * (dprobs - delta)).astype(BF16)
            grad_key = contract(dscores, query, 1, 0) * SCALE
            grad_value = contract(probs, dattn, 1, 0)
            parts = (grad_key, grad_value[:rows], grad_value[rows:])
            for part, targets in zip(parts, (key_parts, value_parts, hist_parts)):
                targets[step][:, features] = part.astype(targets[step].dtype)
            grad_query = contract(dscores, key, 0, 0)
            dquery = grad_query if dquery is None else dquery + grad_query
        dq_own_ref[:, features] = dquery[:rows] * SCALE
        dq_pair_ref[:, features] = (dquery[rows:] * SCALE).astype(BF16)


def pass_values_kernel(near_ref, got_ref, keep_ref, core_ref, value_ref, sum_ref):
    rows = value_ref.shape[0]
    value_ref[...] = (near_ref[...] + got_ref[rows:].astype(F32)).astype(BF16)
    sum_ref[...] = keep_ref[...] + core_ref[...].astype(F32)


def pass_keys_kernel(near_ref, got_ref, key_ref, hist_ref):
    rows = key_ref.shape[0]
    total = near_ref[...] + got_ref[near_ref.shape[0] :].astype(F32)
    key_ref[...] = total[:rows].astype(BF16)
    hist_ref[...] = total[rows:].astype(BF16)


def finish_kernel(
    keep_ref, near_ref, dq_ref, dq_pair_ref,
    dkv_ref, got_y_ref, got_z_ref, rest_k_ref, rest_h_ref, rest_v_ref,
    q_out, k_out, v_out, hk_out, hv_out, out_ref,
):
    rows, capacity = k_out.shape[0], hk_out.shape[0]
    keys = rows + capacity

    def total(first, *others):
        for other in others:
            first = first + other.astype(F32)
        return first.astype(BF16)

    q_out[...] = total(dq_ref[...], dq_pair_ref[...])
    k_out[...] = total(dkv_ref[:rows], got_y_ref[:rows], rest_k_ref[...])
    hk_out[...] = total(dkv_ref[rows:keys], got_y_ref[rows:keys], rest_h_ref[:capacity])
    v_out[...] = total(dkv_ref[keys : keys + rows], got_z_ref[:rows], rest_v_ref[...])
    hv_out[...] = total(
        dkv_ref[keys + rows :], got_y_ref[keys : keys + capacity], rest_h_ref[capacity:]
    )
    out_ref[...] = total(keep_ref[...], near_ref[...])


def blocked(sec_q, sec_k, sec_v, hist_k, hist_v, frame_levels, frame_counts, w_out, grad_out):
    shape = jax.ShapeDtypeStruct
    rows, width = sec_q.shape
    heads = width // HDIM
    capacity = hist_k.shape[0]
    keys = rows + capacity
    share = grad_out.shape[1]

    q_pair = swap(sec_q, "ctx", PAIR)
    grad_near = swap(grad_out, "head", 2)
    grad_core = swap(grad_out, "head", 1)
    weight = load_weight(w_out)
    grad_near, weight = lax.optimization_barrier((grad_near, weight))
    grad_far = swap(grad_near, "head", 1)
    kv0 = load_keys(sec_k, hist_k, sec_v, hist_v)
    kv2 = swap(kv0, "ctx", 2)
    kv1 = swap(kv0, "ctx", 1)
    d_own = local_call(
        dattn_kernel,
        "dattn",
        0.8,
        [shape((rows, width), BF16)],
        (grad_out, grad_core, grad_near, grad_far, weight),
    )[0]
    kv1, kv2, d_own = lax.optimization_barrier((kv1, kv2, d_own))
    pieces = local_call(
        split_heads_kernel, "split_heads", 0.1, [shape((2 * keys, HDIM), BF16)] * heads, (kv2,)
    )
    kvs = (kv0, kv1, kv2, *(swap(piece, "ctx", 1) for piece in pieces))
    d_pair = swap(d_own, "ctx", PAIR)
    limits = local_call(
        limits_kernel,
        "limits",
        0.6,
        [shape((8, 2 * rows), jnp.int32)],
        (frame_levels, frame_counts),
        tables=2,
    )[0]
    lse, probs = local_call(
        scores_kernel,
        "scores",
        0.9,
        [shape((8, 2 * rows), F32), shape((heads * SQUARE * keys, 2 * rows), BF16)],
        (limits, sec_q, q_pair, *kvs),
    )
    attn_own, attn_pair = local_call(
        attn_kernel,
        "attn",
        0.5,
        [shape((width, rows), F32), shape((width, rows), BF16)],
        (probs, *kvs),
    )
    lse, attn_own = lax.optimization_barrier((lse, attn_own))
    stats, dprobs = local_call(
        delta_kernel,
        "delta",
        0.7,
        [shape((16, 2 * rows), F32), shape((heads * SQUARE * keys, 2 * rows), F32)],
        (lse, probs, d_own, d_pair, *kvs),
    )
    stats_pair = swap(stats, "ctx", PAIR)
    wide = keys + capacity
    dq_own, dq_pair, dkv_own, send_y, send_z, near_y, near_z = local_call(
        backward_kernel,
        "backward",
        1.1,
        [shape((rows, width), F32), shape((rows, width), BF16), shape((2 * keys, width), F32)]
        + [shape((2 * wide, width), BF16), shape((2 * rows, width), BF16)]
        + [shape((wide, width), F32), shape((rows, width), F32)],
        (sec_q, q_pair, d_own, d_pair, stats, stats_pair, probs, dprobs, *kvs),
    )
    attn_got = swap(attn_pair, "ctx", PAIR)
    attn_got, send_y, send_z = lax.optimization_barrier((attn_got, send_y, send_z))
    got_y = swap(send_y, "ctx", 1)
    got_z = swap(send_z, "ctx", 2)
    half = share // 2
    out_keep, out_next, out_core, far_left, far_right = local_call(
        project_kernel,
        "project",
        0.6,
        [shape((rows, share), F32)] * 2
        + [shape((rows, share), BF16)]
        + [shape((rows, half), BF16)] * 2,
        (attn_own, attn_got, stats, stats_pair, w_out),
    )
    far_left, far_right = (swap(part, "head", 1) for part in (far_left, far_right))
    out_near = swap(
        local_call(
            add_near_kernel,
            "add_near",
            0.1,
            [shape((rows, share), BF16)],
            (out_next, far_left, far_right),
        )[0],
        "head",
        2,
    )
    dq_got = swap(dq_pair, "ctx", PAIR)
    out_core = swap(out_core, "head", 1)
    rest_v, out_keep = local_call(
        pass_values_kernel,
        "pass_values",
        0.1,
        [shape((rows, width), BF16), shape((rows, share), F32)],
        (near_z, got_z, out_keep, out_core),
    )
    rest_k, rest_h = local_call(
        pass_keys_kernel,
        "pass_keys",
        0.1,
        [shape((rows, width), BF16), shape((2 * capacity, width), BF16)],
        (near_y, got_y),
    )
    rest_k = swap(rest_k, "ctx", 2)
    rest_h = swap(rest_h, "ctx", 2)
    rest_v = swap(rest_v, "ctx", 1)
    grad_q, grad_k, grad_v, grad_hk, grad_hv, out = local_call(
        finish_kernel,
        "finish",
        0.9,
        [shape((rows, width), BF16)] * 3
        + [shape((capacity, width), BF16)] * 2
        + [shape((rows, share), BF16)],
        (
            out_keep, out_near, dq_own, dq_got,
            dkv_own, got_y, got_z, rest_k, rest_h, rest_v,
        ),
    )
    return out, grad_q, grad_k, grad_v, grad_hk, grad_hv


def gathered(sec_q, sec_k, sec_v, hist_k, hist_v, frame_levels, frame_counts, w_out, grad_out):
    rows = sec_q.shape[0]
    capacity = hist_k.shape[0]
    owners = lax.axis_size("ctx")
    me = lax.axis_index("ctx")
    frames = jnp.arange(FMAX, dtype=jnp.int32)[None, :]
    tokens = jnp.where(
        frames < frame_counts[:, None], jnp.right_shift(jnp.int32(FTOK), 2 * frame_levels), 0
    ).sum(axis=1)
    slots = jnp.arange(capacity, dtype=jnp.int32)
    all_valid = jnp.concatenate(
        [jnp.ones((owners * rows,), bool), (slots[None] < tokens[:, None]).reshape(-1)]
    )
    own_valid = jnp.concatenate(
        [jnp.ones((rows,), bool), slots < lax.dynamic_index_in_dim(tokens, me, keepdims=False)]
    )

    def everyone(block, axis=0):
        return lax.all_gather(block, "ctx", axis=axis, tiled=True)

    own_k, own_v = (jnp.concatenate(a, axis=0) for a in ((sec_k, hist_k), (sec_v, hist_v)))
    all_k = jnp.concatenate([everyone(sec_k), everyone(hist_k)], axis=0)
    all_v = jnp.concatenate([everyone(sec_v), everyone(hist_v)], axis=0)
    d_attn = contract(lax.all_gather(grad_out, "head", axis=1, tiled=True), w_out, 1, 1).astype(BF16)
    all_q, all_d = everyone(sec_q), everyone(d_attn)

    def probs_and_dscores(query, key, value, dattn, valid, lse, delta):
        scores = contract(query, key, 1, 1) * SCALE
        probs = jnp.where(valid[None, :], jnp.exp(scores - lse), 0.0).astype(BF16)
        dprobs = contract(dattn, value, 1, 1)
        return probs, (probs.astype(F32) * (dprobs - delta)).astype(BF16)

    attn_parts, q_parts, k_parts, v_parts = [], [], [], []
    for head in range(sec_q.shape[1] // HDIM):
        query, dattn, key, value = (head_slice(a, head) for a in (sec_q, d_attn, all_k, all_v))
        scores = jnp.where(all_valid[None, :], contract(query, key, 1, 1) * SCALE, NEG_FILL)
        lse = jax.nn.logsumexp(scores, axis=1, keepdims=True)
        probs = jnp.where(all_valid[None, :], jnp.exp(scores - lse), 0.0).astype(BF16)
        attn = contract(probs, value, 1, 0).astype(BF16)
        delta = jnp.sum(attn.astype(F32) * dattn.astype(F32), axis=1, keepdims=True)
        _, dscores = probs_and_dscores(query, key, value, dattn, all_valid, lse, delta)
        attn_parts.append(attn)
        q_parts.append(contract(dscores, key, 1, 0))
        query, dattn, key, value = (head_slice(a, head) for a in (all_q, all_d, own_k, own_v))
        probs, dscores = probs_and_dscores(
            query, key, value, dattn, own_valid, everyone(lse), everyone(delta)
        )
        k_parts.append(contract(dscores, query, 0, 0))
        v_parts.append(contract(probs, dattn, 0, 0))
    partial = contract(jnp.concatenate(attn_parts, axis=1), w_out, 1, 0).astype(BF16)
    out = lax.psum_scatter(partial, "head", scatter_dimension=1, tiled=True)
    grad_q, grad_k = (
        (jnp.concatenate(a, axis=1) * SCALE).astype(BF16) for a in (q_parts, k_parts)
    )
    grad_v = jnp.concatenate(v_parts, axis=1).astype(BF16)
    return out, grad_q, grad_k[:rows], grad_v[:rows], grad_k[rows:], grad_v[rows:]


def solution(mesh):
    split = P("ctx", "head")
    plan = blocked if (mesh.shape["ctx"], mesh.shape["head"]) == (2 * SQUARE, 4) else gathered
    return jax.shard_map(
        plan,
        mesh=mesh,
        in_specs=(split,) * 5 + (P(), P(), P("head", None), split),
        out_specs=(split,) * 6,
        check_vma=False,
    )
```

```python
import functools
import math

import jax
import jax.numpy as jnp
from jax import lax
from jax.experimental import pallas as pl
from jax.experimental.pallas import tpu as pltpu
from jax.sharding import PartitionSpec as P

HDIM = 128
FTOK = 16
FMAX = 2
NEG_FILL = -1e30
SCALE = 1.0 / math.sqrt(HDIM)
F32 = jnp.float32
BF16 = jnp.bfloat16
SQUARE = 4
HBM_BYTES = 3.69e6
PAIR = 4


def contract(left, right, left_dim, right_dim):
    return lax.dot_general(
        left, right, (((left_dim,), (right_dim,)), ((), ())), preferred_element_type=F32
    )


def head_slice(stacked, head):
    return stacked[:, head * HDIM : (head + 1) * HDIM]


def swap(block, axis, bit):
    count = lax.axis_size(axis)
    return lax.ppermute(block, axis, [(i, i ^ bit) for i in range(count)])


def cost_of(micros):
    return pl.CostEstimate(flops=0, bytes_accessed=int(micros * HBM_BYTES), transcendentals=0)


def local_call(body, name, micros, out_shapes, args, tables=0):
    spaces = [pltpu.SMEM] * tables + [pltpu.VMEM] * (len(args) - tables)
    return pl.pallas_call(
        body,
        name=name,
        out_shape=out_shapes,
        in_specs=[pl.BlockSpec(memory_space=space) for space in spaces],
        out_specs=[pl.BlockSpec(memory_space=pltpu.VMEM)] * len(out_shapes),
        compiler_params=pltpu.CompilerParams(vmem_limit_bytes=16 * 2**20),
        cost_estimate=cost_of(micros),
    )(*args)


def load_kernel(k_ref, hk_ref, v_ref, hv_ref, kv_out, kv_ref, sems):
    inward, outward, begin = [], [], 0
    for i, ref in enumerate((k_ref, hk_ref, v_ref, hv_ref)):
        part = pl.ds(begin, ref.shape[0])
        inward.append(pltpu.make_async_copy(ref, kv_ref.at[part], sems.at[0, i]))
        outward.append(pltpu.make_async_copy(kv_ref.at[part], kv_out.at[part], sems.at[1, i]))
        begin += ref.shape[0]
    for copy in inward:
        copy.start()
    for before, after in zip(inward, outward):
        before.wait()
        after.start()
    for copy in outward:
        copy.wait()


def load_keys(*arrays):
    rows = sum(a.shape[0] for a in arrays)
    width = arrays[0].shape[1]
    return pl.pallas_call(
        load_kernel,
        name="load",
        out_shape=jax.ShapeDtypeStruct((rows, width), BF16),
        in_specs=[pl.BlockSpec(memory_space=pl.ANY)] * len(arrays),
        out_specs=pl.BlockSpec(memory_space=pl.ANY),
        scratch_shapes=[pltpu.VMEM((rows, width), BF16), pltpu.SemaphoreType.DMA((2, len(arrays)))],
        compiler_params=pltpu.CompilerParams(vmem_limit_bytes=60 * 2**20),
        cost_estimate=cost_of(1.6),
    )(*arrays)


def split_heads_kernel(kv_ref, *out_refs):
    for head, ref in enumerate(out_refs):
        ref[...] = head_slice(kv_ref[...], head)


def square_keys(head, near, far):
    keys = near[0].shape[0] // 2
    return [head_slice(ref[:keys], head) for ref in near] + [far[head][:keys]]


def square_values(head, near, far):
    keys = near[0].shape[0] // 2
    return [head_slice(ref[keys:], head) for ref in near] + [far[head][keys:]]


def load_weight_kernel(w_ref, w_out, sems):
    copies = []
    for i in range(sems.shape[0]):
        part = pl.ds(i * HDIM, HDIM)
        copies.append(pltpu.make_async_copy(w_ref.at[part], w_out.at[part], sems.at[i]))
    for copy in copies:
        copy.start()
    for copy in copies:
        copy.wait()


def load_weight(w_out):
    return pl.pallas_call(
        load_weight_kernel,
        name="load_w",
        out_shape=jax.ShapeDtypeStruct(w_out.shape, BF16),
        in_specs=[pl.BlockSpec(memory_space=pl.ANY)],
        out_specs=pl.BlockSpec(memory_space=pltpu.VMEM),
        scratch_shapes=[pltpu.SemaphoreType.DMA((w_out.shape[0] // HDIM,))],
        compiler_params=pltpu.CompilerParams(vmem_limit_bytes=50 * 2**20 + 2**19),
        cost_estimate=cost_of(1.6),
    )(w_out)


def limits_kernel(levels_ref, counts_ref, limits_ref):
    me = lax.axis_index("ctx")
    row = lax.broadcasted_iota(jnp.int32, limits_ref.shape, 0)
    limits = jnp.zeros(limits_ref.shape, jnp.int32)
    for step in range(SQUARE):
        total = jnp.int32(0)
        for frame in range(FMAX):
            tokens = lax.shift_right_logical(jnp.int32(FTOK), 2 * levels_ref[me ^ step, frame])
            total += jnp.where(frame < counts_ref[me ^ step], tokens, 0)
        limits = jnp.where(row == step, total, limits)
    limits_ref[...] = limits


def dattn_kernel(own_ref, core_ref, near_ref, far_ref, w_ref, out_ref):
    me = lax.axis_index("head")
    size = own_ref.shape[1]
    total = None
    for step, ref in enumerate((own_ref, core_ref, near_ref, far_ref)):
        columns = pl.ds(pl.multiple_of((me ^ step) * size, HDIM), size)
        part = contract(ref[...], w_ref[:, columns], 1, 1)
        total = part if total is None else total + part
    out_ref[...] = total.astype(BF16)


def both_rows(own_ref, pair_ref, head):
    return jnp.concatenate(
        [head_slice(own_ref[...], head), head_slice(pair_ref[...], head)], axis=0
    )


def scores_kernel(
    limits_ref, q_own_ref, q_pair_ref, kv0, kv1, kv2, *refs
):
    rows = q_own_ref.shape[0]
    *far, lse_ref, probs_ref = refs
    keys = kv0.shape[0] // 2
    lse_ref[...] = jnp.zeros_like(lse_ref)
    for head in range(q_own_ref.shape[1] // HDIM):
        query = both_rows(q_own_ref, q_pair_ref, head)
        scores = []
        for step, key in enumerate(square_keys(head, (kv0, kv1, kv2), far)):
            block = contract(key, query, 1, 1) * SCALE
            slot = lax.broadcasted_iota(jnp.int32, block.shape, 0)
            valid = slot < rows + limits_ref[step : step + 1]
            scores.append(jnp.where(valid, block, NEG_FILL))
        top = functools.reduce(
            jnp.maximum, [jnp.max(block, axis=0, keepdims=True) for block in scores]
        )
        weights = [jnp.exp(block - top) for block in scores]
        total = sum(jnp.sum(block, axis=0, keepdims=True) for block in weights)
        inverse = 1.0 / total
        for step, block in enumerate(weights):
            begin = (head * SQUARE + step) * keys
            probs_ref[begin : begin + keys] = (block * inverse).astype(BF16)
        lse_ref[head : head + 1] = top + jnp.log(total)


def delta_kernel(lse_ref, probs_ref, d_own_ref, d_pair_ref, kv0, kv1, kv2, *refs):
    *far, stats_ref, dprobs_ref = refs
    keys = kv0.shape[0] // 2
    stats_ref[...] = jnp.zeros_like(stats_ref)
    stats_ref[: lse_ref.shape[0]] = lse_ref[...]
    for head in range(d_own_ref.shape[1] // HDIM):
        dattn = both_rows(d_own_ref, d_pair_ref, head)
        delta = None
        for step, value in enumerate(square_values(head, (kv0, kv1, kv2), far)):
            part = pl.ds((head * SQUARE + step) * keys, keys)
            dprobs = contract(value, dattn, 1, 1)
            dprobs_ref[part] = dprobs
            share = jnp.sum(probs_ref[part].astype(F32) * dprobs, axis=0, keepdims=True)
            delta = share if delta is None else delta + share
        stats_ref[8 + head : 9 + head] = delta


def attn_kernel(probs_ref, kv0, kv1, kv2, *refs):
    *far, own_ref, pair_ref = refs
    rows = own_ref.shape[1]
    keys = kv0.shape[0] // 2
    for head in range(own_ref.shape[0] // HDIM):
        attn = None
        for step, value in enumerate(square_values(head, (kv0, kv1, kv2), far)):
            begin = (head * SQUARE + step) * keys
            part = contract(value, probs_ref[begin : begin + keys], 0, 0)
            attn = part if attn is None else attn + part
        features = slice(head * HDIM, (head + 1) * HDIM)
        own_ref[features] = attn[:, :rows]
        pair_ref[features] = attn[:, rows:].astype(BF16)


def merge_parts(mine, theirs):
    top = jnp.maximum(mine, theirs)
    weight, weight_pair = jnp.exp(mine - top), jnp.exp(theirs - top)
    inverse = 1.0 / (weight + weight_pair)
    return weight * inverse, weight_pair * inverse


def project_kernel(
    own_ref, pair_ref, stats_ref, stats_pair_ref, w_ref,
    keep_ref, next_ref, core_ref, far_left_ref, far_right_ref,
):
    rows = own_ref.shape[1]
    parts = []
    for head in range(own_ref.shape[0] // HDIM):
        features = slice(head * HDIM, (head + 1) * HDIM)
        weight, weight_pair = merge_parts(
            stats_ref[head : head + 1, :rows], stats_pair_ref[head : head + 1, rows:]
        )
        parts.append(own_ref[features] * weight + pair_ref[features].astype(F32) * weight_pair)
    attn = jnp.concatenate(parts, axis=0).astype(BF16)
    me = lax.axis_index("head")
    size = keep_ref.shape[1]
    half = size // 2

    def columns_of(step):
        columns = pl.ds(pl.multiple_of((me ^ step) * size, HDIM), size)
        return contract(attn, w_ref[:, columns], 0, 0)

    far = columns_of(3).astype(BF16)
    far_left_ref[...] = far[:, :half]
    far_right_ref[...] = far[:, half:]
    next_ref[...] = columns_of(2)
    core_ref[...] = columns_of(1).astype(BF16)
    keep_ref[...] = columns_of(0)


def add_near_kernel(next_ref, left_ref, right_ref, out_ref):
    half = left_ref.shape[1]
    out_ref[:, :half] = (next_ref[:, :half] + left_ref[...].astype(F32)).astype(BF16)
    out_ref[:, half:] = (next_ref[:, half:] + right_ref[...].astype(F32)).astype(BF16)


def backward_kernel(
    q_own_ref, q_pair_ref, d_own_ref, d_pair_ref, stats_ref, stats_pair_ref, probs_ref, dprobs_ref,
    kv0, kv1, kv2, *refs,
):
    rows = q_own_ref.shape[0]
    *far, dq_own_ref, dq_pair_ref, dkv_ref, send_y_ref, send_z_ref, near_y_ref, near_z_ref = refs
    keys = kv0.shape[0] // 2
    wide = near_y_ref.shape[0]
    key_parts = (
        dkv_ref.at[:keys], send_y_ref.at[:keys], near_y_ref.at[:keys], send_y_ref.at[wide : wide + keys]
    )
    value_parts = (
        dkv_ref.at[keys : keys + rows], near_z_ref, send_z_ref.at[:rows], send_z_ref.at[rows:]
    )
    hist_parts = (
        dkv_ref.at[keys + rows :], send_y_ref.at[keys:wide], near_y_ref.at[keys:], send_y_ref.at[wide + keys :]
    )

    def swapped(row):
        return jnp.concatenate([row[:, rows:], row[:, :rows]], axis=1)

    for head in range(q_own_ref.shape[1] // HDIM):
        query = both_rows(q_own_ref, q_pair_ref, head)
        dattn = both_rows(d_own_ref, d_pair_ref, head)
        weight, weight_pair = merge_parts(
            stats_ref[head : head + 1], swapped(stats_pair_ref[head : head + 1])
        )
        delta = weight * stats_ref[8 + head : 9 + head]
        delta += weight_pair * swapped(stats_pair_ref[8 + head : 9 + head])
        features = slice(head * HDIM, (head + 1) * HDIM)
        dquery = None
        for step, key in enumerate(square_keys(head, (kv0, kv1, kv2), far)):
            begin = (head * SQUARE + step) * keys
            probs = (probs_ref[begin : begin + keys].astype(F32) * weight).astype(BF16)
            dprobs = dprobs_ref[begin : begin + keys]
            dscores = (probs.astype(F32) * (dprobs - delta)).astype(BF16)
            grad_key = contract(dscores, query, 1, 0) * SCALE
            grad_value = contract(probs, dattn, 1, 0)
            parts = (grad_key, grad_value[:rows], grad_value[rows:])
            for part, targets in zip(parts, (key_parts, value_parts, hist_parts)):
                targets[step][:, features] = part.astype(targets[step].dtype)
            grad_query = contract(dscores, key, 0, 0)
            dquery = grad_query if dquery is None else dquery + grad_query
        dq_own_ref[:, features] = dquery[:rows] * SCALE
        dq_pair_ref[:, features] = (dquery[rows:] * SCALE).astype(BF16)


def pass_on_kernel(
    near_y_ref, near_z_ref, got_y_ref, got_z_ref, keep_ref, core_ref,
    key_ref, hist_ref, value_ref, sum_ref,
):
    rows = key_ref.shape[0]
    wide = near_y_ref.shape[0]
    total_y = near_y_ref[...] + got_y_ref[wide:].astype(F32)
    key_ref[...] = total_y[:rows].astype(BF16)
    hist_ref[...] = total_y[rows:].astype(BF16)
    value_ref[...] = (near_z_ref[...] + got_z_ref[rows:].astype(F32)).astype(BF16)
    sum_ref[...] = keep_ref[...] + core_ref[...].astype(F32)


def finish_kernel(
    keep_ref, near_ref, dq_ref, dq_pair_ref,
    dkv_ref, got_y_ref, got_z_ref, rest_k_ref, rest_h_ref, rest_v_ref,
    q_out, k_out, v_out, hk_out, hv_out, out_ref,
):
    rows, capacity = k_out.shape[0], hk_out.shape[0]
    keys = rows + capacity

    def total(first, *others):
        for other in others:
            first = first + other.astype(F32)
        return first.astype(BF16)

    q_out[...] = total(dq_ref[...], dq_pair_ref[...])
    k_out[...] = total(dkv_ref[:rows], got_y_ref[:rows], rest_k_ref[...])
    hk_out[...] = total(dkv_ref[rows:keys], got_y_ref[rows:keys], rest_h_ref[:capacity])
    v_out[...] = total(dkv_ref[keys : keys + rows], got_z_ref[:rows], rest_v_ref[...])
    hv_out[...] = total(
        dkv_ref[keys + rows :], got_y_ref[keys : keys + capacity], rest_h_ref[capacity:]
    )
    out_ref[...] = total(keep_ref[...], near_ref[...])


def blocked(sec_q, sec_k, sec_v, hist_k, hist_v, frame_levels, frame_counts, w_out, grad_out):
    shape = jax.ShapeDtypeStruct
    rows, width = sec_q.shape
    heads = width // HDIM
    capacity = hist_k.shape[0]
    keys = rows + capacity
    share = grad_out.shape[1]

    q_pair = swap(sec_q, "ctx", PAIR)
    grad_near = swap(grad_out, "head", 2)
    grad_core = swap(grad_out, "head", 1)
    weight = load_weight(w_out)
    grad_near, weight = lax.optimization_barrier((grad_near, weight))
    grad_far = swap(grad_near, "head", 1)
    kv0 = load_keys(sec_k, hist_k, sec_v, hist_v)
    kv2 = swap(kv0, "ctx", 2)
    kv1 = swap(kv0, "ctx", 1)
    d_own = local_call(
        dattn_kernel,
        "dattn",
        0.8,
        [shape((rows, width), BF16)],
        (grad_out, grad_core, grad_near, grad_far, weight),
    )[0]
    limits = local_call(
        limits_kernel,
        "limits",
        0.6,
        [shape((8, 2 * rows), jnp.int32)],
        (frame_levels, frame_counts),
        tables=2,
    )[0]
    kv1, kv2, d_own, limits = lax.optimization_barrier((kv1, kv2, d_own, limits))
    pieces = local_call(
        split_heads_kernel, "split_heads", 0.1, [shape((2 * keys, HDIM), BF16)] * heads, (kv2,)
    )
    kvs = (kv0, kv1, kv2, *(swap(piece, "ctx", 1) for piece in pieces))
    d_pair = swap(d_own, "ctx", PAIR)
    lse, probs = local_call(
        scores_kernel,
        "scores",
        0.9,
        [shape((8, 2 * rows), F32), shape((heads * SQUARE * keys, 2 * rows), BF16)],
        (limits, sec_q, q_pair, *kvs),
    )
    attn_own, attn_pair = local_call(
        attn_kernel,
        "attn",
        0.5,
        [shape((width, rows), F32), shape((width, rows), BF16)],
        (probs, *kvs),
    )
    lse, attn_own = lax.optimization_barrier((lse, attn_own))
    stats, dprobs = local_call(
        delta_kernel,
        "delta",
        0.7,
        [shape((16, 2 * rows), F32), shape((heads * SQUARE * keys, 2 * rows), F32)],
        (lse, probs, d_own, d_pair, *kvs),
    )
    stats_pair = swap(stats, "ctx", PAIR)
    wide = keys + capacity
    dq_own, dq_pair, dkv_own, send_y, send_z, near_y, near_z = local_call(
        backward_kernel,
        "backward",
        1.1,
        [shape((rows, width), F32), shape((rows, width), BF16), shape((2 * keys, width), F32)]
        + [shape((2 * wide, width), BF16), shape((2 * rows, width), BF16)]
        + [shape((wide, width), F32), shape((rows, width), F32)],
        (sec_q, q_pair, d_own, d_pair, stats, stats_pair, probs, dprobs, *kvs),
    )
    attn_got = swap(attn_pair, "ctx", PAIR)
    attn_got, send_y, send_z = lax.optimization_barrier((attn_got, send_y, send_z))
    got_y = swap(send_y, "ctx", 1)
    got_z = swap(send_z, "ctx", 2)
    half = share // 2
    out_keep, out_next, out_core, far_left, far_right = local_call(
        project_kernel,
        "project",
        0.6,
        [shape((rows, share), F32)] * 2
        + [shape((rows, share), BF16)]
        + [shape((rows, half), BF16)] * 2,
        (attn_own, attn_got, stats, stats_pair, w_out),
    )
    far_left, far_right = (swap(part, "head", 1) for part in (far_left, far_right))
    out_near = swap(
        local_call(
            add_near_kernel,
            "add_near",
            0.1,
            [shape((rows, share), BF16)],
            (out_next, far_left, far_right),
        )[0],
        "head",
        2,
    )
    dq_got = swap(dq_pair, "ctx", PAIR)
    out_core = swap(out_core, "head", 1)
    rest_k, rest_h, rest_v, out_keep = local_call(
        pass_on_kernel,
        "pass_on",
        0.1,
        [shape((size, width), BF16) for size in (rows, 2 * capacity, rows)]
        + [shape((rows, share), F32)],
        (near_y, near_z, got_y, got_z, out_keep, out_core),
    )
    rest_k = swap(rest_k, "ctx", 2)
    rest_h = swap(rest_h, "ctx", 2)
    rest_v = swap(rest_v, "ctx", 1)
    grad_q, grad_k, grad_v, grad_hk, grad_hv, out = local_call(
        finish_kernel,
        "finish",
        0.9,
        [shape((rows, width), BF16)] * 3
        + [shape((capacity, width), BF16)] * 2
        + [shape((rows, share), BF16)],
        (
            out_keep, out_near, dq_own, dq_got,
            dkv_own, got_y, got_z, rest_k, rest_h, rest_v,
        ),
    )
    return out, grad_q, grad_k, grad_v, grad_hk, grad_hv


def gathered(sec_q, sec_k, sec_v, hist_k, hist_v, frame_levels, frame_counts, w_out, grad_out):
    rows = sec_q.shape[0]
    capacity = hist_k.shape[0]
    owners = lax.axis_size("ctx")
    me = lax.axis_index("ctx")
    frames = jnp.arange(FMAX, dtype=jnp.int32)[None, :]
    tokens = jnp.where(
        frames < frame_counts[:, None], jnp.right_shift(jnp.int32(FTOK), 2 * frame_levels), 0
    ).sum(axis=1)
    slots = jnp.arange(capacity, dtype=jnp.int32)
    all_valid = jnp.concatenate(
        [jnp.ones((owners * rows,), bool), (slots[None] < tokens[:, None]).reshape(-1)]
    )
    own_valid = jnp.concatenate(
        [jnp.ones((rows,), bool), slots < lax.dynamic_index_in_dim(tokens, me, keepdims=False)]
    )

    def everyone(block, axis=0):
        return lax.all_gather(block, "ctx", axis=axis, tiled=True)

    own_k, own_v = (jnp.concatenate(a, axis=0) for a in ((sec_k, hist_k), (sec_v, hist_v)))
    all_k = jnp.concatenate([everyone(sec_k), everyone(hist_k)], axis=0)
    all_v = jnp.concatenate([everyone(sec_v), everyone(hist_v)], axis=0)
    d_attn = contract(lax.all_gather(grad_out, "head", axis=1, tiled=True), w_out, 1, 1).astype(BF16)
    all_q, all_d = everyone(sec_q), everyone(d_attn)

    def probs_and_dscores(query, key, value, dattn, valid, lse, delta):
        scores = contract(query, key, 1, 1) * SCALE
        probs = jnp.where(valid[None, :], jnp.exp(scores - lse), 0.0).astype(BF16)
        dprobs = contract(dattn, value, 1, 1)
        return probs, (probs.astype(F32) * (dprobs - delta)).astype(BF16)

    attn_parts, q_parts, k_parts, v_parts = [], [], [], []
    for head in range(sec_q.shape[1] // HDIM):
        query, dattn, key, value = (head_slice(a, head) for a in (sec_q, d_attn, all_k, all_v))
        scores = jnp.where(all_valid[None, :], contract(query, key, 1, 1) * SCALE, NEG_FILL)
        lse = jax.nn.logsumexp(scores, axis=1, keepdims=True)
        probs = jnp.where(all_valid[None, :], jnp.exp(scores - lse), 0.0).astype(BF16)
        attn = contract(probs, value, 1, 0).astype(BF16)
        delta = jnp.sum(attn.astype(F32) * dattn.astype(F32), axis=1, keepdims=True)
        _, dscores = probs_and_dscores(query, key, value, dattn, all_valid, lse, delta)
        attn_parts.append(attn)
        q_parts.append(contract(dscores, key, 1, 0))
        query, dattn, key, value = (head_slice(a, head) for a in (all_q, all_d, own_k, own_v))
        probs, dscores = probs_and_dscores(
            query, key, value, dattn, own_valid, everyone(lse), everyone(delta)
        )
        k_parts.append(contract(dscores, query, 0, 0))
        v_parts.append(contract(probs, dattn, 0, 0))
    partial = contract(jnp.concatenate(attn_parts, axis=1), w_out, 1, 0).astype(BF16)
    out = lax.psum_scatter(partial, "head", scatter_dimension=1, tiled=True)
    grad_q, grad_k = (
        (jnp.concatenate(a, axis=1) * SCALE).astype(BF16) for a in (q_parts, k_parts)
    )
    grad_v = jnp.concatenate(v_parts, axis=1).astype(BF16)
    return out, grad_q, grad_k[:rows], grad_v[:rows], grad_k[rows:], grad_v[rows:]


def solution(mesh):
    split = P("ctx", "head")
    plan = blocked if (mesh.shape["ctx"], mesh.shape["head"]) == (2 * SQUARE, 4) else gathered
    return jax.shard_map(
        plan,
        mesh=mesh,
        in_specs=(split,) * 5 + (P(), P(), P("head", None), split),
        out_specs=(split,) * 6,
        check_vma=False,
    )
```
